32 devices in a mesh: dp: 8 (over y, x, core), stream: 4 (over z).
Axes of the slice: x: 2, y: 2, z: 4, core: 2. Of those that a mesh axis runs over, the one named last changes fastest.
Arguments:
- tokens: bfloat16 [2, 8, 4, 591, 768], P(None, 'dp', 'stream'), may hold values from -6 to 6
- text_lengths: int32 [2, 8, 24], P(None, 'dp'), may hold values from 1 to 40, 591 in all within a row
- pair_text: int32 [2, 8, 9], P(None, 'dp'), may hold values from -1 to 23, as said below
- ln1_gain: bfloat16 [768], replicated, may hold values from 0.099609375 to 1.8984375
- ln1_bias: bfloat16 [768], replicated, may hold values from -1.75 to 1.75
- w_qkv: bfloat16 [768, 2304], replicated, may hold values from -0.3125 to 0.3125
- q_bias: bfloat16 [768], replicated, may hold values from -1.75 to 1.75
- v_bias: bfloat16 [768], replicated, may hold values from -0.625 to 0.625
- w_out: bfloat16 [768, 768], replicated, may hold values from -1.25 to 1.25
- ln2_gain: bfloat16 [768], replicated, may hold values from 0.099609375 to 1.8984375
- ln2_bias: bfloat16 [768], replicated, may hold values from -1.75 to 1.75
- vis_up: bfloat16 [768, 3072], replicated, may hold values from -0.21875 to 0.21875
- vis_down: bfloat16 [3072, 768], replicated, may hold values from -0.21875 to 0.21875
- vis_bias: bfloat16 [768], replicated, may hold values from -1.75 to 1.75
- txt_up: bfloat16 [768, 3072], replicated, may hold values from -0.21875 to 0.21875
- txt_down: bfloat16 [3072, 768], replicated, may hold values from -0.21875 to 0.21875
- txt_bias: bfloat16 [768], replicated, may hold values from -1.75 to 1.75
- cotangent: bfloat16 [2, 8, 4, 591, 768], P(None, 'dp', 'stream'), may hold values from -6 to 6
Outputs:
- output: bfloat16 [2, 8, 4, 591, 768], P(None, 'dp', 'stream')
- tokens_grad: bfloat16 [2, 8, 4, 591, 768], P(None, 'dp', 'stream')
- ln1_gain_grad: float32 [768], P('dp')
- ln1_bias_grad: float32 [768], P('dp')
- w_qkv_grad: float32 [768, 2304], P('dp', 'stream')
- q_bias_grad: float32 [768], P('dp')
- v_bias_grad: float32 [768], P('dp')
- w_out_grad: float32 [768, 768], P('dp', 'stream')
- ln2_gain_grad: float32 [768], P('dp')
- ln2_bias_grad: float32 [768], P('dp')
- vis_up_grad: float32 [768, 3072], P('dp', 'stream')
- vis_down_grad: float32 [3072, 768], P('dp', 'stream')
- vis_bias_grad: float32 [768], P('dp')
- txt_up_grad: float32 [768, 3072], P('dp', 'stream')
- txt_down_grad: float32 [3072, 768], P('dp', 'stream')
- txt_bias_grad: float32 [768], P('dp')
The draws below stay inside these ranges and needn't reach their ends.
Inputs may be any that keep to these rules, and one draw needn't show every extreme that they name: `text_lengths`: the text lengths of a group sum to 591. `pair_text`: no text item is named twice in a group; in each image block exactly 2 of its 3 images are paired, the others hold -1.
All inputs are finite; a program needn't handle non-finite values.
Results may differ from the reference program's by a relative error of at most 0.015.
Values may be sent and summed in bfloat16 or wider, within the bound.
A program may use at most 576 MiB of HBM per device.

```python
import math
import jax
import jax.numpy as jnp
import numpy as np
from jax import lax

D = 768
HEADS = 12
HEAD = 64
FF = 3072
PATCHES = 197
IMGS = 3
TXT_MOST = 40
MICRO = 2
ROWS = 591
TXT_ITEMS = 24
IMAGES = 9
PAIRED = 2
GROUPS = 8
STREAMS = 4


def draw_pair_text(key, part):
    key = jax.random.fold_in(key, 7)
    pick_key, text_key = jax.random.split(key)
    leading = (MICRO, GROUPS)
    image_scores = jax.random.randint(pick_key, leading + (3, IMGS), 0, 1 << 20) * IMGS + jnp.arange(IMGS, dtype=jnp.int32)
    ranks = jnp.argsort(jnp.argsort(image_scores, axis=-1), axis=-1)
    paired = (ranks < PAIRED).reshape(leading + (IMAGES,))
    slot = jnp.cumsum(paired.astype(jnp.int32), axis=-1) - 1
    text_scores = jax.random.randint(text_key, leading + (TXT_ITEMS,), 0, 1 << 20) * TXT_ITEMS + jnp.arange(TXT_ITEMS, dtype=jnp.int32)
    order = jnp.argsort(text_scores, axis=-1).astype(jnp.int32)
    chosen = jnp.take_along_axis(order, jnp.clip(slot, 0, TXT_ITEMS - 1), axis=-1)
    return jnp.where(paired, chosen, -1).astype(jnp.int32)


def shard_levels(rng, dims, pieces, low, top_value):
    def one(position, shards_of):
        heights = jax.random.uniform(jax.random.fold_in(jax.random.fold_in(rng, 6), position), (shards_of,), jnp.float32, low / len(pieces), top_value / len(pieces))
        return jnp.repeat(jnp.exp(heights), dims[position] // shards_of).reshape((-1,) + (1,) * (len(dims) - position - 1))

    gain = one(*pieces[0])
    for cut in pieces[1:]:
        gain = gain * one(*cut)
    return gain


def profile(amount, total, most, skew):
    weights = [(1 << 20) // math.isqrt(standing ** skew) + 1 for standing in range(2, amount + 1)]
    surplus, holding = total - most - (amount - 1), [1] * (amount - 1)
    while surplus > 0:
        movable = [i for i in range(amount - 1) if holding[i] < most]
        whole, budget = sum([weights[i] for i in movable]), surplus
        for i in movable:
            addition = min(most - holding[i], max(1, budget * weights[i] // whole), surplus)
            holding[i] = holding[i] + addition
            surplus = surplus - addition
    return np.array([most] + holding)


def ragged_sizes(own_key, number_of, total, bound, lean):
    if number_of == 2:
        one = jax.random.randint(own_key, (), max(1, total - bound), min(bound, total - 1) + 1)
        return jnp.stack([one, total - one])
    sizes = jnp.asarray(profile(number_of, total, bound, lean), jnp.int32)
    pairs = (number_of - 1) // 2
    giver, taker = sizes[1:1 + 2 * pairs:2], sizes[2:2 + 2 * pairs:2]
    margin = jnp.minimum(giver - 1, bound - taker)
    shifted = jax.random.randint(jax.random.fold_in(own_key, 1), (pairs,), 0, 1 << 20) % (margin + 1)
    sizes = sizes.at[1:1 + 2 * pairs:2].set(giver - shifted).at[2:2 + 2 * pairs:2].set(taker + shifted)
    return sizes[jax.random.permutation(jax.random.fold_in(own_key, 2), number_of)]


def normal_values(stream_key, shape, scale, most, shards=(), held_as=jnp.bfloat16):
    array = jax.random.normal(stream_key, shape, jnp.float32) * scale
    if len(shards) > 0:
        array = shard_levels(stream_key, shape, shards, -0.22, 0.18) * array
    return jnp.clip(array, min=-most, max=most).astype(held_as)


def setup_inputs(seed: int = 0) -> dict:
    keys = jax.random.split(jax.random.key(seed), 19)
    tokens = normal_values(keys[0], (MICRO, GROUPS, STREAMS, ROWS, D), 1.0, 6.0, ((1, 8), (2, 4)))
    text_lengths = jax.vmap(lambda own: ragged_sizes(own, TXT_ITEMS, ROWS, TXT_MOST, 1))(jax.random.split(keys[1], MICRO * GROUPS)).reshape((MICRO, GROUPS, TXT_ITEMS)).astype(jnp.int32)
    pair_text = draw_pair_text(jax.random.fold_in(keys[18], 71), 0)
    ln1_gain = jnp.clip(1.0 + 0.18 * jax.random.normal(keys[3], (D,), jnp.float32), 0.099609375, 1.8984375).astype(jnp.bfloat16)
    ln1_bias = normal_values(keys[4], (D,), 0.3, 1.75)
    w_qkv = normal_values(keys[5], (D, 3 * D), (D // 2) ** -0.5, 0.3125)
    q_bias = normal_values(keys[6], (D,), 0.3, 1.75)
    v_bias = normal_values(keys[7], (D,), 0.1, 0.625)
    w_out = normal_values(keys[8], (D, D), (D // 32) ** -0.5, 1.25)
    ln2_gain = jnp.clip(1.0 + 0.18 * jax.random.normal(keys[9], (D,), jnp.float32), 0.099609375, 1.8984375).astype(jnp.bfloat16)
    ln2_bias = normal_values(keys[10], (D,), 0.3, 1.75)
    vis_up = normal_values(keys[11], (D, FF), D ** -0.5, 0.21875)
    vis_down = normal_values(keys[12], (FF, D), (FF // 4) ** -0.5, 0.21875)
    vis_bias = normal_values(keys[13], (D,), 0.3, 1.75)
    txt_up = normal_values(keys[14], (D, FF), D ** -0.5, 0.21875)
    txt_down = normal_values(keys[15], (FF, D), (FF // 4) ** -0.5, 0.21875)
    txt_bias = normal_values(keys[16], (D,), 0.3, 1.75)
    cotangent = normal_values(keys[17], (MICRO, GROUPS, STREAMS, ROWS, D), 1.0, 6.0, ((1, 8), (2, 4)))
    return dict(tokens=tokens, text_lengths=text_lengths, pair_text=pair_text, ln1_gain=ln1_gain, ln1_bias=ln1_bias, w_qkv=w_qkv, q_bias=q_bias, v_bias=v_bias, w_out=w_out, ln2_gain=ln2_gain, ln2_bias=ln2_bias, vis_up=vis_up, vis_down=vis_down, vis_bias=vis_bias, txt_up=txt_up, txt_down=txt_down, txt_bias=txt_bias, cotangent=cotangent)


EPSILON = 1e-06
MASKED = -1e+30

@jax.custom_vjp
def low(v):
    return lax.optimization_barrier(v.astype(jnp.bfloat16)).astype(jnp.float32)

@jax.custom_vjp
def low_back(v):
    return v

def low_keep(v):
    return (low(v), None)

def low_pass(kept, grad):
    return (grad,)

def back_keep(v):
    return (v, None)

def back_low(kept, grad):
    return (low(grad),)
low.defvjp(low_keep, low_pass)
low_back.defvjp(back_keep, back_low)

def layer_norm(values, norm_gain, norm_bias):
    centred = values - lax.optimization_barrier(jnp.mean(values, axis=-1, keepdims=True))
    inverse = lax.rsqrt(lax.optimization_barrier(jnp.mean(centred * centred, axis=-1, keepdims=True)) + EPSILON)
    return centred * inverse * norm_gain + norm_bias

def sequence_ids(lengths, pairs, row_count, patches):
    item_count = lengths.shape[0]
    image_count = pairs.shape[0]
    image_ids = jnp.arange(3 * row_count, dtype=jnp.int32) // patches
    finish = jnp.cumsum(lengths).astype(jnp.int32)
    starts = finish - lengths
    places = jnp.arange(row_count, dtype=jnp.int32)[:, None]
    member = (places >= starts[None, :]) & (places < finish[None, :])
    numbers = jnp.arange(item_count, dtype=jnp.int32)
    paired_with = pairs[:, None] == numbers[None, :]
    partner = lax.optimization_barrier(jnp.sum(jnp.where(paired_with, jnp.arange(image_count, dtype=jnp.int32)[:, None], 0), axis=0))
    text_seq = jnp.where(jnp.any(paired_with, axis=0), partner, image_count + numbers).astype(jnp.int32)
    text_ids = lax.optimization_barrier(jnp.sum(jnp.where(member, text_seq[None, :], 0), axis=1)).astype(jnp.int32)
    return jnp.concatenate([image_ids, text_ids])

def group_forward(params, block, lengths, pairs):
    gain1, shift1, w_qkv, q_bias, v_bias, w_out, gain2, shift2, vis_up, vis_down, vis_bias, txt_up, txt_down, txt_bias = params
    highest = lax.Precision.HIGHEST
    row_count = block.shape[1]
    flat = block.reshape(4 * row_count, D)
    seq_ids = sequence_ids(lengths, pairs, row_count, PATCHES)
    allowed = seq_ids[:, None] == seq_ids[None, :]
    hidden1 = low(layer_norm(flat, gain1, shift1))
    qkv_shift = jnp.concatenate([q_bias, jnp.zeros_like(q_bias), v_bias])
    qkv = low_back(low(jnp.dot(hidden1, w_qkv, precision=highest) + qkv_shift))
    queries = qkv[:, :D].reshape(-1, HEADS, HEAD)
    key_heads = qkv[:, D:2 * D].reshape(-1, HEADS, HEAD)
    value_heads = qkv[:, 2 * D:].reshape(-1, HEADS, HEAD)
    raw = jnp.einsum('qhe,khe->hqk', queries, key_heads, precision=highest) * HEAD ** (-0.5)
    scores = low_back(jnp.where(allowed[None], raw, MASKED))
    probs = jax.nn.softmax(scores, axis=-1)
    attended = low_back(jnp.einsum('hqk,khe->qhe', low(probs), value_heads, precision=highest).reshape(-1, D))
    middle = flat + low_back(jnp.dot(low(attended), w_out, precision=highest))
    hidden2 = low(layer_norm(middle, gain2, shift2))
    image_rows = 3 * row_count

    def expert(rows_in, up_w, down_w, bias_w):
        up_val = low_back(jnp.dot(rows_in, up_w, precision=highest))
        activ = low(jax.nn.gelu(up_val, approximate=False))
        return jnp.dot(activ, down_w, precision=highest) + bias_w
    added = jnp.concatenate([expert(hidden2[:image_rows], vis_up, vis_down, vis_bias), expert(hidden2[image_rows:], txt_up, txt_down, txt_bias)])
    return (middle + added).reshape(4, row_count, D)

def reference(tokens, text_lengths, pair_text, ln1_gain, ln1_bias, w_qkv, q_bias, v_bias, w_out, ln2_gain, ln2_bias, vis_up, vis_down, vis_bias, txt_up, txt_down, txt_bias, cotangent):
    params = tuple((weight.astype(jnp.float32) for weight in (ln1_gain, ln1_bias, w_qkv, q_bias, v_bias, w_out, ln2_gain, ln2_bias, vis_up, vis_down, vis_bias, txt_up, txt_down, txt_bias)))
    full_shape = tokens.shape
    lengths_flat = text_lengths.reshape(-1, text_lengths.shape[-1])
    pairs_flat = pair_text.reshape(-1, pair_text.shape[-1])

    def forward(values, *weights):
        blocks = values.reshape((full_shape[0] * full_shape[1],) + full_shape[2:])

        def step(carry, inputs):
            block, group_lengths, group_pairs = inputs
            return (carry, group_forward(weights, block, group_lengths, group_pairs))
        carry, result = lax.scan(jax.checkpoint(step), jnp.float32(0.0), (blocks, lengths_flat, pairs_flat))
        return result.reshape(full_shape)
    result, pullback = jax.vjp(forward, tokens.astype(jnp.float32), *params)
    grads = pullback(cotangent.astype(jnp.float32))
    return (result.astype(jnp.bfloat16), grads[0].astype(jnp.bfloat16), grads[1], grads[2], grads[3], grads[4], grads[5], grads[6], grads[7], grads[8], grads[9], grads[10], grads[11], grads[12], grads[13], grads[14])
```

```python
import functools

import jax
import jax.numpy as jnp
from jax import lax
from jax.experimental import pallas as pl
from jax.experimental.pallas import tpu as pltpu
from jax.sharding import PartitionSpec as P

HEADS = 12
PATCHES = 197
OWN = 208
SLOT = 40
TILE = 256
TILES = 3
EPSILON = 1e-06
MASKED = -1e30
BF = jnp.bfloat16
F32 = jnp.float32
FULL = pl.BlockSpec(memory_space=pltpu.VMEM)
HBM = pl.BlockSpec(memory_space=pl.ANY)


def dot(left, right):
    return jnp.dot(left, right, preferred_element_type=F32)


def dot_t(left, right):
    return lax.dot_general(left, right, (((1,), (1,)), ((), ())), preferred_element_type=F32)


def t_dot(left, right):
    return lax.dot_general(left, right, (((0,), (0,)), ((), ())), preferred_element_type=F32)


def normalize(values):
    centred = values - jnp.mean(values, axis=-1, keepdims=True)
    inverse = lax.rsqrt(jnp.mean(centred * centred, axis=-1, keepdims=True) + EPSILON)
    return centred * inverse, inverse


def norm_back(grad, normed, inverse, gain):
    scaled = grad * gain
    return inverse * (
        scaled
        - jnp.mean(scaled, axis=-1, keepdims=True)
        - normed * jnp.mean(scaled * normed, axis=-1, keepdims=True)
    )


def gelu_parts(up):
    reach = jnp.abs(up) * 0.7071067811865476
    inner = 1.0 / (1.0 + 0.3275911 * reach)
    bell = jnp.exp(-0.5 * up * up)
    poly = inner * (
        0.254829592
        + inner
        * (-0.284496736 + inner * (1.421413741 + inner * (-1.453152027 + inner * 1.061405429)))
    )
    tail = 0.5 * poly * bell
    return jnp.where(up >= 0, 1.0 - tail, tail), bell * 0.3989422804014327


def attend_kernel(x_ref, ids_ref, gain_ref, shift_ref, w_ref, bias_ref, qkv_ref, out_ref, p_ref):
    width = x_ref.shape[2]
    normed, _ = normalize(x_ref[0].astype(F32))
    hidden = (normed * gain_ref[...] + shift_ref[...]).astype(BF)
    qkv = (dot(hidden, w_ref[...]) + bias_ref[...]).astype(BF)
    qkv_ref[0] = qkv
    row_ids = jnp.broadcast_to(ids_ref[0], (TILE, TILE))
    barred = jnp.where((row_ids == row_ids.T) & (row_ids >= 0), 0.0, MASKED)
    lane = lax.broadcasted_iota(jnp.int32, (1, 128), 1)
    low = (lane < 64).astype(BF)
    high = (lane >= 64).astype(BF)
    for pair in range(HEADS // 2):
        at = pair * 128
        q = qkv[:, at : at + 128] * 0.125
        k = qkv[:, width + at : width + at + 128]
        v = qkv[:, 2 * width + at : 2 * width + at + 128]
        out = None
        for side, keep in enumerate((low, high)):
            scores = dot_t(q, k * keep) + barred
            top = jnp.max(scores, axis=-1, keepdims=True)
            expo = jnp.exp(scores - top)
            total = jnp.sum(expo, axis=-1, keepdims=True)
            scale = jnp.where(top > 0.5 * MASKED, 1.0 / total, 0.0)
            probs = (expo * scale).astype(BF)
            p_ref[0, 2 * pair + side] = probs
            part = dot(probs, v * keep)
            out = part if out is None else out + part
        out_ref[0, :, at : at + 128] = out.astype(BF)


def attend(x_tiles, ids, gain, shift, w_qkv, bias):
    tiles, _, width = x_tiles.shape

    def block(*shape):
        return pl.BlockSpec((1,) + shape, lambda i: (i,) + (0,) * len(shape))

    return pl.pallas_call(
        attend_kernel,
        grid=(tiles,),
        in_specs=[block(TILE, width), block(1, TILE), FULL, FULL, FULL, FULL],
        out_specs=[block(TILE, 3 * width), block(TILE, width), block(HEADS, TILE, TILE)],
        out_shape=[
            jax.ShapeDtypeStruct((tiles, TILE, 3 * width), BF),
            jax.ShapeDtypeStruct((tiles, TILE, width), BF),
            jax.ShapeDtypeStruct((tiles, HEADS, TILE, TILE), BF),
        ],
        compiler_params=pltpu.CompilerParams(vmem_limit_bytes=56 * 2**20),
        name="attend",
    )(x_tiles, ids, gain, shift, w_qkv, bias)


def attend_back_kernel(qkv_ref, p_ref, out_ref, grad_ref, dqkv_ref):
    width = out_ref.shape[2]
    lane = lax.broadcasted_iota(jnp.int32, (1, 128), 1)
    low = lane < 64
    for pair in range(HEADS // 2):
        at = pair * 128
        q = qkv_ref[0, :, at : at + 128] * 0.125
        k = qkv_ref[0, :, width + at : width + at + 128]
        v = qkv_ref[0, :, 2 * width + at : 2 * width + at + 128].astype(F32)
        grad = grad_ref[0, :, at : at + 128]
        wide = grad.astype(F32)
        inner = pltpu.roll(wide * out_ref[0, :, at : at + 128].astype(F32), 64, 1)
        dq = dk = dv = None
        for side in range(2):
            mine = low if side == 0 else jnp.logical_not(low)
            keep = mine.astype(BF)
            left = jnp.where(mine, wide, inner).astype(BF)
            right = jnp.where(mine, v, -1.0).astype(BF)
            probs = p_ref[0, 2 * pair + side]
            dscore = (probs.astype(F32) * dot_t(left, right)).astype(BF)
            parts = dot(dscore, k * keep), t_dot(dscore, q * keep), t_dot(probs, grad * keep)
            if dq is None:
                dq, dk, dv = parts
            else:
                dq, dk, dv = dq + parts[0], dk + parts[1], dv + parts[2]
        dqkv_ref[0, :, at : at + 128] = (dq * 0.125).astype(BF)
        dqkv_ref[0, :, width + at : width + at + 128] = dk.astype(BF)
        dqkv_ref[0, :, 2 * width + at : 2 * width + at + 128] = dv.astype(BF)


def attend_back(qkv, probs, out, grad):
    tiles, _, width = out.shape

    def block(*shape):
        return pl.BlockSpec((1,) + shape, lambda i: (i,) + (0,) * len(shape))

    return pl.pallas_call(
        attend_back_kernel,
        grid=(tiles,),
        in_specs=[
            block(TILE, 3 * width),
            block(HEADS, TILE, TILE),
            block(TILE, width),
            block(TILE, width),
        ],
        out_specs=block(TILE, 3 * width),
        out_shape=jax.ShapeDtypeStruct((tiles, TILE, 3 * width), BF),
        compiler_params=pltpu.CompilerParams(vmem_limit_bytes=56 * 2**20),
        name="attend_back",
    )(qkv, probs, out, grad)


def expert_kernel(
    text_at,
    x_ref,
    att_ref,
    dy_ref,
    w_out_ref,
    gain_ref,
    shift_ref,
    bias_ref,
    up_v_ref,
    down_v_ref,
    up_t_ref,
    down_t_ref,
    out_ref,
    dmid_ref,
    datt_ref,
    dwout_ref,
    vec_ref,
    dup_ref,
    ddown_ref,
    hid_t,
    dy_t,
    acc_o,
    acc_h,
    up_w,
    down_w,
    dup_buf,
    ddown_buf,
    sems,
    out_sems,
):
    steps, _, cols = up_w.shape
    mid, hid = dmid_ref, datt_ref
    is_text = lax.axis_index("stream") == text_at

    def fetch(up_src, down_src):
        for j in range(steps):
            at = pl.ds(j * cols, cols)
            pltpu.make_async_copy(up_src.at[:, at], up_w.at[j], sems.at[0, j]).start()
            pltpu.make_async_copy(down_src.at[at, :], down_w.at[j], sems.at[1, j]).start()

    pl.when(is_text)(lambda: fetch(up_t_ref, down_t_ref))
    pl.when(jnp.logical_not(is_text))(lambda: fetch(up_v_ref, down_v_ref))

    mid[...] = x_ref[...].astype(F32) + dot(att_ref[...], w_out_ref[...])
    normed, _ = normalize(mid[...])
    hid[...] = (normed * gain_ref[...] + shift_ref[...]).astype(BF)
    hid_t[...] = hid[...].T
    dy_t[...] = dy_ref[...].T

    def stored(j, slot):
        return pltpu.make_async_copy(dup_buf.at[slot], dup_ref.at[j], out_sems.at[0, slot])

    def stored_down(j, slot):
        return pltpu.make_async_copy(ddown_buf.at[slot], ddown_ref.at[j], out_sems.at[1, slot])

    @pl.loop(0, steps)
    def _(j):
        at = pl.ds(j * cols, cols)
        pltpu.make_async_copy(up_v_ref.at[:, at], up_w.at[j], sems.at[0, j]).wait()
        pltpu.make_async_copy(down_v_ref.at[at, :], down_w.at[j], sems.at[1, j]).wait()
        up = dot(hid[...], up_w[j])
        grad = dot_t(dy_ref[...], down_w[j])
        cdf, pdf = gelu_parts(up)
        activ = (up * cdf).astype(BF)
        grad_up = (grad * (cdf + up * pdf)).astype(BF)
        part_o = dot(activ, down_w[j])
        part_h = dot_t(grad_up, up_w[j])

        @pl.when(j == 0)
        def _():
            acc_o[...] = part_o
            acc_h[...] = part_h

        @pl.when(j > 0)
        def _():
            acc_o[...] += part_o
            acc_h[...] += part_h

        slot = lax.rem(j, 2)

        @pl.when(j > 1)
        def _():
            stored(j - 2, slot).wait()
            stored_down(j - 2, slot).wait()

        dup_buf[slot] = dot(hid_t[...], grad_up).astype(BF)
        stored(j, slot).start()
        ddown_buf[slot] = dot(dy_t[...], activ).astype(BF)
        stored_down(j, slot).start()

    out_ref[...] = (mid[...] + acc_o[...] + bias_ref[...]).astype(BF)
    normed, inverse = normalize(mid[...])
    grad = acc_h[...]
    wide = dy_ref[...].astype(F32)
    vec_ref[0:1, :] = jnp.sum(grad * normed, axis=0, keepdims=True)
    vec_ref[1:2, :] = jnp.sum(grad, axis=0, keepdims=True)
    vec_ref[2:3, :] = jnp.sum(wide, axis=0, keepdims=True)
    grad_mid = wide + norm_back(grad, normed, inverse, gain_ref[...])
    dmid_ref[...] = grad_mid
    branch = grad_mid.astype(BF)
    datt_ref[...] = dot_t(branch, w_out_ref[...]).astype(BF)
    dwout_ref[...] = t_dot(att_ref[...], branch).astype(BF)
    for j in range(steps - 2, steps):
        stored(j, j % 2).wait()
        stored_down(j, j % 2).wait()


def expert(x, att, dy, w_out, gain, shift, bias, vis_up, vis_down, txt_up, txt_down):
    rows, width = x.shape
    ff = vis_up.shape[1]
    steps = 3
    cols = ff // steps
    return pl.pallas_call(
        functools.partial(expert_kernel, 3),
        in_specs=[FULL] * 7 + [HBM] * 4,
        out_specs=[FULL] * 5 + [HBM] * 2,
        out_shape=[
            jax.ShapeDtypeStruct((rows, width), BF),
            jax.ShapeDtypeStruct((rows, width), F32),
            jax.ShapeDtypeStruct((rows, width), BF),
            jax.ShapeDtypeStruct((width, width), BF),
            jax.ShapeDtypeStruct((8, width), F32),
            jax.ShapeDtypeStruct((steps, width, cols), BF),
            jax.ShapeDtypeStruct((steps, width, cols), BF),
        ],
        scratch_shapes=[
            pltpu.VMEM((width, rows), BF),
            pltpu.VMEM((width, rows), BF),
            pltpu.VMEM((rows, width), F32),
            pltpu.VMEM((rows, width), F32),
            pltpu.VMEM((steps, width, cols), BF),
            pltpu.VMEM((steps, cols, width), BF),
            pltpu.VMEM((2, width, cols), BF),
            pltpu.VMEM((2, width, cols), BF),
            pltpu.SemaphoreType.DMA((2, steps)),
            pltpu.SemaphoreType.DMA((2, 2)),
        ],
        compiler_params=pltpu.CompilerParams(vmem_limit_bytes=63 * 2**20),
        name="expert",
    )(x, att, dy, w_out, gain, shift, bias, vis_up, vis_down, txt_up, txt_down)


def project_back_kernel(x_ref, dqkv_ref, gain_ref, shift_ref, w_ref, dx_ref, dw_ref, vec_ref, acc):
    i = pl.program_id(0)
    gain = gain_ref[...]
    normed, inverse = normalize(x_ref[0].astype(F32))
    hidden = (normed * gain + shift_ref[...]).astype(BF)
    dqkv = dqkv_ref[0]
    grad = dot_t(dqkv, w_ref[...])
    dx_ref[0] = norm_back(grad, normed, inverse, gain).astype(BF)
    width = x_ref.shape[2]
    part = t_dot(hidden, dqkv)
    ones = jnp.ones((8, TILE), BF)
    sums = dot(ones, dqkv)[0:1]
    vec = jnp.concatenate(
        [
            jnp.sum(grad * normed, axis=0, keepdims=True),
            jnp.sum(grad, axis=0, keepdims=True),
            sums[:, :width],
            sums[:, 2 * width :],
        ],
        axis=0,
    )

    @pl.when(i == 0)
    def _():
        acc[...] = part
        vec_ref[0:4, :] = vec

    @pl.when(i > 0)
    def _():
        acc[...] += part
        vec_ref[0:4, :] += vec

    @pl.when(i == pl.num_programs(0) - 1)
    def _():
        dw_ref[...] = acc[...].astype(BF)


def project_back(x_tiles, dqkv, gain, shift, w_qkv):
    tiles, _, width = x_tiles.shape

    def block(*shape):
        return pl.BlockSpec((1,) + shape, lambda i: (i,) + (0,) * len(shape))

    return pl.pallas_call(
        project_back_kernel,
        grid=(tiles,),
        in_specs=[block(TILE, width), block(TILE, 3 * width), FULL, FULL, FULL],
        out_specs=[block(TILE, width), FULL, FULL],
        out_shape=[
            jax.ShapeDtypeStruct((tiles, TILE, width), BF),
            jax.ShapeDtypeStruct((width, 3 * width), BF),
            jax.ShapeDtypeStruct((8, width), F32),
        ],
        scratch_shapes=[pltpu.VMEM((width, 3 * width), F32)],
        compiler_params=pltpu.CompilerParams(vmem_limit_bytes=56 * 2**20),
        name="project_back",
    )(x_tiles, dqkv, gain, shift, w_qkv)


def pad_rows(block):
    micro, rows, width = block.shape
    thirds = block.reshape(micro, TILES, PATCHES, width)
    thirds = jnp.pad(thirds, ((0, 0), (0, 0), (0, OWN - PATCHES), (0, 0)))
    return thirds.reshape(micro, TILES * OWN, width)


def unpad_rows(block):
    micro, _, width = block.shape
    thirds = block.reshape(micro, TILES, OWN, width)[:, :, :PATCHES]
    return thirds.reshape(micro, TILES * PATCHES, width)


def plan(lengths, pairs, is_text, own_stream):
    micro, items = lengths.shape
    finish = jnp.cumsum(lengths, axis=1)
    starts = finish - lengths
    numbers = jnp.arange(items, dtype=jnp.int32)
    match = pairs[:, :, None] == numbers
    start = jnp.sum(jnp.where(match, starts[:, None, :], 0), axis=2).reshape(micro, 3, TILES)
    length = jnp.sum(jnp.where(match, lengths[:, None, :], 0), axis=2).reshape(micro, 3, TILES)
    paired = (pairs >= 0).reshape(micro, 3, TILES)
    rank = jnp.where(paired, jnp.cumsum(paired.astype(jnp.int32), axis=2) - 1, -1)
    takes = rank[:, :, :, None] == jnp.arange(2)
    slot_start = jnp.sum(jnp.where(takes, start[..., None], 0), axis=2)
    slot_length = jnp.sum(jnp.where(takes, length[..., None], 0), axis=2)
    step = jnp.arange(SLOT, dtype=jnp.int32)
    slot_rows = jnp.where(step < slot_length[..., None], slot_start[..., None] + step, -1)
    next_rows = jnp.broadcast_to(
        PATCHES * jnp.arange(1, TILES, dtype=jnp.int32)[:, None] + step, (micro, TILES - 1, SLOT)
    )
    wanted = jnp.concatenate([slot_rows.reshape(micro, -1), next_rows.reshape(micro, -1)], axis=1)
    place = jnp.arange(TILES * OWN, dtype=jnp.int32)
    row_at = jnp.where(place % OWN < PATCHES, place // OWN * PATCHES + place % OWN, -2)
    picks = (wanted[:, :, None] == row_at).astype(BF)
    item_paired = jnp.any(match, axis=1)
    rows = jnp.arange(TILES * PATCHES + SLOT, dtype=jnp.int32)
    member = (rows[:, None] >= starts[:, None, :]) & (rows[:, None] < finish[:, None, :])
    code = jnp.where(item_paired, -1, numbers + items * (starts // PATCHES))
    row_code = jnp.sum(jnp.where(member, code[:, None, :] + 1, 0), axis=2) - 1
    tile = jnp.arange(TILES, dtype=jnp.int32)[:, None]
    own_code = row_code[:, : TILES * PATCHES].reshape(micro, TILES, PATCHES)
    next_code = jnp.stack(
        [row_code[:, PATCHES * (t + 1) : PATCHES * (t + 1) + SLOT] for t in range(TILES)], axis=1
    )

    def here(codes):
        return jnp.where((codes >= 0) & (codes // items == tile), codes, -1)

    def lay(own, extra):
        gap = jnp.full((micro, TILES, OWN - PATCHES), -1, jnp.int32)
        end = jnp.full((micro, TILES, TILE - OWN - SLOT), -1, jnp.int32)
        return jnp.concatenate([own, gap, extra, end], axis=2)

    text_ids = lay(here(own_code), here(next_code))
    own_length = lax.dynamic_index_in_dim(length, jnp.minimum(own_stream, 2), 1, keepdims=False)
    own_takes = lax.dynamic_index_in_dim(takes, jnp.minimum(own_stream, 2), 1, keepdims=False)
    image_ids = lay(
        jnp.zeros((micro, TILES, PATCHES), jnp.int32),
        jnp.where(step < own_length[..., None], 0, -1),
    )
    ids = jnp.where(is_text, text_ids, image_ids)
    return picks, own_takes.astype(BF), ids.reshape(micro * TILES, 1, TILE)


def spread(padded, picks, own_takes, is_text):
    micro, _, width = padded.shape
    picked = lax.dot_general(
        picks, padded, (((2,), (1,)), ((0,), (0,))), preferred_element_type=F32
    ).astype(BF)
    near = picked[:, 6 * SLOT :].reshape(micro, TILES - 1, SLOT, width)
    near = jnp.concatenate([near, jnp.zeros((micro, 1, SLOT, width), BF)], axis=1)
    sent = picked[:, : 6 * SLOT].reshape(micro, 3, 2 * SLOT, width)
    far = sum(lax.ppermute(sent[:, s], "stream", [(3, s)]) for s in range(3))
    far = far.reshape(micro, 1, 2, SLOT, width) * own_takes[:, :, :, None, None]
    return jnp.where(is_text, near, far[:, :, 0] + far[:, :, 1])


def collect(extra, picks, own_takes, is_text):
    micro, _, _, width = extra.shape
    mine = extra[:, :, None] * own_takes[:, :, :, None, None]
    mine = (mine[:, 0] + mine[:, 1] + mine[:, 2]).reshape(micro, 2 * SLOT, width)
    parts = [lax.ppermute(mine, "stream", [(s, 3)]) for s in range(3)]
    parts.append(extra[:, : TILES - 1].reshape(micro, (TILES - 1) * SLOT, width))
    rows = jnp.concatenate(parts, axis=1)
    scale = jnp.where(is_text, 1.0, 0.0).astype(BF)
    return lax.dot_general(
        picks * scale, rows, (((1,), (1,)), ((0,), (0,))), preferred_element_type=F32
    ).astype(BF)


def reduce_all(vectors, dw_qkv, dw_out, dup, ddown):
    width = dw_qkv.shape[0]
    shard = width // lax.axis_size("dp")
    vectors = lax.psum(vectors, ("dp", "stream"))
    vectors = lax.dynamic_slice_in_dim(vectors, lax.axis_index("dp") * shard, shard, axis=1)

    def over_items(grad, dim):
        return lax.psum_scatter(grad, "dp", scatter_dimension=dim, tiled=True)

    def over_blocks(grad):
        return lax.psum_scatter(grad, "stream", scatter_dimension=1, tiled=True).astype(F32)

    dup = over_items(dup, 0)
    ddown = over_items(ddown, 1)
    qkv = over_blocks(over_items(dw_qkv, 0))
    out = over_blocks(over_items(dw_out, 0))
    up = dup.reshape(dup.shape[0], 4, -1).transpose(1, 0, 2)
    down = ddown.reshape(4, -1, ddown.shape[1])
    up = lax.all_to_all(up, "stream", 0, 0).astype(F32)
    down = lax.all_to_all(down, "stream", 0, 0).astype(F32)
    return (
        vectors,
        qkv,
        out,
        up[0] + up[1] + up[2],
        (down[0] + down[1] + down[2]).T,
        up[3],
        down[3].T,
    )


def shards(
    tokens,
    text_lengths,
    pair_text,
    ln1_gain,
    ln1_bias,
    w_qkv,
    q_bias,
    v_bias,
    w_out,
    ln2_gain,
    ln2_bias,
    vis_up,
    vis_down,
    vis_bias,
    txt_up,
    txt_down,
    txt_bias,
    cotangent,
):
    micro = tokens.shape[0]
    width = tokens.shape[4]
    own_stream = lax.axis_index("stream")
    is_text = own_stream == 3
    gain1, shift1, gain2, shift2 = (
        v.astype(F32)[None] for v in (ln1_gain, ln1_bias, ln2_gain, ln2_bias)
    )
    bias = jnp.where(is_text, txt_bias, vis_bias).astype(F32)[None]
    qkv_bias = jnp.concatenate([q_bias, jnp.zeros_like(q_bias), v_bias]).astype(F32)[None]
    picks, own_takes, ids = plan(text_lengths[:, 0], pair_text[:, 0], is_text, own_stream)

    def tiled(own, extra):
        own = own.reshape(micro, TILES, OWN, width)
        extra = jnp.pad(extra, ((0, 0), (0, 0), (0, TILE - OWN - SLOT), (0, 0)))
        return jnp.concatenate([own, extra], axis=2).reshape(micro * TILES, TILE, width)

    def parted(tiles):
        tiles = tiles.reshape(micro, TILES, TILE, width)
        return tiles[:, :, :OWN].reshape(micro, TILES * OWN, width), tiles[:, :, OWN : OWN + SLOT]

    x = pad_rows(tokens[:, 0, 0])
    dy = pad_rows(cotangent[:, 0, 0])
    x_tiles = tiled(x, spread(x, picks, own_takes, is_text))
    qkv, att_tiles, probs = attend(x_tiles, ids, gain1, shift1, w_qkv, qkv_bias)
    att_own, att_extra = parted(att_tiles)
    att = att_own + collect(att_extra, picks, own_takes, is_text)
    flat = (micro * TILES * OWN, width)
    out, dmid, datt, dw_out, vec2, dup, ddown = expert(
        x.reshape(flat),
        att.reshape(flat),
        dy.reshape(flat),
        w_out,
        gain2,
        shift2,
        bias,
        vis_up,
        vis_down,
        txt_up,
        txt_down,
    )
    datt = datt.reshape(micro, TILES * OWN, width)
    datt_tiles = tiled(datt, spread(datt, picks, own_takes, is_text))
    dqkv = attend_back(qkv, probs, att_tiles, datt_tiles)
    dx_tiles, dw_qkv, vec1 = project_back(x_tiles, dqkv, gain1, shift1, w_qkv)
    dx_own, dx_extra = parted(dx_tiles)
    dx = (
        dmid.reshape(micro, TILES * OWN, width)
        + dx_own.astype(F32)
        + collect(dx_extra, picks, own_takes, is_text).astype(F32)
    )
    text_scale = jnp.where(is_text, 1.0, 0.0)
    vectors = jnp.concatenate(
        [vec1[0:4], vec2[0:2], vec2[2:3] * (1.0 - text_scale), vec2[2:3] * text_scale], axis=0
    )
    dup = jnp.concatenate(list(dup), axis=1)
    ddown = jnp.concatenate(list(ddown), axis=1)
    vectors, g_qkv, g_out, g_vup, g_vdown, g_tup, g_tdown = reduce_all(
        vectors, dw_qkv, dw_out, dup, ddown
    )
    return (
        unpad_rows(out.reshape(micro, TILES * OWN, width)).reshape(tokens.shape),
        unpad_rows(dx).astype(BF).reshape(tokens.shape),
        vectors[0],
        vectors[1],
        g_qkv,
        vectors[2],
        vectors[3],
        g_out,
        vectors[4],
        vectors[5],
        g_vup,
        g_vdown,
        vectors[6],
        g_tup,
        g_tdown,
        vectors[7],
    )


def solution(mesh):
    rows = P(None, "dp", "stream", None, None)
    lists = P(None, "dp", None)
    vector, matrix = P("dp"), P("dp", "stream")
    in_specs = (rows, lists, lists) + (P(),) * 14 + (rows,)
    out_specs = (
        rows,
        rows,
        vector,
        vector,
        matrix,
        vector,
        vector,
        matrix,
        vector,
        vector,
        matrix,
        matrix,
        vector,
        matrix,
        matrix,
        vector,
    )
    return jax.shard_map(shards, mesh=mesh, in_specs=in_specs, out_specs=out_specs, check_vma=False)
```

```python
import functools

import jax
import jax.numpy as jnp
from jax import lax
from jax.experimental import pallas as pl
from jax.experimental.pallas import tpu as pltpu
from jax.sharding import PartitionSpec as P

HEADS = 12
PATCHES = 197
OWN = 208
SLOT = 40
TILE = 256
TILES = 3
EPSILON = 1e-06
MASKED = -1e30
BF = jnp.bfloat16
F32 = jnp.float32
FULL = pl.BlockSpec(memory_space=pltpu.VMEM)
HBM = pl.BlockSpec(memory_space=pl.ANY)


def dot(left, right):
    return jnp.dot(left, right, preferred_element_type=F32)


def dot_t(left, right):
    return lax.dot_general(left, right, (((1,), (1,)), ((), ())), preferred_element_type=F32)


def t_dot(left, right):
    return lax.dot_general(left, right, (((0,), (0,)), ((), ())), preferred_element_type=F32)


def normalize(values):
    centred = values - jnp.mean(values, axis=-1, keepdims=True)
    inverse = lax.rsqrt(jnp.mean(centred * centred, axis=-1, keepdims=True) + EPSILON)
    return centred * inverse, inverse


def norm_back(grad, normed, inverse, gain):
    scaled = grad * gain
    return inverse * (
        scaled
        - jnp.mean(scaled, axis=-1, keepdims=True)
        - normed * jnp.mean(scaled * normed, axis=-1, keepdims=True)
    )


def gelu_parts(up):
    reach = jnp.abs(up) * 0.7071067811865476
    inner = 1.0 / (1.0 + 0.3275911 * reach)
    bell = jnp.exp(-0.5 * up * up)
    poly = inner * (
        0.254829592
        + inner
        * (-0.284496736 + inner * (1.421413741 + inner * (-1.453152027 + inner * 1.061405429)))
    )
    tail = 0.5 * poly * bell
    return jnp.where(up >= 0, 1.0 - tail, tail), bell * 0.3989422804014327


def attend_kernel(x_ref, ids_ref, gain_ref, shift_ref, w_ref, bias_ref, qkv_ref, out_ref, p_ref):
    width = x_ref.shape[2]
    normed, _ = normalize(x_ref[0].astype(F32))
    hidden = (normed * gain_ref[...] + shift_ref[...]).astype(BF)
    qkv = (dot(hidden, w_ref[...]) + bias_ref[...]).astype(BF)
    qkv_ref[0] = qkv
    row_ids = jnp.broadcast_to(ids_ref[0], (TILE, TILE))
    barred = jnp.where((row_ids == row_ids.T) & (row_ids >= 0), 0.0, MASKED)
    lane = lax.broadcasted_iota(jnp.int32, (1, 128), 1)
    low = (lane < 64).astype(BF)
    high = (lane >= 64).astype(BF)
    for pair in range(HEADS // 2):
        at = pair * 128
        q = qkv[:, at : at + 128] * 0.125
        k = qkv[:, width + at : width + at + 128]
        v = qkv[:, 2 * width + at : 2 * width + at + 128]
        out = None
        for side, keep in enumerate((low, high)):
            scores = dot_t(q, k * keep) + barred
            top = jnp.max(scores, axis=-1, keepdims=True)
            expo = jnp.exp(scores - top)
            total = jnp.sum(expo, axis=-1, keepdims=True)
            scale = jnp.where(top > 0.5 * MASKED, 1.0 / total, 0.0)
            probs = (expo * scale).astype(BF)
            p_ref[0, 2 * pair + side] = probs
            part = dot(probs, v * keep)
            out = part if out is None else out + part
        out_ref[0, :, at : at + 128] = out.astype(BF)


def attend(x_tiles, ids, gain, shift, w_qkv, bias):
    tiles, _, width = x_tiles.shape

    def block(*shape):
        return pl.BlockSpec((1,) + shape, lambda i: (i,) + (0,) * len(shape))

    return pl.pallas_call(
        attend_kernel,
        grid=(tiles,),
        in_specs=[block(TILE, width), block(1, TILE), FULL, FULL, FULL, FULL],
        out_specs=[block(TILE, 3 * width), block(TILE, width), block(HEADS, TILE, TILE)],
        out_shape=[
            jax.ShapeDtypeStruct((tiles, TILE, 3 * width), BF),
            jax.ShapeDtypeStruct((tiles, TILE, width), BF),
            jax.ShapeDtypeStruct((tiles, HEADS, TILE, TILE), BF),
        ],
        compiler_params=pltpu.CompilerParams(vmem_limit_bytes=56 * 2**20),
        name="attend",
    )(x_tiles, ids, gain, shift, w_qkv, bias)


def attend_back_kernel(qkv_ref, p_ref, out_ref, grad_ref, dqkv_ref):
    width = out_ref.shape[2]
    lane = lax.broadcasted_iota(jnp.int32, (1, 128), 1)
    low = lane < 64
    for pair in range(HEADS // 2):
        at = pair * 128
        q = qkv_ref[0, :, at : at + 128] * 0.125
        k = qkv_ref[0, :, width + at : width + at + 128]
        v = qkv_ref[0, :, 2 * width + at : 2 * width + at + 128].astype(F32)
        grad = grad_ref[0, :, at : at + 128]
        wide = grad.astype(F32)
        inner = pltpu.roll(wide * out_ref[0, :, at : at + 128].astype(F32), 64, 1)
        dq = dk = dv = None
        for side in range(2):
            mine = low if side == 0 else jnp.logical_not(low)
            keep = mine.astype(BF)
            left = jnp.where(mine, wide, inner).astype(BF)
            right = jnp.where(mine, v, -1.0).astype(BF)
            probs = p_ref[0, 2 * pair + side]
            dscore = (probs.astype(F32) * dot_t(left, right)).astype(BF)
            parts = dot(dscore, k * keep), t_dot(dscore, q * keep), t_dot(probs, grad * keep)
            if dq is None:
                dq, dk, dv = parts
            else:
                dq, dk, dv = dq + parts[0], dk + parts[1], dv + parts[2]
        dqkv_ref[0, :, at : at + 128] = (dq * 0.125).astype(BF)
        dqkv_ref[0, :, width + at : width + at + 128] = dk.astype(BF)
        dqkv_ref[0, :, 2 * width + at : 2 * width + at + 128] = dv.astype(BF)


def attend_back(qkv, probs, out, grad):
    tiles, _, width = out.shape

    def block(*shape):
        return pl.BlockSpec((1,) + shape, lambda i: (i,) + (0,) * len(shape))

    return pl.pallas_call(
        attend_back_kernel,
        grid=(tiles,),
        in_specs=[
            block(TILE, 3 * width),
            block(HEADS, TILE, TILE),
            block(TILE, width),
            block(TILE, width),
        ],
        out_specs=block(TILE, 3 * width),
        out_shape=jax.ShapeDtypeStruct((tiles, TILE, 3 * width), BF),
        compiler_params=pltpu.CompilerParams(vmem_limit_bytes=56 * 2**20),
        name="attend_back",
    )(qkv, probs, out, grad)


MESH = pl.DeviceIdType.MESH
STEPS = 3
PARTS = 3


def add_into(ref, at, other):
    ref[at] = (ref[at].astype(F32) + other.astype(F32)).astype(BF)


class ItemSum:
    def __init__(self, up, down, got, got_one, got_two, sems):
        self.grads = (up, down)
        self.got, self.got_one, self.got_two, self.sems = got, got_one, got_two, sems
        me = lax.axis_index("dp")
        self.me = me
        self.core, self.x, self.y = lax.rem(me, 2), lax.rem(lax.div(me, 2), 2), lax.div(me, 4)
        self.near = me + 1 - 2 * self.core
        self.over_x = me + 2 - 4 * self.x
        self.over_y = me + 4 - 8 * self.y

    def _copy(self, src, dst, stage, which, slot, device):
        return pltpu.make_async_remote_copy(
            src_ref=src,
            dst_ref=dst,
            send_sem=self.sems.at[stage, which, 0, slot],
            recv_sem=self.sems.at[stage, which, 1, slot],
            device_id={"dp": device},
            device_id_type=MESH,
        )

    def core_copy(self, which, slot):
        src = self.grads[which].at[slot, :, :, 1 - self.core]
        return self._copy(src, self.got[which].at[slot], 0, which, slot, self.near)

    def one_copy(self, which, slot):
        grad = self.grads[which]
        if which == 0:
            src, device = grad.at[slot, :, 1 - self.x, self.core], self.over_x
        else:
            src, device = grad.at[slot, 1 - self.y, :, self.core], self.over_y
        return self._copy(src, self.got_one[which].at[slot], 1, which, slot, device)

    def two_copy(self, which, slot):
        grad = self.grads[which]
        if which == 0:
            src, device = grad.at[slot, 1 - self.y, self.x, self.core], self.over_y
        else:
            src, device = grad.at[slot, self.y, 1 - self.x, self.core], self.over_x
        return self._copy(src, self.got_two[which].at[slot], 2, which, slot, device)

    def start(self, which, slot):
        self.core_copy(which, slot).start()

    def after_core(self, slot):
        for which in range(2):
            self.core_copy(which, slot).wait()
            for y in range(2):
                for x in range(2):
                    at = (slot, y, x, self.core)
                    add_into(self.grads[which], at, self.got[which][slot, y, x])
            self.one_copy(which, slot).start()

    def after_one(self, slot):
        for which in range(2):
            self.one_copy(which, slot).wait()
            for side in range(2):
                at = (slot, side, self.x, self.core) if which == 0 else (slot, self.y, side, self.core)
                add_into(self.grads[which], at, self.got_one[which][slot, side])
            self.two_copy(which, slot).start()

    def after_two(self, slot):
        sums = []
        for which in range(2):
            self.two_copy(which, slot).wait()
            own = self.grads[which][slot, self.y, self.x, self.core].astype(F32)
            sums.append((own + self.got_two[which][slot].astype(F32)).astype(BF))
        return sums


def meet(devices):
    barrier = pltpu.get_barrier_semaphore()
    for device in devices:
        pl.semaphore_signal(barrier, inc=1, device_id=device, device_id_type=MESH)
    pl.semaphore_wait(barrier, len(devices))


def expert_kernel(
    remote,
    x_ref,
    att_ref,
    dy_ref,
    w_out_ref,
    gain_ref,
    shift_ref,
    bias_ref,
    up_v_ref,
    down_v_ref,
    up_t_ref,
    down_t_ref,
    out_ref,
    dmid_ref,
    datt_ref,
    dwout_ref,
    vec_ref,
    dup_ref,
    ddown_ref,
    hid_t,
    dy_t,
    acc_o,
    acc_h,
    up_w,
    down_w,
    act,
    gup,
    dup_buf,
    ddown_buf,
    sems,
    *more,
):
    mid, hid = dmid_ref, datt_ref
    rows, width = mid.shape
    cols = act.shape[1]
    is_text = lax.axis_index("stream") == 3
    pieces = 8 if remote else 1
    piece = cols // pieces
    ff = up_v_ref.shape[1]

    x_copy = pltpu.make_async_copy(x_ref, act.at[:, 0:width], sems.at[2, 0])
    x_copy.start()

    def fetch(j, slot):
        def go(up_src, down_src):
            for d in range(pieces):
                at = pl.ds(pl.multiple_of(j * piece + d * (ff // pieces), 128), piece)
                here = pl.ds(d * piece, piece)
                pltpu.make_async_copy(
                    up_src.at[:, at], up_w.at[slot, :, here], sems.at[0, slot]
                ).start()
                pltpu.make_async_copy(
                    down_src.at[at, :], down_w.at[slot, here, :], sems.at[1, slot]
                ).start()

        pl.when(is_text)(lambda: go(up_t_ref, down_t_ref))
        pl.when(jnp.logical_not(is_text))(lambda: go(up_v_ref, down_v_ref))

    def fetched(slot):
        pltpu.make_async_copy(up_w.at[slot], up_w.at[slot], sems.at[0, slot]).wait()
        pltpu.make_async_copy(down_w.at[slot], down_w.at[slot], sems.at[1, slot]).wait()

    fetch(0, 0)
    if remote:
        got, got_one, got_two, sum_sems = more[0:2], more[2:4], more[4:6], more[6]
        total = ItemSum(dup_buf, ddown_buf, got, got_one, got_two, sum_sems)
        meet([{"dp": total.near}, {"dp": total.over_x}, {"dp": total.over_y}])
    x_copy.wait()
    part_rows = rows // PARTS

    @pl.loop(0, PARTS)
    def _(part):
        at = pl.ds(pl.multiple_of(part * part_rows, 16), part_rows)
        middle = act[at, 0:width].astype(F32) + dot(att_ref[at], w_out_ref[...])
        mid[at] = middle
        normed, _ = normalize(middle)
        hid[at] = (normed * gain_ref[...] + shift_ref[...]).astype(BF)
        acc_o[at] = middle + bias_ref[...]
        acc_h[at] = jnp.zeros_like(middle)

    hid_t[...] = hid[...].T
    dy_t[...] = dy_ref[...].T

    def deliver(slot, j):
        up, down = total.after_two(slot)
        for t in range(4):
            dup_ref[j, t] = up[:, t * (cols // 4) : (t + 1) * (cols // 4)]
            ddown_ref[j, t] = down[t * (width // 4) : (t + 1) * (width // 4)]

    def stored(j, slot):
        return (
            pltpu.make_async_copy(dup_buf.at[slot], dup_ref.at[j], sems.at[3, slot]),
            pltpu.make_async_copy(ddown_buf.at[slot], ddown_ref.at[j], sems.at[4, slot]),
        )

    @pl.loop(0, STEPS)
    def _(j):
        slot = lax.rem(j, 2)
        other = 1 - slot
        pl.when(j < STEPS - 1)(lambda: fetch(j + 1, other))
        fetched(slot)

        @pl.loop(0, PARTS)
        def _(part):
            at = pl.ds(pl.multiple_of(part * part_rows, 16), part_rows)
            up = dot(hid[at], up_w[slot])
            grad = dot_t(dy_ref[at], down_w[slot])
            cdf, pdf = gelu_parts(up)
            activ = (up * cdf).astype(BF)
            grad_up = (grad * (cdf + up * pdf)).astype(BF)
            act[at] = activ
            gup[at] = grad_up
            acc_o[at] += dot(activ, down_w[slot])
            acc_h[at] += dot_t(grad_up, up_w[slot])
            if remote:

                @pl.when(part == 0)
                def _():
                    pl.when(j > 1)(lambda: deliver(slot, j - 2))
                    pl.when(j > 0)(lambda: total.after_core(other))

        if not remote:

            @pl.when(j > 1)
            def _():
                for copy in stored(j - 2, slot):
                    copy.wait()

        grad = dot(hid_t[...], gup[...]).astype(BF)
        if remote:
            dup_buf[slot] = grad.reshape(dup_buf.shape[1:])
            total.start(0, slot)
            pl.when(j > 0)(lambda: total.after_one(other))
        else:
            dup_buf[slot] = grad
        grad = dot(dy_t[...], act[...]).astype(BF)
        if remote:
            for d in range(8):
                ddown_buf[slot, d // 4, d // 2 % 2, d % 2] = grad[:, d * piece : (d + 1) * piece]
            total.start(1, slot)
        else:
            ddown_buf[slot] = grad
            for copy in stored(j, slot):
                copy.start()

    last = (STEPS - 1) % 2
    vec_ref[...] = jnp.zeros_like(vec_ref)

    @pl.loop(0, PARTS)
    def _(part):
        at = pl.ds(pl.multiple_of(part * part_rows, 16), part_rows)
        out_ref[at] = acc_o[at].astype(BF)
        normed, inverse = normalize(mid[at])
        grad = acc_h[at]
        wide = dy_ref[at].astype(F32)
        vec_ref[0:1, :] += jnp.sum(grad * normed, axis=0, keepdims=True)
        vec_ref[1:2, :] += jnp.sum(grad, axis=0, keepdims=True)
        vec_ref[2:3, :] += jnp.sum(wide, axis=0, keepdims=True)
        grad_mid = wide + norm_back(grad, normed, inverse, gain_ref[...])
        dmid_ref[at] = grad_mid
        branch = grad_mid.astype(BF)
        gup[at, 0:width] = branch
        datt_ref[at] = dot_t(branch, w_out_ref[...]).astype(BF)
        if remote:

            @pl.when(part == 0)
            def _():
                deliver(1 - last, STEPS - 2)
                total.after_core(last)

    dwout_ref[...] = t_dot(att_ref[...], gup[:, 0:width]).astype(BF)
    if remote:
        total.after_one(last)
        deliver(last, STEPS - 1)
    else:
        for j in range(STEPS - 2, STEPS):
            for copy in stored(j, j % 2):
                copy.wait()


def expert(remote, x, att, dy, w_out, gain, shift, bias, vis_up, vis_down, txt_up, txt_down):
    rows, width = x.shape
    cols = vis_up.shape[1] // STEPS
    if remote:
        shard, piece = width // 8, cols // 8
        buffers = (2, 2, 2, 2, shard, cols), (2, 2, 2, 2, width, piece)
        outs = (STEPS, 4, shard, cols // 4), (STEPS, 4, width // 4, piece)
        more = [
            pltpu.VMEM((2, 2, 2, shard, cols), BF),
            pltpu.VMEM((2, 2, 2, width, piece), BF),
            pltpu.VMEM((2, 2, shard, cols), BF),
            pltpu.VMEM((2, 2, width, piece), BF),
            pltpu.VMEM((2, shard, cols), BF),
            pltpu.VMEM((2, width, piece), BF),
            pltpu.SemaphoreType.DMA((3, 2, 2, 2)),
        ]
        params = dict(collective_id=1, has_side_effects=True)
    else:
        buffers = ((2, width, cols),) * 2
        outs = ((STEPS, width, cols),) * 2
        more, params = [], {}
    return pl.pallas_call(
        functools.partial(expert_kernel, remote),
        in_specs=[HBM] + [FULL] * 6 + [HBM] * 4,
        out_specs=[FULL] * 5 + [FULL if remote else HBM] * 2,
        out_shape=[
            jax.ShapeDtypeStruct((rows, width), BF),
            jax.ShapeDtypeStruct((rows, width), F32),
            jax.ShapeDtypeStruct((rows, width), BF),
            jax.ShapeDtypeStruct((width, width), BF),
            jax.ShapeDtypeStruct((8, width), F32),
        ]
        + [jax.ShapeDtypeStruct(shape, BF) for shape in outs],
        scratch_shapes=[
            pltpu.VMEM((width, rows), BF),
            pltpu.VMEM((width, rows), BF),
            pltpu.VMEM((rows, width), F32),
            pltpu.VMEM((rows, width), F32),
            pltpu.VMEM((2, width, cols), BF),
            pltpu.VMEM((2, cols, width), BF),
            pltpu.VMEM((rows, cols), BF),
            pltpu.VMEM((rows, cols), BF),
            pltpu.VMEM(buffers[0], BF),
            pltpu.VMEM(buffers[1], BF),
            pltpu.SemaphoreType.DMA((5, 2)),
        ]
        + more,
        compiler_params=pltpu.CompilerParams(vmem_limit_bytes=63 * 2**20, **params),
        name="expert",
    )(x, att, dy, w_out, gain, shift, bias, vis_up, vis_down, txt_up, txt_down)


def project_back_kernel(x_ref, dqkv_ref, gain_ref, shift_ref, w_ref, dx_ref, dw_ref, vec_ref, acc):
    i = pl.program_id(0)
    gain = gain_ref[...]
    normed, inverse = normalize(x_ref[0].astype(F32))
    hidden = (normed * gain + shift_ref[...]).astype(BF)
    dqkv = dqkv_ref[0]
    grad = dot_t(dqkv, w_ref[...])
    dx_ref[0] = norm_back(grad, normed, inverse, gain).astype(BF)
    width = x_ref.shape[2]
    part = t_dot(hidden, dqkv)
    ones = jnp.ones((8, TILE), BF)
    sums = dot(ones, dqkv)[0:1]
    vec = jnp.concatenate(
        [
            jnp.sum(grad * normed, axis=0, keepdims=True),
            jnp.sum(grad, axis=0, keepdims=True),
            sums[:, :width],
            sums[:, 2 * width :],
        ],
        axis=0,
    )

    @pl.when(i == 0)
    def _():
        acc[...] = part
        vec_ref[0:4, :] = vec

    @pl.when(i > 0)
    def _():
        acc[...] += part
        vec_ref[0:4, :] += vec

    @pl.when(i == pl.num_programs(0) - 1)
    def _():
        dw_ref[...] = acc[...].astype(BF)


def project_back(x_tiles, dqkv, gain, shift, w_qkv):
    tiles, _, width = x_tiles.shape

    def block(*shape):
        return pl.BlockSpec((1,) + shape, lambda i: (i,) + (0,) * len(shape))

    return pl.pallas_call(
        project_back_kernel,
        grid=(tiles,),
        in_specs=[block(TILE, width), block(TILE, 3 * width), FULL, FULL, FULL],
        out_specs=[block(TILE, width), FULL, FULL],
        out_shape=[
            jax.ShapeDtypeStruct((tiles, TILE, width), BF),
            jax.ShapeDtypeStruct((width, 3 * width), BF),
            jax.ShapeDtypeStruct((8, width), F32),
        ],
        scratch_shapes=[pltpu.VMEM((width, 3 * width), F32)],
        compiler_params=pltpu.CompilerParams(vmem_limit_bytes=56 * 2**20),
        name="project_back",
    )(x_tiles, dqkv, gain, shift, w_qkv)


def pad_rows(block):
    micro, rows, width = block.shape
    thirds = block.reshape(micro, TILES, PATCHES, width)
    thirds = jnp.pad(thirds, ((0, 0), (0, 0), (0, OWN - PATCHES), (0, 0)))
    return thirds.reshape(micro, TILES * OWN, width)


def unpad_rows(block):
    micro, _, width = block.shape
    thirds = block.reshape(micro, TILES, OWN, width)[:, :, :PATCHES]
    return thirds.reshape(micro, TILES * PATCHES, width)


def plan(lengths, pairs, is_text, own_stream):
    micro, items = lengths.shape
    finish = jnp.cumsum(lengths, axis=1)
    starts = finish - lengths
    numbers = jnp.arange(items, dtype=jnp.int32)
    match = pairs[:, :, None] == numbers
    start = jnp.sum(jnp.where(match, starts[:, None, :], 0), axis=2).reshape(micro, 3, TILES)
    length = jnp.sum(jnp.where(match, lengths[:, None, :], 0), axis=2).reshape(micro, 3, TILES)
    paired = (pairs >= 0).reshape(micro, 3, TILES)
    rank = jnp.where(paired, jnp.cumsum(paired.astype(jnp.int32), axis=2) - 1, -1)
    takes = rank[:, :, :, None] == jnp.arange(2)
    slot_start = jnp.sum(jnp.where(takes, start[..., None], 0), axis=2)
    slot_length = jnp.sum(jnp.where(takes, length[..., None], 0), axis=2)
    step = jnp.arange(SLOT, dtype=jnp.int32)
    slot_rows = jnp.where(step < slot_length[..., None], slot_start[..., None] + step, -1)
    next_rows = jnp.broadcast_to(
        PATCHES * jnp.arange(1, TILES, dtype=jnp.int32)[:, None] + step, (micro, TILES - 1, SLOT)
    )
    wanted = jnp.concatenate([slot_rows.reshape(micro, -1), next_rows.reshape(micro, -1)], axis=1)
    place = jnp.arange(TILES * OWN, dtype=jnp.int32)
    row_at = jnp.where(place % OWN < PATCHES, place // OWN * PATCHES + place % OWN, -2)
    picks = (wanted[:, :, None] == row_at).astype(BF)
    item_paired = jnp.any(match, axis=1)
    rows = jnp.arange(TILES * PATCHES + SLOT, dtype=jnp.int32)
    member = (rows[:, None] >= starts[:, None, :]) & (rows[:, None] < finish[:, None, :])
    code = jnp.where(item_paired, -1, numbers + items * (starts // PATCHES))
    row_code = jnp.sum(jnp.where(member, code[:, None, :] + 1, 0), axis=2) - 1
    tile = jnp.arange(TILES, dtype=jnp.int32)[:, None]
    own_code = row_code[:, : TILES * PATCHES].reshape(micro, TILES, PATCHES)
    next_code = jnp.stack(
        [row_code[:, PATCHES * (t + 1) : PATCHES * (t + 1) + SLOT] for t in range(TILES)], axis=1
    )

    def here(codes):
        return jnp.where((codes >= 0) & (codes // items == tile), codes, -1)

    def lay(own, extra):
        gap = jnp.full((micro, TILES, OWN - PATCHES), -1, jnp.int32)
        end = jnp.full((micro, TILES, TILE - OWN - SLOT), -1, jnp.int32)
        return jnp.concatenate([own, gap, extra, end], axis=2)

    text_ids = lay(here(own_code), here(next_code))
    own_length = lax.dynamic_index_in_dim(length, jnp.minimum(own_stream, 2), 1, keepdims=False)
    own_takes = lax.dynamic_index_in_dim(takes, jnp.minimum(own_stream, 2), 1, keepdims=False)
    image_ids = lay(
        jnp.zeros((micro, TILES, PATCHES), jnp.int32),
        jnp.where(step < own_length[..., None], 0, -1),
    )
    ids = jnp.where(is_text, text_ids, image_ids)
    return picks, own_takes.astype(BF), ids.reshape(micro * TILES, 1, TILE)


def spread(padded, picks, own_takes, is_text):
    micro, _, width = padded.shape
    picked = lax.dot_general(
        picks, padded, (((2,), (1,)), ((0,), (0,))), preferred_element_type=F32
    ).astype(BF)
    near = picked[:, 6 * SLOT :].reshape(micro, TILES - 1, SLOT, width)
    near = jnp.concatenate([near, jnp.zeros((micro, 1, SLOT, width), BF)], axis=1)
    sent = picked[:, : 6 * SLOT].reshape(micro, 3, 2 * SLOT, width)
    far = sum(lax.ppermute(sent[:, s], "stream", [(3, s)]) for s in range(3))
    far = far.reshape(micro, 1, 2, SLOT, width) * own_takes[:, :, :, None, None]
    return jnp.where(is_text, near, far[:, :, 0] + far[:, :, 1])


def collect(extra, picks, own_takes, is_text):
    micro, _, _, width = extra.shape
    mine = extra[:, :, None] * own_takes[:, :, :, None, None]
    mine = (mine[:, 0] + mine[:, 1] + mine[:, 2]).reshape(micro, 2 * SLOT, width)
    parts = [lax.ppermute(mine, "stream", [(s, 3)]) for s in range(3)]
    parts.append(extra[:, : TILES - 1].reshape(micro, (TILES - 1) * SLOT, width))
    rows = jnp.concatenate(parts, axis=1)
    scale = jnp.where(is_text, 1.0, 0.0).astype(BF)
    return lax.dot_general(
        picks * scale, rows, (((1,), (1,)), ((0,), (0,))), preferred_element_type=F32
    ).astype(BF)


def reduce_all(remote, vectors, dw_qkv, dw_out, dup, ddown):
    width = dw_qkv.shape[0]
    shard = width // lax.axis_size("dp")
    vectors = lax.psum(vectors, ("dp", "stream"))
    vectors = lax.dynamic_slice_in_dim(vectors, lax.axis_index("dp") * shard, shard, axis=1)

    def over_items(grad, dim):
        return lax.psum_scatter(grad, "dp", scatter_dimension=dim, tiled=True)

    def over_blocks(grad):
        return lax.psum_scatter(grad, "stream", scatter_dimension=1, tiled=True).astype(F32)

    qkv = over_blocks(over_items(dw_qkv, 0))
    out = over_blocks(over_items(dw_out, 0))
    if remote:
        up = dup.transpose(1, 0, 2, 3)
        down = ddown.transpose(1, 0, 2, 3)
    else:
        dup = over_items(jnp.concatenate(list(dup), axis=1), 0)
        ddown = over_items(jnp.concatenate(list(ddown), axis=1), 1)
        up = dup.reshape(dup.shape[0], 4, -1).transpose(1, 0, 2)
        down = ddown.reshape(4, -1, ddown.shape[1])
    up = lax.all_to_all(up, "stream", 0, 0).astype(F32)
    down = lax.all_to_all(down, "stream", 0, 0).astype(F32)

    def place_up(sums):
        if remote:
            steps, rows, cols = sums.shape
            sums = sums.reshape(steps, rows, 2, cols // 2).transpose(1, 2, 0, 3)
            sums = sums.reshape(rows, steps * cols)
        return sums

    def place_down(sums):
        if remote:
            return sums.transpose(0, 2, 1).reshape(-1, sums.shape[1])
        return sums.T

    return (
        vectors,
        qkv,
        out,
        place_up(up[0] + up[1] + up[2]),
        place_down(down[0] + down[1] + down[2]),
        place_up(up[3]),
        place_down(down[3]),
    )


def shards(
    remote,
    tokens,
    text_lengths,
    pair_text,
    ln1_gain,
    ln1_bias,
    w_qkv,
    q_bias,
    v_bias,
    w_out,
    ln2_gain,
    ln2_bias,
    vis_up,
    vis_down,
    vis_bias,
    txt_up,
    txt_down,
    txt_bias,
    cotangent,
):
    micro = tokens.shape[0]
    width = tokens.shape[4]
    own_stream = lax.axis_index("stream")
    is_text = own_stream == 3
    gain1, shift1, gain2, shift2 = (
        v.astype(F32)[None] for v in (ln1_gain, ln1_bias, ln2_gain, ln2_bias)
    )
    bias = jnp.where(is_text, txt_bias, vis_bias).astype(F32)[None]
    qkv_bias = jnp.concatenate([q_bias, jnp.zeros_like(q_bias), v_bias]).astype(F32)[None]
    picks, own_takes, ids = plan(text_lengths[:, 0], pair_text[:, 0], is_text, own_stream)

    def tiled(own, extra):
        own = own.reshape(micro, TILES, OWN, width)
        extra = jnp.pad(extra, ((0, 0), (0, 0), (0, TILE - OWN - SLOT), (0, 0)))
        return jnp.concatenate([own, extra], axis=2).reshape(micro * TILES, TILE, width)

    def parted(tiles):
        tiles = tiles.reshape(micro, TILES, TILE, width)
        return tiles[:, :, :OWN].reshape(micro, TILES * OWN, width), tiles[:, :, OWN : OWN + SLOT]

    x = pad_rows(tokens[:, 0, 0])
    dy = pad_rows(cotangent[:, 0, 0])
    x_tiles = tiled(x, spread(x, picks, own_takes, is_text))
    qkv, att_tiles, probs = attend(x_tiles, ids, gain1, shift1, w_qkv, qkv_bias)
    att_own, att_extra = parted(att_tiles)
    att = att_own + collect(att_extra, picks, own_takes, is_text)
    flat = (micro * TILES * OWN, width)
    out, dmid, datt, dw_out, vec2, dup, ddown = expert(
        remote,
        x.reshape(flat),
        att.reshape(flat),
        dy.reshape(flat),
        w_out,
        gain2,
        shift2,
        bias,
        vis_up,
        vis_down,
        txt_up,
        txt_down,
    )
    datt = datt.reshape(micro, TILES * OWN, width)
    datt_tiles = tiled(datt, spread(datt, picks, own_takes, is_text))
    dqkv = attend_back(qkv, probs, att_tiles, datt_tiles)
    dx_tiles, dw_qkv, vec1 = project_back(x_tiles, dqkv, gain1, shift1, w_qkv)
    dx_own, dx_extra = parted(dx_tiles)
    dx = (
        dmid.reshape(micro, TILES * OWN, width)
        + dx_own.astype(F32)
        + collect(dx_extra, picks, own_takes, is_text).astype(F32)
    )
    text_scale = jnp.where(is_text, 1.0, 0.0)
    vectors = jnp.concatenate(
        [vec1[0:4], vec2[0:2], vec2[2:3] * (1.0 - text_scale), vec2[2:3] * text_scale], axis=0
    )
    vectors, g_qkv, g_out, g_vup, g_vdown, g_tup, g_tdown = reduce_all(
        remote, vectors, dw_qkv, dw_out, dup, ddown
    )
    return (
        unpad_rows(out.reshape(micro, TILES * OWN, width)).reshape(tokens.shape),
        unpad_rows(dx).astype(BF).reshape(tokens.shape),
        vectors[0],
        vectors[1],
        g_qkv,
        vectors[2],
        vectors[3],
        g_out,
        vectors[4],
        vectors[5],
        g_vup,
        g_vdown,
        vectors[6],
        g_tup,
        g_tdown,
        vectors[7],
    )


def solution(mesh):
    rows = P(None, "dp", "stream", None, None)
    lists = P(None, "dp", None)
    vector, matrix = P("dp"), P("dp", "stream")
    in_specs = (rows, lists, lists) + (P(),) * 14 + (rows,)
    out_specs = (
        rows,
        rows,
        vector,
        vector,
        matrix,
        vector,
        vector,
        matrix,
        vector,
        vector,
        matrix,
        matrix,
        vector,
        matrix,
        matrix,
        vector,
    )
    remote = mesh.shape["dp"] == 8
    body = functools.partial(shards, remote)
    return jax.shard_map(body, mesh=mesh, in_specs=in_specs, out_specs=out_specs, check_vma=False)
```

```python
import functools

import jax
import jax.numpy as jnp
from jax import lax
from jax.experimental import pallas as pl
from jax.experimental.pallas import tpu as pltpu
from jax.sharding import PartitionSpec as P

HEADS = 12
PATCHES = 197
OWN = 208
SLOT = 40
TILE = 256
TILES = 3
EPSILON = 1e-06
MASKED = -1e30
BF = jnp.bfloat16
F32 = jnp.float32
FULL = pl.BlockSpec(memory_space=pltpu.VMEM)
HBM = pl.BlockSpec(memory_space=pl.ANY)


def dot(left, right):
    return jnp.dot(left, right, preferred_element_type=F32)


def dot_t(left, right):
    return lax.dot_general(left, right, (((1,), (1,)), ((), ())), preferred_element_type=F32)


def t_dot(left, right):
    return lax.dot_general(left, right, (((0,), (0,)), ((), ())), preferred_element_type=F32)


def normalize(values):
    centred = values - jnp.mean(values, axis=-1, keepdims=True)
    inverse = lax.rsqrt(jnp.mean(centred * centred, axis=-1, keepdims=True) + EPSILON)
    return centred * inverse, inverse


def norm_back(grad, normed, inverse, gain):
    scaled = grad * gain
    return inverse * (
        scaled
        - jnp.mean(scaled, axis=-1, keepdims=True)
        - normed * jnp.mean(scaled * normed, axis=-1, keepdims=True)
    )


def gelu_parts(up):
    reach = jnp.abs(up) * 0.7071067811865476
    inner = 1.0 / (1.0 + 0.3275911 * reach)
    bell = jnp.exp(-0.5 * up * up)
    poly = inner * (
        0.254829592
        + inner
        * (-0.284496736 + inner * (1.421413741 + inner * (-1.453152027 + inner * 1.061405429)))
    )
    tail = 0.5 * poly * bell
    return jnp.where(up >= 0, 1.0 - tail, tail), bell * 0.3989422804014327


def halves(block, low, high):
    return jnp.concatenate([block * low, block * high], axis=0)


def pair_lanes():
    lane = lax.broadcasted_iota(jnp.int32, (1, 128), 1)
    return (lane < 64).astype(BF), (lane >= 64).astype(BF)


def attend_pair(q, k, v, barred, low, high):
    scores = dot_t(halves(k, low, high), q * 0.125)
    yield
    expos = []
    for side in range(2):
        part = scores[TILE * side : TILE * (side + 1)] + barred
        top = jnp.maximum(jnp.max(part, axis=0, keepdims=True), 0.1 * MASKED)
        expos.append(jnp.exp(part - top).astype(BF))
    ones = [jnp.broadcast_to(keep, (TILE, 128)) for keep in (low, high)]
    right = jnp.concatenate([halves(v, low, high), jnp.concatenate(ones, axis=0)], axis=1)
    sums = t_dot(jnp.concatenate(expos, axis=0), right)
    inverse = jnp.where(sums[:, 128:] > 0.0, 1.0 / sums[:, 128:], 0.0)
    yield expos, sums[:, :128] * inverse, inverse


def attend_back_pair(q, k, v, expos, out, inverse, grad, low, high):
    scaled = grad.astype(F32) * inverse.astype(F32)
    inner = (scaled * out.astype(F32)).astype(BF)
    scaled = scaled.astype(BF)
    minus = [jnp.broadcast_to(-keep, (TILE, 128)) for keep in (low, high)]
    right = jnp.concatenate([halves(v, low, high), jnp.concatenate(minus, axis=0)], axis=1)
    slopes = dot_t(right, jnp.concatenate([scaled, inner], axis=1))
    yield
    parts = [
        (expos[side].astype(F32) * slopes[TILE * side : TILE * (side + 1)]).astype(BF)
        for side in range(2)
    ]
    dq = t_dot(jnp.concatenate(parts, axis=0), halves(k, low, high)) * 0.125
    dk = dot(jnp.concatenate(parts, axis=1), halves(q * 0.125, low, high))
    dv = dot(jnp.concatenate(expos, axis=1), halves(scaled, low, high))
    yield dq.astype(BF), dk.astype(BF), dv.astype(BF)


def staggered(makers, finish):
    held = None
    for n, make in enumerate(makers):
        step = make()
        next(step)
        if held is not None:
            finish(n - 1, next(held))
        held = step
    finish(len(makers) - 1, next(held))


def bars(ids_ref):
    ids = jnp.broadcast_to(ids_ref, (TILE, TILE))
    return jnp.where((ids == ids.T) & (ids >= 0), 0.0, MASKED)


def attend_kernel(
    x_ref, ids_ref, gain_ref, shift_ref, w_ref, bias_ref, qkv_ref, out_ref, p_ref, inv_ref
):
    width = x_ref.shape[2]
    normed, _ = normalize(x_ref[0].astype(F32))
    hidden = (normed * gain_ref[...] + shift_ref[...]).astype(BF)
    qkv = (dot(hidden, w_ref[...]) + bias_ref[...]).astype(BF)
    qkv_ref[0] = qkv
    barred = bars(ids_ref[0])
    low, high = pair_lanes()

    def maker(pair):
        cols = [qkv_ref[0, :, part * width + pair * 128 :][:, :128] for part in range(3)]
        return lambda: attend_pair(*cols, barred, low, high)

    def finish(pair, results):
        expos, out, inverse = results
        at = pair * 128
        for side in range(2):
            p_ref[0, 2 * pair + side] = expos[side]
        out_ref[0, :, at : at + 128] = out.astype(BF)
        inv_ref[0, :, at : at + 128] = inverse.astype(BF)

    staggered([maker(pair) for pair in range(HEADS // 2)], finish)


def attend(x_tiles, ids, gain, shift, w_qkv, bias):
    tiles, _, width = x_tiles.shape

    def block(*shape):
        return pl.BlockSpec((1,) + shape, lambda i: (i,) + (0,) * len(shape))

    return pl.pallas_call(
        attend_kernel,
        grid=(tiles,),
        in_specs=[block(TILE, width), block(1, TILE), FULL, FULL, FULL, FULL],
        out_specs=[
            block(TILE, 3 * width),
            block(TILE, width),
            block(HEADS, TILE, TILE),
            block(TILE, width),
        ],
        out_shape=[
            jax.ShapeDtypeStruct((tiles, TILE, 3 * width), BF),
            jax.ShapeDtypeStruct((tiles, TILE, width), BF),
            jax.ShapeDtypeStruct((tiles, HEADS, TILE, TILE), BF),
            jax.ShapeDtypeStruct((tiles, TILE, width), BF),
        ],
        compiler_params=pltpu.CompilerParams(vmem_limit_bytes=56 * 2**20),
        name="attend",
    )(x_tiles, ids, gain, shift, w_qkv, bias)


def attend_back_kernel(qkv_ref, p_ref, out_ref, inv_ref, grad_ref, dqkv_ref):
    width = out_ref.shape[2]
    low, high = pair_lanes()

    def maker(pair):
        at = pl.ds(pair * 128, 128)
        return lambda: attend_back_pair(
            *(qkv_ref[0, :, pl.ds(part * width + pair * 128, 128)] for part in range(3)),
            [p_ref[0, 2 * pair], p_ref[0, 2 * pair + 1]],
            out_ref[0, :, at],
            inv_ref[0, :, at],
            grad_ref[0, :, at],
            low,
            high,
        )

    def finish(pair, results):
        for part, value in enumerate(results):
            dqkv_ref[0, :, pl.ds(part * width + pair * 128, 128)] = value

    staggered([maker(pair) for pair in range(HEADS // 2)], finish)


def attend_back(qkv, probs, out, inverse, grad):
    tiles, _, width = out.shape

    def block(*shape):
        return pl.BlockSpec((1,) + shape, lambda i: (i,) + (0,) * len(shape))

    return pl.pallas_call(
        attend_back_kernel,
        grid=(tiles,),
        in_specs=[
            block(TILE, 3 * width),
            block(HEADS, TILE, TILE),
            block(TILE, width),
            block(TILE, width),
            block(TILE, width),
        ],
        out_specs=block(TILE, 3 * width),
        out_shape=jax.ShapeDtypeStruct((tiles, TILE, 3 * width), BF),
        compiler_params=pltpu.CompilerParams(vmem_limit_bytes=56 * 2**20),
        name="attend_back",
    )(qkv, probs, out, inverse, grad)


MESH = pl.DeviceIdType.MESH
STEPS = 3
PARTS = 3


def add_into(ref, at, other):
    ref[at] = (ref[at].astype(F32) + other.astype(F32)).astype(BF)


class ItemSum:
    def __init__(self, up, down, got, got_one, got_two, sems):
        self.grads = (up, down)
        self.got, self.got_one, self.got_two, self.sems = got, got_one, got_two, sems
        me = lax.axis_index("dp")
        self.me = me
        self.core, self.x, self.y = lax.rem(me, 2), lax.rem(lax.div(me, 2), 2), lax.div(me, 4)
        self.near = me + 1 - 2 * self.core
        self.over_x = me + 2 - 4 * self.x
        self.over_y = me + 4 - 8 * self.y

    def _copy(self, src, dst, stage, which, slot, device):
        return pltpu.make_async_remote_copy(
            src_ref=src,
            dst_ref=dst,
            send_sem=self.sems.at[stage, which, 0, slot],
            recv_sem=self.sems.at[stage, which, 1, slot],
            device_id={"dp": device},
            device_id_type=MESH,
        )

    def core_copy(self, which, slot):
        src = self.grads[which].at[slot, :, :, 1 - self.core]
        return self._copy(src, self.got[which].at[slot], 0, which, slot, self.near)

    def one_copy(self, which, slot):
        grad = self.grads[which]
        if which == 0:
            src, device = grad.at[slot, :, 1 - self.x, self.core], self.over_x
        else:
            src, device = grad.at[slot, 1 - self.y, :, self.core], self.over_y
        return self._copy(src, self.got_one[which].at[slot], 1, which, slot, device)

    def two_copy(self, which, slot):
        grad = self.grads[which]
        if which == 0:
            src, device = grad.at[slot, 1 - self.y, self.x, self.core], self.over_y
        else:
            src, device = grad.at[slot, self.y, 1 - self.x, self.core], self.over_x
        return self._copy(src, self.got_two[which].at[slot], 2, which, slot, device)

    def start(self, which, slot):
        self.core_copy(which, slot).start()

    def after_core(self, slot):
        for which in range(2):
            self.core_copy(which, slot).wait()
            for y in range(2):
                for x in range(2):
                    at = (slot, y, x, self.core)
                    add_into(self.grads[which], at, self.got[which][slot, y, x])
            self.one_copy(which, slot).start()

    def after_one(self, slot):
        for which in range(2):
            self.one_copy(which, slot).wait()
            for side in range(2):
                at = (slot, side, self.x, self.core) if which == 0 else (slot, self.y, side, self.core)
                add_into(self.grads[which], at, self.got_one[which][slot, side])
            self.two_copy(which, slot).start()

    def after_two(self, slot):
        sums = []
        for which in range(2):
            self.two_copy(which, slot).wait()
            own = self.grads[which][slot, self.y, self.x, self.core].astype(F32)
            sums.append((own + self.got_two[which][slot].astype(F32)).astype(BF))
        return sums


def meet(devices):
    barrier = pltpu.get_barrier_semaphore()
    for device in devices:
        pl.semaphore_signal(barrier, inc=1, device_id=device, device_id_type=MESH)
    pl.semaphore_wait(barrier, len(devices))


def expert_kernel(
    remote,
    x_ref,
    att_ref,
    dy_ref,
    w_out_ref,
    gain_ref,
    shift_ref,
    bias_ref,
    up_v_ref,
    down_v_ref,
    up_t_ref,
    down_t_ref,
    out_ref,
    dmid_ref,
    datt_ref,
    dwout_ref,
    vec_ref,
    dup_ref,
    ddown_ref,
    hid_t,
    dy_t,
    acc_o,
    acc_h,
    up_w,
    down_w,
    act,
    gup,
    dup_buf,
    ddown_buf,
    sems,
    *more,
):
    mid, hid = dmid_ref, datt_ref
    rows, width = mid.shape
    cols = act.shape[1]
    is_text = lax.axis_index("stream") == 3
    pieces = 8 if remote else 1
    piece = cols // pieces
    ff = up_v_ref.shape[1]

    x_copy = pltpu.make_async_copy(x_ref, act.at[:, 0:width], sems.at[2, 0])
    x_copy.start()

    def fetch(j, slot):
        def go(up_src, down_src):
            for d in range(pieces):
                at = pl.ds(pl.multiple_of(j * piece + d * (ff // pieces), 128), piece)
                here = pl.ds(d * piece, piece)
                pltpu.make_async_copy(
                    up_src.at[:, at], up_w.at[slot, :, here], sems.at[0, slot]
                ).start()
                pltpu.make_async_copy(
                    down_src.at[at, :], down_w.at[slot, here, :], sems.at[1, slot]
                ).start()

        pl.when(is_text)(lambda: go(up_t_ref, down_t_ref))
        pl.when(jnp.logical_not(is_text))(lambda: go(up_v_ref, down_v_ref))

    def fetched(slot):
        pltpu.make_async_copy(up_w.at[slot], up_w.at[slot], sems.at[0, slot]).wait()
        pltpu.make_async_copy(down_w.at[slot], down_w.at[slot], sems.at[1, slot]).wait()

    fetch(0, 0)
    if remote:
        got, got_one, got_two, sum_sems = more[0:2], more[2:4], more[4:6], more[6]
        total = ItemSum(dup_buf, ddown_buf, got, got_one, got_two, sum_sems)
        meet([{"dp": total.near}, {"dp": total.over_x}, {"dp": total.over_y}])
    x_copy.wait()
    part_rows = rows // PARTS

    @pl.loop(0, PARTS)
    def _(part):
        at = pl.ds(pl.multiple_of(part * part_rows, 16), part_rows)
        middle = act[at, 0:width].astype(F32) + dot(att_ref[at], w_out_ref[...])
        mid[at] = middle
        normed, _ = normalize(middle)
        hid[at] = (normed * gain_ref[...] + shift_ref[...]).astype(BF)
        acc_o[at] = middle + bias_ref[...]
        acc_h[at] = jnp.zeros_like(middle)

    hid_t[...] = hid[...].T
    dy_t[...] = dy_ref[...].T

    def deliver(slot, j):
        up, down = total.after_two(slot)
        for t in range(4):
            dup_ref[t, j] = up[:, t * (cols // 4) : (t + 1) * (cols // 4)]
            ddown_ref[t, j] = down[t * (width // 4) : (t + 1) * (width // 4)]

    def stored(j, slot):
        return (
            pltpu.make_async_copy(dup_buf.at[slot], dup_ref.at[j], sems.at[3, slot]),
            pltpu.make_async_copy(ddown_buf.at[slot], ddown_ref.at[j], sems.at[4, slot]),
        )

    @pl.loop(0, STEPS)
    def _(j):
        slot = lax.rem(j, 2)
        other = 1 - slot
        pl.when(j < STEPS - 1)(lambda: fetch(j + 1, other))
        fetched(slot)

        @pl.loop(0, PARTS)
        def _(part):
            at = pl.ds(pl.multiple_of(part * part_rows, 16), part_rows)
            up = dot(hid[at], up_w[slot])
            grad = dot_t(dy_ref[at], down_w[slot])
            cdf, pdf = gelu_parts(up)
            activ = (up * cdf).astype(BF)
            grad_up = (grad * (cdf + up * pdf)).astype(BF)
            act[at] = activ
            gup[at] = grad_up
            acc_o[at] += dot(activ, down_w[slot])
            acc_h[at] += dot_t(grad_up, up_w[slot])
            if remote:

                @pl.when(part == 0)
                def _():
                    pl.when(j > 1)(lambda: deliver(slot, j - 2))
                    pl.when(j > 0)(lambda: total.after_core(other))

        if not remote:

            @pl.when(j > 1)
            def _():
                for copy in stored(j - 2, slot):
                    copy.wait()

        grad = dot(hid_t[...], gup[...]).astype(BF)
        if remote:
            dup_buf[slot] = grad.reshape(dup_buf.shape[1:])
            total.start(0, slot)
            pl.when(j > 0)(lambda: total.after_one(other))
        else:
            dup_buf[slot] = grad
        grad = dot(dy_t[...], act[...]).astype(BF)
        if remote:
            for d in range(8):
                ddown_buf[slot, d // 4, d // 2 % 2, d % 2] = grad[:, d * piece : (d + 1) * piece]
            total.start(1, slot)
        else:
            ddown_buf[slot] = grad
            for copy in stored(j, slot):
                copy.start()

    last = (STEPS - 1) % 2
    vec_ref[...] = jnp.zeros_like(vec_ref)

    @pl.loop(0, PARTS)
    def _(part):
        at = pl.ds(pl.multiple_of(part * part_rows, 16), part_rows)
        out_ref[at] = acc_o[at].astype(BF)
        normed, inverse = normalize(mid[at])
        grad = acc_h[at]
        wide = dy_ref[at].astype(F32)
        vec_ref[0:1, :] += jnp.sum(grad * normed, axis=0, keepdims=True)
        vec_ref[1:2, :] += jnp.sum(grad, axis=0, keepdims=True)
        vec_ref[2:3, :] += jnp.sum(wide, axis=0, keepdims=True)
        grad_mid = wide + norm_back(grad, normed, inverse, gain_ref[...])
        dmid_ref[at] = grad_mid
        branch = grad_mid.astype(BF)
        gup[at, 0:width] = branch
        datt_ref[at] = dot_t(branch, w_out_ref[...]).astype(BF)
        if remote:

            @pl.when(part == 0)
            def _():
                deliver(1 - last, STEPS - 2)
                total.after_core(last)

    dwout_ref[...] = t_dot(att_ref[...], gup[:, 0:width]).astype(BF)
    if remote:
        total.after_one(last)
        deliver(last, STEPS - 1)
    else:
        for j in range(STEPS - 2, STEPS):
            for copy in stored(j, j % 2):
                copy.wait()


def expert(remote, x, att, dy, w_out, gain, shift, bias, vis_up, vis_down, txt_up, txt_down):
    rows, width = x.shape
    cols = vis_up.shape[1] // STEPS
    if remote:
        shard, piece = width // 8, cols // 8
        buffers = (2, 2, 2, 2, shard, cols), (2, 2, 2, 2, width, piece)
        outs = (4, STEPS, shard, cols // 4), (4, STEPS, width // 4, piece)
        more = [
            pltpu.VMEM((2, 2, 2, shard, cols), BF),
            pltpu.VMEM((2, 2, 2, width, piece), BF),
            pltpu.VMEM((2, 2, shard, cols), BF),
            pltpu.VMEM((2, 2, width, piece), BF),
            pltpu.VMEM((2, shard, cols), BF),
            pltpu.VMEM((2, width, piece), BF),
            pltpu.SemaphoreType.DMA((3, 2, 2, 2)),
        ]
        params = dict(collective_id=1, has_side_effects=True)
    else:
        buffers = ((2, width, cols),) * 2
        outs = ((STEPS, width, cols),) * 2
        more, params = [], {}
    return pl.pallas_call(
        functools.partial(expert_kernel, remote),
        in_specs=[HBM] + [FULL] * 6 + [HBM] * 4,
        out_specs=[FULL] * 5 + [FULL if remote else HBM] * 2,
        out_shape=[
            jax.ShapeDtypeStruct((rows, width), BF),
            jax.ShapeDtypeStruct((rows, width), F32),
            jax.ShapeDtypeStruct((rows, width), BF),
            jax.ShapeDtypeStruct((width, width), BF),
            jax.ShapeDtypeStruct((8, width), F32),
        ]
        + [jax.ShapeDtypeStruct(shape, BF) for shape in outs],
        scratch_shapes=[
            pltpu.VMEM((width, rows), BF),
            pltpu.VMEM((width, rows), BF),
            pltpu.VMEM((rows, width), F32),
            pltpu.VMEM((rows, width), F32),
            pltpu.VMEM((2, width, cols), BF),
            pltpu.VMEM((2, cols, width), BF),
            pltpu.VMEM((rows, cols), BF),
            pltpu.VMEM((rows, cols), BF),
            pltpu.VMEM(buffers[0], BF),
            pltpu.VMEM(buffers[1], BF),
            pltpu.SemaphoreType.DMA((5, 2)),
        ]
        + more,
        compiler_params=pltpu.CompilerParams(vmem_limit_bytes=63 * 2**20, **params),
        name="expert",
    )(x, att, dy, w_out, gain, shift, bias, vis_up, vis_down, txt_up, txt_down)


def project_back_kernel(x_ref, dqkv_ref, gain_ref, shift_ref, w_ref, dx_ref, dw_ref, vec_ref, acc):
    i = pl.program_id(0)
    gain = gain_ref[...]
    normed, inverse = normalize(x_ref[0].astype(F32))
    hidden = (normed * gain + shift_ref[...]).astype(BF)
    dqkv = dqkv_ref[0]
    grad = dot_t(dqkv, w_ref[...])
    dx_ref[0] = norm_back(grad, normed, inverse, gain).astype(BF)
    width = x_ref.shape[2]
    part = t_dot(hidden, dqkv)
    ones = jnp.ones((8, TILE), BF)
    sums = dot(ones, dqkv)[0:1]
    vec = jnp.concatenate(
        [
            jnp.sum(grad * normed, axis=0, keepdims=True),
            jnp.sum(grad, axis=0, keepdims=True),
            sums[:, :width],
            sums[:, 2 * width :],
        ],
        axis=0,
    )

    @pl.when(i == 0)
    def _():
        acc[...] = part
        vec_ref[0:4, :] = vec

    @pl.when(i > 0)
    def _():
        acc[...] += part
        vec_ref[0:4, :] += vec

    @pl.when(i == pl.num_programs(0) - 1)
    def _():
        dw_ref[...] = acc[...].astype(BF)


def project_back(x_tiles, dqkv, gain, shift, w_qkv):
    tiles, _, width = x_tiles.shape

    def block(*shape):
        return pl.BlockSpec((1,) + shape, lambda i: (i,) + (0,) * len(shape))

    return pl.pallas_call(
        project_back_kernel,
        grid=(tiles,),
        in_specs=[block(TILE, width), block(TILE, 3 * width), FULL, FULL, FULL],
        out_specs=[block(TILE, width), FULL, FULL],
        out_shape=[
            jax.ShapeDtypeStruct((tiles, TILE, width), BF),
            jax.ShapeDtypeStruct((width, 3 * width), BF),
            jax.ShapeDtypeStruct((8, width), F32),
        ],
        scratch_shapes=[pltpu.VMEM((width, 3 * width), F32)],
        compiler_params=pltpu.CompilerParams(vmem_limit_bytes=56 * 2**20),
        name="project_back",
    )(x_tiles, dqkv, gain, shift, w_qkv)


GROUP = 256
GROUPS = 3
BLOCK = 128


def stream_blocks(count, share):
    spans = []
    for t in range(4):
        first, last = t * share // BLOCK, ((t + 1) * share - 1) // BLOCK
        spans.append(list(range(first, last + 1)))
    assert spans[-1][-1] == count - 1
    return spans


def unit_blocks(unit):
    if unit == 0:
        return list(range(6))
    g = unit - 1
    return [6 * part + 2 * g + i for part in range(3) for i in range(2)]


def back_kernel(
    x_ref,
    qkv_ref,
    p_ref,
    att_ref,
    inv_ref,
    datt_ref,
    dmid_ref,
    gain_ref,
    shift_ref,
    w_ref,
    dwout_ref,
    zup_ref,
    zdown_ref,
    vec2_ref,
    picks_ref,
    places_ref,
    dx_ref,
    vecs_ref,
    dqkv_ref,
    dout_ref,
    dvup_ref,
    dvdown_ref,
    dtup_ref,
    dtdown_ref,
    qkv,
    x,
    att,
    inv,
    datt,
    base,
    probs,
    hid_t,
    dqkv,
    acc,
    grad_hid,
    extra,
    mine,
    got_rows,
    buf_a,
    buf_b,
    got_a,
    got_b,
    one_a,
    one_b,
    two_a,
    two_b,
    held,
    got_qkv,
    got_out,
    got_up,
    got_down,
    vec,
    got_vec,
    z_vec,
    load_sems,
    p_sems,
    sum_sems,
    row_send,
    row_recv,
    vec_sems,
    zvec_send,
    zvec_recv,
    expert_send,
    expert_recv,
    block_send,
    block_recv,
):
    micros = qkv.shape[0] // TILES
    width = x.shape[2]
    shard = width // 8
    own_z = lax.axis_index("stream")
    is_text = own_z == 3
    total = ItemSum(buf_a, buf_b, (got_a, got_b), (one_a, one_b), (two_a, two_b), sum_sems)

    def loads(m):
        at = pl.ds(m * TILES, TILES)
        rows = pl.ds(m * TILES * OWN, TILES * OWN)
        return [
            pltpu.make_async_copy(qkv_ref.at[at], qkv.at[at], load_sems.at[m, 0]),
            pltpu.make_async_copy(datt_ref.at[at], datt.at[at], load_sems.at[m, 1]),
            pltpu.make_async_copy(inv_ref.at[at], inv.at[at], load_sems.at[m, 2]),
            pltpu.make_async_copy(att_ref.at[at], att.at[at], load_sems.at[m, 3]),
            pltpu.make_async_copy(x_ref.at[at], x.at[at], load_sems.at[m, 4]),
            pltpu.make_async_copy(dmid_ref.at[rows], base.at[rows], load_sems.at[m, 5]),
        ]

    def probs_load(m, g, slot):
        src = p_ref.at[pl.ds(m * TILES, TILES), pl.ds(g * 4, 4)]
        return pltpu.make_async_copy(src, probs.at[slot], p_sems.at[slot])

    probs_load(0, 0, 0).start()
    for m in range(micros):
        for copy in loads(m):
            copy.start()
    meet(
        [{"dp": total.near}, {"dp": total.over_x}, {"dp": total.over_y}]
        + [{"stream": lax.rem(own_z + k, 4)} for k in range(1, 4)]
    )

    def expert_copy(t, which):
        src, dst = ((zup_ref, got_up), (zdown_ref, got_down))[which]
        return pltpu.make_async_remote_copy(
            src_ref=src.at[t],
            dst_ref=dst.at[own_z],
            send_sem=expert_send.at[t, which],
            recv_sem=expert_recv.at[own_z, which],
            device_id={"stream": t},
            device_id_type=MESH,
        )

    def expert_arrival(src, which):
        dst = (got_up, got_down)[which]
        return pltpu.make_async_remote_copy(
            src_ref=dst.at[src],
            dst_ref=dst.at[src],
            send_sem=expert_send.at[src, which],
            recv_sem=expert_recv.at[src, which],
            device_id={"stream": src},
            device_id_type=MESH,
        )

    for t in range(4):

        @pl.when(own_z != t)
        def _():
            expert_copy(t, 0).start()
            expert_copy(t, 1).start()

        @pl.when(own_z == t)
        def _():
            for which in range(2):
                src, dst = ((zup_ref, got_up), (zdown_ref, got_down))[which]
                pltpu.make_async_copy(src.at[t], dst.at[t], expert_send.at[t, which]).start()

    half = buf_a.shape[-1]

    def put_unit(unit, value):
        slot = lax.rem(unit, 2)
        buf_a[slot] = value[:, :half].reshape(buf_a.shape[1:])
        buf_b[slot] = value[:, half:].reshape(buf_b.shape[1:])
        total.start(0, slot)
        total.start(1, slot)

    def take_unit(unit):
        left, right = total.after_two(lax.rem(unit, 2))
        for n in range(3):
            held[unit, n] = left[:, n * BLOCK : (n + 1) * BLOCK]
            held[unit, n + 3] = right[:, n * BLOCK : (n + 1) * BLOCK]

    def block_copy(unit, n, t, place):
        dst = got_out if unit == 0 else got_qkv
        kind = 0 if unit == 0 else 1
        return pltpu.make_async_remote_copy(
            src_ref=held.at[unit, n],
            dst_ref=dst.at[own_z, place],
            send_sem=block_send.at[kind, t, place],
            recv_sem=block_recv.at[kind, own_z, place],
            device_id={"stream": t},
            device_id_type=MESH,
        )

    out_spans = stream_blocks(6, width // 4)
    qkv_spans = stream_blocks(18, 3 * width // 4)

    def unit_sends(unit, t):
        span = (out_spans if unit == 0 else qkv_spans)[t]
        blocks = unit_blocks(unit)
        return [(n, span.index(b)) for n, b in enumerate(blocks) if b in span]

    def send_unit(unit):
        for t in range(4):

            @pl.when(own_z != t)
            def _():
                for n, place in unit_sends(unit, t):
                    block_copy(unit, n, t, place).start()

            @pl.when(own_z == t)
            def _():
                dst = got_out if unit == 0 else got_qkv
                for n, place in unit_sends(unit, t):
                    dst[t, place] = held[unit, n]

    put_unit(0, dwout_ref[...])

    def row_copy(m, s):
        return pltpu.make_async_remote_copy(
            src_ref=mine.at[m],
            dst_ref=got_rows.at[m, s],
            send_sem=row_send.at[m],
            recv_sem=row_recv.at[m, s],
            device_id={"stream": 3},
            device_id_type=MESH,
        )

    low, high = pair_lanes()
    gain = gain_ref[...]
    vec[...] = jnp.zeros_like(vec)

    def add_vec(row, value):
        for d in range(8):
            vec[d, row : row + 1, 0:shard] += value[:, d * shard : (d + 1) * shard]

    add_vec(4, vec2_ref[0:1, :])
    add_vec(5, vec2_ref[1:2, :])
    text_scale = jnp.where(is_text, 1.0, 0.0)
    add_vec(6, vec2_ref[2:3, :] * (1.0 - text_scale))
    add_vec(7, vec2_ref[2:3, :] * text_scale)

    steps = micros * GROUPS

    @pl.loop(0, steps)
    def _(step):
        m, g = lax.div(step, GROUPS), lax.rem(step, GROUPS)
        slot = lax.rem(step, 2)
        first = m * TILES

        @pl.when(step + 1 < steps)
        def _():
            after = step + 1
            probs_load(lax.div(after, GROUPS), lax.rem(after, GROUPS), 1 - slot).start()

        @pl.when(g == 0)
        def _():
            for copy in loads(m):
                copy.wait()
            for t in range(TILES):
                normed, _ = normalize(x[first + t].astype(F32))
                hidden = (normed * gain + shift_ref[...]).astype(BF)
                hid_t[:, t * TILE : (t + 1) * TILE] = hidden.T

        probs_load(m, g, slot).wait()

        def maker(t, pair):
            at = pl.multiple_of(g * GROUP + pair * BLOCK, BLOCK)
            cols = pl.ds(at, BLOCK)
            return lambda: attend_back_pair(
                *(qkv[first + t, :, pl.ds(part * width + at, BLOCK)] for part in range(3)),
                [probs[slot, t, 2 * pair], probs[slot, t, 2 * pair + 1]],
                att[first + t, :, cols],
                inv[first + t, :, cols],
                datt[first + t, :, cols],
                low,
                high,
            )

        def finish(n, results):
            t, pair = n // 2, n % 2
            for part, value in enumerate(results):
                at = part * GROUP + pair * BLOCK
                dqkv[t * TILE : (t + 1) * TILE, at : at + BLOCK] = value

        staggered([maker(n // 2, n % 2) for n in range(2 * TILES)], finish)

        @pl.when(step == 0)
        def _():
            total.after_core(0)

        @pl.when(step == 1)
        def _():
            total.after_one(0)

        @pl.when(step == 2)
        def _():
            take_unit(0)
            send_unit(0)

        @pl.when(step == steps - 2)
        def _():
            total.after_core(1)

        @pl.when(step == steps - 1)
        def _():
            total.after_one(1)
            total.after_core(0)

        part_w = dot(hid_t[...], dqkv[...])

        @pl.when(m == 0)
        def _():
            acc[g] = part_w

        @pl.when(jnp.logical_and(m > 0, m < micros - 1))
        def _():
            acc[g] += part_w

        pl.when(step == steps - 1)(lambda: take_unit(1))

        @pl.when(m == micros - 1)
        def _():
            put_unit(1 + g, (acc[g] + part_w).astype(BF))

        pl.when(step == steps - 1)(lambda: send_unit(1))

        grad = None
        for part in range(3):
            cols = pl.ds(pl.multiple_of(part * width + g * GROUP, GROUP), GROUP)
            piece = dot_t(dqkv[:, part * GROUP : (part + 1) * GROUP], w_ref[:, cols])
            grad = piece if grad is None else grad + piece

        @pl.when(g == 0)
        def _():
            grad_hid[...] = grad

        @pl.when(g > 0)
        def _():
            grad_hid[...] += grad

        ones = jnp.ones((8, TILES * TILE), BF)
        sums = dot(ones, dqkv[...])[0:1]
        for row, at in ((2, 0), (3, 2 * GROUP)):
            for d in range(8):
                lo, hi = max(d * shard, 0), (d + 1) * shard
                for h in range(GROUPS):
                    a, b = max(lo, h * GROUP), min(hi, (h + 1) * GROUP)
                    if a < b:

                        @pl.when(g == h)
                        def _():
                            vec[d, row : row + 1, a - lo : b - lo] += sums[
                                :, at + a - h * GROUP : at + b - h * GROUP
                            ]

        @pl.when(g == GROUPS - 1)
        def _():
            for t in range(TILES):
                normed, inverse = normalize(x[first + t].astype(F32))
                grad = grad_hid[t * TILE : (t + 1) * TILE]
                add_vec(0, jnp.sum(grad * normed, axis=0, keepdims=True))
                add_vec(1, jnp.sum(grad, axis=0, keepdims=True))
                back = norm_back(grad, normed, inverse, gain)
                rows = pl.ds(pl.multiple_of((m * TILES + t) * OWN, 16), OWN)
                base[rows] += back[:OWN]
                extra[m, t * (TILE - OWN) : (t + 1) * (TILE - OWN)] = back[OWN:].astype(BF)

            @pl.when(jnp.logical_not(is_text))
            def _():
                mine[m] = t_dot(places_ref[m], extra[m]).astype(BF)
                for s in range(3):

                    @pl.when(own_z == s)
                    def _():
                        row_copy(m, s).start()

    def vec_copy(stage):
        device = (total.near, total.over_x, total.over_y)[stage]
        return pltpu.make_async_remote_copy(
            src_ref=vec,
            dst_ref=got_vec.at[stage],
            send_sem=vec_sems.at[stage, 0],
            recv_sem=vec_sems.at[stage, 1],
            device_id={"dp": device},
            device_id_type=MESH,
        )

    def vec_stage(stage):
        vec_copy(stage).wait()
        vec[...] += got_vec[stage]

    def zvec_copy(t):
        return pltpu.make_async_remote_copy(
            src_ref=vec.at[total.me],
            dst_ref=z_vec.at[own_z],
            send_sem=zvec_send.at[t],
            recv_sem=zvec_recv.at[own_z],
            device_id={"stream": t},
            device_id_type=MESH,
        )

    def zvec_arrival(s):
        return pltpu.make_async_remote_copy(
            src_ref=z_vec.at[s],
            dst_ref=z_vec.at[s],
            send_sem=zvec_send.at[s],
            recv_sem=zvec_recv.at[s],
            device_id={"stream": s},
            device_id_type=MESH,
        )

    vec_copy(0).start()
    total.after_one(0)
    total.after_core(1)
    vec_stage(0)
    vec_copy(1).start()

    rows_all = TILES * OWN
    flat = TILES * PATCHES
    row = lax.broadcasted_iota(jnp.int32, (flat, rows_all), 0)
    place = lax.broadcasted_iota(jnp.int32, (flat, rows_all), 1)
    third = (row >= PATCHES).astype(jnp.int32) + (row >= 2 * PATCHES).astype(jnp.int32)
    unpad = (place == row + third * (OWN - PATCHES)).astype(F32).astype(BF)

    def deliver(m, scattered):
        rows = pl.ds(m * rows_all, rows_all)
        value = base[rows]
        if scattered:
            value = value + t_dot(
                picks_ref[m], jnp.concatenate([got_rows[m, s] for s in range(3)] + [extra[m]], axis=0)
            )
        dx_ref[m] = dot(unpad, value.astype(BF)).astype(BF)

    @pl.when(jnp.logical_not(is_text))
    def _():
        for m in range(micros - 1):
            deliver(m, False)

    @pl.when(is_text)
    def _():
        for m in range(micros - 1):
            for s in range(3):
                row_copy(m, s).wait_recv()
            deliver(m, True)

    take_unit(2)
    send_unit(2)
    total.after_one(1)
    vec_stage(1)
    vec_copy(2).start()

    @pl.when(jnp.logical_not(is_text))
    def _():
        deliver(micros - 1, False)

    ff_piece = got_down.shape[3]
    for src in range(4):

        @pl.when(own_z != src)
        def _():
            for which in range(2):
                expert_arrival(src, which).wait_recv()
                expert_copy(src, which).wait_send()

        @pl.when(own_z == src)
        def _():
            for which in range(2):
                ref, dst = ((zup_ref, got_up), (zdown_ref, got_down))[which]
                pltpu.make_async_copy(ref.at[src], dst.at[src], expert_send.at[src, which]).wait()

    for j in range(STEPS):
        vis = sum(got_up[s, j].astype(F32) for s in range(3))
        txt = got_up[3, j].astype(F32)
        for d in range(2):
            at = (d * STEPS + j) * ff_piece
            dvup_ref[:, at : at + ff_piece] = vis[:, d * ff_piece : (d + 1) * ff_piece]
            dtup_ref[:, at : at + ff_piece] = txt[:, d * ff_piece : (d + 1) * ff_piece]
        at = j * ff_piece
        dvdown_ref[at : at + ff_piece] = sum(got_down[s, j].astype(F32) for s in range(3)).T
        dtdown_ref[at : at + ff_piece] = got_down[3, j].astype(F32).T

    take_unit(3)
    send_unit(3)
    vec_stage(2)
    for t in range(4):
        pl.when(own_z != t)(lambda: zvec_copy(t).start())

        @pl.when(own_z == t)
        def _():
            z_vec[t] = vec[total.me]

    @pl.when(is_text)
    def _():
        for s in range(3):
            row_copy(micros - 1, s).wait_recv()
        deliver(micros - 1, True)

    @pl.when(jnp.logical_not(is_text))
    def _():
        for m in range(micros):
            row_copy(m, 0).wait_send()

    for src in range(4):

        @pl.when(own_z != src)
        def _():
            zvec_arrival(src).wait_recv()
            zvec_copy(src).wait_send()
            for unit in range(GROUPS + 1):
                for n, place in unit_sends(unit, src):
                    block_copy(unit, n, src, place).wait_send()
            for kind, dst in ((0, got_out), (1, got_qkv)):
                for place in range(dst.shape[1]):
                    pltpu.make_async_remote_copy(
                        src_ref=dst.at[src, place],
                        dst_ref=dst.at[src, place],
                        send_sem=block_send.at[kind, src, place],
                        recv_sem=block_recv.at[kind, src, place],
                        device_id={"stream": src},
                        device_id_type=MESH,
                    ).wait_recv()

    vecs_ref[...] = sum(z_vec[s] for s in range(4))
    odd = lax.rem(own_z, 2) == 1
    for got, out in ((got_qkv, dqkv_ref), (got_out, dout_ref)):
        blocks = [
            sum(got[s, n].astype(F32) for s in range(4)) for n in range(got.shape[1])
        ]
        whole = jnp.concatenate(blocks, axis=1)
        moved = pltpu.roll(whole, whole.shape[1] - BLOCK // 2, 1)
        out[...] = jnp.where(odd, moved, whole)[:, : out.shape[1]]


def back(x_tiles, qkv, probs, att, inv, datt, dmid, gain, shift, w_qkv, dwout, zup, zdown, vec2, picks, places):
    tiles, _, width = x_tiles.shape
    micros = tiles // TILES
    shard = width // 8
    half = width // 2
    ff = 4 * 2 * STEPS * zdown.shape[3]
    flat = TILES * PATCHES

    def sds(*shape, dtype=F32):
        return jax.ShapeDtypeStruct(shape, dtype)

    dma = pltpu.SemaphoreType.DMA
    return pl.pallas_call(
        back_kernel,
        in_specs=[HBM] * 7 + [FULL] * 4 + [HBM] * 2 + [FULL] * 3,
        out_specs=[FULL] * 8,
        out_shape=[
            sds(micros, flat, width, dtype=BF),
            sds(8, BLOCK),
            sds(shard, 3 * width // 4),
            sds(shard, width // 4),
            sds(shard, ff // 4),
            sds(ff // 8, width // 4),
            sds(shard, ff // 4),
            sds(ff // 8, width // 4),
        ],
        scratch_shapes=[
            pltpu.VMEM((tiles, TILE, 3 * width), BF),
            pltpu.VMEM((tiles, TILE, width), BF),
            pltpu.VMEM((tiles, TILE, width), BF),
            pltpu.VMEM((tiles, TILE, width), BF),
            pltpu.VMEM((tiles, TILE, width), BF),
            pltpu.VMEM((tiles * OWN, width), F32),
            pltpu.VMEM((2, TILES, 4, TILE, TILE), BF),
            pltpu.VMEM((width, TILES * TILE), BF),
            pltpu.VMEM((TILES * TILE, 3 * GROUP), BF),
            pltpu.VMEM((GROUPS, width, 3 * GROUP), F32),
            pltpu.VMEM((TILES * TILE, width), F32),
            pltpu.VMEM((micros, TILES * (TILE - OWN), width), BF),
            pltpu.VMEM((micros, 2 * SLOT, width), BF),
            pltpu.VMEM((micros, 3, 2 * SLOT, width), BF),
            pltpu.VMEM((2, 2, 2, 2, shard, half), BF),
            pltpu.VMEM((2, 2, 2, 2, shard, half), BF),
            pltpu.VMEM((2, 2, 2, shard, half), BF),
            pltpu.VMEM((2, 2, 2, shard, half), BF),
            pltpu.VMEM((2, 2, shard, half), BF),
            pltpu.VMEM((2, 2, shard, half), BF),
            pltpu.VMEM((2, shard, half), BF),
            pltpu.VMEM((2, shard, half), BF),
            pltpu.VMEM((GROUPS + 1, 6, shard, BLOCK), BF),
            pltpu.VMEM((4, 5, shard, BLOCK), BF),
            pltpu.VMEM((4, 2, shard, BLOCK), BF),
            pltpu.VMEM((4,) + zup.shape[1:], BF),
            pltpu.VMEM((4,) + zdown.shape[1:], BF),
            pltpu.VMEM((8, 8, BLOCK), F32),
            pltpu.VMEM((3, 8, 8, BLOCK), F32),
            pltpu.VMEM((4, 8, BLOCK), F32),
            dma((micros, 6)),
            dma((2,)),
            dma((3, 2, 2, 2)),
            dma((micros,)),
            dma((micros, 3)),
            dma((3, 2)),
            dma((4,)),
            dma((4,)),
            dma((4, 2)),
            dma((4, 2)),
            dma((2, 4, 5)),
            dma((2, 4, 5)),
        ],
        compiler_params=pltpu.CompilerParams(
            vmem_limit_bytes=63 * 2**20, collective_id=2, has_side_effects=True
        ),
        name="back",
    )(x_tiles, qkv, probs, att, inv, datt, dmid, gain, shift, w_qkv, dwout, zup, zdown, vec2, picks, places)


def pad_rows(block):
    micro, rows, width = block.shape
    thirds = block.reshape(micro, TILES, PATCHES, width)
    thirds = jnp.pad(thirds, ((0, 0), (0, 0), (0, OWN - PATCHES), (0, 0)))
    return thirds.reshape(micro, TILES * OWN, width)


def unpad_rows(block):
    micro, _, width = block.shape
    thirds = block.reshape(micro, TILES, OWN, width)[:, :, :PATCHES]
    return thirds.reshape(micro, TILES * PATCHES, width)


def plan(lengths, pairs, is_text, own_stream):
    micro, items = lengths.shape
    finish = jnp.cumsum(lengths, axis=1)
    starts = finish - lengths
    numbers = jnp.arange(items, dtype=jnp.int32)
    match = pairs[:, :, None] == numbers
    start = jnp.sum(jnp.where(match, starts[:, None, :], 0), axis=2).reshape(micro, 3, TILES)
    length = jnp.sum(jnp.where(match, lengths[:, None, :], 0), axis=2).reshape(micro, 3, TILES)
    paired = (pairs >= 0).reshape(micro, 3, TILES)
    rank = jnp.where(paired, jnp.cumsum(paired.astype(jnp.int32), axis=2) - 1, -1)
    takes = rank[:, :, :, None] == jnp.arange(2)
    slot_start = jnp.sum(jnp.where(takes, start[..., None], 0), axis=2)
    slot_length = jnp.sum(jnp.where(takes, length[..., None], 0), axis=2)
    step = jnp.arange(SLOT, dtype=jnp.int32)
    slot_rows = jnp.where(step < slot_length[..., None], slot_start[..., None] + step, -1)
    pad = jnp.arange(TILE - OWN, dtype=jnp.int32)
    next_rows = PATCHES * jnp.arange(1, TILES + 1, dtype=jnp.int32)[:, None] + pad
    next_rows = jnp.where((pad < SLOT) & (next_rows < TILES * PATCHES), next_rows, -1)
    next_rows = jnp.broadcast_to(next_rows, (micro, TILES, TILE - OWN))
    wanted = jnp.concatenate([slot_rows.reshape(micro, -1), next_rows.reshape(micro, -1)], axis=1)
    place = jnp.arange(TILES * OWN, dtype=jnp.int32)
    row_at = jnp.where(place % OWN < PATCHES, place // OWN * PATCHES + place % OWN, -2)
    picks = (wanted[:, :, None] == row_at).astype(BF)
    item_paired = jnp.any(match, axis=1)
    rows = jnp.arange(TILES * PATCHES + SLOT, dtype=jnp.int32)
    member = (rows[:, None] >= starts[:, None, :]) & (rows[:, None] < finish[:, None, :])
    code = jnp.where(item_paired, -1, numbers + items * (starts // PATCHES))
    row_code = jnp.sum(jnp.where(member, code[:, None, :] + 1, 0), axis=2) - 1
    tile = jnp.arange(TILES, dtype=jnp.int32)[:, None]
    own_code = row_code[:, : TILES * PATCHES].reshape(micro, TILES, PATCHES)
    next_code = jnp.stack(
        [row_code[:, PATCHES * (t + 1) : PATCHES * (t + 1) + SLOT] for t in range(TILES)], axis=1
    )

    def here(codes):
        return jnp.where((codes >= 0) & (codes // items == tile), codes, -1)

    def lay(own, extra):
        gap = jnp.full((micro, TILES, OWN - PATCHES), -1, jnp.int32)
        end = jnp.full((micro, TILES, TILE - OWN - SLOT), -1, jnp.int32)
        return jnp.concatenate([own, gap, extra, end], axis=2)

    text_ids = lay(here(own_code), here(next_code))
    own_length = lax.dynamic_index_in_dim(length, jnp.minimum(own_stream, 2), 1, keepdims=False)
    own_takes = lax.dynamic_index_in_dim(takes, jnp.minimum(own_stream, 2), 1, keepdims=False)
    image_ids = lay(
        jnp.zeros((micro, TILES, PATCHES), jnp.int32),
        jnp.where(step < own_length[..., None], 0, -1),
    )
    ids = jnp.where(is_text, text_ids, image_ids)
    own_takes = own_takes.astype(BF)
    same = (pad[:, None] == step).astype(BF)
    places = own_takes[:, :, None, :, None] * same[:, None, :]
    places = places.reshape(micro, TILES * (TILE - OWN), 2 * SLOT)
    return picks, places, own_takes, ids.reshape(micro * TILES, 1, TILE)


def spread(padded, picks, own_takes, is_text):
    micro, _, width = padded.shape
    picked = lax.dot_general(
        picks, padded, (((2,), (1,)), ((0,), (0,))), preferred_element_type=F32
    ).astype(BF)
    near = picked[:, 6 * SLOT :].reshape(micro, TILES, TILE - OWN, width)[:, :, :SLOT]
    sent = picked[:, : 6 * SLOT].reshape(micro, 3, 2 * SLOT, width)
    far = sum(lax.ppermute(sent[:, s], "stream", [(3, s)]) for s in range(3))
    far = far.reshape(micro, 1, 2, SLOT, width) * own_takes[:, :, :, None, None]
    return jnp.where(is_text, near, far[:, :, 0] + far[:, :, 1])


def collect(extra, picks, own_takes, is_text):
    micro, _, _, width = extra.shape
    mine = extra[:, :, None] * own_takes[:, :, :, None, None]
    mine = (mine[:, 0] + mine[:, 1] + mine[:, 2]).reshape(micro, 2 * SLOT, width)
    parts = [lax.ppermute(mine, "stream", [(s, 3)]) for s in range(3)]
    extra = jnp.pad(extra, ((0, 0), (0, 0), (0, TILE - OWN - SLOT), (0, 0)))
    parts.append(extra.reshape(micro, TILES * (TILE - OWN), width))
    rows = jnp.concatenate(parts, axis=1)
    scale = jnp.where(is_text, 1.0, 0.0).astype(BF)
    return lax.dot_general(
        picks * scale, rows, (((1,), (1,)), ((0,), (0,))), preferred_element_type=F32
    ).astype(BF)


def reduce_all(vectors, dw_qkv, dw_out, dup, ddown):
    width = dw_qkv.shape[0]
    shard = width // lax.axis_size("dp")
    vectors = lax.psum(vectors, ("dp", "stream"))
    vectors = lax.dynamic_slice_in_dim(vectors, lax.axis_index("dp") * shard, shard, axis=1)

    def over_items(grad, dim):
        return lax.psum_scatter(grad, "dp", scatter_dimension=dim, tiled=True)

    def over_blocks(grad):
        return lax.psum_scatter(grad, "stream", scatter_dimension=1, tiled=True).astype(F32)

    qkv = over_blocks(over_items(dw_qkv, 0))
    out = over_blocks(over_items(dw_out, 0))
    dup = over_items(jnp.concatenate(list(dup), axis=1), 0)
    ddown = over_items(jnp.concatenate(list(ddown), axis=1), 1)
    up = dup.reshape(dup.shape[0], 4, -1).transpose(1, 0, 2)
    down = ddown.reshape(4, -1, ddown.shape[1])
    up = lax.all_to_all(up, "stream", 0, 0).astype(F32)
    down = lax.all_to_all(down, "stream", 0, 0).astype(F32)
    return (
        vectors,
        qkv,
        out,
        up[0] + up[1] + up[2],
        (down[0] + down[1] + down[2]).T,
        up[3],
        down[3].T,
    )


def shards(
    remote,
    tokens,
    text_lengths,
    pair_text,
    ln1_gain,
    ln1_bias,
    w_qkv,
    q_bias,
    v_bias,
    w_out,
    ln2_gain,
    ln2_bias,
    vis_up,
    vis_down,
    vis_bias,
    txt_up,
    txt_down,
    txt_bias,
    cotangent,
):
    micro = tokens.shape[0]
    width = tokens.shape[4]
    own_stream = lax.axis_index("stream")
    is_text = own_stream == 3
    gain1, shift1, gain2, shift2 = (
        v.astype(F32)[None] for v in (ln1_gain, ln1_bias, ln2_gain, ln2_bias)
    )
    bias = jnp.where(is_text, txt_bias, vis_bias).astype(F32)[None]
    qkv_bias = jnp.concatenate([q_bias, jnp.zeros_like(q_bias), v_bias]).astype(F32)[None]
    picks, places, own_takes, ids = plan(text_lengths[:, 0], pair_text[:, 0], is_text, own_stream)

    def tiled(own, extra):
        own = own.reshape(micro, TILES, OWN, width)
        extra = jnp.pad(extra, ((0, 0), (0, 0), (0, TILE - OWN - SLOT), (0, 0)))
        return jnp.concatenate([own, extra], axis=2).reshape(micro * TILES, TILE, width)

    def parted(tiles):
        tiles = tiles.reshape(micro, TILES, TILE, width)
        return tiles[:, :, :OWN].reshape(micro, TILES * OWN, width), tiles[:, :, OWN : OWN + SLOT]

    x = pad_rows(tokens[:, 0, 0])
    dy = pad_rows(cotangent[:, 0, 0])
    x_tiles = tiled(x, spread(x, picks, own_takes, is_text))
    qkv, att_tiles, probs, inverse = attend(x_tiles, ids, gain1, shift1, w_qkv, qkv_bias)
    att_own, att_extra = parted(att_tiles)
    att = att_own + collect(att_extra, picks, own_takes, is_text)
    flat = (micro * TILES * OWN, width)
    out, dmid, datt, dw_out, vec2, dup, ddown = expert(
        remote,
        x.reshape(flat),
        att.reshape(flat),
        dy.reshape(flat),
        w_out,
        gain2,
        shift2,
        bias,
        vis_up,
        vis_down,
        txt_up,
        txt_down,
    )
    datt = datt.reshape(micro, TILES * OWN, width)
    datt_tiles = tiled(datt, spread(datt, picks, own_takes, is_text))
    out = unpad_rows(out.reshape(micro, TILES * OWN, width)).reshape(tokens.shape)
    if remote:
        dx, vectors, g_qkv, g_out, g_vup, g_vdown, g_tup, g_tdown = back(
            x_tiles,
            qkv,
            probs,
            att_tiles,
            inverse,
            datt_tiles,
            dmid,
            gain1,
            shift1,
            w_qkv,
            dw_out,
            dup,
            ddown,
            vec2,
            picks,
            places,
        )
        vectors = vectors[:, : width // 8]
    else:
        dqkv = attend_back(qkv, probs, att_tiles, inverse, datt_tiles)
        dx_tiles, dw_qkv, vec1 = project_back(x_tiles, dqkv, gain1, shift1, w_qkv)
        dx_own, dx_extra = parted(dx_tiles)
        dx = (
            dmid.reshape(micro, TILES * OWN, width)
            + dx_own.astype(F32)
            + collect(dx_extra, picks, own_takes, is_text).astype(F32)
        )
        dx = unpad_rows(dx).astype(BF)
        text_scale = jnp.where(is_text, 1.0, 0.0)
        vectors = jnp.concatenate(
            [vec1[0:4], vec2[0:2], vec2[2:3] * (1.0 - text_scale), vec2[2:3] * text_scale], axis=0
        )
        vectors, g_qkv, g_out, g_vup, g_vdown, g_tup, g_tdown = reduce_all(
            vectors, dw_qkv, dw_out, dup, ddown
        )
    return (
        out,
        dx.reshape(tokens.shape),
        vectors[0],
        vectors[1],
        g_qkv,
        vectors[2],
        vectors[3],
        g_out,
        vectors[4],
        vectors[5],
        g_vup,
        g_vdown,
        vectors[6],
        g_tup,
        g_tdown,
        vectors[7],
    )


def solution(mesh):
    rows = P(None, "dp", "stream", None, None)
    lists = P(None, "dp", None)
    vector, matrix = P("dp"), P("dp", "stream")
    in_specs = (rows, lists, lists) + (P(),) * 14 + (rows,)
    out_specs = (
        rows,
        rows,
        vector,
        vector,
        matrix,
        vector,
        vector,
        matrix,
        vector,
        vector,
        matrix,
        matrix,
        vector,
        matrix,
        matrix,
        vector,
    )
    remote = mesh.shape["dp"] == 8
    body = functools.partial(shards, remote)
    return jax.shard_map(body, mesh=mesh, in_specs=in_specs, out_specs=out_specs, check_vma=False)
```

```python
import functools

import jax
import jax.numpy as jnp
from jax import lax
from jax.experimental import pallas as pl
from jax.experimental.pallas import tpu as pltpu
from jax.sharding import PartitionSpec as P

HEADS = 12
PATCHES = 197
OWN = 208
SLOT = 40
TILE = 256
TILES = 3
EPSILON = 1e-06
MASKED = -1e30
BF = jnp.bfloat16
F32 = jnp.float32
FULL = pl.BlockSpec(memory_space=pltpu.VMEM)
HBM = pl.BlockSpec(memory_space=pl.ANY)
MESH = pl.DeviceIdType.MESH
BLOCK = 128


def dot(left, right):
    return jnp.dot(left, right, preferred_element_type=F32)


def dot_t(left, right):
    return lax.dot_general(left, right, (((1,), (1,)), ((), ())), preferred_element_type=F32)


def t_dot(left, right):
    return lax.dot_general(left, right, (((0,), (0,)), ((), ())), preferred_element_type=F32)


def normalize(values):
    centred = values - jnp.mean(values, axis=-1, keepdims=True)
    inverse = lax.rsqrt(jnp.mean(centred * centred, axis=-1, keepdims=True) + EPSILON)
    return centred * inverse, inverse


def norm_back(grad, normed, inverse, gain):
    scaled = grad * gain
    return inverse * (
        scaled
        - jnp.mean(scaled, axis=-1, keepdims=True)
        - normed * jnp.mean(scaled * normed, axis=-1, keepdims=True)
    )


def gelu_parts(up):
    reach = jnp.abs(up) * 0.7071067811865476
    inner = 1.0 / (1.0 + 0.3275911 * reach)
    bell = jnp.exp(-0.5 * up * up)
    poly = inner * (
        0.254829592
        + inner
        * (-0.284496736 + inner * (1.421413741 + inner * (-1.453152027 + inner * 1.061405429)))
    )
    tail = 0.5 * poly * bell
    return jnp.where(up >= 0, 1.0 - tail, tail), bell * 0.3989422804014327


def halves(block, low, high):
    return jnp.concatenate([block * low, block * high], axis=0)


def pair_lanes():
    lane = lax.broadcasted_iota(jnp.int32, (1, 128), 1)
    return (lane < 64).astype(BF), (lane >= 64).astype(BF)


def attend_pair(q, k, v, barred, low, high):
    scores = dot_t(halves(k, low, high), q * 0.125)
    yield
    expos = []
    for side in range(2):
        part = scores[TILE * side : TILE * (side + 1)] + barred
        top = jnp.maximum(jnp.max(part, axis=0, keepdims=True), 0.1 * MASKED)
        expos.append(jnp.exp(part - top).astype(BF))
    ones = [jnp.broadcast_to(keep, (TILE, 128)) for keep in (low, high)]
    right = jnp.concatenate([halves(v, low, high), jnp.concatenate(ones, axis=0)], axis=1)
    sums = t_dot(jnp.concatenate(expos, axis=0), right)
    inverse = jnp.where(sums[:, 128:] > 0.0, 1.0 / sums[:, 128:], 0.0)
    yield expos, sums[:, :128] * inverse, inverse


def attend_back_pair(q, k, v, expos, out, inverse, grad, low, high):
    scaled = grad.astype(F32) * inverse.astype(F32)
    inner = (scaled * out.astype(F32)).astype(BF)
    scaled = scaled.astype(BF)
    minus = [jnp.broadcast_to(-keep, (TILE, 128)) for keep in (low, high)]
    right = jnp.concatenate([halves(v, low, high), jnp.concatenate(minus, axis=0)], axis=1)
    slopes = dot_t(right, jnp.concatenate([scaled, inner], axis=1))
    yield
    parts = [
        (expos[side].astype(F32) * slopes[TILE * side : TILE * (side + 1)]).astype(BF)
        for side in range(2)
    ]
    dq = t_dot(jnp.concatenate(parts, axis=0), halves(k, low, high)) * 0.125
    dk = dot(jnp.concatenate(parts, axis=1), halves(q * 0.125, low, high))
    dv = dot(jnp.concatenate(expos, axis=1), halves(scaled, low, high))
    yield dq.astype(BF), dk.astype(BF), dv.astype(BF)


def staggered(makers, finish):
    held = None
    for n, make in enumerate(makers):
        step = make()
        next(step)
        if held is not None:
            finish(n - 1, next(held))
        held = step
    finish(len(makers) - 1, next(held))


def bars(ids_ref):
    ids = jnp.broadcast_to(ids_ref, (TILE, TILE))
    return jnp.where((ids == ids.T) & (ids >= 0), 0.0, MASKED)


GAIN1, SHIFT1, Q_BIAS, V_BIAS, GAIN2, SHIFT2, VIS_BIAS, TXT_BIAS = range(8)


def row_of(vecs_ref, at):
    return vecs_ref[at : at + 1, :]


def project(values, vecs_ref, w_ref):
    normed, _ = normalize(values.astype(F32))
    hidden = (normed * row_of(vecs_ref, GAIN1) + row_of(vecs_ref, SHIFT1)).astype(BF)
    q_bias, v_bias = row_of(vecs_ref, Q_BIAS), row_of(vecs_ref, V_BIAS)
    bias = jnp.concatenate([q_bias, jnp.zeros_like(q_bias), v_bias], axis=1)
    return (dot(hidden, w_ref[...]) + bias).astype(BF)


def attend_kernel(x_ref, ids_ref, vecs_ref, w_ref, qkv_ref, out_ref, p_ref, inv_ref):
    width = x_ref.shape[2]
    qkv_ref[0] = project(x_ref[0], vecs_ref, w_ref)
    barred = bars(ids_ref[0])
    low, high = pair_lanes()

    def maker(pair):
        cols = [qkv_ref[0, :, part * width + pair * 128 :][:, :128] for part in range(3)]
        return lambda: attend_pair(*cols, barred, low, high)

    def finish(pair, results):
        expos, out, inverse = results
        at = pair * 128
        for side in range(2):
            p_ref[0, 2 * pair + side] = expos[side]
        out_ref[0, :, at : at + 128] = out.astype(BF)
        inv_ref[0, :, at : at + 128] = inverse.astype(BF)

    staggered([maker(pair) for pair in range(HEADS // 2)], finish)


def attend(x_tiles, ids, vecs, w_qkv):
    tiles, _, width = x_tiles.shape

    def block(*shape):
        return pl.BlockSpec((1,) + shape, lambda i: (i,) + (0,) * len(shape))

    return pl.pallas_call(
        attend_kernel,
        grid=(tiles,),
        in_specs=[block(TILE, width), block(1, TILE), FULL, FULL],
        out_specs=[
            block(TILE, 3 * width),
            block(TILE, width),
            block(HEADS, TILE, TILE),
            block(TILE, width),
        ],
        out_shape=[
            jax.ShapeDtypeStruct((tiles, TILE, 3 * width), BF),
            jax.ShapeDtypeStruct((tiles, TILE, width), BF),
            jax.ShapeDtypeStruct((tiles, HEADS, TILE, TILE), BF),
            jax.ShapeDtypeStruct((tiles, TILE, width), BF),
        ],
        compiler_params=pltpu.CompilerParams(vmem_limit_bytes=56 * 2**20),
        name="attend",
    )(x_tiles, ids, vecs, w_qkv)


def third_of(row, size):
    return (row >= size).astype(jnp.int32) + (row >= 2 * size).astype(jnp.int32)


def padding(flip):
    rows, places = TILES * PATCHES, TILES * OWN
    shape = (rows, places) if flip else (places, rows)
    row = lax.broadcasted_iota(jnp.int32, shape, 0 if flip else 1)
    place = lax.broadcasted_iota(jnp.int32, shape, 1 if flip else 0)
    return (place == row + third_of(row, PATCHES) * (OWN - PATCHES)).astype(F32).astype(BF)


def attend_rows_kernel(
    tok_ref,
    picks_ref,
    places_ref,
    ids_ref,
    vecs_ref,
    w_hbm,
    x_out,
    qkv_out,
    p_out,
    inv_out,
    att_out,
    rows_ref,
    tok,
    w,
    x,
    qkv,
    probs,
    inv,
    att,
    sent,
    got,
    mine,
    got_back,
    tok_sems,
    w_sem,
    out_sems,
    p_sems,
    row_send,
    row_recv,
    back_send,
    back_recv,
):
    micros = tok.shape[0]
    width = tok.shape[2]
    own_z = lax.axis_index("stream")
    is_text = own_z == 3
    is_image = jnp.logical_not(is_text)
    side = TILE - OWN

    def tok_copy(m):
        return pltpu.make_async_copy(tok_ref.at[m], tok.at[m], tok_sems.at[m])

    for m in range(micros):
        tok_copy(m).start()
    w_copy = pltpu.make_async_copy(w_hbm, w, w_sem)
    w_copy.start()
    meet([{"stream": lax.rem(own_z + k, 4)} for k in range(1, 4)])

    def row_copy(m, s):
        return pltpu.make_async_remote_copy(
            src_ref=sent.at[m, s],
            dst_ref=got.at[m],
            send_sem=row_send.at[m, s],
            recv_sem=row_recv.at[m],
            device_id={"stream": s},
            device_id_type=MESH,
        )

    def back_copy(m, s):
        return pltpu.make_async_remote_copy(
            src_ref=mine.at[m],
            dst_ref=got_back.at[m, s],
            send_sem=back_send.at[m],
            recv_sem=back_recv.at[m, s],
            device_id={"stream": 3},
            device_id_type=MESH,
        )

    def outs(m):
        at = pl.ds(m * TILES, TILES)
        pairs = ((x, x_out), (qkv, qkv_out), (inv, inv_out), (att, att_out))
        return [
            pltpu.make_async_copy(src.at[at], dst.at[at], out_sems.at[m, n])
            for n, (src, dst) in enumerate(pairs)
        ]

    def probs_store(tile, slot):
        return pltpu.make_async_copy(probs.at[slot], p_out.at[tile], p_sems.at[slot])

    def own_rows(ref, m):
        return jnp.concatenate([ref[m * TILES + t, 0:OWN] for t in range(TILES)], axis=0)

    def beside(ref, m, value):
        for t in range(TILES):
            ref[m * TILES + t, OWN:TILE] = value[t * side : (t + 1) * side]

    pad = padding(False)
    for m in range(micros):
        tok_copy(m).wait()
        padded = dot(pad, tok[m]).astype(BF)
        for t in range(TILES):
            x[m * TILES + t, 0:OWN] = padded[t * OWN : (t + 1) * OWN]

        @pl.when(is_text)
        def _():
            picked = dot(picks_ref[m], own_rows(x, m)).astype(BF)
            for s in range(3):
                sent[m, s] = picked[s * 2 * SLOT : (s + 1) * 2 * SLOT]
                row_copy(m, s).start()
            beside(x, m, picked[6 * SLOT :])

    w_copy.wait()
    for m in range(micros):
        rows = project(own_rows(x, m), vecs_ref, w)
        for t in range(TILES):
            qkv[m * TILES + t, 0:OWN] = rows[t * OWN : (t + 1) * OWN]

    low, high = pair_lanes()

    @pl.loop(0, micros)
    def _(m):
        @pl.when(is_image)
        def _():
            row_copy(m, 0).wait_recv()
            beside(x, m, dot(places_ref[m], got[m]).astype(BF))

        extra = [x[m * TILES + t, OWN:TILE] for t in range(TILES)]
        beside(qkv, m, project(jnp.concatenate(extra, axis=0), vecs_ref, w))

        @pl.loop(0, TILES)
        def _(t):
            tile = m * TILES + t
            slot = lax.rem(tile, 2)
            pl.when(tile > 1)(lambda: probs_store(tile - 2, slot).wait())
            barred = bars(ids_ref[tile])

            def maker(pair):
                at = pair * BLOCK
                cols = [qkv[tile, :, pl.ds(part * width + at, BLOCK)] for part in range(3)]
                return lambda: attend_pair(*cols, barred, low, high)

            def finish(pair, results):
                expos, out, inverse = results
                at = pair * BLOCK
                for n in range(2):
                    probs[slot, 2 * pair + n] = expos[n]
                att[tile, :, at : at + BLOCK] = out.astype(BF)
                inv[tile, :, at : at + BLOCK] = inverse.astype(BF)

            staggered([maker(pair) for pair in range(HEADS // 2)], finish)
            probs_store(tile, slot).start()

        for copy in outs(m):
            copy.start()

        @pl.when(is_image)
        def _():
            extra = [att[m * TILES + t, OWN:TILE] for t in range(TILES)]
            mine[m] = t_dot(places_ref[m], jnp.concatenate(extra, axis=0)).astype(BF)
            for s in range(3):

                @pl.when(own_z == s)
                def _():
                    back_copy(m, s).start()

        at = pl.multiple_of(m * TILES * OWN, 16)
        rows_ref[pl.ds(at, TILES * OWN)] = own_rows(att, m)

    for m in range(micros):

        @pl.when(is_text)
        def _():
            for s in range(3):
                back_copy(m, s).wait_recv()
                row_copy(m, s).wait_send()
            parts = [got_back[m, s] for s in range(3)]
            parts += [att[m * TILES + t, OWN:TILE] for t in range(TILES)]
            moved = t_dot(picks_ref[m], jnp.concatenate(parts, axis=0)).astype(BF)
            at = pl.ds(m * TILES * OWN, TILES * OWN)
            rows_ref[at] = (rows_ref[at].astype(F32) + moved.astype(F32)).astype(BF)

        pl.when(is_image)(lambda: back_copy(m, 0).wait_send())
        for copy in outs(m):
            copy.wait()
    for slot in range(2):
        tile = micros * TILES - 2 + slot
        probs_store(tile, tile % 2).wait()


def attend_rows(tokens, picks, places, ids, vecs, w_qkv):
    micros, _, width = tokens.shape
    tiles = micros * TILES
    dma = pltpu.SemaphoreType.DMA

    def sds(*shape):
        return jax.ShapeDtypeStruct(shape, BF)

    return pl.pallas_call(
        attend_rows_kernel,
        in_specs=[HBM] + [FULL] * 4 + [HBM],
        out_specs=[HBM] * 5 + [FULL],
        out_shape=[
            sds(tiles, TILE, width),
            sds(tiles, TILE, 3 * width),
            sds(tiles, HEADS, TILE, TILE),
            sds(tiles, TILE, width),
            sds(tiles, TILE, width),
            sds(tiles * OWN, width),
        ],
        scratch_shapes=[
            pltpu.VMEM(tokens.shape, BF),
            pltpu.VMEM(w_qkv.shape, BF),
            pltpu.VMEM((tiles, TILE, width), BF),
            pltpu.VMEM((tiles, TILE, 3 * width), BF),
            pltpu.VMEM((2, HEADS, TILE, TILE), BF),
            pltpu.VMEM((tiles, TILE, width), BF),
            pltpu.VMEM((tiles, TILE, width), BF),
            pltpu.VMEM((micros, 3, 2 * SLOT, width), BF),
            pltpu.VMEM((micros, 2 * SLOT, width), BF),
            pltpu.VMEM((micros, 2 * SLOT, width), BF),
            pltpu.VMEM((micros, 3, 2 * SLOT, width), BF),
            dma((micros,)),
            dma,
            dma((micros, 4)),
            dma((2,)),
            dma((micros, 3)),
            dma((micros,)),
            dma((micros,)),
            dma((micros, 3)),
        ],
        compiler_params=pltpu.CompilerParams(
            vmem_limit_bytes=56 * 2**20, collective_id=3, has_side_effects=True
        ),
        name="attend_rows",
    )(tokens, picks, places, ids, vecs, w_qkv)


def attend_back_kernel(qkv_ref, p_ref, out_ref, inv_ref, grad_ref, dqkv_ref):
    width = out_ref.shape[2]
    low, high = pair_lanes()

    def maker(pair):
        at = pl.ds(pair * 128, 128)
        return lambda: attend_back_pair(
            *(qkv_ref[0, :, pl.ds(part * width + pair * 128, 128)] for part in range(3)),
            [p_ref[0, 2 * pair], p_ref[0, 2 * pair + 1]],
            out_ref[0, :, at],
            inv_ref[0, :, at],
            grad_ref[0, :, at],
            low,
            high,
        )

    def finish(pair, results):
        for part, value in enumerate(results):
            dqkv_ref[0, :, pl.ds(part * width + pair * 128, 128)] = value

    staggered([maker(pair) for pair in range(HEADS // 2)], finish)


def attend_back(qkv, probs, out, inverse, grad):
    tiles, _, width = out.shape

    def block(*shape):
        return pl.BlockSpec((1,) + shape, lambda i: (i,) + (0,) * len(shape))

    return pl.pallas_call(
        attend_back_kernel,
        grid=(tiles,),
        in_specs=[
            block(TILE, 3 * width),
            block(HEADS, TILE, TILE),
            block(TILE, width),
            block(TILE, width),
            block(TILE, width),
        ],
        out_specs=block(TILE, 3 * width),
        out_shape=jax.ShapeDtypeStruct((tiles, TILE, 3 * width), BF),
        compiler_params=pltpu.CompilerParams(vmem_limit_bytes=56 * 2**20),
        name="attend_back",
    )(qkv, probs, out, inverse, grad)


STEPS = 3
PARTS = 3


def add_into(ref, at, other):
    ref[at] = (ref[at].astype(F32) + other.astype(F32)).astype(BF)


class ItemSum:
    def __init__(self, up, down, got, got_one, got_two, sems):
        self.grads = (up, down)
        self.got, self.got_one, self.got_two, self.sems = got, got_one, got_two, sems
        me = lax.axis_index("dp")
        self.me = me
        self.core, self.x, self.y = lax.rem(me, 2), lax.rem(lax.div(me, 2), 2), lax.div(me, 4)
        self.near = me + 1 - 2 * self.core
        self.over_x = me + 2 - 4 * self.x
        self.over_y = me + 4 - 8 * self.y

    def _copy(self, src, dst, stage, which, slot, device):
        return pltpu.make_async_remote_copy(
            src_ref=src,
            dst_ref=dst,
            send_sem=self.sems.at[stage, which, 0, slot],
            recv_sem=self.sems.at[stage, which, 1, slot],
            device_id={"dp": device},
            device_id_type=MESH,
        )

    def core_copy(self, which, slot):
        src = self.grads[which].at[slot, :, :, 1 - self.core]
        return self._copy(src, self.got[which].at[slot], 0, which, slot, self.near)

    def one_copy(self, which, slot):
        grad = self.grads[which]
        if which == 0:
            src, device = grad.at[slot, :, 1 - self.x, self.core], self.over_x
        else:
            src, device = grad.at[slot, 1 - self.y, :, self.core], self.over_y
        return self._copy(src, self.got_one[which].at[slot], 1, which, slot, device)

    def two_copy(self, which, slot):
        grad = self.grads[which]
        if which == 0:
            src, device = grad.at[slot, 1 - self.y, self.x, self.core], self.over_y
        else:
            src, device = grad.at[slot, self.y, 1 - self.x, self.core], self.over_x
        return self._copy(src, self.got_two[which].at[slot], 2, which, slot, device)

    def start(self, which, slot):
        self.core_copy(which, slot).start()

    def after_core(self, slot):
        for which in range(2):
            self.core_copy(which, slot).wait()
            for y in range(2):
                for x in range(2):
                    at = (slot, y, x, self.core)
                    add_into(self.grads[which], at, self.got[which][slot, y, x])
            self.one_copy(which, slot).start()

    def after_one(self, slot):
        for which in range(2):
            self.one_copy(which, slot).wait()
            for side in range(2):
                at = (slot, side, self.x, self.core) if which == 0 else (slot, self.y, side, self.core)
                add_into(self.grads[which], at, self.got_one[which][slot, side])
            self.two_copy(which, slot).start()

    def after_two(self, slot):
        sums = []
        for which in range(2):
            self.two_copy(which, slot).wait()
            own = self.grads[which][slot, self.y, self.x, self.core].astype(F32)
            sums.append((own + self.got_two[which][slot].astype(F32)).astype(BF))
        return sums


def meet(devices):
    barrier = pltpu.get_barrier_semaphore()
    for device in devices:
        pl.semaphore_signal(barrier, inc=1, device_id=device, device_id_type=MESH)
    pl.semaphore_wait(barrier, len(devices))


def expert_kernel(
    remote,
    x_ref,
    att_ref,
    dy_ref,
    w_out_ref,
    vecs_ref,
    picks_ref,
    places_ref,
    up_v_ref,
    down_v_ref,
    up_t_ref,
    down_t_ref,
    out_ref,
    dmid_ref,
    datt_ref,
    dwout_ref,
    vec_ref,
    dup_ref,
    ddown_ref,
    dy,
    hid_t,
    dy_t,
    acc_o,
    acc_h,
    up_w,
    down_w,
    act,
    gup,
    dup_buf,
    ddown_buf,
    sems,
    *more,
):
    mid, hid = dmid_ref, datt_ref
    rows, width = mid.shape
    part_tiles = rows // OWN // PARTS

    def put_rows(part, value):
        for n in range(part_tiles):
            datt_ref[part * part_tiles + n, 0:OWN] = value[n * OWN : (n + 1) * OWN]

    def hid_rows(part):
        tiles = [hid[part * part_tiles + n, 0:OWN] for n in range(part_tiles)]
        return jnp.concatenate(tiles, axis=0)

    cols = act.shape[1]
    is_text = lax.axis_index("stream") == 3
    pieces = 8 if remote else 1
    piece = cols // pieces
    ff = up_v_ref.shape[1]

    padded_rows = TILES * OWN
    blocks = rows // padded_rows

    def x_copies():
        for tile in range(rows // OWN):
            dst = act.at[pl.ds(tile * OWN, OWN), 0:width]
            yield pltpu.make_async_copy(x_ref.at[tile, 0:OWN], dst, sems.at[2, tile])

    def dy_copies():
        for m in range(blocks):
            yield pltpu.make_async_copy(dy_ref.at[m], out_ref.at[m], sems.at[5, m])

    for copy in [*x_copies(), *dy_copies()]:
        copy.start()

    def fetch(j, slot):
        def go(up_src, down_src):
            for d in range(pieces):
                at = pl.ds(pl.multiple_of(j * piece + d * (ff // pieces), 128), piece)
                here = pl.ds(d * piece, piece)
                pltpu.make_async_copy(
                    up_src.at[:, at], up_w.at[slot, :, here], sems.at[0, slot]
                ).start()
                pltpu.make_async_copy(
                    down_src.at[at, :], down_w.at[slot, here, :], sems.at[1, slot]
                ).start()

        pl.when(is_text)(lambda: go(up_t_ref, down_t_ref))
        pl.when(jnp.logical_not(is_text))(lambda: go(up_v_ref, down_v_ref))

    def fetched(slot):
        pltpu.make_async_copy(up_w.at[slot], up_w.at[slot], sems.at[0, slot]).wait()
        pltpu.make_async_copy(down_w.at[slot], down_w.at[slot], sems.at[1, slot]).wait()

    fetch(0, 0)
    if remote:
        got, got_one, got_two, sum_sems = more[0:2], more[2:4], more[4:6], more[6]
        total = ItemSum(dup_buf, ddown_buf, got, got_one, got_two, sum_sems)
        own_z = lax.axis_index("stream")
        meet(
            [{"dp": total.near}, {"dp": total.over_x}, {"dp": total.over_y}]
            + [{"stream": lax.rem(own_z + k, 4)} for k in range(1, 4)]
        )
        sent, got_rows, row_send, row_recv = more[7:]
    gain, shift = row_of(vecs_ref, GAIN2), row_of(vecs_ref, SHIFT2)
    bias = jnp.where(is_text, row_of(vecs_ref, TXT_BIAS), row_of(vecs_ref, VIS_BIAS))
    for copy in [*x_copies(), *dy_copies()]:
        copy.wait()
    pad = padding(False)
    for m in range(blocks):
        dy[m * padded_rows : (m + 1) * padded_rows] = dot(pad, out_ref[m]).astype(BF)
    part_rows = rows // PARTS

    @pl.loop(0, PARTS)
    def _(part):
        at = pl.ds(pl.multiple_of(part * part_rows, 16), part_rows)
        middle = act[at, 0:width].astype(F32) + dot(att_ref[at], w_out_ref[...])
        mid[at] = middle
        normed, _ = normalize(middle)
        put_rows(part, (normed * gain + shift).astype(BF))
        acc_o[at] = middle + bias
        acc_h[at] = jnp.zeros_like(middle)

    for part in range(PARTS):
        hid_t[:, part * part_rows : (part + 1) * part_rows] = hid_rows(part).T
    dy_t[...] = dy[...].T

    def deliver(slot, j):
        up, down = total.after_two(slot)
        for t in range(4):
            dup_ref[t, j] = up[:, t * (cols // 4) : (t + 1) * (cols // 4)]
            ddown_ref[t, j] = down[t * (width // 4) : (t + 1) * (width // 4)]

    def stored(j, slot):
        return (
            pltpu.make_async_copy(dup_buf.at[slot], dup_ref.at[j], sems.at[3, slot]),
            pltpu.make_async_copy(ddown_buf.at[slot], ddown_ref.at[j], sems.at[4, slot]),
        )

    @pl.loop(0, STEPS)
    def _(j):
        slot = lax.rem(j, 2)
        other = 1 - slot
        pl.when(j < STEPS - 1)(lambda: fetch(j + 1, other))
        fetched(slot)

        @pl.loop(0, PARTS)
        def _(part):
            at = pl.ds(pl.multiple_of(part * part_rows, 16), part_rows)
            up = dot(hid_rows(part), up_w[slot])
            grad = dot_t(dy[at], down_w[slot])
            cdf, pdf = gelu_parts(up)
            activ = (up * cdf).astype(BF)
            grad_up = (grad * (cdf + up * pdf)).astype(BF)
            act[at] = activ
            gup[at] = grad_up
            acc_o[at] += dot(activ, down_w[slot])
            acc_h[at] += dot_t(grad_up, up_w[slot])
            if remote:

                @pl.when(part == 0)
                def _():
                    pl.when(j > 1)(lambda: deliver(slot, j - 2))
                    pl.when(j > 0)(lambda: total.after_core(other))

        if not remote:

            @pl.when(j > 1)
            def _():
                for copy in stored(j - 2, slot):
                    copy.wait()

        grad = dot(hid_t[...], gup[...]).astype(BF)
        if remote:
            dup_buf[slot] = grad.reshape(dup_buf.shape[1:])
            total.start(0, slot)
            pl.when(j > 0)(lambda: total.after_one(other))
        else:
            dup_buf[slot] = grad
        grad = dot(dy_t[...], act[...]).astype(BF)
        if remote:
            for d in range(8):
                ddown_buf[slot, d // 4, d // 2 % 2, d % 2] = grad[:, d * piece : (d + 1) * piece]
            total.start(1, slot)
        else:
            ddown_buf[slot] = grad
            for copy in stored(j, slot):
                copy.start()

    last = (STEPS - 1) % 2
    vec_ref[...] = jnp.zeros_like(vec_ref)

    @pl.loop(0, PARTS)
    def _(part):
        at = pl.ds(pl.multiple_of(part * part_rows, 16), part_rows)
        act[at, 0:width] = acc_o[at].astype(BF)
        normed, inverse = normalize(mid[at])
        grad = acc_h[at]
        wide = dy[at].astype(F32)
        vec_ref[0:1, :] += jnp.sum(grad * normed, axis=0, keepdims=True)
        vec_ref[1:2, :] += jnp.sum(grad, axis=0, keepdims=True)
        vec_ref[2:3, :] += jnp.sum(wide, axis=0, keepdims=True)
        grad_mid = wide + norm_back(grad, normed, inverse, gain)
        dmid_ref[at] = grad_mid
        branch = grad_mid.astype(BF)
        gup[at, 0:width] = branch
        put_rows(part, dot_t(branch, w_out_ref[...]).astype(BF))
        if remote:

            @pl.when(part == 0)
            def _():
                deliver(1 - last, STEPS - 2)
                total.after_core(last)

    unpad = padding(True)
    for m in range(blocks):
        done = act[m * padded_rows : (m + 1) * padded_rows, 0:width]
        out_ref[m] = dot(unpad, done).astype(BF)

    def beside(m, value):
        for t in range(TILES):
            part = value[t * (TILE - OWN) : (t + 1) * (TILE - OWN)]
            datt_ref[m * TILES + t, OWN:TILE] = part

    if remote:
        micros = got_rows.shape[0]

        def row_copy(m, s):
            return pltpu.make_async_remote_copy(
                src_ref=sent.at[m, s],
                dst_ref=got_rows.at[m],
                send_sem=row_send.at[m, s],
                recv_sem=row_recv.at[m],
                device_id={"stream": s},
                device_id_type=MESH,
            )

        @pl.when(is_text)
        def _():
            for m in range(micros):
                own = [datt_ref[m * TILES + t, 0:OWN] for t in range(TILES)]
                picked = dot(picks_ref[m], jnp.concatenate(own, axis=0)).astype(BF)
                for s in range(3):
                    sent[m, s] = picked[s * 2 * SLOT : (s + 1) * 2 * SLOT]
                    row_copy(m, s).start()
                beside(m, picked[6 * SLOT :])

    dwout_ref[...] = t_dot(att_ref[...], gup[:, 0:width]).astype(BF)
    if remote:
        total.after_one(last)

        @pl.when(is_text)
        def _():
            for m in range(micros):
                for s in range(3):
                    row_copy(m, s).wait_send()

        @pl.when(jnp.logical_not(is_text))
        def _():
            for m in range(micros):
                row_copy(m, 0).wait_recv()
                beside(m, dot(places_ref[m], got_rows[m]).astype(BF))

        deliver(last, STEPS - 1)
    else:
        for j in range(STEPS - 2, STEPS):
            for copy in stored(j, j % 2):
                copy.wait()


def expert(
    remote, x_tiles, att, dy, w_out, vecs, picks, places, vis_up, vis_down, txt_up, txt_down
):
    rows, width = att.shape
    cols = vis_up.shape[1] // STEPS
    micros = rows // OWN // TILES
    if remote:
        shard, piece = width // 8, cols // 8
        buffers = (2, 2, 2, 2, shard, cols), (2, 2, 2, 2, width, piece)
        outs = (4, STEPS, shard, cols // 4), (4, STEPS, width // 4, piece)
        more = [
            pltpu.VMEM((2, 2, 2, shard, cols), BF),
            pltpu.VMEM((2, 2, 2, width, piece), BF),
            pltpu.VMEM((2, 2, shard, cols), BF),
            pltpu.VMEM((2, 2, width, piece), BF),
            pltpu.VMEM((2, shard, cols), BF),
            pltpu.VMEM((2, width, piece), BF),
            pltpu.SemaphoreType.DMA((3, 2, 2, 2)),
            pltpu.VMEM((micros, 3, 2 * SLOT, width), BF),
            pltpu.VMEM((micros, 2 * SLOT, width), BF),
            pltpu.SemaphoreType.DMA((micros, 3)),
            pltpu.SemaphoreType.DMA((micros,)),
        ]
        params = dict(collective_id=1, has_side_effects=True)
    else:
        buffers = ((2, width, cols),) * 2
        outs = ((STEPS, width, cols),) * 2
        more, params = [], {}
    return pl.pallas_call(
        functools.partial(expert_kernel, remote),
        in_specs=[HBM, FULL, HBM] + [FULL] * 4 + [HBM] * 4,
        out_specs=[FULL] * 5 + [FULL if remote else HBM] * 2,
        out_shape=[
            jax.ShapeDtypeStruct(dy.shape, BF),
            jax.ShapeDtypeStruct((rows, width), F32),
            jax.ShapeDtypeStruct((rows // OWN, TILE, width), BF),
            jax.ShapeDtypeStruct((width, width), BF),
            jax.ShapeDtypeStruct((8, width), F32),
        ]
        + [jax.ShapeDtypeStruct(shape, BF) for shape in outs],
        scratch_shapes=[
            pltpu.VMEM((rows, width), BF),
            pltpu.VMEM((width, rows), BF),
            pltpu.VMEM((width, rows), BF),
            pltpu.VMEM((rows, width), F32),
            pltpu.VMEM((rows, width), F32),
            pltpu.VMEM((2, width, cols), BF),
            pltpu.VMEM((2, cols, width), BF),
            pltpu.VMEM((rows, cols), BF),
            pltpu.VMEM((rows, cols), BF),
            pltpu.VMEM(buffers[0], BF),
            pltpu.VMEM(buffers[1], BF),
            pltpu.SemaphoreType.DMA((6, max(2, rows // OWN))),
        ]
        + more,
        compiler_params=pltpu.CompilerParams(vmem_limit_bytes=63 * 2**20, **params),
        name="expert",
    )(x_tiles, att, dy, w_out, vecs, picks, places, vis_up, vis_down, txt_up, txt_down)


def project_back_kernel(x_ref, dqkv_ref, vecs_ref, w_ref, dx_ref, dw_ref, vec_ref, acc):
    i = pl.program_id(0)
    gain, shift = row_of(vecs_ref, GAIN1), row_of(vecs_ref, SHIFT1)
    normed, inverse = normalize(x_ref[0].astype(F32))
    hidden = (normed * gain + shift).astype(BF)
    dqkv = dqkv_ref[0]
    grad = dot_t(dqkv, w_ref[...])
    dx_ref[0] = norm_back(grad, normed, inverse, gain).astype(BF)
    width = x_ref.shape[2]
    part = t_dot(hidden, dqkv)
    ones = jnp.ones((8, TILE), BF)
    sums = dot(ones, dqkv)[0:1]
    vec = jnp.concatenate(
        [
            jnp.sum(grad * normed, axis=0, keepdims=True),
            jnp.sum(grad, axis=0, keepdims=True),
            sums[:, :width],
            sums[:, 2 * width :],
        ],
        axis=0,
    )

    @pl.when(i == 0)
    def _():
        acc[...] = part
        vec_ref[0:4, :] = vec

    @pl.when(i > 0)
    def _():
        acc[...] += part
        vec_ref[0:4, :] += vec

    @pl.when(i == pl.num_programs(0) - 1)
    def _():
        dw_ref[...] = acc[...].astype(BF)


def project_back(x_tiles, dqkv, vecs, w_qkv):
    tiles, _, width = x_tiles.shape

    def block(*shape):
        return pl.BlockSpec((1,) + shape, lambda i: (i,) + (0,) * len(shape))

    return pl.pallas_call(
        project_back_kernel,
        grid=(tiles,),
        in_specs=[block(TILE, width), block(TILE, 3 * width), FULL, FULL],
        out_specs=[block(TILE, width), FULL, FULL],
        out_shape=[
            jax.ShapeDtypeStruct((tiles, TILE, width), BF),
            jax.ShapeDtypeStruct((width, 3 * width), BF),
            jax.ShapeDtypeStruct((8, width), F32),
        ],
        scratch_shapes=[pltpu.VMEM((width, 3 * width), F32)],
        compiler_params=pltpu.CompilerParams(vmem_limit_bytes=56 * 2**20),
        name="project_back",
    )(x_tiles, dqkv, vecs, w_qkv)


GROUP = 256
GROUPS = 3


def stream_blocks(count, share):
    spans = []
    for t in range(4):
        first, last = t * share // BLOCK, ((t + 1) * share - 1) // BLOCK
        spans.append(list(range(first, last + 1)))
    assert spans[-1][-1] == count - 1
    return spans


def unit_blocks(unit):
    if unit == 0:
        return list(range(6))
    g = unit - 1
    return [6 * part + 2 * g + i for part in range(3) for i in range(2)]


def back_kernel(
    x_ref,
    qkv_ref,
    p_ref,
    att_ref,
    inv_ref,
    datt_ref,
    dmid_ref,
    vecs_ref,
    w_ref,
    dwout_ref,
    zup_ref,
    zdown_ref,
    vec2_ref,
    picks_ref,
    places_ref,
    dx_ref,
    sums_ref,
    dqkv_ref,
    dout_ref,
    dvup_ref,
    dvdown_ref,
    dtup_ref,
    dtdown_ref,
    qkv,
    x,
    att,
    inv,
    datt,
    base,
    probs,
    hid_t,
    dqkv,
    w,
    sums,
    grad_hid,
    extra,
    mine,
    got_rows,
    buf_a,
    buf_b,
    got_a,
    got_b,
    one_a,
    one_b,
    two_a,
    two_b,
    held,
    got_qkv,
    got_out,
    got_up,
    got_down,
    vec,
    got_vec,
    z_vec,
    load_sems,
    p_sems,
    w_sem,
    sum_sems,
    row_send,
    row_recv,
    vec_sems,
    zvec_send,
    zvec_recv,
    expert_send,
    expert_recv,
    block_send,
    block_recv,
):
    micros = qkv.shape[0] // TILES
    width = x.shape[2]
    shard = width // 8
    own_z = lax.axis_index("stream")
    is_text = own_z == 3
    total = ItemSum(buf_a, buf_b, (got_a, got_b), (one_a, one_b), (two_a, two_b), sum_sems)

    def loads(m):
        at = pl.ds(m * TILES, TILES)
        rows = pl.ds(m * TILES * OWN, TILES * OWN)
        return [
            pltpu.make_async_copy(qkv_ref.at[at], qkv.at[at], load_sems.at[m, 0]),
            pltpu.make_async_copy(datt_ref.at[at], datt.at[at], load_sems.at[m, 1]),
            pltpu.make_async_copy(inv_ref.at[at], inv.at[at], load_sems.at[m, 2]),
            pltpu.make_async_copy(att_ref.at[at], att.at[at], load_sems.at[m, 3]),
            pltpu.make_async_copy(x_ref.at[at], x.at[at], load_sems.at[m, 4]),
            pltpu.make_async_copy(dmid_ref.at[rows], base.at[rows], load_sems.at[m, 5]),
        ]

    def probs_load(m, g, slot):
        src = p_ref.at[pl.ds(m * TILES, TILES), pl.ds(g * 4, 4)]
        return pltpu.make_async_copy(src, probs.at[slot], p_sems.at[slot])

    w_copies = []
    for g in range(GROUPS):
        for part in range(3):
            src = w_ref.at[:, pl.ds(part * width + g * GROUP, GROUP)]
            dst = w.at[:, pl.ds((g * 3 + part) * GROUP, GROUP)]
            w_copies.append(pltpu.make_async_copy(src, dst, w_sem))
    probs_load(0, 0, 0).start()
    for copy in loads(0) + w_copies:
        copy.start()
    meet(
        [{"dp": total.near}, {"dp": total.over_x}, {"dp": total.over_y}]
        + [{"stream": lax.rem(own_z + k, 4)} for k in range(1, 4)]
    )

    def expert_copy(t, which):
        src, dst = ((zup_ref, got_up), (zdown_ref, got_down))[which]
        return pltpu.make_async_remote_copy(
            src_ref=src.at[t],
            dst_ref=dst.at[own_z],
            send_sem=expert_send.at[t, which],
            recv_sem=expert_recv.at[own_z, which],
            device_id={"stream": t},
            device_id_type=MESH,
        )

    def expert_arrival(src, which):
        dst = (got_up, got_down)[which]
        return pltpu.make_async_remote_copy(
            src_ref=dst.at[src],
            dst_ref=dst.at[src],
            send_sem=expert_send.at[src, which],
            recv_sem=expert_recv.at[src, which],
            device_id={"stream": src},
            device_id_type=MESH,
        )

    for t in range(4):

        @pl.when(own_z != t)
        def _():
            expert_copy(t, 0).start()
            expert_copy(t, 1).start()

        @pl.when(own_z == t)
        def _():
            for which in range(2):
                src, dst = ((zup_ref, got_up), (zdown_ref, got_down))[which]
                pltpu.make_async_copy(src.at[t], dst.at[t], expert_send.at[t, which]).start()

    half = buf_a.shape[-1]

    def put_unit(unit, value):
        slot = lax.rem(unit, 2)
        buf_a[slot] = value[:, :half].reshape(buf_a.shape[1:])
        buf_b[slot] = value[:, half:].reshape(buf_b.shape[1:])
        total.start(0, slot)
        total.start(1, slot)

    def take_unit(unit):
        left, right = total.after_two(lax.rem(unit, 2))
        for n in range(3):
            held[unit, n] = left[:, n * BLOCK : (n + 1) * BLOCK]
            held[unit, n + 3] = right[:, n * BLOCK : (n + 1) * BLOCK]

    def block_copy(unit, n, t, place):
        dst = got_out if unit == 0 else got_qkv
        kind = 0 if unit == 0 else 1
        return pltpu.make_async_remote_copy(
            src_ref=held.at[unit, n],
            dst_ref=dst.at[own_z, place],
            send_sem=block_send.at[kind, t, place],
            recv_sem=block_recv.at[kind, own_z, place],
            device_id={"stream": t},
            device_id_type=MESH,
        )

    out_spans = stream_blocks(6, width // 4)
    qkv_spans = stream_blocks(18, 3 * width // 4)

    def unit_sends(unit, t):
        span = (out_spans if unit == 0 else qkv_spans)[t]
        blocks = unit_blocks(unit)
        return [(n, span.index(b)) for n, b in enumerate(blocks) if b in span]

    def send_unit(unit):
        for t in range(4):

            @pl.when(own_z != t)
            def _():
                for n, place in unit_sends(unit, t):
                    block_copy(unit, n, t, place).start()

            @pl.when(own_z == t)
            def _():
                dst = got_out if unit == 0 else got_qkv
                for n, place in unit_sends(unit, t):
                    dst[t, place] = held[unit, n]

    put_unit(0, dwout_ref[...])

    def row_copy(m, s):
        return pltpu.make_async_remote_copy(
            src_ref=mine.at[m],
            dst_ref=got_rows.at[m, s],
            send_sem=row_send.at[m],
            recv_sem=row_recv.at[m, s],
            device_id={"stream": 3},
            device_id_type=MESH,
        )

    low, high = pair_lanes()
    gain, shift = row_of(vecs_ref, GAIN1), row_of(vecs_ref, SHIFT1)
    vec[...] = jnp.zeros_like(vec)

    def add_vec(row, value):
        for d in range(8):
            vec[d, row : row + 1, 0:shard] += value[:, d * shard : (d + 1) * shard]

    add_vec(4, vec2_ref[0:1, :])
    add_vec(5, vec2_ref[1:2, :])
    text_scale = jnp.where(is_text, 1.0, 0.0)
    add_vec(6, vec2_ref[2:3, :] * (1.0 - text_scale))
    add_vec(7, vec2_ref[2:3, :] * text_scale)

    steps = micros * GROUPS
    span = 3 * GROUP
    lasts = TILES * TILE
    hid_t[width:] = jnp.ones_like(hid_t[width:])

    @pl.loop(0, steps)
    def _(step):
        m, g = lax.div(step, GROUPS), lax.rem(step, GROUPS)
        slot = lax.rem(step, 2)
        first = m * TILES
        here = pl.ds(pl.multiple_of(m * lasts, lasts), lasts)
        there = pl.multiple_of(g * span, span)

        @pl.when(step + 1 < steps)
        def _():
            after = step + 1
            probs_load(lax.div(after, GROUPS), lax.rem(after, GROUPS), 1 - slot).start()

        @pl.when(g == 0)
        def _():
            for copy in loads(m):
                copy.wait()

            @pl.when(m + 1 < micros)
            def _():
                for copy in loads(m + 1):
                    copy.start()

            for t in range(TILES):
                normed, _ = normalize(x[first + t].astype(F32))
                hidden = (normed * gain + shift).astype(BF)
                at = pl.multiple_of((first + t) * TILE, TILE)
                hid_t[0:width, pl.ds(at, TILE)] = hidden.T

        probs_load(m, g, slot).wait()

        def maker(t, pair):
            at = pl.multiple_of(g * GROUP + pair * BLOCK, BLOCK)
            cols = pl.ds(at, BLOCK)
            return lambda: attend_back_pair(
                *(qkv[first + t, :, pl.ds(part * width + at, BLOCK)] for part in range(3)),
                [probs[slot, t, 2 * pair], probs[slot, t, 2 * pair + 1]],
                att[first + t, :, cols],
                inv[first + t, :, cols],
                datt[first + t, :, cols],
                low,
                high,
            )

        def finish(n, results):
            t, pair = n // 2, n % 2
            rows = pl.ds(pl.multiple_of((first + t) * TILE, TILE), TILE)
            for part, value in enumerate(results):
                at = pl.multiple_of(there + part * GROUP + pair * BLOCK, BLOCK)
                dqkv[rows, pl.ds(at, BLOCK)] = value

        staggered([maker(n // 2, n % 2) for n in range(2 * TILES)], finish)

        @pl.when(step == 0)
        def _():
            total.after_core(0)

        @pl.when(step == 1)
        def _():
            total.after_one(0)

        @pl.when(step == 2)
        def _():
            take_unit(0)
            send_unit(0)

        @pl.when(step == steps - 2)
        def _():
            total.after_core(1)

        @pl.when(step == steps - 1)
        def _():
            total.after_one(1)
            total.after_core(0)

        @pl.when(m == micros - 1)
        def _():
            grad = dot(hid_t[...], dqkv[:, pl.ds(there, span)])
            sums[g] = grad[width : width + 8]
            pl.when(step == steps - 1)(lambda: take_unit(1))
            put_unit(1 + g, grad[:width].astype(BF))
            pl.when(step == steps - 1)(lambda: send_unit(1))

        @pl.when(step == GROUPS - 1)
        def _():
            pltpu.make_async_copy(w, w, w_sem).wait()

        @pl.when(g == GROUPS - 1)
        def _():
            grad_hid[...] = dot_t(dqkv[here, :], w[...])
            for t in range(TILES):
                normed, inverse = normalize(x[first + t].astype(F32))
                grad = grad_hid[t * TILE : (t + 1) * TILE]
                add_vec(0, jnp.sum(grad * normed, axis=0, keepdims=True))
                add_vec(1, jnp.sum(grad, axis=0, keepdims=True))
                back = norm_back(grad, normed, inverse, gain)
                rows = pl.ds(pl.multiple_of((first + t) * OWN, 16), OWN)
                base[rows] += back[:OWN]
                extra[m, t * (TILE - OWN) : (t + 1) * (TILE - OWN)] = back[OWN:].astype(BF)

            @pl.when(jnp.logical_not(is_text))
            def _():
                mine[m] = t_dot(places_ref[m], extra[m]).astype(BF)
                for s in range(3):

                    @pl.when(own_z == s)
                    def _():
                        row_copy(m, s).start()

    for row, at in ((2, 0), (3, 2 * GROUP)):
        cols = [sums[g, 0:1, at : at + GROUP] for g in range(GROUPS)]
        add_vec(row, jnp.concatenate(cols, axis=1))

    def vec_copy(stage):
        device = (total.near, total.over_x, total.over_y)[stage]
        return pltpu.make_async_remote_copy(
            src_ref=vec,
            dst_ref=got_vec.at[stage],
            send_sem=vec_sems.at[stage, 0],
            recv_sem=vec_sems.at[stage, 1],
            device_id={"dp": device},
            device_id_type=MESH,
        )

    def vec_stage(stage):
        vec_copy(stage).wait()
        vec[...] += got_vec[stage]

    def zvec_copy(t):
        return pltpu.make_async_remote_copy(
            src_ref=vec.at[total.me],
            dst_ref=z_vec.at[own_z],
            send_sem=zvec_send.at[t],
            recv_sem=zvec_recv.at[own_z],
            device_id={"stream": t},
            device_id_type=MESH,
        )

    def zvec_arrival(s):
        return pltpu.make_async_remote_copy(
            src_ref=z_vec.at[s],
            dst_ref=z_vec.at[s],
            send_sem=zvec_send.at[s],
            recv_sem=zvec_recv.at[s],
            device_id={"stream": s},
            device_id_type=MESH,
        )

    vec_copy(0).start()
    total.after_one(0)
    total.after_core(1)
    vec_stage(0)
    vec_copy(1).start()

    rows_all = TILES * OWN
    unpad = padding(True)

    def deliver(m, scattered):
        rows = pl.ds(m * rows_all, rows_all)
        value = base[rows]
        if scattered:
            value = value + t_dot(
                picks_ref[m], jnp.concatenate([got_rows[m, s] for s in range(3)] + [extra[m]], axis=0)
            )
        dx_ref[m] = dot(unpad, value.astype(BF)).astype(BF)

    @pl.when(jnp.logical_not(is_text))
    def _():
        for m in range(micros - 1):
            deliver(m, False)

    @pl.when(is_text)
    def _():
        for m in range(micros - 1):
            for s in range(3):
                row_copy(m, s).wait_recv()
            deliver(m, True)

    take_unit(2)
    send_unit(2)
    total.after_one(1)
    vec_stage(1)
    vec_copy(2).start()

    @pl.when(jnp.logical_not(is_text))
    def _():
        deliver(micros - 1, False)

    ff_piece = got_down.shape[3]
    for src in range(4):

        @pl.when(own_z != src)
        def _():
            for which in range(2):
                expert_arrival(src, which).wait_recv()
                expert_copy(src, which).wait_send()

        @pl.when(own_z == src)
        def _():
            for which in range(2):
                ref, dst = ((zup_ref, got_up), (zdown_ref, got_down))[which]
                pltpu.make_async_copy(ref.at[src], dst.at[src], expert_send.at[src, which]).wait()

    for j in range(STEPS):
        vis = sum(got_up[s, j].astype(F32) for s in range(3))
        txt = got_up[3, j].astype(F32)
        for d in range(2):
            at = (d * STEPS + j) * ff_piece
            dvup_ref[:, at : at + ff_piece] = vis[:, d * ff_piece : (d + 1) * ff_piece]
            dtup_ref[:, at : at + ff_piece] = txt[:, d * ff_piece : (d + 1) * ff_piece]
        at = j * ff_piece
        dvdown_ref[at : at + ff_piece] = sum(got_down[s, j].astype(F32) for s in range(3)).T
        dtdown_ref[at : at + ff_piece] = got_down[3, j].astype(F32).T

    take_unit(3)
    send_unit(3)
    vec_stage(2)
    for t in range(4):
        pl.when(own_z != t)(lambda: zvec_copy(t).start())

        @pl.when(own_z == t)
        def _():
            z_vec[t] = vec[total.me]

    @pl.when(is_text)
    def _():
        for s in range(3):
            row_copy(micros - 1, s).wait_recv()
        deliver(micros - 1, True)

    @pl.when(jnp.logical_not(is_text))
    def _():
        for m in range(micros):
            row_copy(m, 0).wait_send()

    for src in range(4):

        @pl.when(own_z != src)
        def _():
            zvec_arrival(src).wait_recv()
            zvec_copy(src).wait_send()
            for unit in range(GROUPS + 1):
                for n, place in unit_sends(unit, src):
                    block_copy(unit, n, src, place).wait_send()
            for kind, dst in ((0, got_out), (1, got_qkv)):
                for place in range(dst.shape[1]):
                    pltpu.make_async_remote_copy(
                        src_ref=dst.at[src, place],
                        dst_ref=dst.at[src, place],
                        send_sem=block_send.at[kind, src, place],
                        recv_sem=block_recv.at[kind, src, place],
                        device_id={"stream": src},
                        device_id_type=MESH,
                    ).wait_recv()

    sums_ref[...] = sum(z_vec[s] for s in range(4))
    odd = lax.rem(own_z, 2) == 1
    for got, out in ((got_qkv, dqkv_ref), (got_out, dout_ref)):
        blocks = [
            sum(got[s, n].astype(F32) for s in range(4)) for n in range(got.shape[1])
        ]
        whole = jnp.concatenate(blocks, axis=1)
        moved = pltpu.roll(whole, whole.shape[1] - BLOCK // 2, 1)
        out[...] = jnp.where(odd, moved, whole)[:, : out.shape[1]]


def back(
    x_tiles, qkv, probs, att, inv, datt, dmid, vecs, w_qkv, dwout, zup, zdown, vec2, picks, places
):
    tiles, _, width = x_tiles.shape
    micros = tiles // TILES
    shard = width // 8
    half = width // 2
    ff = 4 * 2 * STEPS * zdown.shape[3]
    flat = TILES * PATCHES

    def sds(*shape, dtype=F32):
        return jax.ShapeDtypeStruct(shape, dtype)

    dma = pltpu.SemaphoreType.DMA
    return pl.pallas_call(
        back_kernel,
        in_specs=[HBM] * 7 + [FULL, HBM, FULL] + [HBM] * 2 + [FULL] * 3,
        out_specs=[FULL] * 8,
        out_shape=[
            sds(micros, flat, width, dtype=BF),
            sds(8, BLOCK),
            sds(shard, 3 * width // 4),
            sds(shard, width // 4),
            sds(shard, ff // 4),
            sds(ff // 8, width // 4),
            sds(shard, ff // 4),
            sds(ff // 8, width // 4),
        ],
        scratch_shapes=[
            pltpu.VMEM((tiles, TILE, 3 * width), BF),
            pltpu.VMEM((tiles, TILE, width), BF),
            pltpu.VMEM((tiles, TILE, width), BF),
            pltpu.VMEM((tiles, TILE, width), BF),
            pltpu.VMEM((tiles, TILE, width), BF),
            pltpu.VMEM((tiles * OWN, width), F32),
            pltpu.VMEM((2, TILES, 4, TILE, TILE), BF),
            pltpu.VMEM((width + 16, tiles * TILE), BF),
            pltpu.VMEM((tiles * TILE, 3 * width), BF),
            pltpu.VMEM((width, 3 * width), BF),
            pltpu.VMEM((GROUPS, 8, 3 * GROUP), F32),
            pltpu.VMEM((TILES * TILE, width), F32),
            pltpu.VMEM((micros, TILES * (TILE - OWN), width), BF),
            pltpu.VMEM((micros, 2 * SLOT, width), BF),
            pltpu.VMEM((micros, 3, 2 * SLOT, width), BF),
            pltpu.VMEM((2, 2, 2, 2, shard, half), BF),
            pltpu.VMEM((2, 2, 2, 2, shard, half), BF),
            pltpu.VMEM((2, 2, 2, shard, half), BF),
            pltpu.VMEM((2, 2, 2, shard, half), BF),
            pltpu.VMEM((2, 2, shard, half), BF),
            pltpu.VMEM((2, 2, shard, half), BF),
            pltpu.VMEM((2, shard, half), BF),
            pltpu.VMEM((2, shard, half), BF),
            pltpu.VMEM((GROUPS + 1, 6, shard, BLOCK), BF),
            pltpu.VMEM((4, 5, shard, BLOCK), BF),
            pltpu.VMEM((4, 2, shard, BLOCK), BF),
            pltpu.VMEM((4,) + zup.shape[1:], BF),
            pltpu.VMEM((4,) + zdown.shape[1:], BF),
            pltpu.VMEM((8, 8, BLOCK), F32),
            pltpu.VMEM((3, 8, 8, BLOCK), F32),
            pltpu.VMEM((4, 8, BLOCK), F32),
            dma((micros, 6)),
            dma((2,)),
            dma,
            dma((3, 2, 2, 2)),
            dma((micros,)),
            dma((micros, 3)),
            dma((3, 2)),
            dma((4,)),
            dma((4,)),
            dma((4, 2)),
            dma((4, 2)),
            dma((2, 4, 5)),
            dma((2, 4, 5)),
        ],
        compiler_params=pltpu.CompilerParams(
            vmem_limit_bytes=63 * 2**20, collective_id=2, has_side_effects=True
        ),
        name="back",
    )(x_tiles, qkv, probs, att, inv, datt, dmid, vecs, w_qkv, dwout, zup, zdown, vec2, picks, places)


def pad_rows(block):
    micro, rows, width = block.shape
    thirds = block.reshape(micro, TILES, PATCHES, width)
    thirds = jnp.pad(thirds, ((0, 0), (0, 0), (0, OWN - PATCHES), (0, 0)))
    return thirds.reshape(micro, TILES * OWN, width)


def unpad_rows(block):
    micro, _, width = block.shape
    thirds = block.reshape(micro, TILES, OWN, width)[:, :, :PATCHES]
    return thirds.reshape(micro, TILES * PATCHES, width)


def plan(lengths, pairs, is_text, own_stream):
    micro, items = lengths.shape
    finish = jnp.cumsum(lengths, axis=1)
    starts = finish - lengths
    numbers = jnp.arange(items, dtype=jnp.int32)
    match = pairs[:, :, None] == numbers
    start = jnp.sum(jnp.where(match, starts[:, None, :], 0), axis=2).reshape(micro, 3, TILES)
    length = jnp.sum(jnp.where(match, lengths[:, None, :], 0), axis=2).reshape(micro, 3, TILES)
    paired = (pairs >= 0).reshape(micro, 3, TILES)
    rank = jnp.where(paired, jnp.cumsum(paired.astype(jnp.int32), axis=2) - 1, -1)
    takes = rank[:, :, :, None] == jnp.arange(2)
    slot_start = jnp.sum(jnp.where(takes, start[..., None], 0), axis=2)
    slot_length = jnp.sum(jnp.where(takes, length[..., None], 0), axis=2)
    step = jnp.arange(SLOT, dtype=jnp.int32)
    slot_rows = jnp.where(step < slot_length[..., None], slot_start[..., None] + step, -1)
    pad = jnp.arange(TILE - OWN, dtype=jnp.int32)
    next_rows = PATCHES * jnp.arange(1, TILES + 1, dtype=jnp.int32)[:, None] + pad
    next_rows = jnp.where((pad < SLOT) & (next_rows < TILES * PATCHES), next_rows, -1)
    next_rows = jnp.broadcast_to(next_rows, (micro, TILES, TILE - OWN))
    wanted = jnp.concatenate([slot_rows.reshape(micro, -1), next_rows.reshape(micro, -1)], axis=1)
    place = jnp.arange(TILES * OWN, dtype=jnp.int32)
    row_at = jnp.where(place % OWN < PATCHES, place // OWN * PATCHES + place % OWN, -2)
    picks = (wanted[:, :, None] == row_at).astype(BF)
    item_paired = jnp.any(match, axis=1)
    rows = jnp.arange(TILES * PATCHES + SLOT, dtype=jnp.int32)
    member = (rows[:, None] >= starts[:, None, :]) & (rows[:, None] < finish[:, None, :])
    code = jnp.where(item_paired, -1, numbers + items * (starts // PATCHES))
    row_code = jnp.sum(jnp.where(member, code[:, None, :] + 1, 0), axis=2) - 1
    tile = jnp.arange(TILES, dtype=jnp.int32)[:, None]
    own_code = row_code[:, : TILES * PATCHES].reshape(micro, TILES, PATCHES)
    next_code = jnp.stack(
        [row_code[:, PATCHES * (t + 1) : PATCHES * (t + 1) + SLOT] for t in range(TILES)], axis=1
    )

    def here(codes):
        return jnp.where((codes >= 0) & (codes // items == tile), codes, -1)

    def lay(own, extra):
        gap = jnp.full((micro, TILES, OWN - PATCHES), -1, jnp.int32)
        end = jnp.full((micro, TILES, TILE - OWN - SLOT), -1, jnp.int32)
        return jnp.concatenate([own, gap, extra, end], axis=2)

    text_ids = lay(here(own_code), here(next_code))
    own_length = lax.dynamic_index_in_dim(length, jnp.minimum(own_stream, 2), 1, keepdims=False)
    own_takes = lax.dynamic_index_in_dim(takes, jnp.minimum(own_stream, 2), 1, keepdims=False)
    image_ids = lay(
        jnp.zeros((micro, TILES, PATCHES), jnp.int32),
        jnp.where(step < own_length[..., None], 0, -1),
    )
    ids = jnp.where(is_text, text_ids, image_ids)
    own_takes = own_takes.astype(BF)
    same = (pad[:, None] == step).astype(BF)
    places = own_takes[:, :, None, :, None] * same[:, None, :]
    places = places.reshape(micro, TILES * (TILE - OWN), 2 * SLOT)
    return picks, places, own_takes, ids.reshape(micro * TILES, 1, TILE)


def spread(padded, picks, own_takes, is_text):
    micro, _, width = padded.shape
    picked = lax.dot_general(
        picks, padded, (((2,), (1,)), ((0,), (0,))), preferred_element_type=F32
    ).astype(BF)
    near = picked[:, 6 * SLOT :].reshape(micro, TILES, TILE - OWN, width)[:, :, :SLOT]
    sent = picked[:, : 6 * SLOT].reshape(micro, 3, 2 * SLOT, width)
    far = sum(lax.ppermute(sent[:, s], "stream", [(3, s)]) for s in range(3))
    far = far.reshape(micro, 1, 2, SLOT, width) * own_takes[:, :, :, None, None]
    return jnp.where(is_text, near, far[:, :, 0] + far[:, :, 1])


def collect(extra, picks, own_takes, is_text):
    micro, _, _, width = extra.shape
    mine = extra[:, :, None] * own_takes[:, :, :, None, None]
    mine = (mine[:, 0] + mine[:, 1] + mine[:, 2]).reshape(micro, 2 * SLOT, width)
    parts = [lax.ppermute(mine, "stream", [(s, 3)]) for s in range(3)]
    extra = jnp.pad(extra, ((0, 0), (0, 0), (0, TILE - OWN - SLOT), (0, 0)))
    parts.append(extra.reshape(micro, TILES * (TILE - OWN), width))
    rows = jnp.concatenate(parts, axis=1)
    scale = jnp.where(is_text, 1.0, 0.0).astype(BF)
    return lax.dot_general(
        picks * scale, rows, (((1,), (1,)), ((0,), (0,))), preferred_element_type=F32
    ).astype(BF)


def reduce_all(vectors, dw_qkv, dw_out, dup, ddown):
    width = dw_qkv.shape[0]
    shard = width // lax.axis_size("dp")
    vectors = lax.psum(vectors, ("dp", "stream"))
    vectors = lax.dynamic_slice_in_dim(vectors, lax.axis_index("dp") * shard, shard, axis=1)

    def over_items(grad, dim):
        return lax.psum_scatter(grad, "dp", scatter_dimension=dim, tiled=True)

    def over_blocks(grad):
        return lax.psum_scatter(grad, "stream", scatter_dimension=1, tiled=True).astype(F32)

    qkv = over_blocks(over_items(dw_qkv, 0))
    out = over_blocks(over_items(dw_out, 0))
    dup = over_items(jnp.concatenate(list(dup), axis=1), 0)
    ddown = over_items(jnp.concatenate(list(ddown), axis=1), 1)
    up = dup.reshape(dup.shape[0], 4, -1).transpose(1, 0, 2)
    down = ddown.reshape(4, -1, ddown.shape[1])
    up = lax.all_to_all(up, "stream", 0, 0).astype(F32)
    down = lax.all_to_all(down, "stream", 0, 0).astype(F32)
    return (
        vectors,
        qkv,
        out,
        up[0] + up[1] + up[2],
        (down[0] + down[1] + down[2]).T,
        up[3],
        down[3].T,
    )


def shards(
    remote,
    tokens,
    text_lengths,
    pair_text,
    ln1_gain,
    ln1_bias,
    w_qkv,
    q_bias,
    v_bias,
    w_out,
    ln2_gain,
    ln2_bias,
    vis_up,
    vis_down,
    vis_bias,
    txt_up,
    txt_down,
    txt_bias,
    cotangent,
):
    micro = tokens.shape[0]
    width = tokens.shape[4]
    own_stream = lax.axis_index("stream")
    is_text = own_stream == 3
    vecs = [ln1_gain, ln1_bias, q_bias, v_bias, ln2_gain, ln2_bias, vis_bias, txt_bias]
    vecs = jnp.stack(vecs).astype(F32)
    picks, places, own_takes, ids = plan(text_lengths[:, 0], pair_text[:, 0], is_text, own_stream)

    def tiled(own, extra):
        own = own.reshape(micro, TILES, OWN, width)
        extra = jnp.pad(extra, ((0, 0), (0, 0), (0, TILE - OWN - SLOT), (0, 0)))
        return jnp.concatenate([own, extra], axis=2).reshape(micro * TILES, TILE, width)

    def parted(tiles):
        tiles = tiles.reshape(micro, TILES, TILE, width)
        return tiles[:, :, :OWN].reshape(micro, TILES * OWN, width), tiles[:, :, OWN : OWN + SLOT]

    if remote:
        x_tiles, qkv, probs, inverse, att_tiles, att = attend_rows(
            tokens[:, 0, 0], picks, places, ids, vecs, w_qkv
        )
    else:
        x = pad_rows(tokens[:, 0, 0])
        x_tiles = tiled(x, spread(x, picks, own_takes, is_text))
        qkv, att_tiles, probs, inverse = attend(x_tiles, ids, vecs, w_qkv)
        att_own, att_extra = parted(att_tiles)
        att = att_own + collect(att_extra, picks, own_takes, is_text)
        att = att.reshape(micro * TILES * OWN, width)
    out, dmid, datt_tiles, dw_out, vec2, dup, ddown = expert(
        remote,
        x_tiles,
        att,
        cotangent[:, 0, 0],
        w_out,
        vecs,
        picks,
        places,
        vis_up,
        vis_down,
        txt_up,
        txt_down,
    )
    if remote:
        dx, vectors, g_qkv, g_out, g_vup, g_vdown, g_tup, g_tdown = back(
            x_tiles,
            qkv,
            probs,
            att_tiles,
            inverse,
            datt_tiles,
            dmid,
            vecs,
            w_qkv,
            dw_out,
            dup,
            ddown,
            vec2,
            picks,
            places,
        )
        vectors = vectors[:, : width // 8]
    else:
        datt = parted(datt_tiles)[0]
        datt_tiles = tiled(datt, spread(datt, picks, own_takes, is_text))
        dqkv = attend_back(qkv, probs, att_tiles, inverse, datt_tiles)
        dx_tiles, dw_qkv, vec1 = project_back(x_tiles, dqkv, vecs, w_qkv)
        dx_own, dx_extra = parted(dx_tiles)
        dx = (
            dmid.reshape(micro, TILES * OWN, width)
            + dx_own.astype(F32)
            + collect(dx_extra, picks, own_takes, is_text).astype(F32)
        )
        dx = unpad_rows(dx).astype(BF)
        text_scale = jnp.where(is_text, 1.0, 0.0)
        vectors = jnp.concatenate(
            [vec1[0:4], vec2[0:2], vec2[2:3] * (1.0 - text_scale), vec2[2:3] * text_scale], axis=0
        )
        vectors, g_qkv, g_out, g_vup, g_vdown, g_tup, g_tdown = reduce_all(
            vectors, dw_qkv, dw_out, dup, ddown
        )
    return (
        out.reshape(tokens.shape),
        dx.reshape(tokens.shape),
        vectors[0],
        vectors[1],
        g_qkv,
        vectors[2],
        vectors[3],
        g_out,
        vectors[4],
        vectors[5],
        g_vup,
        g_vdown,
        vectors[6],
        g_tup,
        g_tdown,
        vectors[7],
    )


def solution(mesh):
    rows = P(None, "dp", "stream", None, None)
    lists = P(None, "dp", None)
    vector, matrix = P("dp"), P("dp", "stream")
    in_specs = (rows, lists, lists) + (P(),) * 14 + (rows,)
    out_specs = (
        rows,
        rows,
        vector,
        vector,
        matrix,
        vector,
        vector,
        matrix,
        vector,
        vector,
        matrix,
        matrix,
        vector,
        matrix,
        matrix,
        vector,
    )
    remote = mesh.shape["dp"] == 8
    body = functools.partial(shards, remote)
    return jax.shard_map(body, mesh=mesh, in_specs=in_specs, out_specs=out_specs, check_vma=False)
```

```python
import functools

import jax
import jax.numpy as jnp
from jax import lax
from jax.experimental import pallas as pl
from jax.experimental.pallas import tpu as pltpu
from jax.sharding import PartitionSpec as P

HEADS = 12
PATCHES = 197
OWN = 208
SLOT = 40
TILE = 256
TILES = 3
EPSILON = 1e-06
MASKED = -1e30
BF = jnp.bfloat16
F32 = jnp.float32
FULL = pl.BlockSpec(memory_space=pltpu.VMEM)
HBM = pl.BlockSpec(memory_space=pl.ANY)
MESH = pl.DeviceIdType.MESH
BLOCK = 128


def dot(left, right):
    return jnp.dot(left, right, preferred_element_type=F32)


def dot_t(left, right):
    return lax.dot_general(left, right, (((1,), (1,)), ((), ())), preferred_element_type=F32)


def t_dot(left, right):
    return lax.dot_general(left, right, (((0,), (0,)), ((), ())), preferred_element_type=F32)


def normalize(values):
    centred = values - jnp.mean(values, axis=-1, keepdims=True)
    inverse = lax.rsqrt(jnp.mean(centred * centred, axis=-1, keepdims=True) + EPSILON)
    return centred * inverse, inverse


def norm_back(grad, normed, inverse, gain):
    scaled = grad * gain
    return inverse * (
        scaled
        - jnp.mean(scaled, axis=-1, keepdims=True)
        - normed * jnp.mean(scaled * normed, axis=-1, keepdims=True)
    )


def gelu_parts(up):
    reach = jnp.abs(up) * 0.7071067811865476
    inner = 1.0 / (1.0 + 0.3275911 * reach)
    bell = jnp.exp(-0.5 * up * up)
    poly = inner * (
        0.254829592
        + inner
        * (-0.284496736 + inner * (1.421413741 + inner * (-1.453152027 + inner * 1.061405429)))
    )
    tail = 0.5 * poly * bell
    return jnp.where(up >= 0, 1.0 - tail, tail), bell * 0.3989422804014327


def halves(block, low, high):
    return jnp.concatenate([block * low, block * high], axis=0)


def pair_lanes():
    lane = lax.broadcasted_iota(jnp.int32, (1, 128), 1)
    return (lane < 64).astype(BF), (lane >= 64).astype(BF)


def attend_pair(q, k, v, barred, low, high):
    scores = dot_t(halves(k, low, high), q * 0.125)
    yield
    expos = []
    for side in range(2):
        part = scores[TILE * side : TILE * (side + 1)] + barred
        top = jnp.maximum(jnp.max(part, axis=0, keepdims=True), 0.1 * MASKED)
        expos.append(jnp.exp(part - top).astype(BF))
    ones = [jnp.broadcast_to(keep, (TILE, 128)) for keep in (low, high)]
    right = jnp.concatenate([halves(v, low, high), jnp.concatenate(ones, axis=0)], axis=1)
    sums = t_dot(jnp.concatenate(expos, axis=0), right)
    inverse = jnp.where(sums[:, 128:] > 0.0, 1.0 / sums[:, 128:], 0.0)
    yield expos, sums[:, :128] * inverse, inverse


def attend_back_pair(q, k, v, expos, out, inverse, grad, low, high):
    scaled = grad.astype(F32) * inverse.astype(F32)
    inner = (scaled * out.astype(F32)).astype(BF)
    scaled = scaled.astype(BF)
    minus = [jnp.broadcast_to(-keep, (TILE, 128)) for keep in (low, high)]
    right = jnp.concatenate([halves(v, low, high), jnp.concatenate(minus, axis=0)], axis=1)
    slopes = dot_t(right, jnp.concatenate([scaled, inner], axis=1))
    yield
    parts = [
        (expos[side].astype(F32) * slopes[TILE * side : TILE * (side + 1)]).astype(BF)
        for side in range(2)
    ]
    dq = t_dot(jnp.concatenate(parts, axis=0), halves(k, low, high)) * 0.125
    dk = dot(jnp.concatenate(parts, axis=1), halves(q * 0.125, low, high))
    dv = dot(jnp.concatenate(expos, axis=1), halves(scaled, low, high))
    yield dq.astype(BF), dk.astype(BF), dv.astype(BF)


def staggered(makers, finish):
    held = None
    for n, make in enumerate(makers):
        step = make()
        next(step)
        if held is not None:
            finish(n - 1, next(held))
        held = step
    finish(len(makers) - 1, next(held))


def bars(ids_ref):
    ids = jnp.broadcast_to(ids_ref, (TILE, TILE))
    return jnp.where((ids == ids.T) & (ids >= 0), 0.0, MASKED)


GAIN1, SHIFT1, Q_BIAS, V_BIAS, GAIN2, SHIFT2, VIS_BIAS, TXT_BIAS = range(8)


def row_of(vecs_ref, at):
    rows = vecs_ref.shape[0] // 8
    return jnp.concatenate([vecs_ref[at * rows + n : at * rows + n + 1] for n in range(rows)], axis=1)


def project(values, vecs_ref, w_ref):
    normed, _ = normalize(values.astype(F32))
    hidden = (normed * row_of(vecs_ref, GAIN1) + row_of(vecs_ref, SHIFT1)).astype(BF)
    q_bias, v_bias = row_of(vecs_ref, Q_BIAS), row_of(vecs_ref, V_BIAS)
    bias = jnp.concatenate([q_bias, jnp.zeros_like(q_bias), v_bias], axis=1)
    return (dot(hidden, w_ref[...]) + bias).astype(BF)


def attend_kernel(x_ref, ids_ref, vecs_ref, w_ref, qkv_ref, out_ref, p_ref, inv_ref):
    width = x_ref.shape[2]
    qkv_ref[0] = project(x_ref[0], vecs_ref, w_ref)
    barred = bars(ids_ref[0])
    low, high = pair_lanes()

    def maker(pair):
        cols = [qkv_ref[0, :, part * width + pair * 128 :][:, :128] for part in range(3)]
        return lambda: attend_pair(*cols, barred, low, high)

    def finish(pair, results):
        expos, out, inverse = results
        at = pair * 128
        for side in range(2):
            p_ref[0, 2 * pair + side] = expos[side]
        out_ref[0, :, at : at + 128] = out.astype(BF)
        inv_ref[0, :, at : at + 128] = inverse.astype(BF)

    staggered([maker(pair) for pair in range(HEADS // 2)], finish)


def attend(x_tiles, ids, vecs, w_qkv):
    tiles, _, width = x_tiles.shape

    def block(*shape):
        return pl.BlockSpec((1,) + shape, lambda i: (i,) + (0,) * len(shape))

    return pl.pallas_call(
        attend_kernel,
        grid=(tiles,),
        in_specs=[block(TILE, width), block(1, TILE), FULL, FULL],
        out_specs=[
            block(TILE, 3 * width),
            block(TILE, width),
            block(HEADS, TILE, TILE),
            block(TILE, width),
        ],
        out_shape=[
            jax.ShapeDtypeStruct((tiles, TILE, 3 * width), BF),
            jax.ShapeDtypeStruct((tiles, TILE, width), BF),
            jax.ShapeDtypeStruct((tiles, HEADS, TILE, TILE), BF),
            jax.ShapeDtypeStruct((tiles, TILE, width), BF),
        ],
        compiler_params=pltpu.CompilerParams(vmem_limit_bytes=56 * 2**20),
        name="attend",
    )(x_tiles, ids, vecs, w_qkv)


def third_of(row, size):
    return (row >= size).astype(jnp.int32) + (row >= 2 * size).astype(jnp.int32)


def padding(flip):
    rows, places = TILES * PATCHES, TILES * OWN
    shape = (rows, places) if flip else (places, rows)
    row = lax.broadcasted_iota(jnp.int32, shape, 0 if flip else 1)
    place = lax.broadcasted_iota(jnp.int32, shape, 1 if flip else 0)
    return (place == row + third_of(row, PATCHES) * (OWN - PATCHES)).astype(F32).astype(BF)


def attend_rows_kernel(
    tok_ref,
    picks_ref,
    places_ref,
    ids_ref,
    vecs_ref,
    w_hbm,
    x_out,
    qkv_out,
    p_out,
    inv_out,
    att_out,
    rows_out,
    mine_out,
    tok,
    w,
    x,
    qkv,
    probs,
    inv,
    att,
    rows_ref,
    sent,
    got,
    mine,
    got_back,
    tok_sems,
    w_sem,
    out_sems,
    p_sems,
    rows_sems,
    row_send,
    row_recv,
    back_send,
    back_recv,
):
    micros = tok.shape[0]
    width = tok.shape[2]
    own_z = lax.axis_index("stream")
    is_text = own_z == 3
    is_image = jnp.logical_not(is_text)
    side = TILE - OWN

    def tok_copy(m):
        return pltpu.make_async_copy(tok_ref.at[m], tok.at[m], tok_sems.at[m])

    for m in range(micros):
        tok_copy(m).start()
    w_copy = pltpu.make_async_copy(w_hbm, w, w_sem)
    w_copy.start()
    meet([{"stream": lax.rem(own_z + k, 4)} for k in range(1, 4)])

    def row_copy(m, s):
        return pltpu.make_async_remote_copy(
            src_ref=sent.at[m, s],
            dst_ref=got.at[m],
            send_sem=row_send.at[m, s],
            recv_sem=row_recv.at[m],
            device_id={"stream": s},
            device_id_type=MESH,
        )

    def back_copy(m, s):
        return pltpu.make_async_remote_copy(
            src_ref=mine.at[m],
            dst_ref=got_back.at[m, s],
            send_sem=back_send.at[m],
            recv_sem=back_recv.at[m, s],
            device_id={"stream": 3},
            device_id_type=MESH,
        )

    def outs(m, which):
        at = pl.ds(m * TILES, TILES)
        pairs = ((x, x_out), (qkv, qkv_out), (inv, inv_out), (att, att_out))
        for n in which:
            src, dst = pairs[n]
            yield pltpu.make_async_copy(src.at[at], dst.at[at], out_sems.at[m, n])

    def rows_copy(m):
        at = pl.ds(m * TILES * OWN, TILES * OWN)
        return pltpu.make_async_copy(rows_ref.at[at], rows_out.at[at], rows_sems.at[m])

    mine_copy = pltpu.make_async_copy(mine.at[micros - 1], mine_out, rows_sems.at[micros])

    def probs_store(tile, slot):
        return pltpu.make_async_copy(probs.at[slot], p_out.at[tile], p_sems.at[slot])

    def own_rows(ref, m):
        return jnp.concatenate([ref[m * TILES + t, 0:OWN] for t in range(TILES)], axis=0)

    def beside(ref, m, value):
        for t in range(TILES):
            ref[m * TILES + t, OWN:TILE] = value[t * side : (t + 1) * side]

    pad = padding(False)
    for m in range(micros):
        tok_copy(m).wait()
        padded = dot(pad, tok[m]).astype(BF)
        for t in range(TILES):
            x[m * TILES + t, 0:OWN] = padded[t * OWN : (t + 1) * OWN]

        @pl.when(is_text)
        def _():
            picked = dot(picks_ref[m], own_rows(x, m)).astype(BF)
            for s in range(3):
                sent[m, s] = picked[s * 2 * SLOT : (s + 1) * 2 * SLOT]
                row_copy(m, s).start()
            beside(x, m, picked[6 * SLOT :])

    w_copy.wait()
    for m in range(micros):
        rows = project(own_rows(x, m), vecs_ref, w)
        for t in range(TILES):
            qkv[m * TILES + t, 0:OWN] = rows[t * OWN : (t + 1) * OWN]

    low, high = pair_lanes()

    @pl.loop(0, micros)
    def _(m):
        @pl.when(is_image)
        def _():
            row_copy(m, 0).wait_recv()
            beside(x, m, dot(places_ref[m], got[m]).astype(BF))

        extra = [x[m * TILES + t, OWN:TILE] for t in range(TILES)]
        beside(qkv, m, project(jnp.concatenate(extra, axis=0), vecs_ref, w))
        for copy in outs(m, (0, 1)):
            copy.start()

        @pl.loop(0, TILES)
        def _(t):
            tile = m * TILES + t
            slot = lax.rem(tile, 2)
            pl.when(tile > 1)(lambda: probs_store(tile - 2, slot).wait())
            barred = bars(ids_ref[tile])

            def maker(pair):
                at = pair * BLOCK
                cols = [qkv[tile, :, pl.ds(part * width + at, BLOCK)] for part in range(3)]
                return lambda: attend_pair(*cols, barred, low, high)

            def finish(pair, results):
                expos, out, inverse = results
                at = pair * BLOCK
                for n in range(2):
                    probs[slot, 2 * pair + n] = expos[n]
                att[tile, :, at : at + BLOCK] = out.astype(BF)
                inv[tile, :, at : at + BLOCK] = inverse.astype(BF)

            staggered([maker(pair) for pair in range(HEADS // 2)], finish)
            probs_store(tile, slot).start()

        for copy in outs(m, (2, 3)):
            copy.start()
        at = pl.multiple_of(m * TILES * OWN, 16)
        rows_ref[pl.ds(at, TILES * OWN)] = own_rows(att, m)

        @pl.when(is_image)
        def _():
            extra = [att[m * TILES + t, OWN:TILE] for t in range(TILES)]
            mine[m] = t_dot(places_ref[m], jnp.concatenate(extra, axis=0)).astype(BF)
            for s in range(3):

                @pl.when((own_z == s) & (m < micros - 1))
                def _():
                    back_copy(m, s).start()

        @pl.when(m == micros - 1)
        def _():
            rows_copy(micros - 1).start()
            mine_copy.start()

    for m in range(micros - 1):

        @pl.when(is_text)
        def _():
            for s in range(3):
                back_copy(m, s).wait_recv()
            parts = [got_back[m, s] for s in range(3)]
            parts += [att[m * TILES + t, OWN:TILE] for t in range(TILES)]
            moved = t_dot(picks_ref[m], jnp.concatenate(parts, axis=0)).astype(BF)
            at = pl.ds(m * TILES * OWN, TILES * OWN)
            rows_ref[at] = (rows_ref[at].astype(F32) + moved.astype(F32)).astype(BF)

        rows_copy(m).start()
        pl.when(is_image)(lambda: back_copy(m, 0).wait_send())

    @pl.when(is_text)
    def _():
        for m in range(micros):
            for s in range(3):
                row_copy(m, s).wait_send()

    for m in range(micros):
        rows_copy(m).wait()
        for copy in outs(m, range(4)):
            copy.wait()
    mine_copy.wait()
    for slot in range(2):
        tile = micros * TILES - 2 + slot
        probs_store(tile, tile % 2).wait()


def attend_rows(tokens, picks, places, ids, vecs, w_qkv):
    micros, _, width = tokens.shape
    tiles = micros * TILES
    dma = pltpu.SemaphoreType.DMA

    def sds(*shape):
        return jax.ShapeDtypeStruct(shape, BF)

    return pl.pallas_call(
        attend_rows_kernel,
        in_specs=[HBM] + [FULL] * 4 + [HBM],
        out_specs=[HBM] * 7,
        out_shape=[
            sds(tiles, TILE, width),
            sds(tiles, TILE, 3 * width),
            sds(tiles, HEADS, TILE, TILE),
            sds(tiles, TILE, width),
            sds(tiles, TILE, width),
            sds(tiles * OWN, width),
            sds(2 * SLOT, width),
        ],
        scratch_shapes=[
            pltpu.VMEM(tokens.shape, BF),
            pltpu.VMEM(w_qkv.shape, BF),
            pltpu.VMEM((tiles, TILE, width), BF),
            pltpu.VMEM((tiles, TILE, 3 * width), BF),
            pltpu.VMEM((2, HEADS, TILE, TILE), BF),
            pltpu.VMEM((tiles, TILE, width), BF),
            pltpu.VMEM((tiles, TILE, width), BF),
            pltpu.VMEM((tiles * OWN, width), BF),
            pltpu.VMEM((micros, 3, 2 * SLOT, width), BF),
            pltpu.VMEM((micros, 2 * SLOT, width), BF),
            pltpu.VMEM((micros, 2 * SLOT, width), BF),
            pltpu.VMEM((micros, 3, 2 * SLOT, width), BF),
            dma((micros,)),
            dma,
            dma((micros, 4)),
            dma((2,)),
            dma((micros + 1,)),
            dma((micros, 3)),
            dma((micros,)),
            dma((micros,)),
            dma((micros, 3)),
        ],
        compiler_params=pltpu.CompilerParams(
            vmem_limit_bytes=56 * 2**20, collective_id=3, has_side_effects=True
        ),
        name="attend_rows",
    )(tokens, picks, places, ids, vecs, w_qkv)


def attend_back_kernel(qkv_ref, p_ref, out_ref, inv_ref, grad_ref, dqkv_ref):
    width = out_ref.shape[2]
    low, high = pair_lanes()

    def maker(pair):
        at = pl.ds(pair * 128, 128)
        return lambda: attend_back_pair(
            *(qkv_ref[0, :, pl.ds(part * width + pair * 128, 128)] for part in range(3)),
            [p_ref[0, 2 * pair], p_ref[0, 2 * pair + 1]],
            out_ref[0, :, at],
            inv_ref[0, :, at],
            grad_ref[0, :, at],
            low,
            high,
        )

    def finish(pair, results):
        for part, value in enumerate(results):
            dqkv_ref[0, :, pl.ds(part * width + pair * 128, 128)] = value

    staggered([maker(pair) for pair in range(HEADS // 2)], finish)


def attend_back(qkv, probs, out, inverse, grad):
    tiles, _, width = out.shape

    def block(*shape):
        return pl.BlockSpec((1,) + shape, lambda i: (i,) + (0,) * len(shape))

    return pl.pallas_call(
        attend_back_kernel,
        grid=(tiles,),
        in_specs=[
            block(TILE, 3 * width),
            block(HEADS, TILE, TILE),
            block(TILE, width),
            block(TILE, width),
            block(TILE, width),
        ],
        out_specs=block(TILE, 3 * width),
        out_shape=jax.ShapeDtypeStruct((tiles, TILE, 3 * width), BF),
        compiler_params=pltpu.CompilerParams(vmem_limit_bytes=56 * 2**20),
        name="attend_back",
    )(qkv, probs, out, inverse, grad)


STEPS = 3


def add_into(ref, at, other):
    ref[at] = (ref[at].astype(F32) + other.astype(F32)).astype(BF)


class ItemSum:
    def __init__(self, up, down, got, got_one, got_two, sems):
        self.grads = (up, down)
        self.got, self.got_one, self.got_two, self.sems = got, got_one, got_two, sems
        me = lax.axis_index("dp")
        self.me = me
        self.core, self.x, self.y = lax.rem(me, 2), lax.rem(lax.div(me, 2), 2), lax.div(me, 4)
        self.near = me + 1 - 2 * self.core
        self.over_x = me + 2 - 4 * self.x
        self.over_y = me + 4 - 8 * self.y

    def _copy(self, src, dst, stage, which, slot, device):
        return pltpu.make_async_remote_copy(
            src_ref=src,
            dst_ref=dst,
            send_sem=self.sems.at[stage, which, 0, slot],
            recv_sem=self.sems.at[stage, which, 1, slot],
            device_id={"dp": device},
            device_id_type=MESH,
        )

    def core_copy(self, which, slot):
        src = self.grads[which].at[slot, :, :, 1 - self.core]
        return self._copy(src, self.got[which].at[slot], 0, which, slot, self.near)

    def one_copy(self, which, slot):
        grad = self.grads[which]
        if which == 0:
            src, device = grad.at[slot, :, 1 - self.x, self.core], self.over_x
        else:
            src, device = grad.at[slot, 1 - self.y, :, self.core], self.over_y
        return self._copy(src, self.got_one[which].at[slot], 1, which, slot, device)

    def two_copy(self, which, slot):
        grad = self.grads[which]
        if which == 0:
            src, device = grad.at[slot, 1 - self.y, self.x, self.core], self.over_y
        else:
            src, device = grad.at[slot, self.y, 1 - self.x, self.core], self.over_x
        return self._copy(src, self.got_two[which].at[slot], 2, which, slot, device)

    def start(self, which, slot):
        self.core_copy(which, slot).start()

    def after_core(self, slot):
        for which in range(2):
            self.core_copy(which, slot).wait()
            for y in range(2):
                for x in range(2):
                    at = (slot, y, x, self.core)
                    add_into(self.grads[which], at, self.got[which][slot, y, x])
            self.one_copy(which, slot).start()

    def after_one(self, slot):
        for which in range(2):
            self.one_copy(which, slot).wait()
            for side in range(2):
                at = (slot, side, self.x, self.core) if which == 0 else (slot, self.y, side, self.core)
                add_into(self.grads[which], at, self.got_one[which][slot, side])
            self.two_copy(which, slot).start()

    def after_two(self, slot):
        sums = []
        for which in range(2):
            self.two_copy(which, slot).wait()
            own = self.grads[which][slot, self.y, self.x, self.core].astype(F32)
            sums.append((own + self.got_two[which][slot].astype(F32)).astype(BF))
        return sums


def meet(devices):
    barrier = pltpu.get_barrier_semaphore()
    for device in devices:
        pl.semaphore_signal(barrier, inc=1, device_id=device, device_id_type=MESH)
    pl.semaphore_wait(barrier, len(devices))


def expert_kernel(
    remote,
    x_ref,
    att_ref,
    att_tiles_ref,
    att_last_ref,
    dy_ref,
    w_out_ref,
    vecs_ref,
    picks_ref,
    places_ref,
    up_v_ref,
    down_v_ref,
    up_t_ref,
    down_t_ref,
    out_ref,
    dmid_ref,
    datt_ref,
    dwout_ref,
    vec_ref,
    dup_ref,
    ddown_ref,
    *refs,
):
    if remote:
        dup_last_ref, ddown_last_ref, rows_last_ref, *refs = refs
    raw, dy, att, w_out, mid, tiles, hid_t, dy_t, acc_o, acc_h, up_w, down_w, *refs = refs
    act, gup, dup_buf, ddown_buf, sems, io_sems, *more = refs
    width = att.shape[1]
    cols = act.shape[2]
    micros = raw.shape[0]
    rows = TILES * OWN
    own_z = lax.axis_index("stream")
    is_text = own_z == 3
    is_image = jnp.logical_not(is_text)
    pieces = 8 if remote else 1
    piece = cols // pieces
    ff = up_v_ref.shape[1]

    def rows_of(m):
        return pl.ds(pl.multiple_of(m * rows, 16), rows)

    def loads(m):
        at = pl.ds(m * rows, rows)
        yield pltpu.make_async_copy(att_ref.at[at], att.at[at], io_sems.at[m, 0])
        for t in range(TILES):
            src = x_ref.at[m * TILES + t, 0:OWN]
            dst = act.at[m, t * OWN : (t + 1) * OWN, 0:width]
            yield pltpu.make_async_copy(src, dst, io_sems.at[m, 1 + t])

    def raw_copy(m):
        return pltpu.make_async_copy(dy_ref.at[m], raw.at[m], io_sems.at[m, 4])

    def store(m, n):
        at = rows_of(m)
        tile_at = pl.ds(m * TILES, TILES)
        src, dst = (
            (mid.at[at], dmid_ref.at[at]),
            (tiles.at[tile_at], datt_ref.at[tile_at]),
            (raw.at[m], out_ref.at[m]),
        )[n]
        return pltpu.make_async_copy(src, dst, io_sems.at[m, 5 + n])

    w_out_copy = pltpu.make_async_copy(w_out_ref, w_out, io_sems.at[0, 8])
    dwout = dy_t.at[:, 0:width]
    dwout_copy = pltpu.make_async_copy(dwout, dwout_ref, io_sems.at[0, 8])

    def fetch(j, slot):
        def go(up_src, down_src):
            for d in range(pieces):
                at = pl.ds(pl.multiple_of(j * piece + d * (ff // pieces), 128), piece)
                here = pl.ds(d * piece, piece)
                pltpu.make_async_copy(
                    up_src.at[:, at], up_w.at[slot, :, here], sems.at[0, slot]
                ).start()
                pltpu.make_async_copy(
                    down_src.at[at, :], down_w.at[slot, here, :], sems.at[1, slot]
                ).start()

        pl.when(is_text)(lambda: go(up_t_ref, down_t_ref))
        pl.when(is_image)(lambda: go(up_v_ref, down_v_ref))

    def fetched(slot):
        pltpu.make_async_copy(up_w.at[slot], up_w.at[slot], sems.at[0, slot]).wait()
        pltpu.make_async_copy(down_w.at[slot], down_w.at[slot], sems.at[1, slot]).wait()

    for m in range(micros):
        raw_copy(m).start()
    w_out_copy.start()
    for m in range(micros):
        for copy in loads(m):
            copy.start()
    fetch(0, 0)

    if remote:
        got, got_one, got_two, sum_sems = more[0:2], more[2:4], more[4:6], more[6]
        sent, got_rows, row_send, row_recv, got_att, att_side, att_send, att_recv, side_sem = more[7:]
        total = ItemSum(dup_buf, ddown_buf, got, got_one, got_two, sum_sems)

        def side_copies():
            for t in range(TILES):
                src = att_tiles_ref.at[(micros - 1) * TILES + t, OWN:TILE]
                yield pltpu.make_async_copy(src, att_side.at[t], side_sem.at[t])

        for copy in side_copies():
            copy.start()
        meet(
            [{"dp": total.near}, {"dp": total.over_x}, {"dp": total.over_y}]
            + [{"stream": lax.rem(own_z + k, 4)} for k in range(1, 4)]
        )

        def att_copy(s):
            return pltpu.make_async_remote_copy(
                src_ref=att_last_ref,
                dst_ref=got_att.at[s],
                send_sem=att_send,
                recv_sem=att_recv.at[s],
                device_id={"stream": 3},
                device_id_type=MESH,
            )

        for s in range(3):
            pl.when(own_z == s)(lambda: att_copy(s).start())

        def row_copy(m, s):
            return pltpu.make_async_remote_copy(
                src_ref=sent.at[m, s],
                dst_ref=got_rows.at[m],
                send_sem=row_send.at[m, s],
                recv_sem=row_recv.at[m],
                device_id={"stream": s},
                device_id_type=MESH,
            )

    gain, shift = row_of(vecs_ref, GAIN2), row_of(vecs_ref, SHIFT2)
    bias = jnp.where(is_text, row_of(vecs_ref, TXT_BIAS), row_of(vecs_ref, VIS_BIAS))
    space = dy_t.shape[1] // micros
    for ref in (hid_t, dy_t):
        for m in range(micros):
            lanes = slice(m * space + rows, (m + 1) * space)
            ref[:, lanes] = jnp.zeros((width, space - rows), BF)
    for ref in (act, gup):
        ref[:, rows:space] = jnp.zeros((micros, space - rows, cols), BF)
    pad = padding(False)
    for m in range(micros):
        raw_copy(m).wait()
        dy[m * rows : (m + 1) * rows] = dot(pad, raw[m]).astype(BF)
        dy_t[:, m * space : m * space + rows] = dy[m * rows : (m + 1) * rows].T

    def put_rows(m, value):
        for t in range(TILES):
            tiles[m * TILES + t, 0:OWN] = value[t * OWN : (t + 1) * OWN]

    def own_rows(m):
        return jnp.concatenate([tiles[m * TILES + t, 0:OWN] for t in range(TILES)], axis=0)

    def beside(m, value):
        for t in range(TILES):
            part = value[t * (TILE - OWN) : (t + 1) * (TILE - OWN)]
            tiles[m * TILES + t, OWN:TILE] = part

    def begin(m):
        for copy in loads(m):
            copy.wait()
        if m == 0:
            w_out_copy.wait()
        at = rows_of(m)
        if remote and m == micros - 1:

            @pl.when(is_text)
            def _():
                for s in range(3):
                    att_copy(s).wait_recv()
                parts = [got_att[s] for s in range(3)] + [att_side[t] for t in range(TILES)]
                moved = t_dot(picks_ref[m], jnp.concatenate(parts, axis=0)).astype(BF)
                att[at] = (att[at].astype(F32) + moved.astype(F32)).astype(BF)

        middle = act[m, 0:rows, 0:width].astype(F32) + dot(att[at], w_out[...])
        mid[at] = middle
        normed, _ = normalize(middle)
        hidden = (normed * gain + shift).astype(BF)
        put_rows(m, hidden)
        hid_t[:, m * space : m * space + rows] = hidden.T
        acc_o[at] = middle + bias
        acc_h[at] = jnp.zeros_like(middle)

    if remote:
        for copy in side_copies():
            copy.wait()

    def deliver(slot, j):
        up, down = total.after_two(slot)
        for t in range(4):
            dup_ref[t, j] = up[:, t * (cols // 4) : (t + 1) * (cols // 4)]
            ddown_ref[t, j] = down[t * (width // 4) : (t + 1) * (width // 4)]

    def stored(j, slot):
        return (
            pltpu.make_async_copy(dup_buf.at[slot], dup_ref.at[j], sems.at[2, slot]),
            pltpu.make_async_copy(ddown_buf.at[slot], ddown_ref.at[j], sems.at[3, slot]),
        )

    @pl.loop(0, STEPS)
    def _(j):
        slot = lax.rem(j, 2)
        other = 1 - slot
        pl.when(j < STEPS - 1)(lambda: fetch(j + 1, other))
        fetched(slot)

        @pl.loop(0, micros)
        def _(m):
            for n in range(micros):
                pl.when((j == 0) & (m == n))(lambda: begin(n))
            at = rows_of(m)
            up = dot(own_rows(m), up_w[slot])
            grad = dot_t(dy[at], down_w[slot])
            for t in range(TILES):
                part = slice(t * OWN, (t + 1) * OWN)
                cdf, pdf = gelu_parts(up[part])
                act[m, part] = (up[part] * cdf).astype(BF)
                gup[m, part] = (grad[part] * (cdf + up[part] * pdf)).astype(BF)
            acc_o[at] += dot(act[m, 0:rows], down_w[slot])
            acc_h[at] += dot_t(gup[m, 0:rows], up_w[slot])
            if remote:

                @pl.when(m == 0)
                def _():
                    pl.when(j > 1)(lambda: deliver(slot, j - 2))
                    pl.when(j > 0)(lambda: total.after_core(other))

        if not remote:

            @pl.when(j > 1)
            def _():
                for copy in stored(j - 2, slot):
                    copy.wait()

        grad = dot(hid_t[...], gup[...].reshape(micros * space, cols)).astype(BF)
        if remote:
            dup_buf[slot] = grad.reshape(dup_buf.shape[1:])
            pl.when(j < STEPS - 1)(lambda: total.start(0, slot))
            pl.when(j > 0)(lambda: total.after_one(other))
        else:
            dup_buf[slot] = grad
        grad = dot(dy_t[...], act[...].reshape(micros * space, cols)).astype(BF)
        if remote:
            for d in range(8):
                ddown_buf[slot, d // 4, d // 2 % 2, d % 2] = grad[:, d * piece : (d + 1) * piece]
            pl.when(j < STEPS - 1)(lambda: total.start(1, slot))
        else:
            ddown_buf[slot] = grad
            for copy in stored(j, slot):
                copy.start()

    last = (STEPS - 1) % 2
    if remote:
        last_copies = [
            pltpu.make_async_copy(dup_buf.at[last], dup_last_ref, sems.at[2, 0]),
            pltpu.make_async_copy(ddown_buf.at[last], ddown_last_ref, sems.at[3, 0]),
        ]
        for copy in last_copies:
            copy.start()
    vec_ref[...] = jnp.zeros_like(vec_ref)

    for m in range(micros):
        at = rows_of(m)
        normed, inverse = normalize(mid[at])
        grad = acc_h[at]
        wide = dy[at].astype(F32)
        vec_ref[0:1, :] += jnp.sum(grad * normed, axis=0, keepdims=True)
        vec_ref[1:2, :] += jnp.sum(grad, axis=0, keepdims=True)
        vec_ref[2:3, :] += jnp.sum(wide, axis=0, keepdims=True)
        grad_mid = wide + norm_back(grad, normed, inverse, gain)
        mid[at] = grad_mid
        store(m, 0).start()
        branch = grad_mid.astype(BF)
        gup[m, 0:rows, 0:width] = branch
        put_rows(m, dot_t(branch, w_out[...]).astype(BF))
        if remote:

            @pl.when(is_text)
            def _():
                picked = dot(picks_ref[m], own_rows(m)).astype(BF)
                for s in range(3):
                    part = picked[s * 2 * SLOT : (s + 1) * 2 * SLOT]
                    if m < micros - 1:
                        sent[m, s] = part
                        row_copy(m, s).start()
                    else:
                        rows_last_ref[s] = part
                beside(m, picked[6 * SLOT :])

            if m == micros - 1:

                @pl.when(is_image)
                def _():
                    rows_last_ref[...] = jnp.zeros_like(rows_last_ref)
                    for t in range(TILES):
                        tiles[m * TILES + t, OWN:TILE] = jnp.zeros((TILE - OWN, width), BF)

                store(m, 1).start()
            else:
                pl.when(is_text)(lambda: store(m, 1).start())
        else:
            store(m, 1).start()

    if remote:
        deliver(1 - last, STEPS - 2)
    unpad = padding(True)
    for m in range(micros):
        raw[m] = dot(unpad, acc_o[rows_of(m)].astype(BF)).astype(BF)
        store(m, 2).start()
    branch = gup[:, 0:rows, 0:width].reshape(micros * rows, width)
    dwout[...] = t_dot(att[...], branch).astype(BF)
    dwout_copy.start()
    if remote:

        @pl.when(is_text)
        def _():
            for m in range(micros - 1):
                for s in range(3):
                    row_copy(m, s).wait_send()

        @pl.when(is_image)
        def _():
            for m in range(micros - 1):
                row_copy(m, 0).wait_recv()
                beside(m, dot(places_ref[m], got_rows[m]).astype(BF))
                store(m, 1).start()
            att_copy(0).wait_send()

        for copy in last_copies:
            copy.wait()
    else:
        for j in range(STEPS - 2, STEPS):
            for copy in stored(j, j % 2):
                copy.wait()
    for m in range(micros):
        for n in range(3):
            store(m, n).wait()
    dwout_copy.wait()


def expert(
    remote,
    x_tiles,
    att,
    att_tiles,
    att_last,
    dy,
    w_out,
    vecs,
    picks,
    places,
    vis_up,
    vis_down,
    txt_up,
    txt_down,
):
    rows, width = att.shape
    cols = vis_up.shape[1] // STEPS
    micros = dy.shape[0]
    space = -(-rows // micros // BLOCK) * BLOCK
    dma = pltpu.SemaphoreType.DMA
    if remote:
        shard, piece = width // 8, cols // 8
        buffers = (2, 2, 2, 2, shard, cols), (2, 2, 2, 2, width, piece)
        outs = (4, STEPS - 1, shard, cols // 4), (4, STEPS - 1, width // 4, piece)
        lasts = [buffers[0][1:], buffers[1][1:], (3, 2 * SLOT, width)]
        out_specs = [HBM] * 4 + [FULL] * 3 + [HBM] * 2 + [FULL]
        more = [
            pltpu.VMEM((2, 2, 2, shard, cols), BF),
            pltpu.VMEM((2, 2, 2, width, piece), BF),
            pltpu.VMEM((2, 2, shard, cols), BF),
            pltpu.VMEM((2, 2, width, piece), BF),
            pltpu.VMEM((2, shard, cols), BF),
            pltpu.VMEM((2, width, piece), BF),
            dma((3, 2, 2, 2)),
            pltpu.VMEM((micros - 1, 3, 2 * SLOT, width), BF),
            pltpu.VMEM((micros - 1, 2 * SLOT, width), BF),
            dma((micros - 1, 3)),
            dma((micros - 1,)),
            pltpu.VMEM((3, 2 * SLOT, width), BF),
            pltpu.VMEM((TILES, TILE - OWN, width), BF),
            dma,
            dma((3,)),
            dma((TILES,)),
        ]
        params = dict(collective_id=1, has_side_effects=True)
    else:
        buffers = ((2, width, cols),) * 2
        outs = ((STEPS, width, cols),) * 2
        lasts, out_specs = [], [HBM] * 4 + [FULL] + [HBM] * 2
        more, params = [], {}
    return pl.pallas_call(
        functools.partial(expert_kernel, remote),
        in_specs=[HBM] * 6 + [FULL] * 3 + [HBM] * 4,
        out_specs=out_specs,
        out_shape=[
            jax.ShapeDtypeStruct(dy.shape, BF),
            jax.ShapeDtypeStruct((rows, width), F32),
            jax.ShapeDtypeStruct((rows // OWN, TILE, width), BF),
            jax.ShapeDtypeStruct((width, width), BF),
            jax.ShapeDtypeStruct((8, width), F32),
        ]
        + [jax.ShapeDtypeStruct(shape, BF) for shape in [*outs, *lasts]],
        scratch_shapes=[
            pltpu.VMEM(dy.shape, BF),
            pltpu.VMEM((rows, width), BF),
            pltpu.VMEM((rows, width), BF),
            pltpu.VMEM((width, width), BF),
            pltpu.VMEM((rows, width), F32),
            pltpu.VMEM((rows // OWN, TILE, width), BF),
            pltpu.VMEM((width, micros * space), BF),
            pltpu.VMEM((width, micros * space), BF),
            pltpu.VMEM((rows, width), F32),
            pltpu.VMEM((rows, width), F32),
            pltpu.VMEM((2, width, cols), BF),
            pltpu.VMEM((2, cols, width), BF),
            pltpu.VMEM((micros, space, cols), BF),
            pltpu.VMEM((micros, space, cols), BF),
            pltpu.VMEM(buffers[0], BF),
            pltpu.VMEM(buffers[1], BF),
            dma((4, 2)),
            dma((micros, 9)),
        ]
        + more,
        compiler_params=pltpu.CompilerParams(vmem_limit_bytes=63 * 2**20, **params),
        name="expert",
    )(
        x_tiles,
        att,
        att_tiles,
        att_last,
        dy,
        w_out,
        vecs,
        picks,
        places,
        vis_up,
        vis_down,
        txt_up,
        txt_down,
    )


def project_back_kernel(x_ref, dqkv_ref, vecs_ref, w_ref, dx_ref, dw_ref, vec_ref, acc):
    i = pl.program_id(0)
    gain, shift = row_of(vecs_ref, GAIN1), row_of(vecs_ref, SHIFT1)
    normed, inverse = normalize(x_ref[0].astype(F32))
    hidden = (normed * gain + shift).astype(BF)
    dqkv = dqkv_ref[0]
    grad = dot_t(dqkv, w_ref[...])
    dx_ref[0] = norm_back(grad, normed, inverse, gain).astype(BF)
    width = x_ref.shape[2]
    part = t_dot(hidden, dqkv)
    ones = jnp.ones((8, TILE), BF)
    sums = dot(ones, dqkv)[0:1]
    vec = jnp.concatenate(
        [
            jnp.sum(grad * normed, axis=0, keepdims=True),
            jnp.sum(grad, axis=0, keepdims=True),
            sums[:, :width],
            sums[:, 2 * width :],
        ],
        axis=0,
    )

    @pl.when(i == 0)
    def _():
        acc[...] = part
        vec_ref[0:4, :] = vec

    @pl.when(i > 0)
    def _():
        acc[...] += part
        vec_ref[0:4, :] += vec

    @pl.when(i == pl.num_programs(0) - 1)
    def _():
        dw_ref[...] = acc[...].astype(BF)


def project_back(x_tiles, dqkv, vecs, w_qkv):
    tiles, _, width = x_tiles.shape

    def block(*shape):
        return pl.BlockSpec((1,) + shape, lambda i: (i,) + (0,) * len(shape))

    return pl.pallas_call(
        project_back_kernel,
        grid=(tiles,),
        in_specs=[block(TILE, width), block(TILE, 3 * width), FULL, FULL],
        out_specs=[block(TILE, width), FULL, FULL],
        out_shape=[
            jax.ShapeDtypeStruct((tiles, TILE, width), BF),
            jax.ShapeDtypeStruct((width, 3 * width), BF),
            jax.ShapeDtypeStruct((8, width), F32),
        ],
        scratch_shapes=[pltpu.VMEM((width, 3 * width), F32)],
        compiler_params=pltpu.CompilerParams(vmem_limit_bytes=56 * 2**20),
        name="project_back",
    )(x_tiles, dqkv, vecs, w_qkv)


GROUP = 256
GROUPS = 3


def stream_blocks(count, share):
    spans = []
    for t in range(4):
        first, last = t * share // BLOCK, ((t + 1) * share - 1) // BLOCK
        spans.append(list(range(first, last + 1)))
    assert spans[-1][-1] == count - 1
    return spans


def unit_blocks(unit):
    if unit == 0:
        return list(range(6))
    g = unit - 1
    return [6 * part + 2 * g + i for part in range(3) for i in range(2)]


def back_kernel(
    x_ref,
    qkv_ref,
    p_ref,
    att_ref,
    inv_ref,
    datt_ref,
    dmid_ref,
    vecs_ref,
    w_ref,
    dwout_ref,
    zup_ref,
    zdown_ref,
    dup_last_ref,
    ddown_last_ref,
    rows_last_ref,
    vec2_ref,
    picks_ref,
    places_ref,
    dx_ref,
    sums_ref,
    dqkv_ref,
    dout_ref,
    dvup_ref,
    dvdown_ref,
    dtup_ref,
    dtdown_ref,
    qkv,
    x,
    att,
    inv,
    datt,
    base,
    probs,
    beside,
    got_last,
    last_a,
    last_b,
    got_last_a,
    got_last_b,
    one_last_a,
    one_last_b,
    two_last_a,
    two_last_b,
    z_last_up,
    z_last_down,
    hid_t,
    dqkv,
    w,
    sums,
    grad_hid,
    extra,
    mine,
    got_rows,
    buf_a,
    buf_b,
    got_a,
    got_b,
    one_a,
    one_b,
    two_a,
    two_b,
    held,
    got_qkv,
    got_out,
    got_up,
    got_down,
    vec,
    got_vec,
    z_vec,
    load_sems,
    x_sems,
    w_sem,
    last_sems,
    last_send,
    last_recv,
    last_sum_sems,
    sum_sems,
    row_send,
    row_recv,
    vec_sems,
    zvec_send,
    zvec_recv,
    expert_send,
    expert_recv,
    block_send,
    block_recv,
):
    micros = x.shape[0] // TILES
    width = x.shape[2]
    shard = width // 8
    own_z = lax.axis_index("stream")
    is_text = own_z == 3
    is_image = jnp.logical_not(is_text)
    total = ItemSum(buf_a, buf_b, (got_a, got_b), (one_a, one_b), (two_a, two_b), sum_sems)

    total_last = ItemSum(
        last_a,
        last_b,
        (got_last_a, got_last_b),
        (one_last_a, one_last_b),
        (two_last_a, two_last_b),
        last_sum_sems,
    )

    def loads(step, slot):
        m, g = lax.div(step, GROUPS), lax.rem(step, GROUPS)
        tiles = pl.ds(m * TILES, TILES)
        at = pl.multiple_of(g * GROUP, GROUP)
        copies = [pltpu.make_async_copy(p_ref.at[tiles, pl.ds(g * 4, 4)], probs.at[slot], load_sems.at[slot, 0])]
        for part in range(3):
            src = qkv_ref.at[tiles, :, pl.ds(part * width + at, GROUP)]
            dst = qkv.at[slot, :, :, pl.ds(part * GROUP, GROUP)]
            copies.append(pltpu.make_async_copy(src, dst, load_sems.at[slot, 1 + part]))
        for n, (src, dst) in enumerate(((att_ref, att), (inv_ref, inv), (datt_ref, datt))):
            src = src.at[tiles, :, pl.ds(at, GROUP)]
            copies.append(pltpu.make_async_copy(src, dst.at[slot], load_sems.at[slot, 4 + n]))
        return copies

    def micro_loads(m):
        at = pl.ds(m * TILES, TILES)
        rows = pl.ds(m * TILES * OWN, TILES * OWN)
        return [
            pltpu.make_async_copy(x_ref.at[at], x.at[at], x_sems.at[m, 0]),
            pltpu.make_async_copy(dmid_ref.at[rows], base.at[rows], x_sems.at[m, 1]),
        ]

    last_loads = [
        pltpu.make_async_copy(dup_last_ref, last_a.at[0], last_sems.at[0]),
        pltpu.make_async_copy(ddown_last_ref, last_b.at[0], last_sems.at[1]),
    ]
    w_copies = []
    for g in range(GROUPS):
        for part in range(3):
            src = w_ref.at[:, pl.ds(part * width + g * GROUP, GROUP)]
            dst = w.at[:, pl.ds((g * 3 + part) * GROUP, GROUP)]
            w_copies.append(pltpu.make_async_copy(src, dst, w_sem))
    for copy in loads(0, 0):
        copy.start()
    meet(
        [{"dp": total.near}, {"dp": total.over_x}, {"dp": total.over_y}]
        + [{"stream": lax.rem(own_z + k, 4)} for k in range(1, 4)]
    )

    def last_row_copy(s):
        return pltpu.make_async_remote_copy(
            src_ref=rows_last_ref.at[s],
            dst_ref=got_last,
            send_sem=last_send.at[s],
            recv_sem=last_recv,
            device_id={"stream": s},
            device_id_type=MESH,
        )

    @pl.when(is_text)
    def _():
        for s in range(3):
            last_row_copy(s).start()

    done = zup_ref.shape[1]

    def expert_ends(which, t, src):
        if which == 0:
            return zup_ref.at[t], got_up.at[src, pl.ds(0, done)]
        if which == 1:
            return zdown_ref.at[t], got_down.at[src, pl.ds(0, done)]
        if which == 2:
            return z_last_up.at[t], got_up.at[src, done]
        return z_last_down.at[t], got_down.at[src, done]

    def expert_copy(t, which):
        src, dst = expert_ends(which, t, own_z)
        return pltpu.make_async_remote_copy(
            src_ref=src,
            dst_ref=dst,
            send_sem=expert_send.at[t, which],
            recv_sem=expert_recv.at[own_z, which],
            device_id={"stream": t},
            device_id_type=MESH,
        )

    def expert_arrival(src, which):
        dst = expert_ends(which, src, src)[1]
        return pltpu.make_async_remote_copy(
            src_ref=dst,
            dst_ref=dst,
            send_sem=expert_send.at[src, which],
            recv_sem=expert_recv.at[src, which],
            device_id={"stream": src},
            device_id_type=MESH,
        )

    def expert_sends(kinds):
        for t in range(4):

            @pl.when(own_z != t)
            def _():
                for which in kinds:
                    expert_copy(t, which).start()

            @pl.when(own_z == t)
            def _():
                for which in kinds:
                    src, dst = expert_ends(which, t, t)
                    pltpu.make_async_copy(src, dst, expert_send.at[t, which]).start()

    def take_last():
        up, down = total_last.after_two(0)
        part_up, part_down = z_last_up.shape[2], z_last_down.shape[1]
        for t in range(4):
            z_last_up[t] = up[:, t * part_up : (t + 1) * part_up]
            z_last_down[t] = down[t * part_down : (t + 1) * part_down]
        expert_sends((2, 3))

    expert_sends((0, 1))

    half = buf_a.shape[-1]

    def put_unit(unit, value):
        slot = lax.rem(unit, 2)
        buf_a[slot] = value[:, :half].reshape(buf_a.shape[1:])
        buf_b[slot] = value[:, half:].reshape(buf_b.shape[1:])
        total.start(0, slot)
        total.start(1, slot)

    def take_unit(unit):
        left, right = total.after_two(lax.rem(unit, 2))
        for n in range(3):
            held[unit, n] = left[:, n * BLOCK : (n + 1) * BLOCK]
            held[unit, n + 3] = right[:, n * BLOCK : (n + 1) * BLOCK]

    def block_copy(unit, n, t, place):
        dst = got_out if unit == 0 else got_qkv
        kind = 0 if unit == 0 else 1
        return pltpu.make_async_remote_copy(
            src_ref=held.at[unit, n],
            dst_ref=dst.at[own_z, place],
            send_sem=block_send.at[kind, t, place],
            recv_sem=block_recv.at[kind, own_z, place],
            device_id={"stream": t},
            device_id_type=MESH,
        )

    out_spans = stream_blocks(6, width // 4)
    qkv_spans = stream_blocks(18, 3 * width // 4)

    def unit_sends(unit, t):
        span = (out_spans if unit == 0 else qkv_spans)[t]
        blocks = unit_blocks(unit)
        return [(n, span.index(b)) for n, b in enumerate(blocks) if b in span]

    def send_unit(unit):
        for t in range(4):

            @pl.when(own_z != t)
            def _():
                for n, place in unit_sends(unit, t):
                    block_copy(unit, n, t, place).start()

            @pl.when(own_z == t)
            def _():
                dst = got_out if unit == 0 else got_qkv
                for n, place in unit_sends(unit, t):
                    dst[t, place] = held[unit, n]

    put_unit(0, dwout_ref[...])

    def row_copy(m, s):
        return pltpu.make_async_remote_copy(
            src_ref=mine.at[m],
            dst_ref=got_rows.at[m, s],
            send_sem=row_send.at[m],
            recv_sem=row_recv.at[m, s],
            device_id={"stream": 3},
            device_id_type=MESH,
        )

    low, high = pair_lanes()
    gain, shift = row_of(vecs_ref, GAIN1), row_of(vecs_ref, SHIFT1)
    vec[...] = jnp.zeros_like(vec)

    def add_vec(row, value):
        for d in range(8):
            vec[d, row : row + 1, 0:shard] += value[:, d * shard : (d + 1) * shard]

    add_vec(4, vec2_ref[0:1, :])
    add_vec(5, vec2_ref[1:2, :])
    text_scale = jnp.where(is_text, 1.0, 0.0)
    add_vec(6, vec2_ref[2:3, :] * (1.0 - text_scale))
    add_vec(7, vec2_ref[2:3, :] * text_scale)

    steps = micros * GROUPS
    span = 3 * GROUP
    lasts = TILES * TILE
    hid_t[width:] = jnp.ones_like(hid_t[width:])

    @pl.loop(0, steps)
    def _(step):
        m, g = lax.div(step, GROUPS), lax.rem(step, GROUPS)
        slot = lax.rem(step, 2)
        first = m * TILES
        here = pl.ds(pl.multiple_of(m * lasts, lasts), lasts)
        there = pl.multiple_of(g * span, span)

        @pl.when(step + 1 < steps)
        def _():
            for copy in loads(step + 1, 1 - slot):
                copy.start()

        @pl.when(step == 0)
        def _():
            for m in range(micros):
                for copy in micro_loads(m):
                    copy.start()
            for copy in last_loads + w_copies:
                copy.start()

        for copy in loads(step, slot):
            copy.wait()

        @pl.when(is_image & (m == micros - 1))
        def _():
            @pl.when(g == 0)
            def _():
                last_row_copy(0).wait_recv()
                beside[...] = dot(places_ref[m], got_last[...]).astype(BF)

            cols = pl.ds(pl.multiple_of(g * GROUP, GROUP), GROUP)
            for t in range(TILES):
                datt[slot, t, OWN:TILE] = beside[t * (TILE - OWN) : (t + 1) * (TILE - OWN), cols]

        @pl.when((step >= 1) & (step <= micros))
        def _():
            first = (step - 1) * TILES
            for copy in micro_loads(step - 1):
                copy.wait()
            for t in range(TILES):
                normed, _ = normalize(x[first + t].astype(F32))
                hidden = (normed * gain + shift).astype(BF)
                at = pl.multiple_of((first + t) * TILE, TILE)
                hid_t[0:width, pl.ds(at, TILE)] = hidden.T

        def maker(t, pair):
            at = pair * BLOCK
            cols = pl.ds(at, BLOCK)
            return lambda: attend_back_pair(
                *(qkv[slot, t, :, pl.ds(part * GROUP + at, BLOCK)] for part in range(3)),
                [probs[slot, t, 2 * pair], probs[slot, t, 2 * pair + 1]],
                att[slot, t, :, cols],
                inv[slot, t, :, cols],
                datt[slot, t, :, cols],
                low,
                high,
            )

        def finish(n, results):
            t, pair = n // 2, n % 2
            rows = pl.ds(pl.multiple_of((first + t) * TILE, TILE), TILE)
            for part, value in enumerate(results):
                at = pl.multiple_of(there + part * GROUP + pair * BLOCK, BLOCK)
                dqkv[rows, pl.ds(at, BLOCK)] = value

        staggered([maker(n // 2, n % 2) for n in range(2 * TILES)], finish)

        @pl.when(step == 0)
        def _():
            total.after_core(0)
            for copy in last_loads:
                copy.wait()
            total_last.start(0, 0)
            total_last.start(1, 0)

        @pl.when(step == 1)
        def _():
            total.after_one(0)
            total_last.after_core(0)

        @pl.when(step == 2)
        def _():
            take_unit(0)
            send_unit(0)

        pl.when(step == 3)(lambda: total_last.after_one(0))
        pl.when(step == 4)(take_last)

        @pl.when(step == steps - 2)
        def _():
            total.after_core(1)

        @pl.when(step == steps - 1)
        def _():
            total.after_one(1)
            total.after_core(0)

        @pl.when(m == micros - 1)
        def _():
            grad = dot(hid_t[...], dqkv[:, pl.ds(there, span)])
            sums[g] = grad[width : width + 8]
            pl.when(step == steps - 1)(lambda: take_unit(1))
            put_unit(1 + g, grad[:width].astype(BF))
            pl.when(step == steps - 1)(lambda: send_unit(1))

        @pl.when(step == GROUPS - 1)
        def _():
            pltpu.make_async_copy(w, w, w_sem).wait()

        @pl.when(g == GROUPS - 1)
        def _():
            grad_hid[...] = dot_t(dqkv[here, :], w[...])
            for t in range(TILES):
                normed, inverse = normalize(x[first + t].astype(F32))
                grad = grad_hid[t * TILE : (t + 1) * TILE]
                add_vec(0, jnp.sum(grad * normed, axis=0, keepdims=True))
                add_vec(1, jnp.sum(grad, axis=0, keepdims=True))
                back = norm_back(grad, normed, inverse, gain)
                rows = pl.ds(pl.multiple_of((first + t) * OWN, 16), OWN)
                base[rows] += back[:OWN]
                extra[m, t * (TILE - OWN) : (t + 1) * (TILE - OWN)] = back[OWN:].astype(BF)

            @pl.when(jnp.logical_not(is_text))
            def _():
                mine[m] = t_dot(places_ref[m], extra[m]).astype(BF)
                for s in range(3):

                    @pl.when(own_z == s)
                    def _():
                        row_copy(m, s).start()

    for row, at in ((2, 0), (3, 2 * GROUP)):
        cols = [sums[g, 0:1, at : at + GROUP] for g in range(GROUPS)]
        add_vec(row, jnp.concatenate(cols, axis=1))

    def vec_copy(stage):
        device = (total.near, total.over_x, total.over_y)[stage]
        return pltpu.make_async_remote_copy(
            src_ref=vec,
            dst_ref=got_vec.at[stage],
            send_sem=vec_sems.at[stage, 0],
            recv_sem=vec_sems.at[stage, 1],
            device_id={"dp": device},
            device_id_type=MESH,
        )

    def vec_stage(stage):
        vec_copy(stage).wait()
        vec[...] += got_vec[stage]

    def zvec_copy(t):
        return pltpu.make_async_remote_copy(
            src_ref=vec.at[total.me],
            dst_ref=z_vec.at[own_z],
            send_sem=zvec_send.at[t],
            recv_sem=zvec_recv.at[own_z],
            device_id={"stream": t},
            device_id_type=MESH,
        )

    def zvec_arrival(s):
        return pltpu.make_async_remote_copy(
            src_ref=z_vec.at[s],
            dst_ref=z_vec.at[s],
            send_sem=zvec_send.at[s],
            recv_sem=zvec_recv.at[s],
            device_id={"stream": s},
            device_id_type=MESH,
        )

    vec_copy(0).start()
    total.after_one(0)
    total.after_core(1)
    vec_stage(0)
    vec_copy(1).start()

    rows_all = TILES * OWN
    unpad = padding(True)

    def deliver(m, scattered):
        rows = pl.ds(m * rows_all, rows_all)
        value = base[rows]
        if scattered:
            value = value + t_dot(
                picks_ref[m], jnp.concatenate([got_rows[m, s] for s in range(3)] + [extra[m]], axis=0)
            )
        dx_ref[m] = dot(unpad, value.astype(BF)).astype(BF)

    @pl.when(jnp.logical_not(is_text))
    def _():
        for m in range(micros - 1):
            deliver(m, False)

    @pl.when(is_text)
    def _():
        for m in range(micros - 1):
            for s in range(3):
                row_copy(m, s).wait_recv()
            deliver(m, True)

    take_unit(2)
    send_unit(2)
    total.after_one(1)
    vec_stage(1)
    vec_copy(2).start()

    @pl.when(jnp.logical_not(is_text))
    def _():
        deliver(micros - 1, False)

    ff_piece = got_down.shape[3]
    for src in range(4):

        @pl.when(own_z != src)
        def _():
            for which in range(4):
                expert_arrival(src, which).wait_recv()
                expert_copy(src, which).wait_send()

        @pl.when(own_z == src)
        def _():
            for which in range(4):
                ref, dst = expert_ends(which, src, src)
                pltpu.make_async_copy(ref, dst, expert_send.at[src, which]).wait()

    for j in range(STEPS):
        vis = sum(got_up[s, j].astype(F32) for s in range(3))
        txt = got_up[3, j].astype(F32)
        for d in range(2):
            at = (d * STEPS + j) * ff_piece
            dvup_ref[:, at : at + ff_piece] = vis[:, d * ff_piece : (d + 1) * ff_piece]
            dtup_ref[:, at : at + ff_piece] = txt[:, d * ff_piece : (d + 1) * ff_piece]
        at = j * ff_piece
        dvdown_ref[at : at + ff_piece] = sum(got_down[s, j].astype(F32) for s in range(3)).T
        dtdown_ref[at : at + ff_piece] = got_down[3, j].astype(F32).T

    take_unit(3)
    send_unit(3)
    vec_stage(2)
    for t in range(4):
        pl.when(own_z != t)(lambda: zvec_copy(t).start())

        @pl.when(own_z == t)
        def _():
            z_vec[t] = vec[total.me]

    @pl.when(is_text)
    def _():
        for s in range(3):
            row_copy(micros - 1, s).wait_recv()
        deliver(micros - 1, True)

        for s in range(3):
            last_row_copy(s).wait_send()

    @pl.when(is_image)
    def _():
        for m in range(micros):
            row_copy(m, 0).wait_send()

    for src in range(4):

        @pl.when(own_z != src)
        def _():
            zvec_arrival(src).wait_recv()
            zvec_copy(src).wait_send()
            for unit in range(GROUPS + 1):
                for n, place in unit_sends(unit, src):
                    block_copy(unit, n, src, place).wait_send()
            for kind, dst in ((0, got_out), (1, got_qkv)):
                for place in range(dst.shape[1]):
                    pltpu.make_async_remote_copy(
                        src_ref=dst.at[src, place],
                        dst_ref=dst.at[src, place],
                        send_sem=block_send.at[kind, src, place],
                        recv_sem=block_recv.at[kind, src, place],
                        device_id={"stream": src},
                        device_id_type=MESH,
                    ).wait_recv()

    sums_ref[...] = sum(z_vec[s] for s in range(4))
    odd = lax.rem(own_z, 2) == 1
    for got, out in ((got_qkv, dqkv_ref), (got_out, dout_ref)):
        blocks = [
            sum(got[s, n].astype(F32) for s in range(4)) for n in range(got.shape[1])
        ]
        whole = jnp.concatenate(blocks, axis=1)
        moved = pltpu.roll(whole, whole.shape[1] - BLOCK // 2, 1)
        out[...] = jnp.where(odd, moved, whole)[:, : out.shape[1]]


def back(
    x_tiles,
    qkv,
    probs,
    att,
    inv,
    datt,
    dmid,
    vecs,
    w_qkv,
    dwout,
    zup,
    zdown,
    dup_last,
    ddown_last,
    rows_last,
    vec2,
    picks,
    places,
):
    tiles, _, width = x_tiles.shape
    micros = tiles // TILES
    shard = width // 8
    half = width // 2
    ff = 4 * 2 * STEPS * zdown.shape[3]
    flat = TILES * PATCHES

    def sds(*shape, dtype=F32):
        return jax.ShapeDtypeStruct(shape, dtype)

    dma = pltpu.SemaphoreType.DMA
    return pl.pallas_call(
        back_kernel,
        in_specs=[HBM] * 7 + [FULL, HBM, FULL] + [HBM] * 5 + [FULL] * 3,
        out_specs=[FULL] * 8,
        out_shape=[
            sds(micros, flat, width, dtype=BF),
            sds(8, BLOCK),
            sds(shard, 3 * width // 4),
            sds(shard, width // 4),
            sds(shard, ff // 4),
            sds(ff // 8, width // 4),
            sds(shard, ff // 4),
            sds(ff // 8, width // 4),
        ],
        scratch_shapes=[
            pltpu.VMEM((2, TILES, TILE, 3 * GROUP), BF),
            pltpu.VMEM((tiles, TILE, width), BF),
            pltpu.VMEM((2, TILES, TILE, GROUP), BF),
            pltpu.VMEM((2, TILES, TILE, GROUP), BF),
            pltpu.VMEM((2, TILES, TILE, GROUP), BF),
            pltpu.VMEM((tiles * OWN, width), F32),
            pltpu.VMEM((2, TILES, 4, TILE, TILE), BF),
            pltpu.VMEM((TILES * (TILE - OWN), width), BF),
            pltpu.VMEM((2 * SLOT, width), BF),
            pltpu.VMEM((1,) + dup_last.shape, BF),
            pltpu.VMEM((1,) + ddown_last.shape, BF),
            pltpu.VMEM((1, 2, 2) + dup_last.shape[3:], BF),
            pltpu.VMEM((1, 2, 2) + ddown_last.shape[3:], BF),
            pltpu.VMEM((1, 2) + dup_last.shape[3:], BF),
            pltpu.VMEM((1, 2) + ddown_last.shape[3:], BF),
            pltpu.VMEM((1,) + dup_last.shape[3:], BF),
            pltpu.VMEM((1,) + ddown_last.shape[3:], BF),
            pltpu.VMEM((4,) + zup.shape[2:], BF),
            pltpu.VMEM((4,) + zdown.shape[2:], BF),
            pltpu.VMEM((width + 16, tiles * TILE), BF),
            pltpu.VMEM((tiles * TILE, 3 * width), BF),
            pltpu.VMEM((width, 3 * width), BF),
            pltpu.VMEM((GROUPS, 8, 3 * GROUP), F32),
            pltpu.VMEM((TILES * TILE, width), F32),
            pltpu.VMEM((micros, TILES * (TILE - OWN), width), BF),
            pltpu.VMEM((micros, 2 * SLOT, width), BF),
            pltpu.VMEM((micros, 3, 2 * SLOT, width), BF),
            pltpu.VMEM((2, 2, 2, 2, shard, half), BF),
            pltpu.VMEM((2, 2, 2, 2, shard, half), BF),
            pltpu.VMEM((2, 2, 2, shard, half), BF),
            pltpu.VMEM((2, 2, 2, shard, half), BF),
            pltpu.VMEM((2, 2, shard, half), BF),
            pltpu.VMEM((2, 2, shard, half), BF),
            pltpu.VMEM((2, shard, half), BF),
            pltpu.VMEM((2, shard, half), BF),
            pltpu.VMEM((GROUPS + 1, 6, shard, BLOCK), BF),
            pltpu.VMEM((4, 5, shard, BLOCK), BF),
            pltpu.VMEM((4, 2, shard, BLOCK), BF),
            pltpu.VMEM((4, STEPS) + zup.shape[2:], BF),
            pltpu.VMEM((4, STEPS) + zdown.shape[2:], BF),
            pltpu.VMEM((8, 8, BLOCK), F32),
            pltpu.VMEM((3, 8, 8, BLOCK), F32),
            pltpu.VMEM((4, 8, BLOCK), F32),
            dma((2, 7)),
            dma((micros, 2)),
            dma,
            dma((2,)),
            dma((3,)),
            dma,
            dma((3, 2, 2, 1)),
            dma((3, 2, 2, 2)),
            dma((micros,)),
            dma((micros, 3)),
            dma((3, 2)),
            dma((4,)),
            dma((4,)),
            dma((4, 4)),
            dma((4, 4)),
            dma((2, 4, 5)),
            dma((2, 4, 5)),
        ],
        compiler_params=pltpu.CompilerParams(
            vmem_limit_bytes=63 * 2**20, collective_id=2, has_side_effects=True
        ),
        name="back",
    )(
        x_tiles,
        qkv,
        probs,
        att,
        inv,
        datt,
        dmid,
        vecs,
        w_qkv,
        dwout,
        zup,
        zdown,
        dup_last,
        ddown_last,
        rows_last,
        vec2,
        picks,
        places,
    )


def pad_rows(block):
    micro, rows, width = block.shape
    thirds = block.reshape(micro, TILES, PATCHES, width)
    thirds = jnp.pad(thirds, ((0, 0), (0, 0), (0, OWN - PATCHES), (0, 0)))
    return thirds.reshape(micro, TILES * OWN, width)


def unpad_rows(block):
    micro, _, width = block.shape
    thirds = block.reshape(micro, TILES, OWN, width)[:, :, :PATCHES]
    return thirds.reshape(micro, TILES * PATCHES, width)


def plan(lengths, pairs, is_text, own_stream):
    micro, items = lengths.shape
    finish = jnp.cumsum(lengths, axis=1)
    starts = finish - lengths
    numbers = jnp.arange(items, dtype=jnp.int32)
    match = pairs[:, :, None] == numbers
    start = jnp.sum(jnp.where(match, starts[:, None, :], 0), axis=2).reshape(micro, 3, TILES)
    length = jnp.sum(jnp.where(match, lengths[:, None, :], 0), axis=2).reshape(micro, 3, TILES)
    paired = (pairs >= 0).reshape(micro, 3, TILES)
    rank = jnp.where(paired, jnp.cumsum(paired.astype(jnp.int32), axis=2) - 1, -1)
    takes = rank[:, :, :, None] == jnp.arange(2)
    slot_start = jnp.sum(jnp.where(takes, start[..., None], 0), axis=2)
    slot_length = jnp.sum(jnp.where(takes, length[..., None], 0), axis=2)
    step = jnp.arange(SLOT, dtype=jnp.int32)
    slot_rows = jnp.where(step < slot_length[..., None], slot_start[..., None] + step, -1)
    pad = jnp.arange(TILE - OWN, dtype=jnp.int32)
    next_rows = PATCHES * jnp.arange(1, TILES + 1, dtype=jnp.int32)[:, None] + pad
    next_rows = jnp.where((pad < SLOT) & (next_rows < TILES * PATCHES), next_rows, -1)
    next_rows = jnp.broadcast_to(next_rows, (micro, TILES, TILE - OWN))
    wanted = jnp.concatenate([slot_rows.reshape(micro, -1), next_rows.reshape(micro, -1)], axis=1)
    place = jnp.arange(TILES * OWN, dtype=jnp.int32)
    row_at = jnp.where(place % OWN < PATCHES, place // OWN * PATCHES + place % OWN, -2)
    picks = (wanted[:, :, None] == row_at).astype(BF)
    item_paired = jnp.any(match, axis=1)
    rows = jnp.arange(TILES * PATCHES + SLOT, dtype=jnp.int32)
    member = (rows[:, None] >= starts[:, None, :]) & (rows[:, None] < finish[:, None, :])
    code = jnp.where(item_paired, -1, numbers + items * (starts // PATCHES))
    row_code = jnp.sum(jnp.where(member, code[:, None, :] + 1, 0), axis=2) - 1
    tile = jnp.arange(TILES, dtype=jnp.int32)[:, None]
    own_code = row_code[:, : TILES * PATCHES].reshape(micro, TILES, PATCHES)
    next_code = jnp.stack(
        [row_code[:, PATCHES * (t + 1) : PATCHES * (t + 1) + SLOT] for t in range(TILES)], axis=1
    )

    def here(codes):
        return jnp.where((codes >= 0) & (codes // items == tile), codes, -1)

    def lay(own, extra):
        gap = jnp.full((micro, TILES, OWN - PATCHES), -1, jnp.int32)
        end = jnp.full((micro, TILES, TILE - OWN - SLOT), -1, jnp.int32)
        return jnp.concatenate([own, gap, extra, end], axis=2)

    text_ids = lay(here(own_code), here(next_code))
    own_length = lax.dynamic_index_in_dim(length, jnp.minimum(own_stream, 2), 1, keepdims=False)
    own_takes = lax.dynamic_index_in_dim(takes, jnp.minimum(own_stream, 2), 1, keepdims=False)
    image_ids = lay(
        jnp.zeros((micro, TILES, PATCHES), jnp.int32),
        jnp.where(step < own_length[..., None], 0, -1),
    )
    ids = jnp.where(is_text, text_ids, image_ids)
    own_takes = own_takes.astype(BF)
    same = (pad[:, None] == step).astype(BF)
    places = own_takes[:, :, None, :, None] * same[:, None, :]
    places = places.reshape(micro, TILES * (TILE - OWN), 2 * SLOT)
    return picks, places, own_takes, ids.reshape(micro * TILES, 1, TILE)


def plan_kernel(length_ref, pair_ref, *refs):
    vec_refs, (picks_ref, places_ref, ids_ref, vecs_ref, starts, codes) = refs[:8], refs[8:]
    for n, ref in enumerate(vec_refs):
        rows = ref.shape[0] // BLOCK
        vecs_ref[n * rows : (n + 1) * rows] = ref[...].astype(F32).reshape(rows, BLOCK)
    micros, items = length_ref.shape
    own_z = lax.axis_index("stream")
    is_text = own_z == 3
    block = jnp.minimum(own_z, 2)
    side = TILE - OWN
    place = lax.broadcasted_iota(jnp.int32, (1, TILES * OWN), 1)
    third = third_of(place, OWN)
    inside = place - OWN * third
    row_at = jnp.where(inside < PATCHES, PATCHES * third + inside, -2)
    lane = lax.broadcasted_iota(jnp.int32, (1, TILE), 1)
    far = lax.broadcasted_iota(jnp.int32, (6 * SLOT, 1), 0)
    near = lax.broadcasted_iota(jnp.int32, (TILES * side, 1), 0)
    near_tile = third_of(near, side)
    near_step = near - side * near_tile
    near_row = PATCHES * (near_tile + 1) + near_step
    near_row = jnp.where((near_step < SLOT) & (near_row < TILES * PATCHES), near_row, -1)
    slot_at = lax.broadcasted_iota(jnp.int32, (1, 2 * SLOT), 1)
    slot_of = (slot_at >= SLOT).astype(jnp.int32)
    slot_step = slot_at - SLOT * slot_of
    for m in range(micros):
        start = jnp.int32(0)
        for item in range(items):
            starts[m, item] = start
            codes[m, item] = item + items * third_of(start, PATCHES)
            start = start + length_ref[m, item]

        def pair_of(image):
            item = pair_ref[m, image]
            known = jnp.maximum(item, 0)
            paired = item >= 0
            return paired, starts[m, known], jnp.where(paired, length_ref[m, known], 0)

        wanted = jnp.full(far.shape, -1, jnp.int32)
        for s in range(3):
            rank = jnp.int32(0)
            for t in range(TILES):
                paired, start, length = pair_of(TILES * s + t)
                step = far - SLOT * (2 * s + rank)
                wanted = jnp.where((step >= 0) & (step < length), start + step, wanted)
                rank = rank + paired.astype(jnp.int32)
        picks_ref[m, 0 : 6 * SLOT] = (wanted == row_at).astype(F32).astype(BF)
        picks_ref[m, 6 * SLOT :] = (near_row == row_at).astype(F32).astype(BF)

        rank = jnp.int32(0)
        ranks = jnp.full(near.shape, -1, jnp.int32)
        lengths = []
        for t in range(TILES):
            paired, _, length = pair_of(TILES * block + t)
            lengths.append(length)
            ranks = jnp.where((near_tile == t) & paired, rank, ranks)
            rank = rank + paired.astype(jnp.int32)
        chosen = (near_step == slot_step) & (ranks == slot_of)
        places_ref[m] = chosen.astype(F32).astype(BF)

        for image in range(3 * TILES):

            @pl.when(pair_ref[m, image] >= 0)
            def _():
                codes[m, pair_ref[m, image]] = -1

        for t in range(TILES):
            beside = lane - OWN
            image_ids = jnp.where((lane < PATCHES) | ((beside >= 0) & (beside < lengths[t])), 0, -1)
            row = jnp.where(lane < PATCHES, PATCHES * t + lane, -1)
            row = jnp.where((beside >= 0) & (beside < SLOT), PATCHES * (t + 1) + beside, row)
            text_ids = jnp.full(lane.shape, -1, jnp.int32)
            for item in range(items):
                start, code = starts[m, item], codes[m, item]
                code = jnp.where(third_of(start, PATCHES) == t, code, -1)
                member = (row >= start) & (row < start + length_ref[m, item])
                text_ids = jnp.where(member, code, text_ids)
            ids_ref[m * TILES + t] = jnp.where(is_text, text_ids, image_ids)


def plan_rows(lengths, pairs, vectors):
    micros, items = lengths.shape
    smem = pl.BlockSpec(memory_space=pltpu.SMEM)
    return pl.pallas_call(
        plan_kernel,
        in_specs=[smem, smem] + [FULL] * 8,
        out_specs=[FULL] * 4,
        out_shape=[
            jax.ShapeDtypeStruct((micros, 6 * SLOT + TILES * (TILE - OWN), TILES * OWN), BF),
            jax.ShapeDtypeStruct((micros, TILES * (TILE - OWN), 2 * SLOT), BF),
            jax.ShapeDtypeStruct((micros * TILES, 1, TILE), jnp.int32),
            jax.ShapeDtypeStruct((8 * vectors[0].shape[0] // BLOCK, BLOCK), F32),
        ],
        scratch_shapes=[
            pltpu.SMEM((micros, items), jnp.int32),
            pltpu.SMEM((micros, items), jnp.int32),
        ],
        name="plan_rows",
    )(lengths, pairs, *vectors)


def spread(padded, picks, own_takes, is_text):
    micro, _, width = padded.shape
    picked = lax.dot_general(
        picks, padded, (((2,), (1,)), ((0,), (0,))), preferred_element_type=F32
    ).astype(BF)
    near = picked[:, 6 * SLOT :].reshape(micro, TILES, TILE - OWN, width)[:, :, :SLOT]
    sent = picked[:, : 6 * SLOT].reshape(micro, 3, 2 * SLOT, width)
    far = sum(lax.ppermute(sent[:, s], "stream", [(3, s)]) for s in range(3))
    far = far.reshape(micro, 1, 2, SLOT, width) * own_takes[:, :, :, None, None]
    return jnp.where(is_text, near, far[:, :, 0] + far[:, :, 1])


def collect(extra, picks, own_takes, is_text):
    micro, _, _, width = extra.shape
    mine = extra[:, :, None] * own_takes[:, :, :, None, None]
    mine = (mine[:, 0] + mine[:, 1] + mine[:, 2]).reshape(micro, 2 * SLOT, width)
    parts = [lax.ppermute(mine, "stream", [(s, 3)]) for s in range(3)]
    extra = jnp.pad(extra, ((0, 0), (0, 0), (0, TILE - OWN - SLOT), (0, 0)))
    parts.append(extra.reshape(micro, TILES * (TILE - OWN), width))
    rows = jnp.concatenate(parts, axis=1)
    scale = jnp.where(is_text, 1.0, 0.0).astype(BF)
    return lax.dot_general(
        picks * scale, rows, (((1,), (1,)), ((0,), (0,))), preferred_element_type=F32
    ).astype(BF)


def reduce_all(vectors, dw_qkv, dw_out, dup, ddown):
    width = dw_qkv.shape[0]
    shard = width // lax.axis_size("dp")
    vectors = lax.psum(vectors, ("dp", "stream"))
    vectors = lax.dynamic_slice_in_dim(vectors, lax.axis_index("dp") * shard, shard, axis=1)

    def over_items(grad, dim):
        return lax.psum_scatter(grad, "dp", scatter_dimension=dim, tiled=True)

    def over_blocks(grad):
        return lax.psum_scatter(grad, "stream", scatter_dimension=1, tiled=True).astype(F32)

    qkv = over_blocks(over_items(dw_qkv, 0))
    out = over_blocks(over_items(dw_out, 0))
    dup = over_items(jnp.concatenate(list(dup), axis=1), 0)
    ddown = over_items(jnp.concatenate(list(ddown), axis=1), 1)
    up = dup.reshape(dup.shape[0], 4, -1).transpose(1, 0, 2)
    down = ddown.reshape(4, -1, ddown.shape[1])
    up = lax.all_to_all(up, "stream", 0, 0).astype(F32)
    down = lax.all_to_all(down, "stream", 0, 0).astype(F32)
    return (
        vectors,
        qkv,
        out,
        up[0] + up[1] + up[2],
        (down[0] + down[1] + down[2]).T,
        up[3],
        down[3].T,
    )


def shards(
    remote,
    tokens,
    text_lengths,
    pair_text,
    ln1_gain,
    ln1_bias,
    w_qkv,
    q_bias,
    v_bias,
    w_out,
    ln2_gain,
    ln2_bias,
    vis_up,
    vis_down,
    vis_bias,
    txt_up,
    txt_down,
    txt_bias,
    cotangent,
):
    micro = tokens.shape[0]
    width = tokens.shape[4]
    own_stream = lax.axis_index("stream")
    is_text = own_stream == 3
    vecs = [ln1_gain, ln1_bias, q_bias, v_bias, ln2_gain, ln2_bias, vis_bias, txt_bias]
    if remote:
        picks, places, ids, vecs = plan_rows(text_lengths[:, 0], pair_text[:, 0], vecs)
    else:
        vecs = jnp.concatenate(vecs).astype(F32).reshape(-1, BLOCK)
        picks, places, own_takes, ids = plan(
            text_lengths[:, 0], pair_text[:, 0], is_text, own_stream
        )

    def tiled(own, extra):
        own = own.reshape(micro, TILES, OWN, width)
        extra = jnp.pad(extra, ((0, 0), (0, 0), (0, TILE - OWN - SLOT), (0, 0)))
        return jnp.concatenate([own, extra], axis=2).reshape(micro * TILES, TILE, width)

    def parted(tiles):
        tiles = tiles.reshape(micro, TILES, TILE, width)
        return tiles[:, :, :OWN].reshape(micro, TILES * OWN, width), tiles[:, :, OWN : OWN + SLOT]

    if remote:
        x_tiles, qkv, probs, inverse, att_tiles, att, att_last = attend_rows(
            tokens[:, 0, 0], picks, places, ids, vecs, w_qkv
        )
    else:
        x = pad_rows(tokens[:, 0, 0])
        x_tiles = tiled(x, spread(x, picks, own_takes, is_text))
        qkv, att_tiles, probs, inverse = attend(x_tiles, ids, vecs, w_qkv)
        att_own, att_extra = parted(att_tiles)
        att = att_own + collect(att_extra, picks, own_takes, is_text)
        att = att.reshape(micro * TILES * OWN, width)
        att_last = jnp.zeros((2 * SLOT, width), BF)
    out, dmid, datt_tiles, dw_out, vec2, dup, ddown, *lasts = expert(
        remote,
        x_tiles,
        att,
        att_tiles,
        att_last,
        cotangent[:, 0, 0],
        w_out,
        vecs,
        picks,
        places,
        vis_up,
        vis_down,
        txt_up,
        txt_down,
    )
    if remote:
        dx, vectors, g_qkv, g_out, g_vup, g_vdown, g_tup, g_tdown = back(
            x_tiles,
            qkv,
            probs,
            att_tiles,
            inverse,
            datt_tiles,
            dmid,
            vecs,
            w_qkv,
            dw_out,
            dup,
            ddown,
            *lasts,
            vec2,
            picks,
            places,
        )
        vectors = vectors[:, : width // 8]
    else:
        datt = parted(datt_tiles)[0]
        datt_tiles = tiled(datt, spread(datt, picks, own_takes, is_text))
        dqkv = attend_back(qkv, probs, att_tiles, inverse, datt_tiles)
        dx_tiles, dw_qkv, vec1 = project_back(x_tiles, dqkv, vecs, w_qkv)
        dx_own, dx_extra = parted(dx_tiles)
        dx = (
            dmid.reshape(micro, TILES * OWN, width)
            + dx_own.astype(F32)
            + collect(dx_extra, picks, own_takes, is_text).astype(F32)
        )
        dx = unpad_rows(dx).astype(BF)
        text_scale = jnp.where(is_text, 1.0, 0.0)
        vectors = jnp.concatenate(
            [vec1[0:4], vec2[0:2], vec2[2:3] * (1.0 - text_scale), vec2[2:3] * text_scale], axis=0
        )
        vectors, g_qkv, g_out, g_vup, g_vdown, g_tup, g_tdown = reduce_all(
            vectors, dw_qkv, dw_out, dup, ddown
        )
    return (
        out.reshape(tokens.shape),
        dx.reshape(tokens.shape),
        vectors[0],
        vectors[1],
        g_qkv,
        vectors[2],
        vectors[3],
        g_out,
        vectors[4],
        vectors[5],
        g_vup,
        g_vdown,
        vectors[6],
        g_tup,
        g_tdown,
        vectors[7],
    )


def solution(mesh):
    rows = P(None, "dp", "stream", None, None)
    lists = P(None, "dp", None)
    vector, matrix = P("dp"), P("dp", "stream")
    in_specs = (rows, lists, lists) + (P(),) * 14 + (rows,)
    out_specs = (
        rows,
        rows,
        vector,
        vector,
        matrix,
        vector,
        vector,
        matrix,
        vector,
        vector,
        matrix,
        matrix,
        vector,
        matrix,
        matrix,
        vector,
    )
    remote = mesh.shape["dp"] == 8
    body = functools.partial(shards, remote)
    return jax.shard_map(body, mesh=mesh, in_specs=in_specs, out_specs=out_specs, check_vma=False)
```

```python
import functools

import jax
import jax.numpy as jnp
from jax import lax
from jax.experimental import pallas as pl
from jax.experimental.pallas import tpu as pltpu
from jax.sharding import PartitionSpec as P

HEADS = 12
PATCHES = 197
OWN = 208
SLOT = 40
TILE = 256
TILES = 3
EPSILON = 1e-06
MASKED = -1e30
BF = jnp.bfloat16
F32 = jnp.float32
FULL = pl.BlockSpec(memory_space=pltpu.VMEM)
HBM = pl.BlockSpec(memory_space=pl.ANY)
MESH = pl.DeviceIdType.MESH
BLOCK = 128


def dot(left, right):
    return jnp.dot(left, right, preferred_element_type=F32)


def dot_t(left, right):
    return lax.dot_general(left, right, (((1,), (1,)), ((), ())), preferred_element_type=F32)


def t_dot(left, right):
    return lax.dot_general(left, right, (((0,), (0,)), ((), ())), preferred_element_type=F32)


def normalize(values):
    centred = values - jnp.mean(values, axis=-1, keepdims=True)
    inverse = lax.rsqrt(jnp.mean(centred * centred, axis=-1, keepdims=True) + EPSILON)
    return centred * inverse, inverse


def norm_back(grad, normed, inverse, gain):
    scaled = grad * gain
    return inverse * (
        scaled
        - jnp.mean(scaled, axis=-1, keepdims=True)
        - normed * jnp.mean(scaled * normed, axis=-1, keepdims=True)
    )


def gelu_parts(up):
    rise = 1.0 + 0.2316418882663604 * jnp.abs(up)
    inner = 1.0 / rise
    bell = jnp.exp2(up * up * -0.7213475204444817)
    poly = inner * (
        0.127414796
        + inner
        * (-0.142248368 + inner * (0.7107068705 + inner * (-0.7265760135 + inner * 0.5307027145)))
    )
    tail = poly * bell
    return jnp.where(up >= 0, 1.0 - tail, tail), bell * 0.3989422804014327


def halves(block, low, high):
    return jnp.concatenate([block * low, block * high], axis=0)


def pair_lanes():
    lane = lax.broadcasted_iota(jnp.int32, (1, 128), 1)
    return (lane < 64).astype(BF), (lane >= 64).astype(BF)


def attend_pair(q, k, v, barred, low, high):
    scores = dot_t(halves(k, low, high), q * 0.125)
    yield
    expos = []
    for side in range(2):
        part = scores[TILE * side : TILE * (side + 1)] + barred
        top = jnp.maximum(jnp.max(part, axis=0, keepdims=True), 0.1 * MASKED)
        expos.append(jnp.exp(part - top).astype(BF))
    ones = [jnp.broadcast_to(keep, (TILE, 128)) for keep in (low, high)]
    right = jnp.concatenate([halves(v, low, high), jnp.concatenate(ones, axis=0)], axis=1)
    sums = t_dot(jnp.concatenate(expos, axis=0), right)
    inverse = jnp.where(sums[:, 128:] > 0.0, 1.0 / sums[:, 128:], 0.0)
    yield expos, sums[:, :128] * inverse, inverse


def attend_back_pair(q, k, v, expos, out, inverse, grad, low, high):
    scaled = grad.astype(F32) * inverse.astype(F32)
    inner = (scaled * out.astype(F32)).astype(BF)
    scaled = scaled.astype(BF)
    minus = [jnp.broadcast_to(-keep, (TILE, 128)) for keep in (low, high)]
    right = jnp.concatenate([halves(v, low, high), jnp.concatenate(minus, axis=0)], axis=1)
    slopes = dot_t(right, jnp.concatenate([scaled, inner], axis=1))
    yield
    parts = [
        (expos[side].astype(F32) * slopes[TILE * side : TILE * (side + 1)]).astype(BF)
        for side in range(2)
    ]
    dq = t_dot(jnp.concatenate(parts, axis=0), halves(k, low, high)) * 0.125
    dk = dot(jnp.concatenate(parts, axis=1), halves(q * 0.125, low, high))
    dv = dot(jnp.concatenate(expos, axis=1), halves(scaled, low, high))
    yield dq.astype(BF), dk.astype(BF), dv.astype(BF)


def staggered(makers, finish):
    held = None
    for n, make in enumerate(makers):
        step = make()
        next(step)
        if held is not None:
            finish(n - 1, next(held))
        held = step
    finish(len(makers) - 1, next(held))


def bars(ids_ref):
    ids = jnp.broadcast_to(ids_ref, (TILE, TILE))
    return jnp.where((ids == ids.T) & (ids >= 0), 0.0, MASKED)


GAIN1, SHIFT1, Q_BIAS, V_BIAS, GAIN2, SHIFT2, VIS_BIAS, TXT_BIAS = range(8)


def row_of(vecs_ref, at):
    rows = vecs_ref.shape[0] // 8
    return jnp.concatenate([vecs_ref[at * rows + n : at * rows + n + 1] for n in range(rows)], axis=1)


def project(values, vecs_ref, w_ref):
    normed, _ = normalize(values.astype(F32))
    hidden = (normed * row_of(vecs_ref, GAIN1) + row_of(vecs_ref, SHIFT1)).astype(BF)
    q_bias, v_bias = row_of(vecs_ref, Q_BIAS), row_of(vecs_ref, V_BIAS)
    bias = jnp.concatenate([q_bias, jnp.zeros_like(q_bias), v_bias], axis=1)
    return (dot(hidden, w_ref[...]) + bias).astype(BF)


def attend_kernel(x_ref, ids_ref, vecs_ref, w_ref, qkv_ref, out_ref, p_ref, inv_ref):
    width = x_ref.shape[2]
    qkv_ref[0] = project(x_ref[0], vecs_ref, w_ref)
    barred = bars(ids_ref[0])
    low, high = pair_lanes()

    def maker(pair):
        cols = [qkv_ref[0, :, part * width + pair * 128 :][:, :128] for part in range(3)]
        return lambda: attend_pair(*cols, barred, low, high)

    def finish(pair, results):
        expos, out, inverse = results
        at = pair * 128
        for side in range(2):
            p_ref[0, 2 * pair + side] = expos[side]
        out_ref[0, :, at : at + 128] = out.astype(BF)
        inv_ref[0, :, at : at + 128] = inverse.astype(BF)

    staggered([maker(pair) for pair in range(HEADS // 2)], finish)


def attend(x_tiles, ids, vecs, w_qkv):
    tiles, _, width = x_tiles.shape

    def block(*shape):
        return pl.BlockSpec((1,) + shape, lambda i: (i,) + (0,) * len(shape))

    return pl.pallas_call(
        attend_kernel,
        grid=(tiles,),
        in_specs=[block(TILE, width), block(1, TILE), FULL, FULL],
        out_specs=[
            block(TILE, 3 * width),
            block(TILE, width),
            block(HEADS, TILE, TILE),
            block(TILE, width),
        ],
        out_shape=[
            jax.ShapeDtypeStruct((tiles, TILE, 3 * width), BF),
            jax.ShapeDtypeStruct((tiles, TILE, width), BF),
            jax.ShapeDtypeStruct((tiles, HEADS, TILE, TILE), BF),
            jax.ShapeDtypeStruct((tiles, TILE, width), BF),
        ],
        compiler_params=pltpu.CompilerParams(vmem_limit_bytes=56 * 2**20),
        name="attend",
    )(x_tiles, ids, vecs, w_qkv)


def third_of(row, size):
    return (row >= size).astype(jnp.int32) + (row >= 2 * size).astype(jnp.int32)


def padding(micros, flip):
    count = micros * (OWN if flip else PATCHES)
    at = lax.broadcasted_iota(jnp.int32, (1, count), 1)
    rows = lax.broadcasted_iota(jnp.int32, (micros * (PATCHES if flip else OWN), 1), 0)
    if flip:
        wanted = lax.rem(rows, micros) * OWN + lax.div(rows, micros)
    else:
        micro = sum((rows >= m * OWN).astype(jnp.int32) for m in range(1, micros))
        row = rows - micro * OWN
        wanted = jnp.where(row < PATCHES, row * micros + micro, -1)
    return (wanted == at).astype(F32).astype(BF)


def pad_third(pad, third):
    rows, micros, width = third.shape
    return dot(pad, third.reshape(rows * micros, width)).astype(BF)


def attend_rows_kernel(
    tok_ref,
    picks_ref,
    places_ref,
    ids_ref,
    vecs_ref,
    w_hbm,
    x_out,
    qkv_out,
    p_out,
    inv_out,
    att_out,
    rows_out,
    mine_out,
    tok,
    w,
    x,
    qkv,
    probs,
    inv,
    att,
    rows_ref,
    sent,
    got,
    mine,
    got_back,
    tok_sems,
    w_sem,
    out_sems,
    p_sems,
    rows_sems,
    row_send,
    row_recv,
    back_send,
    back_recv,
):
    micros = tok.shape[1]
    width = tok.shape[2]
    own_z = lax.axis_index("stream")
    is_text = own_z == 3
    is_image = jnp.logical_not(is_text)
    side = TILE - OWN

    def tok_copy(t):
        at = pl.ds(t * PATCHES, PATCHES)
        return pltpu.make_async_copy(tok_ref.at[at], tok.at[at], tok_sems.at[t])

    for t in range(TILES):
        tok_copy(t).start()
    w_copy = pltpu.make_async_copy(w_hbm, w, w_sem)
    w_copy.start()
    meet([{"stream": lax.rem(own_z + k, 4)} for k in range(1, 4)])

    def row_copy(m, s):
        return pltpu.make_async_remote_copy(
            src_ref=sent.at[m, s],
            dst_ref=got.at[m],
            send_sem=row_send.at[m, s],
            recv_sem=row_recv.at[m],
            device_id={"stream": s},
            device_id_type=MESH,
        )

    def back_copy(m, s):
        return pltpu.make_async_remote_copy(
            src_ref=mine.at[m],
            dst_ref=got_back.at[m, s],
            send_sem=back_send.at[m],
            recv_sem=back_recv.at[m, s],
            device_id={"stream": 3},
            device_id_type=MESH,
        )

    def outs(m, which):
        at = pl.ds(m * TILES, TILES)
        pairs = ((x, x_out), (qkv, qkv_out), (inv, inv_out), (att, att_out))
        for n in which:
            src, dst = pairs[n]
            yield pltpu.make_async_copy(src.at[at], dst.at[at], out_sems.at[m, n])

    def rows_copy(m):
        at = pl.ds(m * TILES * OWN, TILES * OWN)
        return pltpu.make_async_copy(rows_ref.at[at], rows_out.at[at], rows_sems.at[m])

    mine_copy = pltpu.make_async_copy(mine.at[micros - 1], mine_out, rows_sems.at[micros])

    def probs_store(tile, slot):
        return pltpu.make_async_copy(probs.at[slot], p_out.at[tile], p_sems.at[slot])

    def own_rows(ref, m):
        return jnp.concatenate([ref[m * TILES + t, 0:OWN] for t in range(TILES)], axis=0)

    def beside(ref, m, value):
        for t in range(TILES):
            ref[m * TILES + t, OWN:TILE] = value[t * side : (t + 1) * side]

    pad = padding(micros, False)
    for t in range(TILES):
        tok_copy(t).wait()
        padded = pad_third(pad, tok[t * PATCHES : (t + 1) * PATCHES])
        for m in range(micros):
            x[m * TILES + t, 0:OWN] = padded[m * OWN : (m + 1) * OWN]
    for m in range(micros):

        @pl.when(is_text)
        def _():
            picked = dot(picks_ref[m], own_rows(x, m)).astype(BF)
            for s in range(3):
                sent[m, s] = picked[s * 2 * SLOT : (s + 1) * 2 * SLOT]
                row_copy(m, s).start()
            beside(x, m, picked[6 * SLOT :])

    w_copy.wait()
    for m in range(micros):
        rows = project(own_rows(x, m), vecs_ref, w)
        for t in range(TILES):
            qkv[m * TILES + t, 0:OWN] = rows[t * OWN : (t + 1) * OWN]

    low, high = pair_lanes()

    @pl.loop(0, micros)
    def _(m):
        @pl.when(is_image)
        def _():
            row_copy(m, 0).wait_recv()
            beside(x, m, dot(places_ref[m], got[m]).astype(BF))

        extra = [x[m * TILES + t, OWN:TILE] for t in range(TILES)]
        beside(qkv, m, project(jnp.concatenate(extra, axis=0), vecs_ref, w))
        for copy in outs(m, (0, 1)):
            copy.start()

        @pl.loop(0, TILES)
        def _(t):
            tile = m * TILES + t
            slot = lax.rem(tile, 2)
            pl.when(tile > 1)(lambda: probs_store(tile - 2, slot).wait())
            barred = bars(ids_ref[tile])

            def maker(pair):
                at = pair * BLOCK
                cols = [qkv[tile, :, pl.ds(part * width + at, BLOCK)] for part in range(3)]
                return lambda: attend_pair(*cols, barred, low, high)

            def finish(pair, results):
                expos, out, inverse = results
                at = pair * BLOCK
                for n in range(2):
                    probs[slot, 2 * pair + n] = expos[n]
                att[tile, :, at : at + BLOCK] = out.astype(BF)
                inv[tile, :, at : at + BLOCK] = inverse.astype(BF)

            staggered([maker(pair) for pair in range(HEADS // 2)], finish)
            probs_store(tile, slot).start()

        for copy in outs(m, (2, 3)):
            copy.start()
        at = pl.multiple_of(m * TILES * OWN, 16)
        rows_ref[pl.ds(at, TILES * OWN)] = own_rows(att, m)

        @pl.when(is_image)
        def _():
            extra = [att[m * TILES + t, OWN:TILE] for t in range(TILES)]
            mine[m] = t_dot(places_ref[m], jnp.concatenate(extra, axis=0)).astype(BF)
            for s in range(3):

                @pl.when((own_z == s) & (m < micros - 1))
                def _():
                    back_copy(m, s).start()

        @pl.when(m == micros - 1)
        def _():
            rows_copy(micros - 1).start()
            mine_copy.start()

    for m in range(micros - 1):

        @pl.when(is_text)
        def _():
            for s in range(3):
                back_copy(m, s).wait_recv()
            parts = [got_back[m, s] for s in range(3)]
            parts += [att[m * TILES + t, OWN:TILE] for t in range(TILES)]
            moved = t_dot(picks_ref[m], jnp.concatenate(parts, axis=0)).astype(BF)
            at = pl.ds(m * TILES * OWN, TILES * OWN)
            rows_ref[at] = (rows_ref[at].astype(F32) + moved.astype(F32)).astype(BF)

        rows_copy(m).start()
        pl.when(is_image)(lambda: back_copy(m, 0).wait_send())

    @pl.when(is_text)
    def _():
        for m in range(micros):
            for s in range(3):
                row_copy(m, s).wait_send()

    for m in range(micros):
        rows_copy(m).wait()
        for copy in outs(m, range(4)):
            copy.wait()
    mine_copy.wait()
    for slot in range(2):
        tile = micros * TILES - 2 + slot
        probs_store(tile, tile % 2).wait()


def attend_rows(tokens, picks, places, ids, vecs, w_qkv):
    _, micros, width = tokens.shape
    tiles = micros * TILES
    dma = pltpu.SemaphoreType.DMA

    def sds(*shape):
        return jax.ShapeDtypeStruct(shape, BF)

    return pl.pallas_call(
        attend_rows_kernel,
        in_specs=[HBM] + [FULL] * 4 + [HBM],
        out_specs=[HBM] * 7,
        out_shape=[
            sds(tiles, TILE, width),
            sds(tiles, TILE, 3 * width),
            sds(tiles, HEADS, TILE, TILE),
            sds(tiles, TILE, width),
            sds(tiles, TILE, width),
            sds(tiles * OWN, width),
            sds(2 * SLOT, width),
        ],
        scratch_shapes=[
            pltpu.VMEM(tokens.shape, BF),
            pltpu.VMEM(w_qkv.shape, BF),
            pltpu.VMEM((tiles, TILE, width), BF),
            pltpu.VMEM((tiles, TILE, 3 * width), BF),
            pltpu.VMEM((2, HEADS, TILE, TILE), BF),
            pltpu.VMEM((tiles, TILE, width), BF),
            pltpu.VMEM((tiles, TILE, width), BF),
            pltpu.VMEM((tiles * OWN, width), BF),
            pltpu.VMEM((micros, 3, 2 * SLOT, width), BF),
            pltpu.VMEM((micros, 2 * SLOT, width), BF),
            pltpu.VMEM((micros, 2 * SLOT, width), BF),
            pltpu.VMEM((micros, 3, 2 * SLOT, width), BF),
            dma((TILES,)),
            dma,
            dma((micros, 4)),
            dma((2,)),
            dma((micros + 1,)),
            dma((micros, 3)),
            dma((micros,)),
            dma((micros,)),
            dma((micros, 3)),
        ],
        compiler_params=pltpu.CompilerParams(
            vmem_limit_bytes=63 * 2**20, collective_id=3, has_side_effects=True
        ),
        name="attend_rows",
    )(tokens, picks, places, ids, vecs, w_qkv)


def attend_back_kernel(qkv_ref, p_ref, out_ref, inv_ref, grad_ref, dqkv_ref):
    width = out_ref.shape[2]
    low, high = pair_lanes()

    def maker(pair):
        at = pl.ds(pair * 128, 128)
        return lambda: attend_back_pair(
            *(qkv_ref[0, :, pl.ds(part * width + pair * 128, 128)] for part in range(3)),
            [p_ref[0, 2 * pair], p_ref[0, 2 * pair + 1]],
            out_ref[0, :, at],
            inv_ref[0, :, at],
            grad_ref[0, :, at],
            low,
            high,
        )

    def finish(pair, results):
        for part, value in enumerate(results):
            dqkv_ref[0, :, pl.ds(part * width + pair * 128, 128)] = value

    staggered([maker(pair) for pair in range(HEADS // 2)], finish)


def attend_back(qkv, probs, out, inverse, grad):
    tiles, _, width = out.shape

    def block(*shape):
        return pl.BlockSpec((1,) + shape, lambda i: (i,) + (0,) * len(shape))

    return pl.pallas_call(
        attend_back_kernel,
        grid=(tiles,),
        in_specs=[
            block(TILE, 3 * width),
            block(HEADS, TILE, TILE),
            block(TILE, width),
            block(TILE, width),
            block(TILE, width),
        ],
        out_specs=block(TILE, 3 * width),
        out_shape=jax.ShapeDtypeStruct((tiles, TILE, 3 * width), BF),
        compiler_params=pltpu.CompilerParams(vmem_limit_bytes=56 * 2**20),
        name="attend_back",
    )(qkv, probs, out, inverse, grad)


STEPS = 3


def add_into(ref, at, other):
    ref[at] = (ref[at].astype(F32) + other.astype(F32)).astype(BF)


class ItemSum:
    def __init__(self, up, down, got, got_one, got_two, sems):
        self.grads = (up, down)
        self.got, self.got_one, self.got_two, self.sems = got, got_one, got_two, sems
        me = lax.axis_index("dp")
        self.me = me
        self.core, self.x, self.y = lax.rem(me, 2), lax.rem(lax.div(me, 2), 2), lax.div(me, 4)
        self.near = me + 1 - 2 * self.core
        self.over_x = me + 2 - 4 * self.x
        self.over_y = me + 4 - 8 * self.y

    def _copy(self, src, dst, stage, which, slot, device):
        return pltpu.make_async_remote_copy(
            src_ref=src,
            dst_ref=dst,
            send_sem=self.sems.at[stage, which, 0, slot],
            recv_sem=self.sems.at[stage, which, 1, slot],
            device_id={"dp": device},
            device_id_type=MESH,
        )

    def core_copy(self, which, slot):
        src = self.grads[which].at[slot, :, :, 1 - self.core]
        return self._copy(src, self.got[which].at[slot], 0, which, slot, self.near)

    def one_copy(self, which, slot):
        grad = self.grads[which]
        if which == 0:
            src, device = grad.at[slot, :, 1 - self.x, self.core], self.over_x
        else:
            src, device = grad.at[slot, 1 - self.y, :, self.core], self.over_y
        return self._copy(src, self.got_one[which].at[slot], 1, which, slot, device)

    def two_copy(self, which, slot):
        grad = self.grads[which]
        if which == 0:
            src, device = grad.at[slot, 1 - self.y, self.x, self.core], self.over_y
        else:
            src, device = grad.at[slot, self.y, 1 - self.x, self.core], self.over_x
        return self._copy(src, self.got_two[which].at[slot], 2, which, slot, device)

    def start(self, which, slot):
        self.core_copy(which, slot).start()

    def after_core(self, slot):
        for which in range(2):
            self.core_copy(which, slot).wait()
            for y in range(2):
                for x in range(2):
                    at = (slot, y, x, self.core)
                    add_into(self.grads[which], at, self.got[which][slot, y, x])
            self.one_copy(which, slot).start()

    def after_one(self, slot):
        for which in range(2):
            self.one_copy(which, slot).wait()
            for side in range(2):
                at = (slot, side, self.x, self.core) if which == 0 else (slot, self.y, side, self.core)
                add_into(self.grads[which], at, self.got_one[which][slot, side])
            self.two_copy(which, slot).start()

    def after_two(self, slot):
        sums = []
        for which in range(2):
            self.two_copy(which, slot).wait()
            own = self.grads[which][slot, self.y, self.x, self.core].astype(F32)
            sums.append((own + self.got_two[which][slot].astype(F32)).astype(BF))
        return sums


def meet(devices):
    barrier = pltpu.get_barrier_semaphore()
    for device in devices:
        pl.semaphore_signal(barrier, inc=1, device_id=device, device_id_type=MESH)
    pl.semaphore_wait(barrier, len(devices))


def expert_kernel(
    remote,
    x_ref,
    att_ref,
    att_tiles_ref,
    att_last_ref,
    dy_ref,
    w_out_ref,
    vecs_ref,
    picks_ref,
    places_ref,
    up_v_ref,
    down_v_ref,
    up_t_ref,
    down_t_ref,
    out_ref,
    dmid_ref,
    datt_ref,
    dwout_ref,
    vec_ref,
    dup_ref,
    ddown_ref,
    *refs,
):
    if remote:
        dup_last_ref, ddown_last_ref, rows_last_ref, *refs = refs
    raw, dy, att, w_out, mid, tiles, hid_t, dy_t, acc_o, acc_h, up_w, down_w, *refs = refs
    act, gup, dup_buf, ddown_buf, sems, io_sems, raw_sems, *more = refs
    width = att.shape[1]
    cols = act.shape[2]
    micros = raw.shape[1]
    rows = TILES * OWN
    own_z = lax.axis_index("stream")
    is_text = own_z == 3
    is_image = jnp.logical_not(is_text)
    pieces = 8 if remote else 1
    piece = cols // pieces
    ff = up_v_ref.shape[1]

    def rows_of(m):
        return pl.ds(pl.multiple_of(m * rows, 16), rows)

    def loads(m):
        at = pl.ds(m * rows, rows)
        yield pltpu.make_async_copy(att_ref.at[at], att.at[at], io_sems.at[m, 0])
        for t in range(TILES):
            src = x_ref.at[m * TILES + t, 0:OWN]
            dst = act.at[m, t * OWN : (t + 1) * OWN, 0:width]
            yield pltpu.make_async_copy(src, dst, io_sems.at[m, 1 + t])

    def raw_copy(t):
        at = pl.ds(t * PATCHES, PATCHES)
        return pltpu.make_async_copy(dy_ref.at[at], raw.at[at], raw_sems.at[t])

    def store(m, n):
        at = rows_of(m)
        tile_at = pl.ds(m * TILES, TILES)
        src, dst = (
            (mid.at[at], dmid_ref.at[at]),
            (tiles.at[tile_at], datt_ref.at[tile_at]),
            (act.at[m, 0:rows, 0:width], out_ref.at[at]),
        )[n]
        return pltpu.make_async_copy(src, dst, io_sems.at[m, 5 + n])

    w_out_copy = pltpu.make_async_copy(w_out_ref, w_out, io_sems.at[0, 8])
    dwout = dy_t.at[:, 0:width]
    dwout_copy = pltpu.make_async_copy(dwout, dwout_ref, io_sems.at[0, 8])

    def fetch(j, slot):
        def go(up_src, down_src):
            for d in range(pieces):
                at = pl.ds(pl.multiple_of(j * piece + d * (ff // pieces), 128), piece)
                here = pl.ds(d * piece, piece)
                pltpu.make_async_copy(
                    up_src.at[:, at], up_w.at[slot, :, here], sems.at[0, slot]
                ).start()
                pltpu.make_async_copy(
                    down_src.at[at, :], down_w.at[slot, here, :], sems.at[1, slot]
                ).start()

        pl.when(is_text)(lambda: go(up_t_ref, down_t_ref))
        pl.when(is_image)(lambda: go(up_v_ref, down_v_ref))

    def fetched(slot):
        pltpu.make_async_copy(up_w.at[slot], up_w.at[slot], sems.at[0, slot]).wait()
        pltpu.make_async_copy(down_w.at[slot], down_w.at[slot], sems.at[1, slot]).wait()

    for t in range(TILES):
        raw_copy(t).start()
    w_out_copy.start()
    for m in range(micros):
        for copy in loads(m):
            copy.start()
    fetch(0, 0)

    if remote:
        got, got_one, got_two, sum_sems = more[0:2], more[2:4], more[4:6], more[6]
        sent, got_rows, row_send, row_recv, got_att, att_side, att_send, att_recv, side_sem = more[7:]
        total = ItemSum(dup_buf, ddown_buf, got, got_one, got_two, sum_sems)

        def side_copies():
            for t in range(TILES):
                src = att_tiles_ref.at[(micros - 1) * TILES + t, OWN:TILE]
                yield pltpu.make_async_copy(src, att_side.at[t], side_sem.at[t])

        for copy in side_copies():
            copy.start()
        meet(
            [{"dp": total.near}, {"dp": total.over_x}, {"dp": total.over_y}]
            + [{"stream": lax.rem(own_z + k, 4)} for k in range(1, 4)]
        )

        def att_copy(s):
            return pltpu.make_async_remote_copy(
                src_ref=att_last_ref,
                dst_ref=got_att.at[s],
                send_sem=att_send,
                recv_sem=att_recv.at[s],
                device_id={"stream": 3},
                device_id_type=MESH,
            )

        for s in range(3):
            pl.when(own_z == s)(lambda: att_copy(s).start())

        def row_copy(m, s):
            return pltpu.make_async_remote_copy(
                src_ref=sent.at[m, s],
                dst_ref=got_rows.at[m],
                send_sem=row_send.at[m, s],
                recv_sem=row_recv.at[m],
                device_id={"stream": s},
                device_id_type=MESH,
            )

    gain, shift = row_of(vecs_ref, GAIN2), row_of(vecs_ref, SHIFT2)
    bias = jnp.where(is_text, row_of(vecs_ref, TXT_BIAS), row_of(vecs_ref, VIS_BIAS))
    space = dy_t.shape[1] // micros
    for ref in (hid_t, dy_t):
        for m in range(micros):
            lanes = slice(m * space + rows, (m + 1) * space)
            ref[:, lanes] = jnp.zeros((width, space - rows), BF)
    for ref in (act, gup):
        ref[:, rows:space] = jnp.zeros((micros, space - rows, cols), BF)
    pad = padding(micros, False)
    for t in range(TILES):
        raw_copy(t).wait()
        padded = pad_third(pad, raw[t * PATCHES : (t + 1) * PATCHES])
        for m in range(micros):
            at = m * rows + t * OWN
            dy[at : at + OWN] = padded[m * OWN : (m + 1) * OWN]
    for m in range(micros):
        dy_t[:, m * space : m * space + rows] = dy[m * rows : (m + 1) * rows].T

    def put_rows(m, value):
        for t in range(TILES):
            tiles[m * TILES + t, 0:OWN] = value[t * OWN : (t + 1) * OWN]

    def own_rows(m):
        return jnp.concatenate([tiles[m * TILES + t, 0:OWN] for t in range(TILES)], axis=0)

    def beside(m, value):
        for t in range(TILES):
            part = value[t * (TILE - OWN) : (t + 1) * (TILE - OWN)]
            tiles[m * TILES + t, OWN:TILE] = part

    def begin(m):
        for copy in loads(m):
            copy.wait()
        if m == 0:
            w_out_copy.wait()
        at = rows_of(m)
        if remote and m == micros - 1:

            @pl.when(is_text)
            def _():
                for s in range(3):
                    att_copy(s).wait_recv()
                parts = [got_att[s] for s in range(3)] + [att_side[t] for t in range(TILES)]
                moved = t_dot(picks_ref[m], jnp.concatenate(parts, axis=0)).astype(BF)
                att[at] = (att[at].astype(F32) + moved.astype(F32)).astype(BF)

        middle = act[m, 0:rows, 0:width].astype(F32) + dot(att[at], w_out[...])
        mid[at] = middle
        normed, _ = normalize(middle)
        hidden = (normed * gain + shift).astype(BF)
        put_rows(m, hidden)
        hid_t[:, m * space : m * space + rows] = hidden.T
        acc_o[at] = middle + bias
        acc_h[at] = jnp.zeros_like(middle)

    if remote:
        for copy in side_copies():
            copy.wait()

    def deliver(slot, j):
        up, down = total.after_two(slot)
        for t in range(4):
            dup_ref[t, j] = up[:, t * (cols // 4) : (t + 1) * (cols // 4)]
            ddown_ref[t, j] = down[t * (width // 4) : (t + 1) * (width // 4)]

    def stored(j, slot):
        return (
            pltpu.make_async_copy(dup_buf.at[slot], dup_ref.at[j], sems.at[2, slot]),
            pltpu.make_async_copy(ddown_buf.at[slot], ddown_ref.at[j], sems.at[3, slot]),
        )

    vec_ref[...] = jnp.zeros_like(vec_ref)

    def finish(m):
        at = rows_of(m)
        normed, inverse = normalize(mid[at])
        grad = acc_h[at]
        wide = dy[at].astype(F32)
        vec_ref[0:1, :] += jnp.sum(grad * normed, axis=0, keepdims=True)
        vec_ref[1:2, :] += jnp.sum(grad, axis=0, keepdims=True)
        vec_ref[2:3, :] += jnp.sum(wide, axis=0, keepdims=True)
        grad_mid = wide + norm_back(grad, normed, inverse, gain)
        mid[at] = grad_mid
        store(m, 0).start()
        branch = grad_mid.astype(BF)
        dy[at] = branch
        put_rows(m, dot_t(branch, w_out[...]).astype(BF))
        if remote:

            @pl.when(is_text)
            def _():
                picked = dot(picks_ref[m], own_rows(m)).astype(BF)
                for s in range(3):
                    part = picked[s * 2 * SLOT : (s + 1) * 2 * SLOT]
                    if m < micros - 1:
                        sent[m, s] = part
                        row_copy(m, s).start()
                    else:
                        rows_last_ref[s] = part
                beside(m, picked[6 * SLOT :])

            if m == micros - 1:

                @pl.when(is_image)
                def _():
                    rows_last_ref[...] = jnp.zeros_like(rows_last_ref)
                    for t in range(TILES):
                        tiles[m * TILES + t, OWN:TILE] = jnp.zeros((TILE - OWN, width), BF)

                store(m, 1).start()
            else:
                pl.when(is_text)(lambda: store(m, 1).start())
        else:
            store(m, 1).start()

    @pl.loop(0, STEPS)
    def _(j):
        slot = lax.rem(j, 2)
        other = 1 - slot
        pl.when(j < STEPS - 1)(lambda: fetch(j + 1, other))
        fetched(slot)

        @pl.loop(0, micros)
        def _(m):
            for n in range(micros):
                pl.when((j == 0) & (m == n))(lambda: begin(n))
            at = rows_of(m)
            up = dot(own_rows(m), up_w[slot])
            grad = dot_t(dy[at], down_w[slot])
            for t in range(TILES):
                part = slice(t * OWN, (t + 1) * OWN)
                cdf, pdf = gelu_parts(up[part])
                act[m, part] = (up[part] * cdf).astype(BF)
                gup[m, part] = (grad[part] * (cdf + up[part] * pdf)).astype(BF)
            acc_o[at] += dot(act[m, 0:rows], down_w[slot])
            acc_h[at] += dot_t(gup[m, 0:rows], up_w[slot])
            if remote:

                @pl.when(m == 0)
                def _():
                    pl.when(j > 1)(lambda: deliver(slot, j - 2))
                    pl.when(j > 0)(lambda: total.after_core(other))


        if not remote:

            @pl.when(j > 1)
            def _():
                for copy in stored(j - 2, slot):
                    copy.wait()

        grad = dot(hid_t[...], gup[...].reshape(micros * space, cols)).astype(BF)
        if remote:
            dup_buf[slot] = grad.reshape(dup_buf.shape[1:])
            pl.when(j < STEPS - 1)(lambda: total.start(0, slot))
            pl.when(j > 0)(lambda: total.after_one(other))
        else:
            dup_buf[slot] = grad
        grad = dot(dy_t[...], act[...].reshape(micros * space, cols)).astype(BF)
        if remote:
            for d in range(8):
                ddown_buf[slot, d // 4, d // 2 % 2, d % 2] = grad[:, d * piece : (d + 1) * piece]
            pl.when(j < STEPS - 1)(lambda: total.start(1, slot))
        else:
            ddown_buf[slot] = grad
            for copy in stored(j, slot):
                copy.start()

    last = (STEPS - 1) % 2
    if remote:
        last_copies = [
            pltpu.make_async_copy(dup_buf.at[last], dup_last_ref, sems.at[2, 0]),
            pltpu.make_async_copy(ddown_buf.at[last], ddown_last_ref, sems.at[3, 0]),
        ]
        for copy in last_copies:
            copy.start()
    for n in range(micros):
        finish(n)
    if remote:
        deliver(1 - last, STEPS - 2)
    for m in range(micros):
        act[m, 0:rows, 0:width] = acc_o[rows_of(m)].astype(BF)
        store(m, 2).start()
    dwout[...] = t_dot(att[...], dy[...]).astype(BF)
    dwout_copy.start()
    if remote:

        @pl.when(is_text)
        def _():
            for m in range(micros - 1):
                for s in range(3):
                    row_copy(m, s).wait_send()

        @pl.when(is_image)
        def _():
            for m in range(micros - 1):
                row_copy(m, 0).wait_recv()
                beside(m, dot(places_ref[m], got_rows[m]).astype(BF))
                store(m, 1).start()
            att_copy(0).wait_send()

        for copy in last_copies:
            copy.wait()
    else:
        for j in range(STEPS - 2, STEPS):
            for copy in stored(j, j % 2):
                copy.wait()
    for m in range(micros):
        for n in range(3):
            store(m, n).wait()
    dwout_copy.wait()


def expert(
    remote,
    x_tiles,
    att,
    att_tiles,
    att_last,
    dy,
    w_out,
    vecs,
    picks,
    places,
    vis_up,
    vis_down,
    txt_up,
    txt_down,
):
    rows, width = att.shape
    cols = vis_up.shape[1] // STEPS
    micros = dy.shape[1]
    space = -(-rows // micros // BLOCK) * BLOCK
    dma = pltpu.SemaphoreType.DMA
    if remote:
        shard, piece = width // 8, cols // 8
        buffers = (2, 2, 2, 2, shard, cols), (2, 2, 2, 2, width, piece)
        outs = (4, STEPS - 1, shard, cols // 4), (4, STEPS - 1, width // 4, piece)
        lasts = [buffers[0][1:], buffers[1][1:], (3, 2 * SLOT, width)]
        out_specs = [HBM] * 4 + [FULL] * 3 + [HBM] * 2 + [FULL]
        more = [
            pltpu.VMEM((2, 2, 2, shard, cols), BF),
            pltpu.VMEM((2, 2, 2, width, piece), BF),
            pltpu.VMEM((2, 2, shard, cols), BF),
            pltpu.VMEM((2, 2, width, piece), BF),
            pltpu.VMEM((2, shard, cols), BF),
            pltpu.VMEM((2, width, piece), BF),
            dma((3, 2, 2, 2)),
            pltpu.VMEM((micros - 1, 3, 2 * SLOT, width), BF),
            pltpu.VMEM((micros - 1, 2 * SLOT, width), BF),
            dma((micros - 1, 3)),
            dma((micros - 1,)),
            pltpu.VMEM((3, 2 * SLOT, width), BF),
            pltpu.VMEM((TILES, TILE - OWN, width), BF),
            dma,
            dma((3,)),
            dma((TILES,)),
        ]
        params = dict(collective_id=1, has_side_effects=True)
    else:
        buffers = ((2, width, cols),) * 2
        outs = ((STEPS, width, cols),) * 2
        lasts, out_specs = [], [HBM] * 4 + [FULL] + [HBM] * 2
        more, params = [], {}
    return pl.pallas_call(
        functools.partial(expert_kernel, remote),
        in_specs=[HBM] * 6 + [FULL] * 3 + [HBM] * 4,
        out_specs=out_specs,
        out_shape=[
            jax.ShapeDtypeStruct((rows, width), BF),
            jax.ShapeDtypeStruct((rows, width), F32),
            jax.ShapeDtypeStruct((rows // OWN, TILE, width), BF),
            jax.ShapeDtypeStruct((width, width), BF),
            jax.ShapeDtypeStruct((8, width), F32),
        ]
        + [jax.ShapeDtypeStruct(shape, BF) for shape in [*outs, *lasts]],
        scratch_shapes=[
            pltpu.VMEM(dy.shape, BF),
            pltpu.VMEM((rows, width), BF),
            pltpu.VMEM((rows, width), BF),
            pltpu.VMEM((width, width), BF),
            pltpu.VMEM((rows, width), F32),
            pltpu.VMEM((rows // OWN, TILE, width), BF),
            pltpu.VMEM((width, micros * space), BF),
            pltpu.VMEM((width, micros * space), BF),
            pltpu.VMEM((rows, width), F32),
            pltpu.VMEM((rows, width), F32),
            pltpu.VMEM((2, width, cols), BF),
            pltpu.VMEM((2, cols, width), BF),
            pltpu.VMEM((micros, space, cols), BF),
            pltpu.VMEM((micros, space, cols), BF),
            pltpu.VMEM(buffers[0], BF),
            pltpu.VMEM(buffers[1], BF),
            dma((4, 2)),
            dma((micros, 9)),
            dma((TILES,)),
        ]
        + more,
        compiler_params=pltpu.CompilerParams(vmem_limit_bytes=63 * 2**20, **params),
        name="expert",
    )(
        x_tiles,
        att,
        att_tiles,
        att_last,
        dy,
        w_out,
        vecs,
        picks,
        places,
        vis_up,
        vis_down,
        txt_up,
        txt_down,
    )


def project_back_kernel(x_ref, dqkv_ref, vecs_ref, w_ref, dx_ref, dw_ref, vec_ref, acc):
    i = pl.program_id(0)
    gain, shift = row_of(vecs_ref, GAIN1), row_of(vecs_ref, SHIFT1)
    normed, inverse = normalize(x_ref[0].astype(F32))
    hidden = (normed * gain + shift).astype(BF)
    dqkv = dqkv_ref[0]
    grad = dot_t(dqkv, w_ref[...])
    dx_ref[0] = norm_back(grad, normed, inverse, gain).astype(BF)
    width = x_ref.shape[2]
    part = t_dot(hidden, dqkv)
    ones = jnp.ones((8, TILE), BF)
    sums = dot(ones, dqkv)[0:1]
    vec = jnp.concatenate(
        [
            jnp.sum(grad * normed, axis=0, keepdims=True),
            jnp.sum(grad, axis=0, keepdims=True),
            sums[:, :width],
            sums[:, 2 * width :],
        ],
        axis=0,
    )

    @pl.when(i == 0)
    def _():
        acc[...] = part
        vec_ref[0:4, :] = vec

    @pl.when(i > 0)
    def _():
        acc[...] += part
        vec_ref[0:4, :] += vec

    @pl.when(i == pl.num_programs(0) - 1)
    def _():
        dw_ref[...] = acc[...].astype(BF)


def project_back(x_tiles, dqkv, vecs, w_qkv):
    tiles, _, width = x_tiles.shape

    def block(*shape):
        return pl.BlockSpec((1,) + shape, lambda i: (i,) + (0,) * len(shape))

    return pl.pallas_call(
        project_back_kernel,
        grid=(tiles,),
        in_specs=[block(TILE, width), block(TILE, 3 * width), FULL, FULL],
        out_specs=[block(TILE, width), FULL, FULL],
        out_shape=[
            jax.ShapeDtypeStruct((tiles, TILE, width), BF),
            jax.ShapeDtypeStruct((width, 3 * width), BF),
            jax.ShapeDtypeStruct((8, width), F32),
        ],
        scratch_shapes=[pltpu.VMEM((width, 3 * width), F32)],
        compiler_params=pltpu.CompilerParams(vmem_limit_bytes=56 * 2**20),
        name="project_back",
    )(x_tiles, dqkv, vecs, w_qkv)


GROUP = 256
GROUPS = 3


def stream_blocks(count, share):
    spans = []
    for t in range(4):
        first, last = t * share // BLOCK, ((t + 1) * share - 1) // BLOCK
        spans.append(list(range(first, last + 1)))
    assert spans[-1][-1] == count - 1
    return spans


def unit_blocks(unit):
    if unit == 0:
        return list(range(6))
    g = unit - 1
    return [6 * part + 2 * g + i for part in range(3) for i in range(2)]


def back_kernel(
    x_ref,
    qkv_ref,
    p_ref,
    att_ref,
    inv_ref,
    datt_ref,
    dmid_ref,
    vecs_ref,
    w_ref,
    dwout_ref,
    zup_ref,
    zdown_ref,
    dup_last_ref,
    ddown_last_ref,
    rows_last_ref,
    vec2_ref,
    picks_ref,
    places_ref,
    dx_ref,
    sums_ref,
    got_qkv,
    got_out,
    got_up,
    got_down,
    qkv,
    x,
    att,
    inv,
    datt,
    base,
    probs,
    beside,
    got_last,
    last_a,
    last_b,
    got_last_a,
    got_last_b,
    one_last_a,
    one_last_b,
    two_last_a,
    two_last_b,
    z_last_up,
    z_last_down,
    hid_t,
    dqkv,
    w,
    sums,
    extra,
    mine,
    got_rows,
    buf_a,
    buf_b,
    got_a,
    got_b,
    one_a,
    one_b,
    two_a,
    two_b,
    held,
    dx,
    vec,
    got_vec,
    z_vec,
    load_sems,
    x_sems,
    w_sem,
    last_sems,
    last_send,
    last_recv,
    last_sum_sems,
    sum_sems,
    row_send,
    row_recv,
    vec_sems,
    zvec_send,
    zvec_recv,
    expert_send,
    expert_recv,
    block_send,
    block_recv,
    dx_sems,
):
    micros = x.shape[0] // TILES
    width = x.shape[2]
    shard = width // 8
    own_z = lax.axis_index("stream")
    is_text = own_z == 3
    is_image = jnp.logical_not(is_text)
    total = ItemSum(buf_a, buf_b, (got_a, got_b), (one_a, one_b), (two_a, two_b), sum_sems)

    total_last = ItemSum(
        last_a,
        last_b,
        (got_last_a, got_last_b),
        (one_last_a, one_last_b),
        (two_last_a, two_last_b),
        last_sum_sems,
    )

    def loads(step, slot):
        m, g = lax.div(step, GROUPS), lax.rem(step, GROUPS)
        tiles = pl.ds(m * TILES, TILES)
        at = pl.multiple_of(g * GROUP, GROUP)
        copies = [pltpu.make_async_copy(p_ref.at[tiles, pl.ds(g * 4, 4)], probs.at[slot], load_sems.at[slot, 0])]
        for part in range(3):
            src = qkv_ref.at[tiles, :, pl.ds(part * width + at, GROUP)]
            dst = qkv.at[slot, :, :, pl.ds(part * GROUP, GROUP)]
            copies.append(pltpu.make_async_copy(src, dst, load_sems.at[slot, 1 + part]))
        for n, (src, dst) in enumerate(((att_ref, att), (inv_ref, inv), (datt_ref, datt))):
            src = src.at[tiles, :, pl.ds(at, GROUP)]
            copies.append(pltpu.make_async_copy(src, dst.at[slot], load_sems.at[slot, 4 + n]))
        return copies

    def micro_loads(m):
        at = pl.ds(m * TILES, TILES)
        rows = pl.ds(m * TILES * OWN, TILES * OWN)
        return [
            pltpu.make_async_copy(x_ref.at[at], x.at[at], x_sems.at[m, 0]),
            pltpu.make_async_copy(dmid_ref.at[rows], base.at[rows], x_sems.at[m, 1]),
        ]

    last_loads = [
        pltpu.make_async_copy(dup_last_ref, last_a.at[0], last_sems.at[0]),
        pltpu.make_async_copy(ddown_last_ref, last_b.at[0], last_sems.at[1]),
    ]
    w_copies = []
    for g in range(GROUPS):
        for part in range(3):
            src = w_ref.at[:, pl.ds(part * width + g * GROUP, GROUP)]
            dst = w.at[:, pl.ds((g * 3 + part) * GROUP, GROUP)]
            w_copies.append(pltpu.make_async_copy(src, dst, w_sem))
    for copy in loads(0, 0):
        copy.start()
    meet(
        [{"dp": total.near}, {"dp": total.over_x}, {"dp": total.over_y}]
        + [{"stream": lax.rem(own_z + k, 4)} for k in range(1, 4)]
    )

    def last_row_copy(s):
        return pltpu.make_async_remote_copy(
            src_ref=rows_last_ref.at[s],
            dst_ref=got_last,
            send_sem=last_send.at[s],
            recv_sem=last_recv,
            device_id={"stream": s},
            device_id_type=MESH,
        )

    @pl.when(is_text)
    def _():
        for s in range(3):
            last_row_copy(s).start()

    done = zup_ref.shape[1]

    def expert_ends(which, t, src):
        if which == 0:
            return zup_ref.at[t], got_up.at[src, pl.ds(0, done)]
        if which == 1:
            return zdown_ref.at[t], got_down.at[src, pl.ds(0, done)]
        if which == 2:
            return z_last_up.at[t], got_up.at[src, done]
        return z_last_down.at[t], got_down.at[src, done]

    def expert_copy(t, which):
        src, dst = expert_ends(which, t, own_z)
        return pltpu.make_async_remote_copy(
            src_ref=src,
            dst_ref=dst,
            send_sem=expert_send.at[t, which],
            recv_sem=expert_recv.at[own_z, which],
            device_id={"stream": t},
            device_id_type=MESH,
        )

    def expert_arrival(src, which):
        dst = expert_ends(which, src, src)[1]
        return pltpu.make_async_remote_copy(
            src_ref=dst,
            dst_ref=dst,
            send_sem=expert_send.at[src, which],
            recv_sem=expert_recv.at[src, which],
            device_id={"stream": src},
            device_id_type=MESH,
        )

    def expert_sends(kinds):
        for t in range(4):

            @pl.when(own_z != t)
            def _():
                for which in kinds:
                    expert_copy(t, which).start()

            @pl.when(own_z == t)
            def _():
                for which in kinds:
                    src, dst = expert_ends(which, t, t)
                    pltpu.make_async_copy(src, dst, expert_send.at[t, which]).start()

    def take_last():
        up, down = total_last.after_two(0)
        part_up, part_down = z_last_up.shape[2], z_last_down.shape[1]
        for t in range(4):
            z_last_up[t] = up[:, t * part_up : (t + 1) * part_up]
            z_last_down[t] = down[t * part_down : (t + 1) * part_down]
        expert_sends((2, 3))

    expert_sends((0, 1))

    half = buf_a.shape[-1]

    def put_unit(unit, value):
        slot = lax.rem(unit, 2)
        buf_a[slot] = value[:, :half].reshape(buf_a.shape[1:])
        buf_b[slot] = value[:, half:].reshape(buf_b.shape[1:])
        total.start(0, slot)
        total.start(1, slot)

    def take_unit(unit):
        left, right = total.after_two(lax.rem(unit, 2))
        for n in range(3):
            held[unit, n] = left[:, n * BLOCK : (n + 1) * BLOCK]
            held[unit, n + 3] = right[:, n * BLOCK : (n + 1) * BLOCK]

    def block_copy(unit, n, t, place):
        dst = got_out if unit == 0 else got_qkv
        kind = 0 if unit == 0 else 1
        return pltpu.make_async_remote_copy(
            src_ref=held.at[unit, n],
            dst_ref=dst.at[own_z, place],
            send_sem=block_send.at[kind, t, place],
            recv_sem=block_recv.at[kind, own_z, place],
            device_id={"stream": t},
            device_id_type=MESH,
        )

    def own_block_copy(unit, n, t, place):
        dst = got_out if unit == 0 else got_qkv
        kind = 0 if unit == 0 else 1
        return pltpu.make_async_copy(
            held.at[unit, n], dst.at[t, place], block_send.at[kind, t, place]
        )

    out_spans = stream_blocks(6, width // 4)
    qkv_spans = stream_blocks(18, 3 * width // 4)

    def unit_sends(unit, t):
        span = (out_spans if unit == 0 else qkv_spans)[t]
        blocks = unit_blocks(unit)
        return [(n, span.index(b)) for n, b in enumerate(blocks) if b in span]

    def send_unit(unit):
        for t in range(4):

            @pl.when(own_z != t)
            def _():
                for n, place in unit_sends(unit, t):
                    block_copy(unit, n, t, place).start()

            @pl.when(own_z == t)
            def _():
                for n, place in unit_sends(unit, t):
                    own_block_copy(unit, n, t, place).start()

    put_unit(0, dwout_ref[...])

    def row_copy(m, s):
        return pltpu.make_async_remote_copy(
            src_ref=mine.at[m],
            dst_ref=got_rows.at[m, s],
            send_sem=row_send.at[m],
            recv_sem=row_recv.at[m, s],
            device_id={"stream": 3},
            device_id_type=MESH,
        )

    low, high = pair_lanes()
    gain, shift = row_of(vecs_ref, GAIN1), row_of(vecs_ref, SHIFT1)
    vec[...] = jnp.zeros_like(vec)

    def add_vec(row, value):
        for d in range(8):
            vec[d, row : row + 1, 0:shard] += value[:, d * shard : (d + 1) * shard]

    add_vec(4, vec2_ref[0:1, :])
    add_vec(5, vec2_ref[1:2, :])
    text_scale = jnp.where(is_text, 1.0, 0.0)
    add_vec(6, vec2_ref[2:3, :] * (1.0 - text_scale))
    add_vec(7, vec2_ref[2:3, :] * text_scale)

    steps = micros * GROUPS
    span = 3 * GROUP
    hid_t[width:] = jnp.ones_like(hid_t[width:])

    @pl.loop(0, steps)
    def _(step):
        m, g = lax.div(step, GROUPS), lax.rem(step, GROUPS)
        slot = lax.rem(step, 2)
        first = m * TILES
        there = pl.multiple_of(g * span, span)

        @pl.when(step + 1 < steps)
        def _():
            for copy in loads(step + 1, 1 - slot):
                copy.start()

        @pl.when(step == 0)
        def _():
            for m in range(micros):
                for copy in micro_loads(m):
                    copy.start()
            for copy in last_loads + w_copies:
                copy.start()

        for copy in loads(step, slot):
            copy.wait()

        @pl.when(is_image & (m == micros - 1))
        def _():
            @pl.when(g == 0)
            def _():
                last_row_copy(0).wait_recv()
                beside[...] = dot(places_ref[m], got_last[...]).astype(BF)

            cols = pl.ds(pl.multiple_of(g * GROUP, GROUP), GROUP)
            for t in range(TILES):
                datt[slot, t, OWN:TILE] = beside[t * (TILE - OWN) : (t + 1) * (TILE - OWN), cols]

        @pl.when((step >= 1) & (step <= micros))
        def _():
            first = (step - 1) * TILES
            for copy in micro_loads(step - 1):
                copy.wait()
            for t in range(TILES):
                normed, _ = normalize(x[first + t].astype(F32))
                hidden = (normed * gain + shift).astype(BF)
                at = pl.multiple_of((first + t) * TILE, TILE)
                hid_t[0:width, pl.ds(at, TILE)] = hidden.T

        def maker(t, pair):
            at = pair * BLOCK
            cols = pl.ds(at, BLOCK)
            return lambda: attend_back_pair(
                *(qkv[slot, t, :, pl.ds(part * GROUP + at, BLOCK)] for part in range(3)),
                [probs[slot, t, 2 * pair], probs[slot, t, 2 * pair + 1]],
                att[slot, t, :, cols],
                inv[slot, t, :, cols],
                datt[slot, t, :, cols],
                low,
                high,
            )

        def finish(n, results):
            t, pair = n // 2, n % 2
            rows = pl.ds(pl.multiple_of((first + t) * TILE, TILE), TILE)
            for part, value in enumerate(results):
                at = pl.multiple_of(there + part * GROUP + pair * BLOCK, BLOCK)
                dqkv[rows, pl.ds(at, BLOCK)] = value

        staggered([maker(n // 2, n % 2) for n in range(2 * TILES)], finish)

        @pl.when(step == 0)
        def _():
            total.after_core(0)
            for copy in last_loads:
                copy.wait()
            total_last.start(0, 0)
            total_last.start(1, 0)

        @pl.when(step == 1)
        def _():
            total.after_one(0)
            total_last.after_core(0)

        @pl.when(step == 2)
        def _():
            take_unit(0)
            send_unit(0)

        pl.when(step == 3)(lambda: total_last.after_one(0))
        pl.when(step == 4)(take_last)

        @pl.when(step == steps - 2)
        def _():
            total.after_core(1)

        @pl.when(step == steps - 1)
        def _():
            total.after_one(1)
            total.after_core(0)

        @pl.when(m == micros - 1)
        def _():
            grad = dot(hid_t[...], dqkv[:, pl.ds(there, span)])
            sums[g] = grad[width : width + 8]
            pl.when(step == steps - 1)(lambda: take_unit(1))
            put_unit(1 + g, grad[:width].astype(BF))
            pl.when(step == steps - 1)(lambda: send_unit(1))

        @pl.when(step == GROUPS - 1)
        def _():
            pltpu.make_async_copy(w, w, w_sem).wait()

        @pl.when(g == GROUPS - 1)
        def _():
            for side in ((OWN, TILE), (0, OWN)):
                count = side[1] - side[0]

                grads = [
                    dqkv[pl.ds(pl.multiple_of((first + t) * TILE + side[0], 16), count), :]
                    for t in range(TILES)
                ]
                grad = dot_t(jnp.concatenate(grads, axis=0), w[...])
                rows = [x[first + t, side[0] : side[1]] for t in range(TILES)]
                normed, inverse = normalize(jnp.concatenate(rows, axis=0).astype(F32))
                add_vec(0, jnp.sum(grad * normed, axis=0, keepdims=True))
                add_vec(1, jnp.sum(grad, axis=0, keepdims=True))
                back = norm_back(grad, normed, inverse, gain)
                if side[0] == 0:
                    own = pl.ds(pl.multiple_of(first * OWN, 16), TILES * OWN)
                    base[own] += back
                    continue
                extra[m] = back.astype(BF)

                @pl.when(is_image)
                def _():
                    mine[m] = t_dot(places_ref[m], extra[m]).astype(BF)
                    for s in range(3):

                        @pl.when(own_z == s)
                        def _():
                            row_copy(m, s).start()

    for row, at in ((2, 0), (3, 2 * GROUP)):
        cols = [sums[g, 0:1, at : at + GROUP] for g in range(GROUPS)]
        add_vec(row, jnp.concatenate(cols, axis=1))

    def vec_copy(stage):
        device = (total.near, total.over_x, total.over_y)[stage]
        return pltpu.make_async_remote_copy(
            src_ref=vec,
            dst_ref=got_vec.at[stage],
            send_sem=vec_sems.at[stage, 0],
            recv_sem=vec_sems.at[stage, 1],
            device_id={"dp": device},
            device_id_type=MESH,
        )

    def vec_stage(stage):
        vec_copy(stage).wait()
        vec[...] += got_vec[stage]

    def zvec_copy(t):
        return pltpu.make_async_remote_copy(
            src_ref=vec.at[total.me],
            dst_ref=z_vec.at[own_z],
            send_sem=zvec_send.at[t],
            recv_sem=zvec_recv.at[own_z],
            device_id={"stream": t},
            device_id_type=MESH,
        )

    def zvec_arrival(s):
        return pltpu.make_async_remote_copy(
            src_ref=z_vec.at[s],
            dst_ref=z_vec.at[s],
            send_sem=zvec_send.at[s],
            recv_sem=zvec_recv.at[s],
            device_id={"stream": s},
            device_id_type=MESH,
        )

    vec_copy(0).start()
    total.after_one(0)
    total.after_core(1)
    vec_stage(0)
    vec_copy(1).start()

    rows_all = TILES * OWN

    def dx_copy(m):
        rows = pl.ds(m * rows_all, rows_all)
        return pltpu.make_async_copy(dx.at[rows], dx_ref.at[rows], dx_sems.at[m])

    def deliver(m, scattered):
        rows = pl.ds(m * rows_all, rows_all)
        value = base[rows]
        if scattered:
            value = value + t_dot(
                picks_ref[m], jnp.concatenate([got_rows[m, s] for s in range(3)] + [extra[m]], axis=0)
            )
        dx[rows] = value.astype(BF)
        dx_copy(m).start()

    @pl.when(jnp.logical_not(is_text))
    def _():
        for m in range(micros - 1):
            deliver(m, False)

    @pl.when(is_text)
    def _():
        for m in range(micros - 1):
            for s in range(3):
                row_copy(m, s).wait_recv()
            deliver(m, True)

    take_unit(2)
    send_unit(2)
    total.after_one(1)
    vec_stage(1)
    vec_copy(2).start()

    @pl.when(jnp.logical_not(is_text))
    def _():
        deliver(micros - 1, False)

    for src in range(4):

        @pl.when(own_z != src)
        def _():
            for which in range(4):
                expert_arrival(src, which).wait_recv()
                expert_copy(src, which).wait_send()

        @pl.when(own_z == src)
        def _():
            for which in range(4):
                ref, dst = expert_ends(which, src, src)
                pltpu.make_async_copy(ref, dst, expert_send.at[src, which]).wait()

    take_unit(3)
    send_unit(3)
    vec_stage(2)
    for t in range(4):
        pl.when(own_z != t)(lambda: zvec_copy(t).start())

        @pl.when(own_z == t)
        def _():
            z_vec[t] = vec[total.me]

    @pl.when(is_text)
    def _():
        for s in range(3):
            row_copy(micros - 1, s).wait_recv()
        deliver(micros - 1, True)

        for s in range(3):
            last_row_copy(s).wait_send()

    @pl.when(is_image)
    def _():
        for m in range(micros):
            row_copy(m, 0).wait_send()

    for src in range(4):

        @pl.when(own_z != src)
        def _():
            zvec_arrival(src).wait_recv()
            zvec_copy(src).wait_send()
            for unit in range(GROUPS + 1):
                for n, place in unit_sends(unit, src):
                    block_copy(unit, n, src, place).wait_send()
            for kind, dst in ((0, got_out), (1, got_qkv)):
                for place in range(dst.shape[1]):
                    pltpu.make_async_remote_copy(
                        src_ref=dst.at[src, place],
                        dst_ref=dst.at[src, place],
                        send_sem=block_send.at[kind, src, place],
                        recv_sem=block_recv.at[kind, src, place],
                        device_id={"stream": src},
                        device_id_type=MESH,
                    ).wait_recv()

        @pl.when(own_z == src)
        def _():
            for unit in range(GROUPS + 1):
                for n, place in unit_sends(unit, src):
                    own_block_copy(unit, n, src, place).wait()

    sums_ref[...] = sum(z_vec[s] for s in range(4))
    for m in range(micros):
        dx_copy(m).wait()


def back(
    x_tiles,
    qkv,
    probs,
    att,
    inv,
    datt,
    dmid,
    vecs,
    w_qkv,
    dwout,
    zup,
    zdown,
    dup_last,
    ddown_last,
    rows_last,
    vec2,
    picks,
    places,
):
    tiles, _, width = x_tiles.shape
    micros = tiles // TILES
    shard = width // 8
    half = width // 2

    def sds(*shape, dtype=F32):
        return jax.ShapeDtypeStruct(shape, dtype)

    dma = pltpu.SemaphoreType.DMA
    return pl.pallas_call(
        back_kernel,
        in_specs=[HBM] * 7 + [FULL, HBM, FULL] + [HBM] * 5 + [FULL] * 3,
        out_specs=[HBM, FULL] + [HBM] * 4,
        out_shape=[
            sds(tiles * OWN, width, dtype=BF),
            sds(8, BLOCK),
            sds(4, 5, shard, BLOCK, dtype=BF),
            sds(4, 2, shard, BLOCK, dtype=BF),
            sds(4, STEPS, *zup.shape[2:], dtype=BF),
            sds(4, STEPS, *zdown.shape[2:], dtype=BF),
        ],
        scratch_shapes=[
            pltpu.VMEM((2, TILES, TILE, 3 * GROUP), BF),
            pltpu.VMEM((tiles, TILE, width), BF),
            pltpu.VMEM((2, TILES, TILE, GROUP), BF),
            pltpu.VMEM((2, TILES, TILE, GROUP), BF),
            pltpu.VMEM((2, TILES, TILE, GROUP), BF),
            pltpu.VMEM((tiles * OWN, width), F32),
            pltpu.VMEM((2, TILES, 4, TILE, TILE), BF),
            pltpu.VMEM((TILES * (TILE - OWN), width), BF),
            pltpu.VMEM((2 * SLOT, width), BF),
            pltpu.VMEM((1,) + dup_last.shape, BF),
            pltpu.VMEM((1,) + ddown_last.shape, BF),
            pltpu.VMEM((1, 2, 2) + dup_last.shape[3:], BF),
            pltpu.VMEM((1, 2, 2) + ddown_last.shape[3:], BF),
            pltpu.VMEM((1, 2) + dup_last.shape[3:], BF),
            pltpu.VMEM((1, 2) + ddown_last.shape[3:], BF),
            pltpu.VMEM((1,) + dup_last.shape[3:], BF),
            pltpu.VMEM((1,) + ddown_last.shape[3:], BF),
            pltpu.VMEM((4,) + zup.shape[2:], BF),
            pltpu.VMEM((4,) + zdown.shape[2:], BF),
            pltpu.VMEM((width + 16, tiles * TILE), BF),
            pltpu.VMEM((tiles * TILE, 3 * width), BF),
            pltpu.VMEM((width, 3 * width), BF),
            pltpu.VMEM((GROUPS, 8, 3 * GROUP), F32),
            pltpu.VMEM((micros, TILES * (TILE - OWN), width), BF),
            pltpu.VMEM((micros, 2 * SLOT, width), BF),
            pltpu.VMEM((micros, 3, 2 * SLOT, width), BF),
            pltpu.VMEM((2, 2, 2, 2, shard, half), BF),
            pltpu.VMEM((2, 2, 2, 2, shard, half), BF),
            pltpu.VMEM((2, 2, 2, shard, half), BF),
            pltpu.VMEM((2, 2, 2, shard, half), BF),
            pltpu.VMEM((2, 2, shard, half), BF),
            pltpu.VMEM((2, 2, shard, half), BF),
            pltpu.VMEM((2, shard, half), BF),
            pltpu.VMEM((2, shard, half), BF),
            pltpu.VMEM((GROUPS + 1, 6, shard, BLOCK), BF),
            pltpu.VMEM((tiles * OWN, width), BF),
            pltpu.VMEM((8, 8, BLOCK), F32),
            pltpu.VMEM((3, 8, 8, BLOCK), F32),
            pltpu.VMEM((4, 8, BLOCK), F32),
            dma((2, 7)),
            dma((micros, 2)),
            dma,
            dma((2,)),
            dma((3,)),
            dma,
            dma((3, 2, 2, 1)),
            dma((3, 2, 2, 2)),
            dma((micros,)),
            dma((micros, 3)),
            dma((3, 2)),
            dma((4,)),
            dma((4,)),
            dma((4, 4)),
            dma((4, 4)),
            dma((2, 4, 5)),
            dma((2, 4, 5)),
            dma((micros,)),
        ],
        compiler_params=pltpu.CompilerParams(
            vmem_limit_bytes=63 * 2**20, collective_id=2, has_side_effects=True
        ),
        name="back",
    )(
        x_tiles,
        qkv,
        probs,
        att,
        inv,
        datt,
        dmid,
        vecs,
        w_qkv,
        dwout,
        zup,
        zdown,
        dup_last,
        ddown_last,
        rows_last,
        vec2,
        picks,
        places,
    )


def results_kernel(
    out_hbm,
    dx_hbm,
    qkv_hbm,
    o_hbm,
    up_hbm,
    down_hbm,
    out_rows_hbm,
    dx_rows_hbm,
    dqkv_ref,
    dout_ref,
    dvup_ref,
    dvdown_ref,
    dtup_ref,
    dtdown_ref,
    out_ref,
    dx_ref,
    got_qkv,
    got_out,
    got_up,
    got_down,
    out_rows,
    dx_rows,
    sems,
):
    _, micros, width = out_rows.shape
    ins = (
        (out_hbm, out_ref),
        (dx_hbm, dx_ref),
        (up_hbm, got_up),
        (down_hbm, got_down),
        (qkv_hbm, got_qkv),
        (o_hbm, got_out),
    )
    loads = [pltpu.make_async_copy(src, dst, sems.at[n]) for n, (src, dst) in enumerate(ins)]
    outs = ((out_rows, out_rows_hbm), (dx_rows, dx_rows_hbm))
    stores = [pltpu.make_async_copy(src, dst, sems.at[6 + n]) for n, (src, dst) in enumerate(outs)]
    for load in loads:
        load.start()
    unpad = padding(micros, True)
    for n, (src, dst) in enumerate(((out_ref, out_rows), (dx_ref, dx_rows))):
        loads[n].wait()
        for t in range(TILES):
            tiles = [src[(m * TILES + t) * OWN : (m * TILES + t + 1) * OWN] for m in range(micros)]
            rows = dot(unpad, jnp.concatenate(tiles, axis=0)).astype(BF)
            dst[t * PATCHES : (t + 1) * PATCHES] = rows.reshape(PATCHES, micros, width)
        stores[n].start()

    for load in loads[2:]:
        load.wait()
    ff_piece = got_down.shape[3]
    for j in range(STEPS):
        vis = sum(got_up[s, j].astype(F32) for s in range(3))
        txt = got_up[3, j].astype(F32)
        for d in range(2):
            at = (d * STEPS + j) * ff_piece
            dvup_ref[:, at : at + ff_piece] = vis[:, d * ff_piece : (d + 1) * ff_piece]
            dtup_ref[:, at : at + ff_piece] = txt[:, d * ff_piece : (d + 1) * ff_piece]
        at = j * ff_piece
        dvdown_ref[:, at : at + ff_piece] = sum(got_down[s, j].astype(F32) for s in range(3))
        dtdown_ref[:, at : at + ff_piece] = got_down[3, j].astype(F32)

    odd = lax.rem(lax.axis_index("stream"), 2) == 1
    for got, out in ((got_qkv, dqkv_ref), (got_out, dout_ref)):
        blocks = [sum(got[s, n].astype(F32) for s in range(4)) for n in range(got.shape[1])]
        whole = jnp.concatenate(blocks, axis=1)
        moved = pltpu.roll(whole, whole.shape[1] - BLOCK // 2, 1)
        out[...] = jnp.where(odd, moved, whole)[:, : out.shape[1]]
    for store in stores:
        store.wait()


def results(micros, out, dx, got_qkv, got_out, got_up, got_down):
    width = out.shape[1]
    shard = got_up.shape[2]
    ff = 8 * STEPS * got_down.shape[3]
    rows = jax.ShapeDtypeStruct((TILES * PATCHES, micros, width), BF)
    grads = [
        (shard, 3 * width // 4),
        (shard, width // 4),
        (shard, ff // 4),
        (width // 4, ff // 8),
        (shard, ff // 4),
        (width // 4, ff // 8),
    ]
    return pl.pallas_call(
        results_kernel,
        in_specs=[HBM] * 6,
        out_specs=[HBM] * 2 + [FULL] * 6,
        out_shape=[rows, rows] + [jax.ShapeDtypeStruct(shape, F32) for shape in grads],
        scratch_shapes=[
            pltpu.VMEM(array.shape, BF) for array in (out, dx, got_qkv, got_out, got_up, got_down)
        ]
        + [pltpu.VMEM(rows.shape, BF)] * 2
        + [pltpu.SemaphoreType.DMA((8,))],
        compiler_params=pltpu.CompilerParams(vmem_limit_bytes=63 * 2**20),
        name="results",
    )(out, dx, got_qkv, got_out, got_up, got_down)


def pad_rows(block):
    micro, rows, width = block.shape
    thirds = block.reshape(micro, TILES, PATCHES, width)
    thirds = jnp.pad(thirds, ((0, 0), (0, 0), (0, OWN - PATCHES), (0, 0)))
    return thirds.reshape(micro, TILES * OWN, width)


def unpad_rows(block):
    micro, _, width = block.shape
    thirds = block.reshape(micro, TILES, OWN, width)[:, :, :PATCHES]
    return thirds.reshape(micro, TILES * PATCHES, width)


def plan(lengths, pairs, is_text, own_stream):
    micro, items = lengths.shape
    finish = jnp.cumsum(lengths, axis=1)
    starts = finish - lengths
    numbers = jnp.arange(items, dtype=jnp.int32)
    match = pairs[:, :, None] == numbers
    start = jnp.sum(jnp.where(match, starts[:, None, :], 0), axis=2).reshape(micro, 3, TILES)
    length = jnp.sum(jnp.where(match, lengths[:, None, :], 0), axis=2).reshape(micro, 3, TILES)
    paired = (pairs >= 0).reshape(micro, 3, TILES)
    rank = jnp.where(paired, jnp.cumsum(paired.astype(jnp.int32), axis=2) - 1, -1)
    takes = rank[:, :, :, None] == jnp.arange(2)
    slot_start = jnp.sum(jnp.where(takes, start[..., None], 0), axis=2)
    slot_length = jnp.sum(jnp.where(takes, length[..., None], 0), axis=2)
    step = jnp.arange(SLOT, dtype=jnp.int32)
    slot_rows = jnp.where(step < slot_length[..., None], slot_start[..., None] + step, -1)
    pad = jnp.arange(TILE - OWN, dtype=jnp.int32)
    next_rows = PATCHES * jnp.arange(1, TILES + 1, dtype=jnp.int32)[:, None] + pad
    next_rows = jnp.where((pad < SLOT) & (next_rows < TILES * PATCHES), next_rows, -1)
    next_rows = jnp.broadcast_to(next_rows, (micro, TILES, TILE - OWN))
    wanted = jnp.concatenate([slot_rows.reshape(micro, -1), next_rows.reshape(micro, -1)], axis=1)
    place = jnp.arange(TILES * OWN, dtype=jnp.int32)
    row_at = jnp.where(place % OWN < PATCHES, place // OWN * PATCHES + place % OWN, -2)
    picks = (wanted[:, :, None] == row_at).astype(BF)
    item_paired = jnp.any(match, axis=1)
    rows = jnp.arange(TILES * PATCHES + SLOT, dtype=jnp.int32)
    member = (rows[:, None] >= starts[:, None, :]) & (rows[:, None] < finish[:, None, :])
    code = jnp.where(item_paired, -1, numbers + items * (starts // PATCHES))
    row_code = jnp.sum(jnp.where(member, code[:, None, :] + 1, 0), axis=2) - 1
    tile = jnp.arange(TILES, dtype=jnp.int32)[:, None]
    own_code = row_code[:, : TILES * PATCHES].reshape(micro, TILES, PATCHES)
    next_code = jnp.stack(
        [row_code[:, PATCHES * (t + 1) : PATCHES * (t + 1) + SLOT] for t in range(TILES)], axis=1
    )

    def here(codes):
        return jnp.where((codes >= 0) & (codes // items == tile), codes, -1)

    def lay(own, extra):
        gap = jnp.full((micro, TILES, OWN - PATCHES), -1, jnp.int32)
        end = jnp.full((micro, TILES, TILE - OWN - SLOT), -1, jnp.int32)
        return jnp.concatenate([own, gap, extra, end], axis=2)

    text_ids = lay(here(own_code), here(next_code))
    own_length = lax.dynamic_index_in_dim(length, jnp.minimum(own_stream, 2), 1, keepdims=False)
    own_takes = lax.dynamic_index_in_dim(takes, jnp.minimum(own_stream, 2), 1, keepdims=False)
    image_ids = lay(
        jnp.zeros((micro, TILES, PATCHES), jnp.int32),
        jnp.where(step < own_length[..., None], 0, -1),
    )
    ids = jnp.where(is_text, text_ids, image_ids)
    own_takes = own_takes.astype(BF)
    same = (pad[:, None] == step).astype(BF)
    places = own_takes[:, :, None, :, None] * same[:, None, :]
    places = places.reshape(micro, TILES * (TILE - OWN), 2 * SLOT)
    return picks, places, own_takes, ids.reshape(micro * TILES, 1, TILE)


def plan_kernel(length_ref, pair_ref, *refs):
    vec_refs, (picks_ref, places_ref, ids_ref, vecs_ref, starts, codes) = refs[:8], refs[8:]
    for n, ref in enumerate(vec_refs):
        rows = ref.shape[0] // BLOCK
        vecs_ref[n * rows : (n + 1) * rows] = ref[...].astype(F32).reshape(rows, BLOCK)
    micros, items = length_ref.shape
    own_z = lax.axis_index("stream")
    is_text = own_z == 3
    block = jnp.minimum(own_z, 2)
    side = TILE - OWN
    place = lax.broadcasted_iota(jnp.int32, (1, TILES * OWN), 1)
    third = third_of(place, OWN)
    inside = place - OWN * third
    row_at = jnp.where(inside < PATCHES, PATCHES * third + inside, -2)
    lane = lax.broadcasted_iota(jnp.int32, (1, TILE), 1)
    far = lax.broadcasted_iota(jnp.int32, (6 * SLOT, 1), 0)
    near = lax.broadcasted_iota(jnp.int32, (TILES * side, 1), 0)
    near_tile = third_of(near, side)
    near_step = near - side * near_tile
    near_row = PATCHES * (near_tile + 1) + near_step
    near_row = jnp.where((near_step < SLOT) & (near_row < TILES * PATCHES), near_row, -1)
    slot_at = lax.broadcasted_iota(jnp.int32, (1, 2 * SLOT), 1)
    slot_of = (slot_at >= SLOT).astype(jnp.int32)
    slot_step = slot_at - SLOT * slot_of
    for m in range(micros):
        start = jnp.int32(0)
        for item in range(items):
            starts[m, item] = start
            codes[m, item] = item + items * third_of(start, PATCHES)
            start = start + length_ref[m, item]

        def pair_of(image):
            item = pair_ref[m, image]
            known = jnp.maximum(item, 0)
            paired = item >= 0
            return paired, starts[m, known], jnp.where(paired, length_ref[m, known], 0)

        wanted = jnp.full(far.shape, -1, jnp.int32)
        for s in range(3):
            rank = jnp.int32(0)
            for t in range(TILES):
                paired, start, length = pair_of(TILES * s + t)
                step = far - SLOT * (2 * s + rank)
                wanted = jnp.where((step >= 0) & (step < length), start + step, wanted)
                rank = rank + paired.astype(jnp.int32)
        picks_ref[m, 0 : 6 * SLOT] = (wanted == row_at).astype(F32).astype(BF)
        picks_ref[m, 6 * SLOT :] = (near_row == row_at).astype(F32).astype(BF)

        rank = jnp.int32(0)
        ranks = jnp.full(near.shape, -1, jnp.int32)
        lengths = []
        for t in range(TILES):
            paired, _, length = pair_of(TILES * block + t)
            lengths.append(length)
            ranks = jnp.where((near_tile == t) & paired, rank, ranks)
            rank = rank + paired.astype(jnp.int32)
        chosen = (near_step == slot_step) & (ranks == slot_of)
        places_ref[m] = chosen.astype(F32).astype(BF)

        for image in range(3 * TILES):

            @pl.when(pair_ref[m, image] >= 0)
            def _():
                codes[m, pair_ref[m, image]] = -1

        for t in range(TILES):
            beside = lane - OWN
            image_ids = jnp.where((lane < PATCHES) | ((beside >= 0) & (beside < lengths[t])), 0, -1)
            row = jnp.where(lane < PATCHES, PATCHES * t + lane, -1)
            row = jnp.where((beside >= 0) & (beside < SLOT), PATCHES * (t + 1) + beside, row)
            text_ids = jnp.full(lane.shape, -1, jnp.int32)
            for item in range(items):
                start, code = starts[m, item], codes[m, item]
                code = jnp.where(third_of(start, PATCHES) == t, code, -1)
                member = (row >= start) & (row < start + length_ref[m, item])
                text_ids = jnp.where(member, code, text_ids)
            ids_ref[m * TILES + t] = jnp.where(is_text, text_ids, image_ids)


def plan_rows(lengths, pairs, vectors):
    micros, items = lengths.shape
    smem = pl.BlockSpec(memory_space=pltpu.SMEM)
    return pl.pallas_call(
        plan_kernel,
        in_specs=[smem, smem] + [FULL] * 8,
        out_specs=[FULL] * 4,
        out_shape=[
            jax.ShapeDtypeStruct((micros, 6 * SLOT + TILES * (TILE - OWN), TILES * OWN), BF),
            jax.ShapeDtypeStruct((micros, TILES * (TILE - OWN), 2 * SLOT), BF),
            jax.ShapeDtypeStruct((micros * TILES, 1, TILE), jnp.int32),
            jax.ShapeDtypeStruct((8 * vectors[0].shape[0] // BLOCK, BLOCK), F32),
        ],
        scratch_shapes=[
            pltpu.SMEM((micros, items), jnp.int32),
            pltpu.SMEM((micros, items), jnp.int32),
        ],
        compiler_params=pltpu.CompilerParams(vmem_limit_bytes=63 * 2**20),
        name="plan_rows",
    )(lengths, pairs, *vectors)


def spread(padded, picks, own_takes, is_text):
    micro, _, width = padded.shape
    picked = lax.dot_general(
        picks, padded, (((2,), (1,)), ((0,), (0,))), preferred_element_type=F32
    ).astype(BF)
    near = picked[:, 6 * SLOT :].reshape(micro, TILES, TILE - OWN, width)[:, :, :SLOT]
    sent = picked[:, : 6 * SLOT].reshape(micro, 3, 2 * SLOT, width)
    far = sum(lax.ppermute(sent[:, s], "stream", [(3, s)]) for s in range(3))
    far = far.reshape(micro, 1, 2, SLOT, width) * own_takes[:, :, :, None, None]
    return jnp.where(is_text, near, far[:, :, 0] + far[:, :, 1])


def collect(extra, picks, own_takes, is_text):
    micro, _, _, width = extra.shape
    mine = extra[:, :, None] * own_takes[:, :, :, None, None]
    mine = (mine[:, 0] + mine[:, 1] + mine[:, 2]).reshape(micro, 2 * SLOT, width)
    parts = [lax.ppermute(mine, "stream", [(s, 3)]) for s in range(3)]
    extra = jnp.pad(extra, ((0, 0), (0, 0), (0, TILE - OWN - SLOT), (0, 0)))
    parts.append(extra.reshape(micro, TILES * (TILE - OWN), width))
    rows = jnp.concatenate(parts, axis=1)
    scale = jnp.where(is_text, 1.0, 0.0).astype(BF)
    return lax.dot_general(
        picks * scale, rows, (((1,), (1,)), ((0,), (0,))), preferred_element_type=F32
    ).astype(BF)


def reduce_all(vectors, dw_qkv, dw_out, dup, ddown):
    width = dw_qkv.shape[0]
    shard = width // lax.axis_size("dp")
    vectors = lax.psum(vectors, ("dp", "stream"))
    vectors = lax.dynamic_slice_in_dim(vectors, lax.axis_index("dp") * shard, shard, axis=1)

    def over_items(grad, dim):
        return lax.psum_scatter(grad, "dp", scatter_dimension=dim, tiled=True)

    def over_blocks(grad):
        return lax.psum_scatter(grad, "stream", scatter_dimension=1, tiled=True).astype(F32)

    qkv = over_blocks(over_items(dw_qkv, 0))
    out = over_blocks(over_items(dw_out, 0))
    dup = over_items(jnp.concatenate(list(dup), axis=1), 0)
    ddown = over_items(jnp.concatenate(list(ddown), axis=1), 1)
    up = dup.reshape(dup.shape[0], 4, -1).transpose(1, 0, 2)
    down = ddown.reshape(4, -1, ddown.shape[1])
    up = lax.all_to_all(up, "stream", 0, 0).astype(F32)
    down = lax.all_to_all(down, "stream", 0, 0).astype(F32)
    return (
        vectors,
        qkv,
        out,
        up[0] + up[1] + up[2],
        (down[0] + down[1] + down[2]).T,
        up[3],
        down[3].T,
    )


def shards(
    remote,
    tokens,
    text_lengths,
    pair_text,
    ln1_gain,
    ln1_bias,
    w_qkv,
    q_bias,
    v_bias,
    w_out,
    ln2_gain,
    ln2_bias,
    vis_up,
    vis_down,
    vis_bias,
    txt_up,
    txt_down,
    txt_bias,
    cotangent,
):
    micro = tokens.shape[0]
    width = tokens.shape[4]
    own_stream = lax.axis_index("stream")
    is_text = own_stream == 3
    vecs = [ln1_gain, ln1_bias, q_bias, v_bias, ln2_gain, ln2_bias, vis_bias, txt_bias]
    if remote:
        picks, places, ids, vecs = plan_rows(text_lengths[:, 0], pair_text[:, 0], vecs)
    else:
        vecs = jnp.concatenate(vecs).astype(F32).reshape(-1, BLOCK)
        picks, places, own_takes, ids = plan(
            text_lengths[:, 0], pair_text[:, 0], is_text, own_stream
        )

    def tiled(own, extra):
        own = own.reshape(micro, TILES, OWN, width)
        extra = jnp.pad(extra, ((0, 0), (0, 0), (0, TILE - OWN - SLOT), (0, 0)))
        return jnp.concatenate([own, extra], axis=2).reshape(micro * TILES, TILE, width)

    def parted(tiles):
        tiles = tiles.reshape(micro, TILES, TILE, width)
        return tiles[:, :, :OWN].reshape(micro, TILES * OWN, width), tiles[:, :, OWN : OWN + SLOT]

    if remote:
        x_tiles, qkv, probs, inverse, att_tiles, att, att_last = attend_rows(
            tokens[:, 0, 0].transpose(1, 0, 2), picks, places, ids, vecs, w_qkv
        )
    else:
        x = pad_rows(tokens[:, 0, 0])
        x_tiles = tiled(x, spread(x, picks, own_takes, is_text))
        qkv, att_tiles, probs, inverse = attend(x_tiles, ids, vecs, w_qkv)
        att_own, att_extra = parted(att_tiles)
        att = att_own + collect(att_extra, picks, own_takes, is_text)
        att = att.reshape(micro * TILES * OWN, width)
        att_last = jnp.zeros((2 * SLOT, width), BF)
    out, dmid, datt_tiles, dw_out, vec2, dup, ddown, *lasts = expert(
        remote,
        x_tiles,
        att,
        att_tiles,
        att_last,
        cotangent[:, 0, 0].transpose(1, 0, 2),
        w_out,
        vecs,
        picks,
        places,
        vis_up,
        vis_down,
        txt_up,
        txt_down,
    )
    if remote:
        dx, vectors, *shares = back(
            x_tiles,
            qkv,
            probs,
            att_tiles,
            inverse,
            datt_tiles,
            dmid,
            vecs,
            w_qkv,
            dw_out,
            dup,
            ddown,
            *lasts,
            vec2,
            picks,
            places,
        )
        vectors = vectors[:, : width // 8]
        out, dx, g_qkv, g_out, g_vup, g_vdown, g_tup, g_tdown = results(micro, out, dx, *shares)
        out, dx = out.transpose(1, 0, 2), dx.transpose(1, 0, 2)
        g_vdown, g_tdown = g_vdown.T, g_tdown.T
    else:
        datt = parted(datt_tiles)[0]
        datt_tiles = tiled(datt, spread(datt, picks, own_takes, is_text))
        dqkv = attend_back(qkv, probs, att_tiles, inverse, datt_tiles)
        dx_tiles, dw_qkv, vec1 = project_back(x_tiles, dqkv, vecs, w_qkv)
        dx_own, dx_extra = parted(dx_tiles)
        dx = (
            dmid.reshape(micro, TILES * OWN, width)
            + dx_own.astype(F32)
            + collect(dx_extra, picks, own_takes, is_text).astype(F32)
        )
        dx = unpad_rows(dx).astype(BF)
        out = unpad_rows(out.reshape(micro, TILES * OWN, width))
        text_scale = jnp.where(is_text, 1.0, 0.0)
        vectors = jnp.concatenate(
            [vec1[0:4], vec2[0:2], vec2[2:3] * (1.0 - text_scale), vec2[2:3] * text_scale], axis=0
        )
        vectors, g_qkv, g_out, g_vup, g_vdown, g_tup, g_tdown = reduce_all(
            vectors, dw_qkv, dw_out, dup, ddown
        )
    return (
        out.reshape(tokens.shape),
        dx.reshape(tokens.shape),
        vectors[0],
        vectors[1],
        g_qkv,
        vectors[2],
        vectors[3],
        g_out,
        vectors[4],
        vectors[5],
        g_vup,
        g_vdown,
        vectors[6],
        g_tup,
        g_tdown,
        vectors[7],
    )


def solution(mesh):
    rows = P(None, "dp", "stream", None, None)
    lists = P(None, "dp", None)
    vector, matrix = P("dp"), P("dp", "stream")
    in_specs = (rows, lists, lists) + (P(),) * 14 + (rows,)
    out_specs = (
        rows,
        rows,
        vector,
        vector,
        matrix,
        vector,
        vector,
        matrix,
        vector,
        vector,
        matrix,
        matrix,
        vector,
        matrix,
        matrix,
        vector,
    )
    remote = mesh.shape["dp"] == 8
    body = functools.partial(shards, remote)
    return jax.shard_map(body, mesh=mesh, in_specs=in_specs, out_specs=out_specs, check_vma=False)
```

```python
import functools

import jax
import jax.numpy as jnp
from jax import lax
from jax.experimental import pallas as pl
from jax.experimental.pallas import tpu as pltpu
from jax.sharding import PartitionSpec as P

HEADS = 12
PATCHES = 197
OWN = 208
SLOT = 40
TILE = 256
TILES = 3
EPSILON = 1e-06
MASKED = -1e30
BF = jnp.bfloat16
F32 = jnp.float32
FULL = pl.BlockSpec(memory_space=pltpu.VMEM)
HBM = pl.BlockSpec(memory_space=pl.ANY)
MESH = pl.DeviceIdType.MESH
BLOCK = 128


def dot(left, right):
    return jnp.dot(left, right, preferred_element_type=F32)


def dot_t(left, right):
    return lax.dot_general(left, right, (((1,), (1,)), ((), ())), preferred_element_type=F32)


def t_dot(left, right):
    return lax.dot_general(left, right, (((0,), (0,)), ((), ())), preferred_element_type=F32)


def normalize(values):
    centred = values - jnp.mean(values, axis=-1, keepdims=True)
    inverse = lax.rsqrt(jnp.mean(centred * centred, axis=-1, keepdims=True) + EPSILON)
    return centred * inverse, inverse


def norm_back(grad, normed, inverse, gain):
    scaled = grad * gain
    return inverse * (
        scaled
        - jnp.mean(scaled, axis=-1, keepdims=True)
        - normed * jnp.mean(scaled * normed, axis=-1, keepdims=True)
    )


def gelu_parts(up):
    rise = 1.0 + 0.2316418882663604 * jnp.abs(up)
    inner = 1.0 / rise
    bell = jnp.exp2(up * up * -0.7213475204444817)
    poly = inner * (
        0.127414796
        + inner
        * (-0.142248368 + inner * (0.7107068705 + inner * (-0.7265760135 + inner * 0.5307027145)))
    )
    tail = poly * bell
    return jnp.where(up >= 0, 1.0 - tail, tail), bell * 0.3989422804014327


def halves(block, low, high):
    return jnp.concatenate([block * low, block * high], axis=0)


def pair_lanes():
    lane = lax.broadcasted_iota(jnp.int32, (1, 128), 1)
    return (lane < 64).astype(BF), (lane >= 64).astype(BF)


def attend_pair(q, k, v, barred, low, high):
    scores = dot_t(halves(k, low, high), q * 0.125)
    yield
    expos = []
    for side in range(2):
        part = scores[TILE * side : TILE * (side + 1)] + barred
        top = jnp.maximum(jnp.max(part, axis=0, keepdims=True), 0.1 * MASKED)
        expos.append(jnp.exp(part - top).astype(BF))
    ones = [jnp.broadcast_to(keep, (TILE, 128)) for keep in (low, high)]
    right = jnp.concatenate([halves(v, low, high), jnp.concatenate(ones, axis=0)], axis=1)
    sums = t_dot(jnp.concatenate(expos, axis=0), right)
    inverse = jnp.where(sums[:, 128:] > 0.0, 1.0 / sums[:, 128:], 0.0)
    yield expos, sums[:, :128] * inverse, inverse


def attend_back_pair(q, k, v, expos, out, inverse, grad, low, high):
    scaled = grad.astype(F32) * inverse.astype(F32)
    inner = (scaled * out.astype(F32)).astype(BF)
    scaled = scaled.astype(BF)
    minus = [jnp.broadcast_to(-keep, (TILE, 128)) for keep in (low, high)]
    right = jnp.concatenate([halves(v, low, high), jnp.concatenate(minus, axis=0)], axis=1)
    slopes = dot_t(right, jnp.concatenate([scaled, inner], axis=1))
    yield
    parts = [
        (expos[side].astype(F32) * slopes[TILE * side : TILE * (side + 1)]).astype(BF)
        for side in range(2)
    ]
    dq = t_dot(jnp.concatenate(parts, axis=0), halves(k, low, high)) * 0.125
    dk = dot(jnp.concatenate(parts, axis=1), halves(q * 0.125, low, high))
    dv = dot(jnp.concatenate(expos, axis=1), halves(scaled, low, high))
    yield dq.astype(BF), dk.astype(BF), dv.astype(BF)


def staggered(makers, finish):
    held = None
    for n, make in enumerate(makers):
        step = make()
        next(step)
        if held is not None:
            finish(n - 1, next(held))
        held = step
    finish(len(makers) - 1, next(held))


def bars(ids_ref):
    ids = jnp.broadcast_to(ids_ref, (TILE, TILE))
    return jnp.where((ids == ids.T) & (ids >= 0), 0.0, MASKED)


GAIN1, SHIFT1, Q_BIAS, V_BIAS, GAIN2, SHIFT2, VIS_BIAS, TXT_BIAS = range(8)


def row_of(vecs_ref, at):
    rows = vecs_ref.shape[0] // 8
    return jnp.concatenate([vecs_ref[at * rows + n : at * rows + n + 1] for n in range(rows)], axis=1)


def project(values, vecs_ref, w_ref):
    normed, _ = normalize(values.astype(F32))
    hidden = (normed * row_of(vecs_ref, GAIN1) + row_of(vecs_ref, SHIFT1)).astype(BF)
    q_bias, v_bias = row_of(vecs_ref, Q_BIAS), row_of(vecs_ref, V_BIAS)
    bias = jnp.concatenate([q_bias, jnp.zeros_like(q_bias), v_bias], axis=1)
    return (dot(hidden, w_ref[...]) + bias).astype(BF)


def attend_kernel(x_ref, ids_ref, vecs_ref, w_ref, qkv_ref, out_ref, p_ref, inv_ref):
    width = x_ref.shape[2]
    qkv_ref[0] = project(x_ref[0], vecs_ref, w_ref)
    barred = bars(ids_ref[0])
    low, high = pair_lanes()

    def maker(pair):
        cols = [qkv_ref[0, :, part * width + pair * 128 :][:, :128] for part in range(3)]
        return lambda: attend_pair(*cols, barred, low, high)

    def finish(pair, results):
        expos, out, inverse = results
        at = pair * 128
        for side in range(2):
            p_ref[0, 2 * pair + side] = expos[side]
        out_ref[0, :, at : at + 128] = out.astype(BF)
        inv_ref[0, :, at : at + 128] = inverse.astype(BF)

    staggered([maker(pair) for pair in range(HEADS // 2)], finish)


def attend(x_tiles, ids, vecs, w_qkv):
    tiles, _, width = x_tiles.shape

    def block(*shape):
        return pl.BlockSpec((1,) + shape, lambda i: (i,) + (0,) * len(shape))

    return pl.pallas_call(
        attend_kernel,
        grid=(tiles,),
        in_specs=[block(TILE, width), block(1, TILE), FULL, FULL],
        out_specs=[
            block(TILE, 3 * width),
            block(TILE, width),
            block(HEADS, TILE, TILE),
            block(TILE, width),
        ],
        out_shape=[
            jax.ShapeDtypeStruct((tiles, TILE, 3 * width), BF),
            jax.ShapeDtypeStruct((tiles, TILE, width), BF),
            jax.ShapeDtypeStruct((tiles, HEADS, TILE, TILE), BF),
            jax.ShapeDtypeStruct((tiles, TILE, width), BF),
        ],
        compiler_params=pltpu.CompilerParams(vmem_limit_bytes=56 * 2**20),
        name="attend",
    )(x_tiles, ids, vecs, w_qkv)


def third_of(row, size):
    return (row >= size).astype(jnp.int32) + (row >= 2 * size).astype(jnp.int32)


def padding(micros, flip):
    count = micros * (OWN if flip else PATCHES)
    at = lax.broadcasted_iota(jnp.int32, (1, count), 1)
    rows = lax.broadcasted_iota(jnp.int32, (micros * (PATCHES if flip else OWN), 1), 0)
    if flip:
        wanted = lax.rem(rows, micros) * OWN + lax.div(rows, micros)
    else:
        micro = sum((rows >= m * OWN).astype(jnp.int32) for m in range(1, micros))
        row = rows - micro * OWN
        wanted = jnp.where(row < PATCHES, row * micros + micro, -1)
    return (wanted == at).astype(F32).astype(BF)


def pad_third(pad, third):
    rows, micros, width = third.shape
    return dot(pad, third.reshape(rows * micros, width)).astype(BF)


def attend_rows_kernel(
    tok_ref,
    picks_ref,
    places_ref,
    ids_ref,
    vecs_ref,
    w_hbm,
    x_out,
    qkv_out,
    p_out,
    inv_out,
    att_out,
    rows_out,
    mine_out,
    tok,
    w,
    x,
    qkv,
    probs,
    inv,
    att,
    rows_ref,
    sent,
    got,
    mine,
    got_back,
    tok_sems,
    w_sem,
    out_sems,
    p_sems,
    rows_sems,
    row_send,
    row_recv,
    back_send,
    back_recv,
):
    micros = tok.shape[1]
    width = tok.shape[2]
    own_z = lax.axis_index("stream")
    is_text = own_z == 3
    is_image = jnp.logical_not(is_text)
    side = TILE - OWN

    def tok_copy(t):
        at = pl.ds(t * PATCHES, PATCHES)
        return pltpu.make_async_copy(tok_ref.at[at], tok.at[at], tok_sems.at[t])

    for t in range(TILES):
        tok_copy(t).start()
    w_copy = pltpu.make_async_copy(w_hbm, w, w_sem)
    w_copy.start()
    meet([{"stream": lax.rem(own_z + k, 4)} for k in range(1, 4)])

    def row_copy(m, s):
        return pltpu.make_async_remote_copy(
            src_ref=sent.at[m, s],
            dst_ref=got.at[m],
            send_sem=row_send.at[m, s],
            recv_sem=row_recv.at[m],
            device_id={"stream": s},
            device_id_type=MESH,
        )

    def back_copy(m, s):
        return pltpu.make_async_remote_copy(
            src_ref=mine.at[m],
            dst_ref=got_back.at[m, s],
            send_sem=back_send.at[m],
            recv_sem=back_recv.at[m, s],
            device_id={"stream": 3},
            device_id_type=MESH,
        )

    def outs(m, which):
        at = pl.ds(m * TILES, TILES)
        pairs = ((x, x_out), (qkv, qkv_out), (inv, inv_out), (att, att_out))
        for n in which:
            src, dst = pairs[n]
            yield pltpu.make_async_copy(src.at[at], dst.at[at], out_sems.at[m, n])

    def rows_copy(m):
        at = pl.ds(m * TILES * OWN, TILES * OWN)
        return pltpu.make_async_copy(rows_ref.at[at], rows_out.at[at], rows_sems.at[m])

    mine_copy = pltpu.make_async_copy(mine.at[micros - 1], mine_out, rows_sems.at[micros])

    def probs_store(tile, slot):
        return pltpu.make_async_copy(probs.at[slot], p_out.at[tile], p_sems.at[slot])

    def own_rows(ref, m):
        return jnp.concatenate([ref[m * TILES + t, 0:OWN] for t in range(TILES)], axis=0)

    def beside(ref, m, value):
        for t in range(TILES):
            ref[m * TILES + t, OWN:TILE] = value[t * side : (t + 1) * side]

    pad = padding(micros, False)
    for t in range(TILES):
        tok_copy(t).wait()
        padded = pad_third(pad, tok[t * PATCHES : (t + 1) * PATCHES])
        for m in range(micros):
            x[m * TILES + t, 0:OWN] = padded[m * OWN : (m + 1) * OWN]
    for m in range(micros):

        @pl.when(is_text)
        def _():
            picked = dot(picks_ref[m], own_rows(x, m)).astype(BF)
            for s in range(3):
                sent[m, s] = picked[s * 2 * SLOT : (s + 1) * 2 * SLOT]
                row_copy(m, s).start()
            beside(x, m, picked[6 * SLOT :])

    w_copy.wait()
    for m in range(micros):
        rows = project(own_rows(x, m), vecs_ref, w)
        for t in range(TILES):
            qkv[m * TILES + t, 0:OWN] = rows[t * OWN : (t + 1) * OWN]

    low, high = pair_lanes()

    @pl.loop(0, micros)
    def _(m):
        @pl.when(is_image)
        def _():
            row_copy(m, 0).wait_recv()
            beside(x, m, dot(places_ref[m], got[m]).astype(BF))

        extra = [x[m * TILES + t, OWN:TILE] for t in range(TILES)]
        beside(qkv, m, project(jnp.concatenate(extra, axis=0), vecs_ref, w))
        for copy in outs(m, (0, 1)):
            copy.start()

        @pl.loop(0, TILES)
        def _(t):
            tile = m * TILES + t
            slot = lax.rem(tile, 2)
            pl.when(tile > 1)(lambda: probs_store(tile - 2, slot).wait())
            barred = bars(ids_ref[tile])

            def maker(pair):
                at = pair * BLOCK
                cols = [qkv[tile, :, pl.ds(part * width + at, BLOCK)] for part in range(3)]
                return lambda: attend_pair(*cols, barred, low, high)

            def finish(pair, results):
                expos, out, inverse = results
                at = pair * BLOCK
                for n in range(2):
                    probs[slot, 2 * pair + n] = expos[n]
                att[tile, :, at : at + BLOCK] = out.astype(BF)
                inv[tile, :, at : at + BLOCK] = inverse.astype(BF)

            staggered([maker(pair) for pair in range(HEADS // 2)], finish)
            probs_store(tile, slot).start()

        for copy in outs(m, (2, 3)):
            copy.start()
        at = pl.multiple_of(m * TILES * OWN, 16)
        rows_ref[pl.ds(at, TILES * OWN)] = own_rows(att, m)

        @pl.when(is_image)
        def _():
            extra = [att[m * TILES + t, OWN:TILE] for t in range(TILES)]
            mine[m] = t_dot(places_ref[m], jnp.concatenate(extra, axis=0)).astype(BF)
            for s in range(3):

                @pl.when((own_z == s) & (m < micros - 1))
                def _():
                    back_copy(m, s).start()

        @pl.when(m == micros - 1)
        def _():
            rows_copy(micros - 1).start()
            mine_copy.start()

    for m in range(micros - 1):

        @pl.when(is_text)
        def _():
            for s in range(3):
                back_copy(m, s).wait_recv()
            parts = [got_back[m, s] for s in range(3)]
            parts += [att[m * TILES + t, OWN:TILE] for t in range(TILES)]
            moved = t_dot(picks_ref[m], jnp.concatenate(parts, axis=0)).astype(BF)
            at = pl.ds(m * TILES * OWN, TILES * OWN)
            rows_ref[at] = (rows_ref[at].astype(F32) + moved.astype(F32)).astype(BF)

        rows_copy(m).start()
        pl.when(is_image)(lambda: back_copy(m, 0).wait_send())

    @pl.when(is_text)
    def _():
        for m in range(micros):
            for s in range(3):
                row_copy(m, s).wait_send()

    for m in range(micros):
        rows_copy(m).wait()
        for copy in outs(m, range(4)):
            copy.wait()
    mine_copy.wait()
    for slot in range(2):
        tile = micros * TILES - 2 + slot
        probs_store(tile, tile % 2).wait()


def attend_rows(tokens, picks, places, ids, vecs, w_qkv):
    _, micros, width = tokens.shape
    tiles = micros * TILES
    dma = pltpu.SemaphoreType.DMA

    def sds(*shape):
        return jax.ShapeDtypeStruct(shape, BF)

    return pl.pallas_call(
        attend_rows_kernel,
        in_specs=[HBM] + [FULL] * 4 + [HBM],
        out_specs=[HBM] * 7,
        out_shape=[
            sds(tiles, TILE, width),
            sds(tiles, TILE, 3 * width),
            sds(tiles, HEADS, TILE, TILE),
            sds(tiles, TILE, width),
            sds(tiles, TILE, width),
            sds(tiles * OWN, width),
            sds(2 * SLOT, width),
        ],
        scratch_shapes=[
            pltpu.VMEM(tokens.shape, BF),
            pltpu.VMEM(w_qkv.shape, BF),
            pltpu.VMEM((tiles, TILE, width), BF),
            pltpu.VMEM((tiles, TILE, 3 * width), BF),
            pltpu.VMEM((2, HEADS, TILE, TILE), BF),
            pltpu.VMEM((tiles, TILE, width), BF),
            pltpu.VMEM((tiles, TILE, width), BF),
            pltpu.VMEM((tiles * OWN, width), BF),
            pltpu.VMEM((micros, 3, 2 * SLOT, width), BF),
            pltpu.VMEM((micros, 2 * SLOT, width), BF),
            pltpu.VMEM((micros, 2 * SLOT, width), BF),
            pltpu.VMEM((micros, 3, 2 * SLOT, width), BF),
            dma((TILES,)),
            dma,
            dma((micros, 4)),
            dma((2,)),
            dma((micros + 1,)),
            dma((micros, 3)),
            dma((micros,)),
            dma((micros,)),
            dma((micros, 3)),
        ],
        compiler_params=pltpu.CompilerParams(
            vmem_limit_bytes=63 * 2**20, collective_id=3, has_side_effects=True
        ),
        name="attend_rows",
    )(tokens, picks, places, ids, vecs, w_qkv)


def attend_back_kernel(qkv_ref, p_ref, out_ref, inv_ref, grad_ref, dqkv_ref):
    width = out_ref.shape[2]
    low, high = pair_lanes()

    def maker(pair):
        at = pl.ds(pair * 128, 128)
        return lambda: attend_back_pair(
            *(qkv_ref[0, :, pl.ds(part * width + pair * 128, 128)] for part in range(3)),
            [p_ref[0, 2 * pair], p_ref[0, 2 * pair + 1]],
            out_ref[0, :, at],
            inv_ref[0, :, at],
            grad_ref[0, :, at],
            low,
            high,
        )

    def finish(pair, results):
        for part, value in enumerate(results):
            dqkv_ref[0, :, pl.ds(part * width + pair * 128, 128)] = value

    staggered([maker(pair) for pair in range(HEADS // 2)], finish)


def attend_back(qkv, probs, out, inverse, grad):
    tiles, _, width = out.shape

    def block(*shape):
        return pl.BlockSpec((1,) + shape, lambda i: (i,) + (0,) * len(shape))

    return pl.pallas_call(
        attend_back_kernel,
        grid=(tiles,),
        in_specs=[
            block(TILE, 3 * width),
            block(HEADS, TILE, TILE),
            block(TILE, width),
            block(TILE, width),
            block(TILE, width),
        ],
        out_specs=block(TILE, 3 * width),
        out_shape=jax.ShapeDtypeStruct((tiles, TILE, 3 * width), BF),
        compiler_params=pltpu.CompilerParams(vmem_limit_bytes=56 * 2**20),
        name="attend_back",
    )(qkv, probs, out, inverse, grad)


STEPS = 3


def add_into(ref, at, other):
    ref[at] = (ref[at].astype(F32) + other.astype(F32)).astype(BF)


class ItemSum:
    def __init__(self, up, down, got, got_one, got_two, sems):
        self.grads = (up, down)
        self.got, self.got_one, self.got_two, self.sems = got, got_one, got_two, sems
        me = lax.axis_index("dp")
        self.me = me
        self.core, self.x, self.y = lax.rem(me, 2), lax.rem(lax.div(me, 2), 2), lax.div(me, 4)
        self.near = me + 1 - 2 * self.core
        self.over_x = me + 2 - 4 * self.x
        self.over_y = me + 4 - 8 * self.y

    def _copy(self, src, dst, stage, which, slot, device):
        return pltpu.make_async_remote_copy(
            src_ref=src,
            dst_ref=dst,
            send_sem=self.sems.at[stage, which, 0, slot],
            recv_sem=self.sems.at[stage, which, 1, slot],
            device_id={"dp": device},
            device_id_type=MESH,
        )

    def core_copy(self, which, slot):
        src = self.grads[which].at[slot, :, :, 1 - self.core]
        return self._copy(src, self.got[which].at[slot], 0, which, slot, self.near)

    def one_copy(self, which, slot):
        grad = self.grads[which]
        if which == 0:
            src, device = grad.at[slot, :, 1 - self.x, self.core], self.over_x
        else:
            src, device = grad.at[slot, 1 - self.y, :, self.core], self.over_y
        return self._copy(src, self.got_one[which].at[slot], 1, which, slot, device)

    def two_copy(self, which, slot):
        grad = self.grads[which]
        if which == 0:
            src, device = grad.at[slot, 1 - self.y, self.x, self.core], self.over_y
        else:
            src, device = grad.at[slot, self.y, 1 - self.x, self.core], self.over_x
        return self._copy(src, self.got_two[which].at[slot], 2, which, slot, device)

    def start(self, which, slot):
        self.core_copy(which, slot).start()

    def after_core(self, slot):
        for which in range(2):
            self.core_copy(which, slot).wait()
            for y in range(2):
                for x in range(2):
                    at = (slot, y, x, self.core)
                    add_into(self.grads[which], at, self.got[which][slot, y, x])
            self.one_copy(which, slot).start()

    def after_one(self, slot):
        for which in range(2):
            self.one_copy(which, slot).wait()
            for side in range(2):
                at = (slot, side, self.x, self.core) if which == 0 else (slot, self.y, side, self.core)
                add_into(self.grads[which], at, self.got_one[which][slot, side])
            self.two_copy(which, slot).start()

    def after_two(self, slot):
        sums = []
        for which in range(2):
            self.two_copy(which, slot).wait()
            own = self.grads[which][slot, self.y, self.x, self.core].astype(F32)
            sums.append((own + self.got_two[which][slot].astype(F32)).astype(BF))
        return sums


def meet(devices):
    barrier = pltpu.get_barrier_semaphore()
    for device in devices:
        pl.semaphore_signal(barrier, inc=1, device_id=device, device_id_type=MESH)
    pl.semaphore_wait(barrier, len(devices))


def expert_kernel(
    remote,
    x_ref,
    att_ref,
    att_tiles_ref,
    att_last_ref,
    dy_ref,
    w_out_ref,
    vecs_ref,
    picks_ref,
    places_ref,
    up_v_ref,
    down_v_ref,
    up_t_ref,
    down_t_ref,
    out_ref,
    dmid_ref,
    datt_ref,
    dwout_ref,
    vec_ref,
    dup_ref,
    ddown_ref,
    *refs,
):
    if remote:
        dup_last_ref, ddown_last_ref, rows_last_ref, got_up, got_down, *refs = refs
    raw, dy, att, w_out, mid, tiles, hid_t, dy_t, acc_o, acc_h, up_w, down_w, *refs = refs
    act, gup, dup_buf, ddown_buf, sems, io_sems, raw_sems, *more = refs
    width = att.shape[1]
    cols = act.shape[2]
    micros = raw.shape[1]
    rows = TILES * OWN
    own_z = lax.axis_index("stream")
    is_text = own_z == 3
    is_image = jnp.logical_not(is_text)
    pieces = 8 if remote else 1
    piece = cols // pieces
    ff = up_v_ref.shape[1]

    def rows_of(m):
        return pl.ds(pl.multiple_of(m * rows, 16), rows)

    def loads(m):
        at = pl.ds(m * rows, rows)
        yield pltpu.make_async_copy(att_ref.at[at], att.at[at], io_sems.at[m, 0])
        for t in range(TILES):
            src = x_ref.at[m * TILES + t, 0:OWN]
            dst = act.at[m, t * OWN : (t + 1) * OWN, 0:width]
            yield pltpu.make_async_copy(src, dst, io_sems.at[m, 1 + t])

    def raw_copy(t):
        at = pl.ds(t * PATCHES, PATCHES)
        return pltpu.make_async_copy(dy_ref.at[at], raw.at[at], raw_sems.at[t])

    def store(m, n):
        at = rows_of(m)
        tile_at = pl.ds(m * TILES, TILES)
        src, dst = (
            (mid.at[at], dmid_ref.at[at]),
            (tiles.at[tile_at], datt_ref.at[tile_at]),
            (act.at[m, 0:rows, 0:width], out_ref.at[at]),
        )[n]
        return pltpu.make_async_copy(src, dst, io_sems.at[m, 5 + n])

    w_out_copy = pltpu.make_async_copy(w_out_ref, w_out, io_sems.at[0, 8])
    dwout = dy_t.at[:, 0:width]
    dwout_copy = pltpu.make_async_copy(dwout, dwout_ref, io_sems.at[0, 8])

    def fetch(j, slot):
        def go(up_src, down_src):
            for d in range(pieces):
                at = pl.ds(pl.multiple_of(j * piece + d * (ff // pieces), 128), piece)
                here = pl.ds(d * piece, piece)
                pltpu.make_async_copy(
                    up_src.at[:, at], up_w.at[slot, :, here], sems.at[0, slot]
                ).start()
                pltpu.make_async_copy(
                    down_src.at[at, :], down_w.at[slot, here, :], sems.at[1, slot]
                ).start()

        pl.when(is_text)(lambda: go(up_t_ref, down_t_ref))
        pl.when(is_image)(lambda: go(up_v_ref, down_v_ref))

    def fetched(slot):
        pltpu.make_async_copy(up_w.at[slot], up_w.at[slot], sems.at[0, slot]).wait()
        pltpu.make_async_copy(down_w.at[slot], down_w.at[slot], sems.at[1, slot]).wait()

    for t in range(TILES):
        raw_copy(t).start()
    w_out_copy.start()
    for m in range(micros):
        for copy in loads(m):
            copy.start()
    fetch(0, 0)

    if remote:
        got, got_one, got_two, sum_sems = more[0:2], more[2:4], more[4:6], more[6]
        sent, got_rows, row_send, row_recv, got_att, att_side = more[7:13]
        att_send, att_recv, side_sem, z_up, z_down, z_send, z_recv = more[13:]
        total = ItemSum(dup_buf, ddown_buf, got, got_one, got_two, sum_sems)

        def side_copies():
            for t in range(TILES):
                src = att_tiles_ref.at[(micros - 1) * TILES + t, OWN:TILE]
                yield pltpu.make_async_copy(src, att_side.at[t], side_sem.at[t])

        for copy in side_copies():
            copy.start()
        meet(
            [{"dp": total.near}, {"dp": total.over_x}, {"dp": total.over_y}]
            + [{"stream": lax.rem(own_z + k, 4)} for k in range(1, 4)]
        )

        def att_copy(s):
            return pltpu.make_async_remote_copy(
                src_ref=att_last_ref,
                dst_ref=got_att.at[s],
                send_sem=att_send,
                recv_sem=att_recv.at[s],
                device_id={"stream": 3},
                device_id_type=MESH,
            )

        for s in range(3):
            pl.when(own_z == s)(lambda: att_copy(s).start())

        def row_copy(m, s):
            return pltpu.make_async_remote_copy(
                src_ref=sent.at[m, s],
                dst_ref=got_rows.at[m],
                send_sem=row_send.at[m, s],
                recv_sem=row_recv.at[m],
                device_id={"stream": s},
                device_id_type=MESH,
            )

    gain, shift = row_of(vecs_ref, GAIN2), row_of(vecs_ref, SHIFT2)
    bias = jnp.where(is_text, row_of(vecs_ref, TXT_BIAS), row_of(vecs_ref, VIS_BIAS))
    space = dy_t.shape[1] // micros
    for ref in (hid_t, dy_t):
        for m in range(micros):
            lanes = slice(m * space + rows, (m + 1) * space)
            ref[:, lanes] = jnp.zeros((width, space - rows), BF)
    for ref in (act, gup):
        ref[:, rows:space] = jnp.zeros((micros, space - rows, cols), BF)
    pad = padding(micros, False)
    for t in range(TILES):
        raw_copy(t).wait()
        padded = pad_third(pad, raw[t * PATCHES : (t + 1) * PATCHES])
        for m in range(micros):
            at = m * rows + t * OWN
            dy[at : at + OWN] = padded[m * OWN : (m + 1) * OWN]
    for m in range(micros):
        dy_t[:, m * space : m * space + rows] = dy[m * rows : (m + 1) * rows].T

    def put_rows(m, value):
        for t in range(TILES):
            tiles[m * TILES + t, 0:OWN] = value[t * OWN : (t + 1) * OWN]

    def own_rows(m):
        return jnp.concatenate([tiles[m * TILES + t, 0:OWN] for t in range(TILES)], axis=0)

    def beside(m, value):
        for t in range(TILES):
            part = value[t * (TILE - OWN) : (t + 1) * (TILE - OWN)]
            tiles[m * TILES + t, OWN:TILE] = part

    def begin(m):
        for copy in loads(m):
            copy.wait()
        if m == 0:
            w_out_copy.wait()
        at = rows_of(m)
        if remote and m == micros - 1:

            @pl.when(is_text)
            def _():
                for s in range(3):
                    att_copy(s).wait_recv()
                parts = [got_att[s] for s in range(3)] + [att_side[t] for t in range(TILES)]
                moved = t_dot(picks_ref[m], jnp.concatenate(parts, axis=0)).astype(BF)
                att[at] = (att[at].astype(F32) + moved.astype(F32)).astype(BF)

        middle = act[m, 0:rows, 0:width].astype(F32) + dot(att[at], w_out[...])
        mid[at] = middle
        normed, _ = normalize(middle)
        hidden = (normed * gain + shift).astype(BF)
        put_rows(m, hidden)
        hid_t[:, m * space : m * space + rows] = hidden.T
        acc_o[at] = middle + bias
        acc_h[at] = jnp.zeros_like(middle)

    if remote:
        for copy in side_copies():
            copy.wait()

    def deliver(slot, up_ref, down_ref):
        up, down = total.after_two(slot)
        for t in range(4):
            up_ref[t] = up[:, t * (cols // 4) : (t + 1) * (cols // 4)]
            down_ref[t] = down[t * (width // 4) : (t + 1) * (width // 4)]

    def share_copy(t, which):
        src, dst = ((z_up, got_up), (z_down, got_down))[which]
        return pltpu.make_async_remote_copy(
            src_ref=src.at[t],
            dst_ref=dst.at[own_z],
            send_sem=z_send.at[t, which],
            recv_sem=z_recv.at[own_z, which],
            device_id={"stream": t},
            device_id_type=MESH,
        )

    def share_arrival(t, which):
        dst = (got_up, got_down)[which]
        return pltpu.make_async_remote_copy(
            src_ref=dst.at[t],
            dst_ref=dst.at[t],
            send_sem=z_send.at[t, which],
            recv_sem=z_recv.at[t, which],
            device_id={"stream": t},
            device_id_type=MESH,
        )

    def own_share(t, which):
        src, dst = ((z_up, got_up), (z_down, got_down))[which]
        return pltpu.make_async_copy(src.at[t], dst.at[t], z_send.at[t, which])

    def deliver_first(slot):
        deliver(slot, z_up, z_down)
        for t in range(4):
            for which in range(2):
                pl.when(own_z != t)(lambda: share_copy(t, which).start())
                pl.when(own_z == t)(lambda: own_share(t, which).start())

    def stored(j, slot):
        return (
            pltpu.make_async_copy(dup_buf.at[slot], dup_ref.at[j], sems.at[2, slot]),
            pltpu.make_async_copy(ddown_buf.at[slot], ddown_ref.at[j], sems.at[3, slot]),
        )

    vec_ref[...] = jnp.zeros_like(vec_ref)

    def finish(m):
        at = rows_of(m)
        normed, inverse = normalize(mid[at])
        grad = acc_h[at]
        wide = dy[at].astype(F32)
        vec_ref[0:1, :] += jnp.sum(grad * normed, axis=0, keepdims=True)
        vec_ref[1:2, :] += jnp.sum(grad, axis=0, keepdims=True)
        vec_ref[2:3, :] += jnp.sum(wide, axis=0, keepdims=True)
        grad_mid = wide + norm_back(grad, normed, inverse, gain)
        mid[at] = grad_mid
        store(m, 0).start()
        branch = grad_mid.astype(BF)
        dy[at] = branch
        put_rows(m, dot_t(branch, w_out[...]).astype(BF))
        if remote:

            @pl.when(is_text)
            def _():
                picked = dot(picks_ref[m], own_rows(m)).astype(BF)
                for s in range(3):
                    part = picked[s * 2 * SLOT : (s + 1) * 2 * SLOT]
                    if m < micros - 1:
                        sent[m, s] = part
                        row_copy(m, s).start()
                    else:
                        rows_last_ref[s] = part
                beside(m, picked[6 * SLOT :])

            if m == micros - 1:

                @pl.when(is_image)
                def _():
                    rows_last_ref[...] = jnp.zeros_like(rows_last_ref)
                    for t in range(TILES):
                        tiles[m * TILES + t, OWN:TILE] = jnp.zeros((TILE - OWN, width), BF)

                store(m, 1).start()
            else:
                pl.when(is_text)(lambda: store(m, 1).start())
        else:
            store(m, 1).start()

    @pl.loop(0, STEPS)
    def _(j):
        slot = lax.rem(j, 2)
        other = 1 - slot
        pl.when(j < STEPS - 1)(lambda: fetch(j + 1, other))
        fetched(slot)

        @pl.loop(0, micros)
        def _(m):
            for n in range(micros):
                pl.when((j == 0) & (m == n))(lambda: begin(n))
            at = rows_of(m)
            up = dot(own_rows(m), up_w[slot])
            grad = dot_t(dy[at], down_w[slot])
            for t in range(TILES):
                part = slice(t * OWN, (t + 1) * OWN)
                cdf, pdf = gelu_parts(up[part])
                act[m, part] = (up[part] * cdf).astype(BF)
                gup[m, part] = (grad[part] * (cdf + up[part] * pdf)).astype(BF)
            acc_o[at] += dot(act[m, 0:rows], down_w[slot])
            acc_h[at] += dot_t(gup[m, 0:rows], up_w[slot])
            if remote:

                @pl.when(m == 0)
                def _():
                    pl.when(j > 1)(lambda: deliver_first(slot))
                    pl.when(j > 0)(lambda: total.after_core(other))


        if not remote:

            @pl.when(j > 1)
            def _():
                for copy in stored(j - 2, slot):
                    copy.wait()

        grad = dot(hid_t[...], gup[...].reshape(micros * space, cols)).astype(BF)
        if remote:
            dup_buf[slot] = grad.reshape(dup_buf.shape[1:])
            pl.when(j < STEPS - 1)(lambda: total.start(0, slot))
        else:
            dup_buf[slot] = grad
        grad = dot(dy_t[...], act[...].reshape(micros * space, cols)).astype(BF)
        if remote:
            for d in range(8):
                ddown_buf[slot, d // 4, d // 2 % 2, d % 2] = grad[:, d * piece : (d + 1) * piece]
            pl.when(j < STEPS - 1)(lambda: total.start(1, slot))
            pl.when(j > 0)(lambda: total.after_one(other))
        else:
            ddown_buf[slot] = grad
            for copy in stored(j, slot):
                copy.start()

    last = (STEPS - 1) % 2
    if remote:
        last_copies = [
            pltpu.make_async_copy(dup_buf.at[last], dup_last_ref, sems.at[2, 0]),
            pltpu.make_async_copy(ddown_buf.at[last], ddown_last_ref, sems.at[3, 0]),
        ]
        for copy in last_copies:
            copy.start()
    for n in range(micros):
        finish(n)
    for m in range(micros):
        act[m, 0:rows, 0:width] = acc_o[rows_of(m)].astype(BF)
        store(m, 2).start()
    dwout[...] = t_dot(att[...], dy[...]).astype(BF)
    dwout_copy.start()
    if remote:
        deliver(1 - last, dup_ref, ddown_ref)

        @pl.when(is_text)
        def _():
            for m in range(micros - 1):
                for s in range(3):
                    row_copy(m, s).wait_send()

        @pl.when(is_image)
        def _():
            for m in range(micros - 1):
                row_copy(m, 0).wait_recv()
                beside(m, dot(places_ref[m], got_rows[m]).astype(BF))
                store(m, 1).start()
            att_copy(0).wait_send()

        for t in range(4):
            for which in range(2):

                @pl.when(own_z != t)
                def _():
                    share_arrival(t, which).wait_recv()
                    share_copy(t, which).wait_send()

                pl.when(own_z == t)(lambda: own_share(t, which).wait())
        for copy in last_copies:
            copy.wait()
    else:
        for j in range(STEPS - 2, STEPS):
            for copy in stored(j, j % 2):
                copy.wait()
    for m in range(micros):
        for n in range(3):
            store(m, n).wait()
    dwout_copy.wait()


def expert(
    remote,
    x_tiles,
    att,
    att_tiles,
    att_last,
    dy,
    w_out,
    vecs,
    picks,
    places,
    vis_up,
    vis_down,
    txt_up,
    txt_down,
):
    rows, width = att.shape
    cols = vis_up.shape[1] // STEPS
    micros = dy.shape[1]
    space = -(-rows // micros // BLOCK) * BLOCK
    dma = pltpu.SemaphoreType.DMA
    if remote:
        shard, piece = width // 8, cols // 8
        buffers = (2, 2, 2, 2, shard, cols), (2, 2, 2, 2, width, piece)
        outs = (4, shard, cols // 4), (4, width // 4, piece)
        lasts = [buffers[0][1:], buffers[1][1:], (3, 2 * SLOT, width), *outs]
        out_specs = [HBM] * 4 + [FULL] * 3 + [HBM] * 2 + [FULL] + [HBM] * 2
        more = [
            pltpu.VMEM((2, 2, 2, shard, cols), BF),
            pltpu.VMEM((2, 2, 2, width, piece), BF),
            pltpu.VMEM((2, 2, shard, cols), BF),
            pltpu.VMEM((2, 2, width, piece), BF),
            pltpu.VMEM((2, shard, cols), BF),
            pltpu.VMEM((2, width, piece), BF),
            dma((3, 2, 2, 2)),
            pltpu.VMEM((micros - 1, 3, 2 * SLOT, width), BF),
            pltpu.VMEM((micros - 1, 2 * SLOT, width), BF),
            dma((micros - 1, 3)),
            dma((micros - 1,)),
            pltpu.VMEM((3, 2 * SLOT, width), BF),
            pltpu.VMEM((TILES, TILE - OWN, width), BF),
            dma,
            dma((3,)),
            dma((TILES,)),
            pltpu.VMEM(outs[0], BF),
            pltpu.VMEM(outs[1], BF),
            dma((4, 2)),
            dma((4, 2)),
        ]
        params = dict(collective_id=1, has_side_effects=True)
    else:
        buffers = ((2, width, cols),) * 2
        outs = ((STEPS, width, cols),) * 2
        lasts, out_specs = [], [HBM] * 4 + [FULL] + [HBM] * 2
        more, params = [], {}
    return pl.pallas_call(
        functools.partial(expert_kernel, remote),
        in_specs=[HBM] * 6 + [FULL] * 3 + [HBM] * 4,
        out_specs=out_specs,
        out_shape=[
            jax.ShapeDtypeStruct((rows, width), BF),
            jax.ShapeDtypeStruct((rows, width), F32),
            jax.ShapeDtypeStruct((rows // OWN, TILE, width), BF),
            jax.ShapeDtypeStruct((width, width), BF),
            jax.ShapeDtypeStruct((8, width), F32),
        ]
        + [jax.ShapeDtypeStruct(shape, BF) for shape in [*outs, *lasts]],
        scratch_shapes=[
            pltpu.VMEM(dy.shape, BF),
            pltpu.VMEM((rows, width), BF),
            pltpu.VMEM((rows, width), BF),
            pltpu.VMEM((width, width), BF),
            pltpu.VMEM((rows, width), F32),
            pltpu.VMEM((rows // OWN, TILE, width), BF),
            pltpu.VMEM((width, micros * space), BF),
            pltpu.VMEM((width, micros * space), BF),
            pltpu.VMEM((rows, width), F32),
            pltpu.VMEM((rows, width), F32),
            pltpu.VMEM((2, width, cols), BF),
            pltpu.VMEM((2, cols, width), BF),
            pltpu.VMEM((micros, space, cols), BF),
            pltpu.VMEM((micros, space, cols), BF),
            pltpu.VMEM(buffers[0], BF),
            pltpu.VMEM(buffers[1], BF),
            dma((4, 2)),
            dma((micros, 9)),
            dma((TILES,)),
        ]
        + more,
        compiler_params=pltpu.CompilerParams(vmem_limit_bytes=63 * 2**20, **params),
        name="expert",
    )(
        x_tiles,
        att,
        att_tiles,
        att_last,
        dy,
        w_out,
        vecs,
        picks,
        places,
        vis_up,
        vis_down,
        txt_up,
        txt_down,
    )


def project_back_kernel(x_ref, dqkv_ref, vecs_ref, w_ref, dx_ref, dw_ref, vec_ref, acc):
    i = pl.program_id(0)
    gain, shift = row_of(vecs_ref, GAIN1), row_of(vecs_ref, SHIFT1)
    normed, inverse = normalize(x_ref[0].astype(F32))
    hidden = (normed * gain + shift).astype(BF)
    dqkv = dqkv_ref[0]
    grad = dot_t(dqkv, w_ref[...])
    dx_ref[0] = norm_back(grad, normed, inverse, gain).astype(BF)
    width = x_ref.shape[2]
    part = t_dot(hidden, dqkv)
    ones = jnp.ones((8, TILE), BF)
    sums = dot(ones, dqkv)[0:1]
    vec = jnp.concatenate(
        [
            jnp.sum(grad * normed, axis=0, keepdims=True),
            jnp.sum(grad, axis=0, keepdims=True),
            sums[:, :width],
            sums[:, 2 * width :],
        ],
        axis=0,
    )

    @pl.when(i == 0)
    def _():
        acc[...] = part
        vec_ref[0:4, :] = vec

    @pl.when(i > 0)
    def _():
        acc[...] += part
        vec_ref[0:4, :] += vec

    @pl.when(i == pl.num_programs(0) - 1)
    def _():
        dw_ref[...] = acc[...].astype(BF)


def project_back(x_tiles, dqkv, vecs, w_qkv):
    tiles, _, width = x_tiles.shape

    def block(*shape):
        return pl.BlockSpec((1,) + shape, lambda i: (i,) + (0,) * len(shape))

    return pl.pallas_call(
        project_back_kernel,
        grid=(tiles,),
        in_specs=[block(TILE, width), block(TILE, 3 * width), FULL, FULL],
        out_specs=[block(TILE, width), FULL, FULL],
        out_shape=[
            jax.ShapeDtypeStruct((tiles, TILE, width), BF),
            jax.ShapeDtypeStruct((width, 3 * width), BF),
            jax.ShapeDtypeStruct((8, width), F32),
        ],
        scratch_shapes=[pltpu.VMEM((width, 3 * width), F32)],
        compiler_params=pltpu.CompilerParams(vmem_limit_bytes=56 * 2**20),
        name="project_back",
    )(x_tiles, dqkv, vecs, w_qkv)


GROUP = 256
GROUPS = 3
SLOTS = 3


def stream_blocks(count, share):
    spans = []
    for t in range(4):
        first, last = t * share // BLOCK, ((t + 1) * share - 1) // BLOCK
        spans.append(list(range(first, last + 1)))
    assert spans[-1][-1] == count - 1
    return spans


def unit_blocks(unit):
    if unit == 0:
        return list(range(6))
    g = unit - 1
    return [6 * part + 2 * g + i for part in range(3) for i in range(2)]


def back_kernel(
    x_ref,
    qkv_ref,
    p_ref,
    att_ref,
    inv_ref,
    datt_ref,
    dmid_ref,
    vecs_ref,
    w_ref,
    dwout_ref,
    zup_ref,
    zdown_ref,
    dup_last_ref,
    ddown_last_ref,
    rows_last_ref,
    vec2_ref,
    picks_ref,
    places_ref,
    dx_ref,
    sums_ref,
    got_qkv,
    got_out,
    got_up,
    got_down,
    qkv,
    x,
    att,
    inv,
    datt,
    base,
    probs,
    beside,
    got_last,
    last_a,
    last_b,
    got_last_a,
    got_last_b,
    one_last_a,
    one_last_b,
    two_last_a,
    two_last_b,
    z_last_up,
    z_last_down,
    hid_t,
    dqkv,
    w,
    sums,
    extra,
    mine,
    got_rows,
    buf_a,
    buf_b,
    got_a,
    got_b,
    one_a,
    one_b,
    two_a,
    two_b,
    held,
    dx,
    vec,
    got_vec,
    own_vec,
    z_vec,
    load_sems,
    x_sems,
    w_sem,
    last_sems,
    last_send,
    last_recv,
    last_sum_sems,
    sum_sems,
    row_send,
    row_recv,
    vec_sems,
    zvec_send,
    zvec_recv,
    expert_send,
    expert_recv,
    block_send,
    block_recv,
    dx_sems,
):
    micros = x.shape[0] // TILES
    width = x.shape[2]
    shard = width // 8
    own_z = lax.axis_index("stream")
    is_text = own_z == 3
    is_image = jnp.logical_not(is_text)
    total = ItemSum(buf_a, buf_b, (got_a, got_b), (one_a, one_b), (two_a, two_b), sum_sems)

    total_last = ItemSum(
        last_a,
        last_b,
        (got_last_a, got_last_b),
        (one_last_a, one_last_b),
        (two_last_a, two_last_b),
        last_sum_sems,
    )

    def loads(step, slot):
        m, g = lax.div(step, GROUPS), lax.rem(step, GROUPS)
        tiles = pl.ds(m * TILES, TILES)
        at = pl.multiple_of(g * GROUP, GROUP)
        copies = [pltpu.make_async_copy(p_ref.at[tiles, pl.ds(g * 4, 4)], probs.at[slot], load_sems.at[slot, 0])]
        for part in range(3):
            src = qkv_ref.at[tiles, :, pl.ds(part * width + at, GROUP)]
            dst = qkv.at[slot, :, :, pl.ds(part * GROUP, GROUP)]
            copies.append(pltpu.make_async_copy(src, dst, load_sems.at[slot, 1 + part]))
        for n, (src, dst) in enumerate(((att_ref, att), (inv_ref, inv), (datt_ref, datt))):
            src = src.at[tiles, :, pl.ds(at, GROUP)]
            copies.append(pltpu.make_async_copy(src, dst.at[slot], load_sems.at[slot, 4 + n]))
        return copies

    def micro_loads(m):
        at = pl.ds(m * TILES, TILES)
        rows = pl.ds(m * TILES * OWN, TILES * OWN)
        return [
            pltpu.make_async_copy(x_ref.at[at], x.at[at], x_sems.at[m, 0]),
            pltpu.make_async_copy(dmid_ref.at[rows], base.at[rows], x_sems.at[m, 1]),
        ]

    last_loads = [
        pltpu.make_async_copy(dup_last_ref, last_a.at[0], last_sems.at[0]),
        pltpu.make_async_copy(ddown_last_ref, last_b.at[0], last_sems.at[1]),
    ]
    w_copies = []
    for g in range(GROUPS):
        for part in range(3):
            src = w_ref.at[:, pl.ds(part * width + g * GROUP, GROUP)]
            dst = w.at[:, pl.ds((g * 3 + part) * GROUP, GROUP)]
            w_copies.append(pltpu.make_async_copy(src, dst, w_sem))
    for copy in [*loads(0, 0), *last_loads]:
        copy.start()
    meet(
        [{"dp": lax.rem(total.me + k, 8)} for k in range(1, 8)]
        + [{"stream": lax.rem(own_z + k, 4)} for k in range(1, 4)]
    )

    def last_row_copy(s):
        return pltpu.make_async_remote_copy(
            src_ref=rows_last_ref.at[s],
            dst_ref=got_last,
            send_sem=last_send.at[s],
            recv_sem=last_recv,
            device_id={"stream": s},
            device_id_type=MESH,
        )

    @pl.when(is_text)
    def _():
        for s in range(3):
            last_row_copy(s).start()

    def expert_ends(which, t, src):
        mine = zup_ref, zdown_ref, z_last_up, z_last_down
        return mine[which].at[t], (got_up, got_down)[which % 2].at[src, which // 2]

    def expert_copy(t, which):
        src, dst = expert_ends(which, t, own_z)
        return pltpu.make_async_remote_copy(
            src_ref=src,
            dst_ref=dst,
            send_sem=expert_send.at[t, which],
            recv_sem=expert_recv.at[own_z, which],
            device_id={"stream": t},
            device_id_type=MESH,
        )

    def expert_arrival(src, which):
        dst = expert_ends(which, src, src)[1]
        return pltpu.make_async_remote_copy(
            src_ref=dst,
            dst_ref=dst,
            send_sem=expert_send.at[src, which],
            recv_sem=expert_recv.at[src, which],
            device_id={"stream": src},
            device_id_type=MESH,
        )

    def expert_sends(kinds):
        for t in range(4):

            @pl.when(own_z != t)
            def _():
                for which in kinds:
                    expert_copy(t, which).start()

            @pl.when(own_z == t)
            def _():
                for which in kinds:
                    src, dst = expert_ends(which, t, t)
                    pltpu.make_async_copy(src, dst, expert_send.at[t, which]).start()

    def take_last():
        up, down = total_last.after_two(0)
        part_up, part_down = z_last_up.shape[2], z_last_down.shape[1]
        for t in range(4):
            z_last_up[t] = up[:, t * part_up : (t + 1) * part_up]
            z_last_down[t] = down[t * part_down : (t + 1) * part_down]
        expert_sends((2, 3))

    expert_sends((0, 1))

    half = buf_a.shape[-1]

    def put_unit(unit, value):
        slot = lax.rem(unit, SLOTS)
        buf_a[slot] = value[:, :half].reshape(buf_a.shape[1:])
        buf_b[slot] = value[:, half:].reshape(buf_b.shape[1:])
        total.start(0, slot)
        total.start(1, slot)

    def take_unit(unit):
        left, right = total.after_two(unit % SLOTS)
        for n in range(3):
            held[unit, n] = left[:, n * BLOCK : (n + 1) * BLOCK]
            held[unit, n + 3] = right[:, n * BLOCK : (n + 1) * BLOCK]

    def block_copy(unit, n, t, place):
        dst = got_out if unit == 0 else got_qkv
        kind = 0 if unit == 0 else 1
        return pltpu.make_async_remote_copy(
            src_ref=held.at[unit, n],
            dst_ref=dst.at[own_z, place],
            send_sem=block_send.at[kind, t, place],
            recv_sem=block_recv.at[kind, own_z, place],
            device_id={"stream": t},
            device_id_type=MESH,
        )

    def own_block_copy(unit, n, t, place):
        dst = got_out if unit == 0 else got_qkv
        kind = 0 if unit == 0 else 1
        return pltpu.make_async_copy(
            held.at[unit, n], dst.at[t, place], block_send.at[kind, t, place]
        )

    out_spans = stream_blocks(6, width // 4)
    qkv_spans = stream_blocks(18, 3 * width // 4)

    def unit_sends(unit, t):
        span = (out_spans if unit == 0 else qkv_spans)[t]
        blocks = unit_blocks(unit)
        return [(n, span.index(b)) for n, b in enumerate(blocks) if b in span]

    def send_unit(unit):
        for t in range(4):

            @pl.when(own_z != t)
            def _():
                for n, place in unit_sends(unit, t):
                    block_copy(unit, n, t, place).start()

            @pl.when(own_z == t)
            def _():
                for n, place in unit_sends(unit, t):
                    own_block_copy(unit, n, t, place).start()

    put_unit(0, dwout_ref[...])

    def row_copy(m, s):
        return pltpu.make_async_remote_copy(
            src_ref=mine.at[m],
            dst_ref=got_rows.at[m, s],
            send_sem=row_send.at[m],
            recv_sem=row_recv.at[m, s],
            device_id={"stream": 3},
            device_id_type=MESH,
        )

    low, high = pair_lanes()
    gain, shift = row_of(vecs_ref, GAIN1), row_of(vecs_ref, SHIFT1)
    vec[...] = jnp.zeros_like(vec)

    def add_vec(row, value):
        for d in range(8):
            vec[d, row : row + 1, 0:shard] += value[:, d * shard : (d + 1) * shard]

    add_vec(4, vec2_ref[0:1, :])
    add_vec(5, vec2_ref[1:2, :])
    text_scale = jnp.where(is_text, 1.0, 0.0)
    add_vec(6, vec2_ref[2:3, :] * (1.0 - text_scale))
    add_vec(7, vec2_ref[2:3, :] * text_scale)

    def input_grad(m, begin, end):
        first = m * TILES
        starts = [pl.multiple_of((first + t) * TILE + begin, 16) for t in range(TILES)]
        grads = [dqkv[pl.ds(start, end - begin), :] for start in starts]
        grad = dot_t(jnp.concatenate(grads, axis=0), w[...])
        rows = [x[first + t, begin:end] for t in range(TILES)]
        normed, inverse = normalize(jnp.concatenate(rows, axis=0).astype(F32))
        add_vec(0, jnp.sum(grad * normed, axis=0, keepdims=True))
        add_vec(1, jnp.sum(grad, axis=0, keepdims=True))
        return norm_back(grad, normed, inverse, gain)

    steps = micros * GROUPS
    span = 3 * GROUP
    hid_t[width:] = jnp.ones_like(hid_t[width:])

    @pl.loop(0, steps)
    def _(step):
        m, g = lax.div(step, GROUPS), lax.rem(step, GROUPS)
        slot = lax.rem(step, 2)
        first = m * TILES
        there = pl.multiple_of(g * span, span)

        @pl.when(step + 1 < steps)
        def _():
            for copy in loads(step + 1, 1 - slot):
                copy.start()

        @pl.when(step == 0)
        def _():
            for m in range(micros):
                for copy in micro_loads(m):
                    copy.start()
            for copy in w_copies:
                copy.start()

        for copy in loads(step, slot):
            copy.wait()

        @pl.when(step == 0)
        def _():
            for copy in last_loads:
                copy.wait()
            total_last.start(0, 0)
            total_last.start(1, 0)

        pl.when(step == 1)(lambda: total_last.after_core(0))

        @pl.when(is_image & (m == micros - 1))
        def _():
            @pl.when(g == 0)
            def _():
                last_row_copy(0).wait_recv()
                beside[...] = dot(places_ref[m], got_last[...]).astype(BF)

            cols = pl.ds(pl.multiple_of(g * GROUP, GROUP), GROUP)
            for t in range(TILES):
                datt[slot, t, OWN:TILE] = beside[t * (TILE - OWN) : (t + 1) * (TILE - OWN), cols]

        @pl.when((step >= 1) & (step <= micros))
        def _():
            first = (step - 1) * TILES
            for copy in micro_loads(step - 1):
                copy.wait()
            for t in range(TILES):
                normed, _ = normalize(x[first + t].astype(F32))
                hidden = (normed * gain + shift).astype(BF)
                at = pl.multiple_of((first + t) * TILE, TILE)
                hid_t[0:width, pl.ds(at, TILE)] = hidden.T

        def maker(t, pair):
            at = pair * BLOCK
            cols = pl.ds(at, BLOCK)
            return lambda: attend_back_pair(
                *(qkv[slot, t, :, pl.ds(part * GROUP + at, BLOCK)] for part in range(3)),
                [probs[slot, t, 2 * pair], probs[slot, t, 2 * pair + 1]],
                att[slot, t, :, cols],
                inv[slot, t, :, cols],
                datt[slot, t, :, cols],
                low,
                high,
            )

        def finish(n, results):
            t, pair = n // 2, n % 2
            rows = pl.ds(pl.multiple_of((first + t) * TILE, TILE), TILE)
            for part, value in enumerate(results):
                at = pl.multiple_of(there + part * GROUP + pair * BLOCK, BLOCK)
                dqkv[rows, pl.ds(at, BLOCK)] = value

        staggered([maker(n // 2, n % 2) for n in range(2 * TILES)], finish)

        pl.when(step == 0)(lambda: total.after_core(0))
        pl.when(step == 2)(lambda: total.after_one(0))

        @pl.when(step == 3)
        def _():
            take_unit(0)
            send_unit(0)
            total_last.after_one(0)

        pl.when(step == steps - 2)(lambda: total.after_core(1))

        @pl.when(step == steps - 1)
        def _():
            total.after_one(1)
            total.after_core(2)

        @pl.when(m == micros - 1)
        def _():
            grad = dot(hid_t[...], dqkv[:, pl.ds(there, span)])
            sums[g] = grad[width : width + 8]
            put_unit(1 + g, grad[:width].astype(BF))

        pl.when(step == steps - 2)(take_last)

        @pl.when(step == GROUPS - 1)
        def _():
            pltpu.make_async_copy(w, w, w_sem).wait()

        @pl.when(g == GROUPS - 1)
        def _():
            extra[m] = input_grad(m, OWN, TILE).astype(BF)

            @pl.when(is_image)
            def _():
                mine[m] = t_dot(places_ref[m], extra[m]).astype(BF)
                for s in range(3):

                    @pl.when(own_z == s)
                    def _():
                        row_copy(m, s).start()

    for row, at in ((2, 0), (3, 2 * GROUP)):
        cols = [sums[g, 0:1, at : at + GROUP] for g in range(GROUPS)]
        add_vec(row, jnp.concatenate(cols, axis=1))

    peers = [lax.rem(total.me + k, 8) for k in range(1, 8)]

    def vec_copy(peer):
        return pltpu.make_async_remote_copy(
            src_ref=vec.at[peer],
            dst_ref=got_vec.at[total.me],
            send_sem=vec_sems.at[0, peer],
            recv_sem=vec_sems.at[1, total.me],
            device_id={"dp": peer},
            device_id_type=MESH,
        )

    def vec_arrival(peer):
        return pltpu.make_async_remote_copy(
            src_ref=got_vec.at[peer],
            dst_ref=got_vec.at[peer],
            send_sem=vec_sems.at[0, peer],
            recv_sem=vec_sems.at[1, peer],
            device_id={"dp": peer},
            device_id_type=MESH,
        )

    def zvec_copy(t):
        return pltpu.make_async_remote_copy(
            src_ref=own_vec,
            dst_ref=z_vec.at[own_z],
            send_sem=zvec_send.at[t],
            recv_sem=zvec_recv.at[own_z],
            device_id={"stream": t},
            device_id_type=MESH,
        )

    def zvec_arrival(s):
        return pltpu.make_async_remote_copy(
            src_ref=z_vec.at[s],
            dst_ref=z_vec.at[s],
            send_sem=zvec_send.at[s],
            recv_sem=zvec_recv.at[s],
            device_id={"stream": s},
            device_id_type=MESH,
        )

    rows_all = TILES * OWN

    def dx_copy(m):
        rows = pl.ds(m * rows_all, rows_all)
        return pltpu.make_async_copy(dx.at[rows], dx_ref.at[rows], dx_sems.at[m])

    def deliver(m, scattered):
        rows = pl.ds(m * rows_all, rows_all)
        value = base[rows]
        if scattered:
            value = value + t_dot(
                picks_ref[m], jnp.concatenate([got_rows[m, s] for s in range(3)] + [extra[m]], axis=0)
            )
        dx[rows] = value.astype(BF)
        dx_copy(m).start()

    def own_part(m):
        own = pl.ds(m * rows_all, rows_all)
        base[own] += input_grad(m, 0, OWN)

    def end_rows(m):
        pl.when(is_image)(lambda: deliver(m, False))

        @pl.when(is_text)
        def _():
            for s in range(3):
                row_copy(m, s).wait_recv()
            deliver(m, True)

    take_unit(1)
    send_unit(1)
    total.after_core(0)
    for m in range(micros - 1):
        own_part(m)
    total.after_one(2)
    for m in range(micros - 1):
        end_rows(m)
    total.after_one(0)
    own_part(micros - 1)
    for peer in peers:
        vec_copy(peer).start()
    take_unit(2)
    send_unit(2)
    take_unit(3)
    send_unit(3)
    for peer in peers:
        vec_arrival(peer).wait_recv()
        vec_copy(peer).wait_send()
    own_vec[...] = vec[total.me] + sum(got_vec[peer] for peer in peers)
    for t in range(4):
        pl.when(own_z != t)(lambda: zvec_copy(t).start())

        @pl.when(own_z == t)
        def _():
            z_vec[t] = own_vec[...]

    end_rows(micros - 1)

    @pl.when(is_text)
    def _():
        for s in range(3):
            last_row_copy(s).wait_send()

    @pl.when(is_image)
    def _():
        for m in range(micros):
            row_copy(m, 0).wait_send()

    for src in range(4):

        @pl.when(own_z != src)
        def _():
            for which in range(4):
                expert_arrival(src, which).wait_recv()
                expert_copy(src, which).wait_send()

        @pl.when(own_z == src)
        def _():
            for which in range(4):
                ref, dst = expert_ends(which, src, src)
                pltpu.make_async_copy(ref, dst, expert_send.at[src, which]).wait()

    for src in range(4):

        @pl.when(own_z != src)
        def _():
            zvec_arrival(src).wait_recv()
            zvec_copy(src).wait_send()
            for unit in range(GROUPS + 1):
                for n, place in unit_sends(unit, src):
                    block_copy(unit, n, src, place).wait_send()
            for kind, dst in ((0, got_out), (1, got_qkv)):
                for place in range(dst.shape[1]):
                    pltpu.make_async_remote_copy(
                        src_ref=dst.at[src, place],
                        dst_ref=dst.at[src, place],
                        send_sem=block_send.at[kind, src, place],
                        recv_sem=block_recv.at[kind, src, place],
                        device_id={"stream": src},
                        device_id_type=MESH,
                    ).wait_recv()

        @pl.when(own_z == src)
        def _():
            for unit in range(GROUPS + 1):
                for n, place in unit_sends(unit, src):
                    own_block_copy(unit, n, src, place).wait()

    sums_ref[...] = sum(z_vec[s] for s in range(4))
    for m in range(micros):
        dx_copy(m).wait()


def back(
    x_tiles,
    qkv,
    probs,
    att,
    inv,
    datt,
    dmid,
    vecs,
    w_qkv,
    dwout,
    zup,
    zdown,
    dup_last,
    ddown_last,
    rows_last,
    vec2,
    picks,
    places,
):
    tiles, _, width = x_tiles.shape
    micros = tiles // TILES
    shard = width // 8
    half = width // 2

    def sds(*shape, dtype=F32):
        return jax.ShapeDtypeStruct(shape, dtype)

    dma = pltpu.SemaphoreType.DMA
    return pl.pallas_call(
        back_kernel,
        in_specs=[HBM] * 7 + [FULL, HBM, FULL] + [HBM] * 5 + [FULL] * 3,
        out_specs=[HBM, FULL] + [HBM] * 4,
        out_shape=[
            sds(tiles * OWN, width, dtype=BF),
            sds(8, BLOCK),
            sds(4, 5, shard, BLOCK, dtype=BF),
            sds(4, 2, shard, BLOCK, dtype=BF),
            sds(4, STEPS - 1, *zup.shape[1:], dtype=BF),
            sds(4, STEPS - 1, *zdown.shape[1:], dtype=BF),
        ],
        scratch_shapes=[
            pltpu.VMEM((2, TILES, TILE, 3 * GROUP), BF),
            pltpu.VMEM((tiles, TILE, width), BF),
            pltpu.VMEM((2, TILES, TILE, GROUP), BF),
            pltpu.VMEM((2, TILES, TILE, GROUP), BF),
            pltpu.VMEM((2, TILES, TILE, GROUP), BF),
            pltpu.VMEM((tiles * OWN, width), F32),
            pltpu.VMEM((2, TILES, 4, TILE, TILE), BF),
            pltpu.VMEM((TILES * (TILE - OWN), width), BF),
            pltpu.VMEM((2 * SLOT, width), BF),
            pltpu.VMEM((1,) + dup_last.shape, BF),
            pltpu.VMEM((1,) + ddown_last.shape, BF),
            pltpu.VMEM((1, 2, 2) + dup_last.shape[3:], BF),
            pltpu.VMEM((1, 2, 2) + ddown_last.shape[3:], BF),
            pltpu.VMEM((1, 2) + dup_last.shape[3:], BF),
            pltpu.VMEM((1, 2) + ddown_last.shape[3:], BF),
            pltpu.VMEM((1,) + dup_last.shape[3:], BF),
            pltpu.VMEM((1,) + ddown_last.shape[3:], BF),
            pltpu.VMEM(zup.shape, BF),
            pltpu.VMEM(zdown.shape, BF),
            pltpu.VMEM((width + 16, tiles * TILE), BF),
            pltpu.VMEM((tiles * TILE, 3 * width), BF),
            pltpu.VMEM((width, 3 * width), BF),
            pltpu.VMEM((GROUPS, 8, 3 * GROUP), F32),
            pltpu.VMEM((micros, TILES * (TILE - OWN), width), BF),
            pltpu.VMEM((micros, 2 * SLOT, width), BF),
            pltpu.VMEM((micros, 3, 2 * SLOT, width), BF),
            pltpu.VMEM((SLOTS, 2, 2, 2, shard, half), BF),
            pltpu.VMEM((SLOTS, 2, 2, 2, shard, half), BF),
            pltpu.VMEM((SLOTS, 2, 2, shard, half), BF),
            pltpu.VMEM((SLOTS, 2, 2, shard, half), BF),
            pltpu.VMEM((SLOTS, 2, shard, half), BF),
            pltpu.VMEM((SLOTS, 2, shard, half), BF),
            pltpu.VMEM((SLOTS, shard, half), BF),
            pltpu.VMEM((SLOTS, shard, half), BF),
            pltpu.VMEM((GROUPS + 1, 6, shard, BLOCK), BF),
            pltpu.VMEM((tiles * OWN, width), BF),
            pltpu.VMEM((8, 8, BLOCK), F32),
            pltpu.VMEM((8, 8, BLOCK), F32),
            pltpu.VMEM((8, BLOCK), F32),
            pltpu.VMEM((4, 8, BLOCK), F32),
            dma((2, 7)),
            dma((micros, 2)),
            dma,
            dma((2,)),
            dma((3,)),
            dma,
            dma((3, 2, 2, 1)),
            dma((3, 2, 2, SLOTS)),
            dma((micros,)),
            dma((micros, 3)),
            dma((2, 8)),
            dma((4,)),
            dma((4,)),
            dma((4, 4)),
            dma((4, 4)),
            dma((2, 4, 5)),
            dma((2, 4, 5)),
            dma((micros,)),
        ],
        compiler_params=pltpu.CompilerParams(
            vmem_limit_bytes=63 * 2**20, collective_id=2, has_side_effects=True
        ),
        name="back",
    )(
        x_tiles,
        qkv,
        probs,
        att,
        inv,
        datt,
        dmid,
        vecs,
        w_qkv,
        dwout,
        zup,
        zdown,
        dup_last,
        ddown_last,
        rows_last,
        vec2,
        picks,
        places,
    )


def results_kernel(
    out_hbm,
    dx_hbm,
    qkv_hbm,
    o_hbm,
    up_hbm,
    down_hbm,
    first_up_hbm,
    first_down_hbm,
    out_rows_hbm,
    dx_rows_hbm,
    dqkv_ref,
    dout_ref,
    dvup_ref,
    dvdown_ref,
    dtup_ref,
    dtdown_ref,
    out_ref,
    dx_ref,
    got_qkv,
    got_out,
    got_up,
    got_down,
    first_up,
    first_down,
    out_rows,
    dx_rows,
    sems,
):
    _, micros, width = out_rows.shape
    ins = (
        (out_hbm, out_ref),
        (dx_hbm, dx_ref),
        (up_hbm, got_up),
        (down_hbm, got_down),
        (first_up_hbm, first_up),
        (first_down_hbm, first_down),
        (qkv_hbm, got_qkv),
        (o_hbm, got_out),
    )
    loads = [pltpu.make_async_copy(src, dst, sems.at[n]) for n, (src, dst) in enumerate(ins)]
    outs = ((out_rows, out_rows_hbm), (dx_rows, dx_rows_hbm))
    stores = [pltpu.make_async_copy(src, dst, sems.at[len(ins) + n]) for n, (src, dst) in enumerate(outs)]
    for load in loads:
        load.start()
    unpad = padding(micros, True)
    for n, (src, dst) in enumerate(((out_ref, out_rows), (dx_ref, dx_rows))):
        loads[n].wait()
        for t in range(TILES):
            tiles = [src[(m * TILES + t) * OWN : (m * TILES + t + 1) * OWN] for m in range(micros)]
            rows = dot(unpad, jnp.concatenate(tiles, axis=0)).astype(BF)
            dst[t * PATCHES : (t + 1) * PATCHES] = rows.reshape(PATCHES, micros, width)
        stores[n].start()

    for load in loads[2:]:
        load.wait()
    ff_piece = got_down.shape[3]
    for j in range(STEPS):
        ups = [(first_up[s] if j == 0 else got_up[s, j - 1]).astype(F32) for s in range(4)]
        downs = [(first_down[s] if j == 0 else got_down[s, j - 1]).astype(F32) for s in range(4)]
        vis, txt = sum(ups[:3]), ups[3]
        for d in range(2):
            at = (d * STEPS + j) * ff_piece
            dvup_ref[:, at : at + ff_piece] = vis[:, d * ff_piece : (d + 1) * ff_piece]
            dtup_ref[:, at : at + ff_piece] = txt[:, d * ff_piece : (d + 1) * ff_piece]
        at = j * ff_piece
        dvdown_ref[:, at : at + ff_piece] = sum(downs[:3])
        dtdown_ref[:, at : at + ff_piece] = downs[3]

    odd = lax.rem(lax.axis_index("stream"), 2) == 1
    for got, out in ((got_qkv, dqkv_ref), (got_out, dout_ref)):
        blocks = [sum(got[s, n].astype(F32) for s in range(4)) for n in range(got.shape[1])]
        whole = jnp.concatenate(blocks, axis=1)
        moved = pltpu.roll(whole, whole.shape[1] - BLOCK // 2, 1)
        out[...] = jnp.where(odd, moved, whole)[:, : out.shape[1]]
    for store in stores:
        store.wait()


def results(micros, out, dx, got_qkv, got_out, got_up, got_down, first_up, first_down):
    arrays = out, dx, got_qkv, got_out, got_up, got_down, first_up, first_down
    width = out.shape[1]
    shard = got_up.shape[2]
    ff = 8 * STEPS * got_down.shape[3]
    rows = jax.ShapeDtypeStruct((TILES * PATCHES, micros, width), BF)
    grads = [
        (shard, 3 * width // 4),
        (shard, width // 4),
        (shard, ff // 4),
        (width // 4, ff // 8),
        (shard, ff // 4),
        (width // 4, ff // 8),
    ]
    return pl.pallas_call(
        results_kernel,
        in_specs=[HBM] * 8,
        out_specs=[HBM] * 2 + [FULL] * 6,
        out_shape=[rows, rows] + [jax.ShapeDtypeStruct(shape, F32) for shape in grads],
        scratch_shapes=[
            pltpu.VMEM(array.shape, BF) for array in arrays
        ]
        + [pltpu.VMEM(rows.shape, BF)] * 2
        + [pltpu.SemaphoreType.DMA((10,))],
        compiler_params=pltpu.CompilerParams(vmem_limit_bytes=63 * 2**20),
        name="results",
    )(*arrays)


def pad_rows(block):
    micro, rows, width = block.shape
    thirds = block.reshape(micro, TILES, PATCHES, width)
    thirds = jnp.pad(thirds, ((0, 0), (0, 0), (0, OWN - PATCHES), (0, 0)))
    return thirds.reshape(micro, TILES * OWN, width)


def unpad_rows(block):
    micro, _, width = block.shape
    thirds = block.reshape(micro, TILES, OWN, width)[:, :, :PATCHES]
    return thirds.reshape(micro, TILES * PATCHES, width)


def plan(lengths, pairs, is_text, own_stream):
    micro, items = lengths.shape
    finish = jnp.cumsum(lengths, axis=1)
    starts = finish - lengths
    numbers = jnp.arange(items, dtype=jnp.int32)
    match = pairs[:, :, None] == numbers
    start = jnp.sum(jnp.where(match, starts[:, None, :], 0), axis=2).reshape(micro, 3, TILES)
    length = jnp.sum(jnp.where(match, lengths[:, None, :], 0), axis=2).reshape(micro, 3, TILES)
    paired = (pairs >= 0).reshape(micro, 3, TILES)
    rank = jnp.where(paired, jnp.cumsum(paired.astype(jnp.int32), axis=2) - 1, -1)
    takes = rank[:, :, :, None] == jnp.arange(2)
    slot_start = jnp.sum(jnp.where(takes, start[..., None], 0), axis=2)
    slot_length = jnp.sum(jnp.where(takes, length[..., None], 0), axis=2)
    step = jnp.arange(SLOT, dtype=jnp.int32)
    slot_rows = jnp.where(step < slot_length[..., None], slot_start[..., None] + step, -1)
    pad = jnp.arange(TILE - OWN, dtype=jnp.int32)
    next_rows = PATCHES * jnp.arange(1, TILES + 1, dtype=jnp.int32)[:, None] + pad
    next_rows = jnp.where((pad < SLOT) & (next_rows < TILES * PATCHES), next_rows, -1)
    next_rows = jnp.broadcast_to(next_rows, (micro, TILES, TILE - OWN))
    wanted = jnp.concatenate([slot_rows.reshape(micro, -1), next_rows.reshape(micro, -1)], axis=1)
    place = jnp.arange(TILES * OWN, dtype=jnp.int32)
    row_at = jnp.where(place % OWN < PATCHES, place // OWN * PATCHES + place % OWN, -2)
    picks = (wanted[:, :, None] == row_at).astype(BF)
    item_paired = jnp.any(match, axis=1)
    rows = jnp.arange(TILES * PATCHES + SLOT, dtype=jnp.int32)
    member = (rows[:, None] >= starts[:, None, :]) & (rows[:, None] < finish[:, None, :])
    code = jnp.where(item_paired, -1, numbers + items * (starts // PATCHES))
    row_code = jnp.sum(jnp.where(member, code[:, None, :] + 1, 0), axis=2) - 1
    tile = jnp.arange(TILES, dtype=jnp.int32)[:, None]
    own_code = row_code[:, : TILES * PATCHES].reshape(micro, TILES, PATCHES)
    next_code = jnp.stack(
        [row_code[:, PATCHES * (t + 1) : PATCHES * (t + 1) + SLOT] for t in range(TILES)], axis=1
    )

    def here(codes):
        return jnp.where((codes >= 0) & (codes // items == tile), codes, -1)

    def lay(own, extra):
        gap = jnp.full((micro, TILES, OWN - PATCHES), -1, jnp.int32)
        end = jnp.full((micro, TILES, TILE - OWN - SLOT), -1, jnp.int32)
        return jnp.concatenate([own, gap, extra, end], axis=2)

    text_ids = lay(here(own_code), here(next_code))
    own_length = lax.dynamic_index_in_dim(length, jnp.minimum(own_stream, 2), 1, keepdims=False)
    own_takes = lax.dynamic_index_in_dim(takes, jnp.minimum(own_stream, 2), 1, keepdims=False)
    image_ids = lay(
        jnp.zeros((micro, TILES, PATCHES), jnp.int32),
        jnp.where(step < own_length[..., None], 0, -1),
    )
    ids = jnp.where(is_text, text_ids, image_ids)
    own_takes = own_takes.astype(BF)
    same = (pad[:, None] == step).astype(BF)
    places = own_takes[:, :, None, :, None] * same[:, None, :]
    places = places.reshape(micro, TILES * (TILE - OWN), 2 * SLOT)
    return picks, places, own_takes, ids.reshape(micro * TILES, 1, TILE)


def plan_kernel(length_ref, pair_ref, *refs):
    vec_refs, (picks_ref, places_ref, ids_ref, vecs_ref, starts, codes) = refs[:8], refs[8:]
    for n, ref in enumerate(vec_refs):
        rows = ref.shape[0] // BLOCK
        vecs_ref[n * rows : (n + 1) * rows] = ref[...].astype(F32).reshape(rows, BLOCK)
    micros, items = length_ref.shape
    own_z = lax.axis_index("stream")
    is_text = own_z == 3
    block = jnp.minimum(own_z, 2)
    side = TILE - OWN
    place = lax.broadcasted_iota(jnp.int32, (1, TILES * OWN), 1)
    third = third_of(place, OWN)
    inside = place - OWN * third
    row_at = jnp.where(inside < PATCHES, PATCHES * third + inside, -2)
    lane = lax.broadcasted_iota(jnp.int32, (1, TILE), 1)
    far = lax.broadcasted_iota(jnp.int32, (6 * SLOT, 1), 0)
    near = lax.broadcasted_iota(jnp.int32, (TILES * side, 1), 0)
    near_tile = third_of(near, side)
    near_step = near - side * near_tile
    near_row = PATCHES * (near_tile + 1) + near_step
    near_row = jnp.where((near_step < SLOT) & (near_row < TILES * PATCHES), near_row, -1)
    slot_at = lax.broadcasted_iota(jnp.int32, (1, 2 * SLOT), 1)
    slot_of = (slot_at >= SLOT).astype(jnp.int32)
    slot_step = slot_at - SLOT * slot_of
    for m in range(micros):
        start = jnp.int32(0)
        for item in range(items):
            starts[m, item] = start
            codes[m, item] = item + items * third_of(start, PATCHES)
            start = start + length_ref[m, item]

        def pair_of(image):
            item = pair_ref[m, image]
            known = jnp.maximum(item, 0)
            paired = item >= 0
            return paired, starts[m, known], jnp.where(paired, length_ref[m, known], 0)

        wanted = jnp.full(far.shape, -1, jnp.int32)
        for s in range(3):
            rank = jnp.int32(0)
            for t in range(TILES):
                paired, start, length = pair_of(TILES * s + t)
                step = far - SLOT * (2 * s + rank)
                wanted = jnp.where((step >= 0) & (step < length), start + step, wanted)
                rank = rank + paired.astype(jnp.int32)
        picks_ref[m, 0 : 6 * SLOT] = (wanted == row_at).astype(F32).astype(BF)
        picks_ref[m, 6 * SLOT :] = (near_row == row_at).astype(F32).astype(BF)

        rank = jnp.int32(0)
        ranks = jnp.full(near.shape, -1, jnp.int32)
        lengths = []
        for t in range(TILES):
            paired, _, length = pair_of(TILES * block + t)
            lengths.append(length)
            ranks = jnp.where((near_tile == t) & paired, rank, ranks)
            rank = rank + paired.astype(jnp.int32)
        chosen = (near_step == slot_step) & (ranks == slot_of)
        places_ref[m] = chosen.astype(F32).astype(BF)

        for image in range(3 * TILES):

            @pl.when(pair_ref[m, image] >= 0)
            def _():
                codes[m, pair_ref[m, image]] = -1

        for t in range(TILES):
            beside = lane - OWN
            image_ids = jnp.where((lane < PATCHES) | ((beside >= 0) & (beside < lengths[t])), 0, -1)
            row = jnp.where(lane < PATCHES, PATCHES * t + lane, -1)
            row = jnp.where((beside >= 0) & (beside < SLOT), PATCHES * (t + 1) + beside, row)
            text_ids = jnp.full(lane.shape, -1, jnp.int32)
            for item in range(items):
                start, code = starts[m, item], codes[m, item]
                code = jnp.where(third_of(start, PATCHES) == t, code, -1)
                member = (row >= start) & (row < start + length_ref[m, item])
                text_ids = jnp.where(member, code, text_ids)
            ids_ref[m * TILES + t] = jnp.where(is_text, text_ids, image_ids)


def plan_rows(lengths, pairs, vectors):
    micros, items = lengths.shape
    smem = pl.BlockSpec(memory_space=pltpu.SMEM)
    return pl.pallas_call(
        plan_kernel,
        in_specs=[smem, smem] + [FULL] * 8,
        out_specs=[FULL] * 4,
        out_shape=[
            jax.ShapeDtypeStruct((micros, 6 * SLOT + TILES * (TILE - OWN), TILES * OWN), BF),
            jax.ShapeDtypeStruct((micros, TILES * (TILE - OWN), 2 * SLOT), BF),
            jax.ShapeDtypeStruct((micros * TILES, 1, TILE), jnp.int32),
            jax.ShapeDtypeStruct((8 * vectors[0].shape[0] // BLOCK, BLOCK), F32),
        ],
        scratch_shapes=[
            pltpu.SMEM((micros, items), jnp.int32),
            pltpu.SMEM((micros, items), jnp.int32),
        ],
        compiler_params=pltpu.CompilerParams(vmem_limit_bytes=63 * 2**20),
        name="plan_rows",
    )(lengths, pairs, *vectors)


def spread(padded, picks, own_takes, is_text):
    micro, _, width = padded.shape
    picked = lax.dot_general(
        picks, padded, (((2,), (1,)), ((0,), (0,))), preferred_element_type=F32
    ).astype(BF)
    near = picked[:, 6 * SLOT :].reshape(micro, TILES, TILE - OWN, width)[:, :, :SLOT]
    sent = picked[:, : 6 * SLOT].reshape(micro, 3, 2 * SLOT, width)
    far = sum(lax.ppermute(sent[:, s], "stream", [(3, s)]) for s in range(3))
    far = far.reshape(micro, 1, 2, SLOT, width) * own_takes[:, :, :, None, None]
    return jnp.where(is_text, near, far[:, :, 0] + far[:, :, 1])


def collect(extra, picks, own_takes, is_text):
    micro, _, _, width = extra.shape
    mine = extra[:, :, None] * own_takes[:, :, :, None, None]
    mine = (mine[:, 0] + mine[:, 1] + mine[:, 2]).reshape(micro, 2 * SLOT, width)
    parts = [lax.ppermute(mine, "stream", [(s, 3)]) for s in range(3)]
    extra = jnp.pad(extra, ((0, 0), (0, 0), (0, TILE - OWN - SLOT), (0, 0)))
    parts.append(extra.reshape(micro, TILES * (TILE - OWN), width))
    rows = jnp.concatenate(parts, axis=1)
    scale = jnp.where(is_text, 1.0, 0.0).astype(BF)
    return lax.dot_general(
        picks * scale, rows, (((1,), (1,)), ((0,), (0,))), preferred_element_type=F32
    ).astype(BF)


def reduce_all(vectors, dw_qkv, dw_out, dup, ddown):
    width = dw_qkv.shape[0]
    shard = width // lax.axis_size("dp")
    vectors = lax.psum(vectors, ("dp", "stream"))
    vectors = lax.dynamic_slice_in_dim(vectors, lax.axis_index("dp") * shard, shard, axis=1)

    def over_items(grad, dim):
        return lax.psum_scatter(grad, "dp", scatter_dimension=dim, tiled=True)

    def over_blocks(grad):
        return lax.psum_scatter(grad, "stream", scatter_dimension=1, tiled=True).astype(F32)

    qkv = over_blocks(over_items(dw_qkv, 0))
    out = over_blocks(over_items(dw_out, 0))
    dup = over_items(jnp.concatenate(list(dup), axis=1), 0)
    ddown = over_items(jnp.concatenate(list(ddown), axis=1), 1)
    up = dup.reshape(dup.shape[0], 4, -1).transpose(1, 0, 2)
    down = ddown.reshape(4, -1, ddown.shape[1])
    up = lax.all_to_all(up, "stream", 0, 0).astype(F32)
    down = lax.all_to_all(down, "stream", 0, 0).astype(F32)
    return (
        vectors,
        qkv,
        out,
        up[0] + up[1] + up[2],
        (down[0] + down[1] + down[2]).T,
        up[3],
        down[3].T,
    )


def shards(
    remote,
    tokens,
    text_lengths,
    pair_text,
    ln1_gain,
    ln1_bias,
    w_qkv,
    q_bias,
    v_bias,
    w_out,
    ln2_gain,
    ln2_bias,
    vis_up,
    vis_down,
    vis_bias,
    txt_up,
    txt_down,
    txt_bias,
    cotangent,
):
    micro = tokens.shape[0]
    width = tokens.shape[4]
    own_stream = lax.axis_index("stream")
    is_text = own_stream == 3
    vecs = [ln1_gain, ln1_bias, q_bias, v_bias, ln2_gain, ln2_bias, vis_bias, txt_bias]
    if remote:
        picks, places, ids, vecs = plan_rows(text_lengths[:, 0], pair_text[:, 0], vecs)
    else:
        vecs = jnp.concatenate(vecs).astype(F32).reshape(-1, BLOCK)
        picks, places, own_takes, ids = plan(
            text_lengths[:, 0], pair_text[:, 0], is_text, own_stream
        )

    def tiled(own, extra):
        own = own.reshape(micro, TILES, OWN, width)
        extra = jnp.pad(extra, ((0, 0), (0, 0), (0, TILE - OWN - SLOT), (0, 0)))
        return jnp.concatenate([own, extra], axis=2).reshape(micro * TILES, TILE, width)

    def parted(tiles):
        tiles = tiles.reshape(micro, TILES, TILE, width)
        return tiles[:, :, :OWN].reshape(micro, TILES * OWN, width), tiles[:, :, OWN : OWN + SLOT]

    if remote:
        x_tiles, qkv, probs, inverse, att_tiles, att, att_last = attend_rows(
            tokens[:, 0, 0].transpose(1, 0, 2), picks, places, ids, vecs, w_qkv
        )
    else:
        x = pad_rows(tokens[:, 0, 0])
        x_tiles = tiled(x, spread(x, picks, own_takes, is_text))
        qkv, att_tiles, probs, inverse = attend(x_tiles, ids, vecs, w_qkv)
        att_own, att_extra = parted(att_tiles)
        att = att_own + collect(att_extra, picks, own_takes, is_text)
        att = att.reshape(micro * TILES * OWN, width)
        att_last = jnp.zeros((2 * SLOT, width), BF)
    out, dmid, datt_tiles, dw_out, vec2, dup, ddown, *more = expert(
        remote,
        x_tiles,
        att,
        att_tiles,
        att_last,
        cotangent[:, 0, 0].transpose(1, 0, 2),
        w_out,
        vecs,
        picks,
        places,
        vis_up,
        vis_down,
        txt_up,
        txt_down,
    )
    if remote:
        dx, vectors, *shares = back(
            x_tiles,
            qkv,
            probs,
            att_tiles,
            inverse,
            datt_tiles,
            dmid,
            vecs,
            w_qkv,
            dw_out,
            dup,
            ddown,
            *more[:3],
            vec2,
            picks,
            places,
        )
        vectors = vectors[:, : width // 8]
        out, dx, g_qkv, g_out, g_vup, g_vdown, g_tup, g_tdown = results(
            micro, out, dx, *shares, *more[3:]
        )
        out, dx = out.transpose(1, 0, 2), dx.transpose(1, 0, 2)
        g_vdown, g_tdown = g_vdown.T, g_tdown.T
    else:
        datt = parted(datt_tiles)[0]
        datt_tiles = tiled(datt, spread(datt, picks, own_takes, is_text))
        dqkv = attend_back(qkv, probs, att_tiles, inverse, datt_tiles)
        dx_tiles, dw_qkv, vec1 = project_back(x_tiles, dqkv, vecs, w_qkv)
        dx_own, dx_extra = parted(dx_tiles)
        dx = (
            dmid.reshape(micro, TILES * OWN, width)
            + dx_own.astype(F32)
            + collect(dx_extra, picks, own_takes, is_text).astype(F32)
        )
        dx = unpad_rows(dx).astype(BF)
        out = unpad_rows(out.reshape(micro, TILES * OWN, width))
        text_scale = jnp.where(is_text, 1.0, 0.0)
        vectors = jnp.concatenate(
            [vec1[0:4], vec2[0:2], vec2[2:3] * (1.0 - text_scale), vec2[2:3] * text_scale], axis=0
        )
        vectors, g_qkv, g_out, g_vup, g_vdown, g_tup, g_tdown = reduce_all(
            vectors, dw_qkv, dw_out, dup, ddown
        )
    return (
        out.reshape(tokens.shape),
        dx.reshape(tokens.shape),
        vectors[0],
        vectors[1],
        g_qkv,
        vectors[2],
        vectors[3],
        g_out,
        vectors[4],
        vectors[5],
        g_vup,
        g_vdown,
        vectors[6],
        g_tup,
        g_tdown,
        vectors[7],
    )


def solution(mesh):
    rows = P(None, "dp", "stream", None, None)
    lists = P(None, "dp", None)
    vector, matrix = P("dp"), P("dp", "stream")
    in_specs = (rows, lists, lists) + (P(),) * 14 + (rows,)
    out_specs = (
        rows,
        rows,
        vector,
        vector,
        matrix,
        vector,
        vector,
        matrix,
        vector,
        vector,
        matrix,
        matrix,
        vector,
        matrix,
        matrix,
        vector,
    )
    remote = mesh.shape["dp"] == 8
    body = functools.partial(shards, remote)
    return jax.shard_map(body, mesh=mesh, in_specs=in_specs, out_specs=out_specs, check_vma=False)
```

```python
import functools

import jax
import jax.numpy as jnp
from jax import lax
from jax.experimental import pallas as pl
from jax.experimental.pallas import tpu as pltpu
from jax.sharding import PartitionSpec as P

HEADS = 12
PATCHES = 197
OWN = 208
SLOT = 40
TILE = 256
TILES = 3
EPSILON = 1e-06
MASKED = -1e30
BF = jnp.bfloat16
F32 = jnp.float32
FULL = pl.BlockSpec(memory_space=pltpu.VMEM)
HBM = pl.BlockSpec(memory_space=pl.ANY)
MESH = pl.DeviceIdType.MESH
BLOCK = 128


def dot(left, right):
    return jnp.dot(left, right, preferred_element_type=F32)


def dot_t(left, right):
    return lax.dot_general(left, right, (((1,), (1,)), ((), ())), preferred_element_type=F32)


def t_dot(left, right):
    return lax.dot_general(left, right, (((0,), (0,)), ((), ())), preferred_element_type=F32)


def normalize(values):
    centred = values - jnp.mean(values, axis=-1, keepdims=True)
    inverse = lax.rsqrt(jnp.mean(centred * centred, axis=-1, keepdims=True) + EPSILON)
    return centred * inverse, inverse


def norm_back(grad, normed, inverse, gain):
    scaled = grad * gain
    return inverse * (
        scaled
        - jnp.mean(scaled, axis=-1, keepdims=True)
        - normed * jnp.mean(scaled * normed, axis=-1, keepdims=True)
    )


def gelu_parts(up):
    rise = 1.0 + 0.2316418882663604 * jnp.abs(up)
    inner = 1.0 / rise
    bell = jnp.exp2(up * up * -0.7213475204444817)
    poly = inner * (
        0.127414796
        + inner
        * (-0.142248368 + inner * (0.7107068705 + inner * (-0.7265760135 + inner * 0.5307027145)))
    )
    tail = poly * bell
    return jnp.where(up >= 0, 1.0 - tail, tail), bell * 0.3989422804014327


def halves(block, low, high):
    return jnp.concatenate([block * low, block * high], axis=0)


def pair_lanes():
    lane = lax.broadcasted_iota(jnp.int32, (1, 128), 1)
    return (lane < 64).astype(BF), (lane >= 64).astype(BF)


def attend_pair(q, k, v, barred, low, high):
    scores = dot_t(halves(k, low, high), q * 0.125)
    yield
    expos = []
    for side in range(2):
        part = scores[TILE * side : TILE * (side + 1)] + barred
        top = jnp.maximum(jnp.max(part, axis=0, keepdims=True), 0.1 * MASKED)
        expos.append(jnp.exp(part - top).astype(BF))
    ones = [jnp.broadcast_to(keep, (TILE, 128)) for keep in (low, high)]
    right = jnp.concatenate([halves(v, low, high), jnp.concatenate(ones, axis=0)], axis=1)
    sums = t_dot(jnp.concatenate(expos, axis=0), right)
    inverse = jnp.where(sums[:, 128:] > 0.0, 1.0 / sums[:, 128:], 0.0)
    yield expos, sums[:, :128] * inverse, inverse


def attend_back_pair(q, k, v, expos, out, inverse, grad, low, high):
    scaled = grad.astype(F32) * inverse.astype(F32)
    inner = (scaled * out.astype(F32)).astype(BF)
    scaled = scaled.astype(BF)
    minus = [jnp.broadcast_to(-keep, (TILE, 128)) for keep in (low, high)]
    right = jnp.concatenate([halves(v, low, high), jnp.concatenate(minus, axis=0)], axis=1)
    slopes = dot_t(right, jnp.concatenate([scaled, inner], axis=1))
    yield
    parts = [
        (expos[side].astype(F32) * slopes[TILE * side : TILE * (side + 1)]).astype(BF)
        for side in range(2)
    ]
    dq = t_dot(jnp.concatenate(parts, axis=0), halves(k, low, high)) * 0.125
    dk = dot(jnp.concatenate(parts, axis=1), halves(q * 0.125, low, high))
    dv = dot(jnp.concatenate(expos, axis=1), halves(scaled, low, high))
    yield dq.astype(BF), dk.astype(BF), dv.astype(BF)


def staggered(makers, finish):
    held = None
    for n, make in enumerate(makers):
        step = make()
        next(step)
        if held is not None:
            finish(n - 1, next(held))
        held = step
    finish(len(makers) - 1, next(held))


def bars(ids_ref):
    ids = jnp.broadcast_to(ids_ref, (TILE, TILE))
    return jnp.where((ids == ids.T) & (ids >= 0), 0.0, MASKED)


GAIN1, SHIFT1, Q_BIAS, V_BIAS, GAIN2, SHIFT2, VIS_BIAS, TXT_BIAS = range(8)


def row_of(vecs_ref, at):
    rows = vecs_ref.shape[0] // 8
    return jnp.concatenate([vecs_ref[at * rows + n : at * rows + n + 1] for n in range(rows)], axis=1)


def project(values, vecs_ref, w_ref):
    normed, _ = normalize(values.astype(F32))
    hidden = (normed * row_of(vecs_ref, GAIN1) + row_of(vecs_ref, SHIFT1)).astype(BF)
    q_bias, v_bias = row_of(vecs_ref, Q_BIAS), row_of(vecs_ref, V_BIAS)
    bias = jnp.concatenate([q_bias, jnp.zeros_like(q_bias), v_bias], axis=1)
    return (dot(hidden, w_ref[...]) + bias).astype(BF)


def attend_kernel(x_ref, ids_ref, vecs_ref, w_ref, qkv_ref, out_ref, p_ref, inv_ref):
    width = x_ref.shape[2]
    qkv_ref[0] = project(x_ref[0], vecs_ref, w_ref)
    barred = bars(ids_ref[0])
    low, high = pair_lanes()

    def maker(pair):
        cols = [qkv_ref[0, :, part * width + pair * 128 :][:, :128] for part in range(3)]
        return lambda: attend_pair(*cols, barred, low, high)

    def finish(pair, results):
        expos, out, inverse = results
        at = pair * 128
        for side in range(2):
            p_ref[0, 2 * pair + side] = expos[side]
        out_ref[0, :, at : at + 128] = out.astype(BF)
        inv_ref[0, :, at : at + 128] = inverse.astype(BF)

    staggered([maker(pair) for pair in range(HEADS // 2)], finish)


def attend(x_tiles, ids, vecs, w_qkv):
    tiles, _, width = x_tiles.shape

    def block(*shape):
        return pl.BlockSpec((1,) + shape, lambda i: (i,) + (0,) * len(shape))

    return pl.pallas_call(
        attend_kernel,
        grid=(tiles,),
        in_specs=[block(TILE, width), block(1, TILE), FULL, FULL],
        out_specs=[
            block(TILE, 3 * width),
            block(TILE, width),
            block(HEADS, TILE, TILE),
            block(TILE, width),
        ],
        out_shape=[
            jax.ShapeDtypeStruct((tiles, TILE, 3 * width), BF),
            jax.ShapeDtypeStruct((tiles, TILE, width), BF),
            jax.ShapeDtypeStruct((tiles, HEADS, TILE, TILE), BF),
            jax.ShapeDtypeStruct((tiles, TILE, width), BF),
        ],
        compiler_params=pltpu.CompilerParams(vmem_limit_bytes=56 * 2**20),
        name="attend",
    )(x_tiles, ids, vecs, w_qkv)


def third_of(row, size):
    return (row >= size).astype(jnp.int32) + (row >= 2 * size).astype(jnp.int32)


def padding(micros, flip):
    count = micros * (OWN if flip else PATCHES)
    at = lax.broadcasted_iota(jnp.int32, (1, count), 1)
    rows = lax.broadcasted_iota(jnp.int32, (micros * (PATCHES if flip else OWN), 1), 0)
    if flip:
        wanted = lax.rem(rows, micros) * OWN + lax.div(rows, micros)
    else:
        micro = sum((rows >= m * OWN).astype(jnp.int32) for m in range(1, micros))
        row = rows - micro * OWN
        wanted = jnp.where(row < PATCHES, row * micros + micro, -1)
    return (wanted == at).astype(F32).astype(BF)


def pad_third(pad, third):
    rows, micros, width = third.shape
    return dot(pad, third.reshape(rows * micros, width)).astype(BF)


def attend_rows_kernel(
    tok_ref,
    picks_ref,
    places_ref,
    ids_ref,
    vecs_ref,
    w_hbm,
    x_out,
    qkv_out,
    p_out,
    inv_out,
    att_out,
    rows_out,
    mine_out,
    tok,
    w,
    x,
    qkv,
    probs,
    inv,
    att,
    rows_ref,
    sent,
    got,
    mine,
    got_back,
    tok_sems,
    w_sem,
    out_sems,
    p_sems,
    rows_sems,
    row_send,
    row_recv,
    back_send,
    back_recv,
):
    micros = tok.shape[1]
    width = tok.shape[2]
    own_z = lax.axis_index("stream")
    is_text = own_z == 3
    is_image = jnp.logical_not(is_text)
    side = TILE - OWN

    def tok_copy(t):
        at = pl.ds(t * PATCHES, PATCHES)
        return pltpu.make_async_copy(tok_ref.at[at], tok.at[at], tok_sems.at[t])

    for t in range(TILES):
        tok_copy(t).start()
    w_copy = pltpu.make_async_copy(w_hbm, w, w_sem)
    w_copy.start()
    meet([{"stream": lax.rem(own_z + k, 4)} for k in range(1, 4)])

    def row_copy(m, s):
        return pltpu.make_async_remote_copy(
            src_ref=sent.at[m, s],
            dst_ref=got.at[m],
            send_sem=row_send.at[m, s],
            recv_sem=row_recv.at[m],
            device_id={"stream": s},
            device_id_type=MESH,
        )

    def back_copy(m, s):
        return pltpu.make_async_remote_copy(
            src_ref=mine.at[m],
            dst_ref=got_back.at[m, s],
            send_sem=back_send.at[m],
            recv_sem=back_recv.at[m, s],
            device_id={"stream": 3},
            device_id_type=MESH,
        )

    def outs(m, which):
        at = pl.ds(m * TILES, TILES)
        pairs = ((x, x_out), (qkv, qkv_out), (inv, inv_out), (att, att_out))
        for n in which:
            src, dst = pairs[n]
            yield pltpu.make_async_copy(src.at[at], dst.at[at], out_sems.at[m, n])

    def rows_copy(m):
        at = pl.ds(m * TILES * OWN, TILES * OWN)
        return pltpu.make_async_copy(rows_ref.at[at], rows_out.at[at], rows_sems.at[m])

    mine_copy = pltpu.make_async_copy(mine.at[micros - 1], mine_out, rows_sems.at[micros])

    def probs_store(tile, slot):
        return pltpu.make_async_copy(probs.at[slot], p_out.at[tile], p_sems.at[slot])

    def own_rows(ref, m):
        return jnp.concatenate([ref[m * TILES + t, 0:OWN] for t in range(TILES)], axis=0)

    def beside(ref, m, value):
        for t in range(TILES):
            ref[m * TILES + t, OWN:TILE] = value[t * side : (t + 1) * side]

    pad = padding(micros, False)
    for t in range(TILES):
        tok_copy(t).wait()
        padded = pad_third(pad, tok[t * PATCHES : (t + 1) * PATCHES])
        for m in range(micros):
            x[m * TILES + t, 0:OWN] = padded[m * OWN : (m + 1) * OWN]
    for m in range(micros):

        @pl.when(is_text)
        def _():
            picked = dot(picks_ref[m], own_rows(x, m)).astype(BF)
            for s in range(3):
                sent[m, s] = picked[s * 2 * SLOT : (s + 1) * 2 * SLOT]
                row_copy(m, s).start()
            beside(x, m, picked[6 * SLOT :])

    w_copy.wait()
    for m in range(micros):
        rows = project(own_rows(x, m), vecs_ref, w)
        for t in range(TILES):
            qkv[m * TILES + t, 0:OWN] = rows[t * OWN : (t + 1) * OWN]

    low, high = pair_lanes()

    @pl.loop(0, micros)
    def _(m):
        @pl.when(is_image)
        def _():
            row_copy(m, 0).wait_recv()
            beside(x, m, dot(places_ref[m], got[m]).astype(BF))

        extra = [x[m * TILES + t, OWN:TILE] for t in range(TILES)]
        beside(qkv, m, project(jnp.concatenate(extra, axis=0), vecs_ref, w))
        for copy in outs(m, (0, 1)):
            copy.start()

        @pl.loop(0, TILES)
        def _(t):
            tile = m * TILES + t
            slot = lax.rem(tile, 2)
            pl.when(tile > 1)(lambda: probs_store(tile - 2, slot).wait())
            barred = bars(ids_ref[tile])

            def maker(pair):
                at = pair * BLOCK
                cols = [qkv[tile, :, pl.ds(part * width + at, BLOCK)] for part in range(3)]
                return lambda: attend_pair(*cols, barred, low, high)

            def finish(pair, results):
                expos, out, inverse = results
                at = pair * BLOCK
                for n in range(2):
                    probs[slot, 2 * pair + n] = expos[n]
                att[tile, :, at : at + BLOCK] = out.astype(BF)
                inv[tile, :, at : at + BLOCK] = inverse.astype(BF)

            staggered([maker(pair) for pair in range(HEADS // 2)], finish)
            probs_store(tile, slot).start()

        for copy in outs(m, (2, 3)):
            copy.start()
        at = pl.multiple_of(m * TILES * OWN, 16)
        rows_ref[pl.ds(at, TILES * OWN)] = own_rows(att, m)

        @pl.when(is_image)
        def _():
            extra = [att[m * TILES + t, OWN:TILE] for t in range(TILES)]
            mine[m] = t_dot(places_ref[m], jnp.concatenate(extra, axis=0)).astype(BF)
            for s in range(3):

                @pl.when((own_z == s) & (m < micros - 1))
                def _():
                    back_copy(m, s).start()

        @pl.when(m == micros - 1)
        def _():
            rows_copy(micros - 1).start()
            mine_copy.start()

    for m in range(micros - 1):

        @pl.when(is_text)
        def _():
            for s in range(3):
                back_copy(m, s).wait_recv()
            parts = [got_back[m, s] for s in range(3)]
            parts += [att[m * TILES + t, OWN:TILE] for t in range(TILES)]
            moved = t_dot(picks_ref[m], jnp.concatenate(parts, axis=0)).astype(BF)
            at = pl.ds(m * TILES * OWN, TILES * OWN)
            rows_ref[at] = (rows_ref[at].astype(F32) + moved.astype(F32)).astype(BF)

        rows_copy(m).start()
        pl.when(is_image)(lambda: back_copy(m, 0).wait_send())

    @pl.when(is_text)
    def _():
        for m in range(micros):
            for s in range(3):
                row_copy(m, s).wait_send()

    for m in range(micros):
        rows_copy(m).wait()
        for copy in outs(m, range(4)):
            copy.wait()
    mine_copy.wait()
    for slot in range(2):
        tile = micros * TILES - 2 + slot
        probs_store(tile, tile % 2).wait()


def attend_rows(tokens, picks, places, ids, vecs, w_qkv):
    _, micros, width = tokens.shape
    tiles = micros * TILES
    dma = pltpu.SemaphoreType.DMA

    def sds(*shape):
        return jax.ShapeDtypeStruct(shape, BF)

    return pl.pallas_call(
        attend_rows_kernel,
        in_specs=[HBM] + [FULL] * 4 + [HBM],
        out_specs=[HBM] * 7,
        out_shape=[
            sds(tiles, TILE, width),
            sds(tiles, TILE, 3 * width),
            sds(tiles, HEADS, TILE, TILE),
            sds(tiles, TILE, width),
            sds(tiles, TILE, width),
            sds(tiles * OWN, width),
            sds(2 * SLOT, width),
        ],
        scratch_shapes=[
            pltpu.VMEM(tokens.shape, BF),
            pltpu.VMEM(w_qkv.shape, BF),
            pltpu.VMEM((tiles, TILE, width), BF),
            pltpu.VMEM((tiles, TILE, 3 * width), BF),
            pltpu.VMEM((2, HEADS, TILE, TILE), BF),
            pltpu.VMEM((tiles, TILE, width), BF),
            pltpu.VMEM((tiles, TILE, width), BF),
            pltpu.VMEM((tiles * OWN, width), BF),
            pltpu.VMEM((micros, 3, 2 * SLOT, width), BF),
            pltpu.VMEM((micros, 2 * SLOT, width), BF),
            pltpu.VMEM((micros, 2 * SLOT, width), BF),
            pltpu.VMEM((micros, 3, 2 * SLOT, width), BF),
            dma((TILES,)),
            dma,
            dma((micros, 4)),
            dma((2,)),
            dma((micros + 1,)),
            dma((micros, 3)),
            dma((micros,)),
            dma((micros,)),
            dma((micros, 3)),
        ],
        compiler_params=pltpu.CompilerParams(
            vmem_limit_bytes=63 * 2**20, collective_id=3, has_side_effects=True
        ),
        name="attend_rows",
    )(tokens, picks, places, ids, vecs, w_qkv)


def attend_back_kernel(qkv_ref, p_ref, out_ref, inv_ref, grad_ref, dqkv_ref):
    width = out_ref.shape[2]
    low, high = pair_lanes()

    def maker(pair):
        at = pl.ds(pair * 128, 128)
        return lambda: attend_back_pair(
            *(qkv_ref[0, :, pl.ds(part * width + pair * 128, 128)] for part in range(3)),
            [p_ref[0, 2 * pair], p_ref[0, 2 * pair + 1]],
            out_ref[0, :, at],
            inv_ref[0, :, at],
            grad_ref[0, :, at],
            low,
            high,
        )

    def finish(pair, results):
        for part, value in enumerate(results):
            dqkv_ref[0, :, pl.ds(part * width + pair * 128, 128)] = value

    staggered([maker(pair) for pair in range(HEADS // 2)], finish)


def attend_back(qkv, probs, out, inverse, grad):
    tiles, _, width = out.shape

    def block(*shape):
        return pl.BlockSpec((1,) + shape, lambda i: (i,) + (0,) * len(shape))

    return pl.pallas_call(
        attend_back_kernel,
        grid=(tiles,),
        in_specs=[
            block(TILE, 3 * width),
            block(HEADS, TILE, TILE),
            block(TILE, width),
            block(TILE, width),
            block(TILE, width),
        ],
        out_specs=block(TILE, 3 * width),
        out_shape=jax.ShapeDtypeStruct((tiles, TILE, 3 * width), BF),
        compiler_params=pltpu.CompilerParams(vmem_limit_bytes=56 * 2**20),
        name="attend_back",
    )(qkv, probs, out, inverse, grad)


STEPS = 3


def add_into(ref, at, other):
    ref[at] = (ref[at].astype(F32) + other.astype(F32)).astype(BF)


class ItemSum:
    def __init__(self, up, down, got, got_one, got_two, sems):
        self.grads = (up, down)
        self.got, self.got_one, self.got_two, self.sems = got, got_one, got_two, sems
        me = lax.axis_index("dp")
        self.me = me
        self.core, self.x, self.y = lax.rem(me, 2), lax.rem(lax.div(me, 2), 2), lax.div(me, 4)
        self.near = me + 1 - 2 * self.core
        self.over_x = me + 2 - 4 * self.x
        self.over_y = me + 4 - 8 * self.y

    def _copy(self, src, dst, stage, which, slot, device):
        return pltpu.make_async_remote_copy(
            src_ref=src,
            dst_ref=dst,
            send_sem=self.sems.at[stage, which, 0, slot],
            recv_sem=self.sems.at[stage, which, 1, slot],
            device_id={"dp": device},
            device_id_type=MESH,
        )

    def core_copy(self, which, slot):
        src = self.grads[which].at[slot, :, :, 1 - self.core]
        return self._copy(src, self.got[which].at[slot], 0, which, slot, self.near)

    def one_copy(self, which, slot):
        grad = self.grads[which]
        if which == 0:
            src, device = grad.at[slot, :, 1 - self.x, self.core], self.over_x
        else:
            src, device = grad.at[slot, 1 - self.y, :, self.core], self.over_y
        return self._copy(src, self.got_one[which].at[slot], 1, which, slot, device)

    def two_copy(self, which, slot):
        grad = self.grads[which]
        if which == 0:
            src, device = grad.at[slot, 1 - self.y, self.x, self.core], self.over_y
        else:
            src, device = grad.at[slot, self.y, 1 - self.x, self.core], self.over_x
        return self._copy(src, self.got_two[which].at[slot], 2, which, slot, device)

    def start(self, which, slot):
        self.core_copy(which, slot).start()

    def after_core(self, slot):
        for which in range(2):
            self.core_copy(which, slot).wait()
            for y in range(2):
                for x in range(2):
                    at = (slot, y, x, self.core)
                    add_into(self.grads[which], at, self.got[which][slot, y, x])
            self.one_copy(which, slot).start()

    def after_one(self, slot):
        for which in range(2):
            self.one_copy(which, slot).wait()
            for side in range(2):
                at = (slot, side, self.x, self.core) if which == 0 else (slot, self.y, side, self.core)
                add_into(self.grads[which], at, self.got_one[which][slot, side])
            self.two_copy(which, slot).start()

    def after_two(self, slot):
        sums = []
        for which in range(2):
            self.two_copy(which, slot).wait()
            own = self.grads[which][slot, self.y, self.x, self.core].astype(F32)
            sums.append((own + self.got_two[which][slot].astype(F32)).astype(BF))
        return sums


def meet(devices):
    barrier = pltpu.get_barrier_semaphore()
    for device in devices:
        pl.semaphore_signal(barrier, inc=1, device_id=device, device_id_type=MESH)
    pl.semaphore_wait(barrier, len(devices))


def expert_kernel(
    remote,
    x_ref,
    att_ref,
    att_tiles_ref,
    att_last_ref,
    dy_ref,
    w_out_ref,
    vecs_ref,
    picks_ref,
    places_ref,
    up_v_ref,
    down_v_ref,
    up_t_ref,
    down_t_ref,
    out_ref,
    dmid_ref,
    datt_ref,
    dwout_ref,
    vec_ref,
    dup_ref,
    ddown_ref,
    *refs,
):
    if remote:
        dup_last_ref, ddown_last_ref, rows_last_ref, got_up, got_down, *refs = refs
    raw, dy, att, w_out, mid, tiles, hid_t, dy_t, acc_o, acc_h, up_w, down_w, *refs = refs
    act, gup, dup_buf, ddown_buf, sems, io_sems, raw_sems, *more = refs
    width = att.shape[1]
    cols = act.shape[2]
    micros = raw.shape[1]
    rows = TILES * OWN
    own_z = lax.axis_index("stream")
    is_text = own_z == 3
    is_image = jnp.logical_not(is_text)
    pieces = 8 if remote else 1
    piece = cols // pieces
    ff = up_v_ref.shape[1]

    def rows_of(m):
        return pl.ds(pl.multiple_of(m * rows, 16), rows)

    def loads(m):
        at = pl.ds(m * rows, rows)
        yield pltpu.make_async_copy(att_ref.at[at], att.at[at], io_sems.at[m, 0])
        for t in range(TILES):
            src = x_ref.at[m * TILES + t, 0:OWN]
            dst = act.at[m, t * OWN : (t + 1) * OWN, 0:width]
            yield pltpu.make_async_copy(src, dst, io_sems.at[m, 1 + t])

    def raw_copy(t):
        at = pl.ds(t * PATCHES, PATCHES)
        return pltpu.make_async_copy(dy_ref.at[at], raw.at[at], raw_sems.at[t])

    def store(m, n):
        at = rows_of(m)
        tile_at = pl.ds(m * TILES, TILES)
        src, dst = (
            (mid.at[at], dmid_ref.at[at]),
            (tiles.at[tile_at], datt_ref.at[tile_at]),
            (act.at[m, 0:rows, 0:width], out_ref.at[at]),
        )[n]
        return pltpu.make_async_copy(src, dst, io_sems.at[m, 5 + n])

    w_out_copy = pltpu.make_async_copy(w_out_ref, w_out, io_sems.at[0, 8])
    dwout = dy_t.at[:, 0:width]
    dwout_copy = pltpu.make_async_copy(dwout, dwout_ref, io_sems.at[0, 8])

    def fetch(j, slot):
        def go(up_src, down_src):
            for d in range(pieces):
                at = pl.ds(pl.multiple_of(j * piece + d * (ff // pieces), 128), piece)
                here = pl.ds(d * piece, piece)
                pltpu.make_async_copy(
                    up_src.at[:, at], up_w.at[slot, :, here], sems.at[0, slot]
                ).start()
                pltpu.make_async_copy(
                    down_src.at[at, :], down_w.at[slot, here, :], sems.at[1, slot]
                ).start()

        pl.when(is_text)(lambda: go(up_t_ref, down_t_ref))
        pl.when(is_image)(lambda: go(up_v_ref, down_v_ref))

    def fetched(slot):
        pltpu.make_async_copy(up_w.at[slot], up_w.at[slot], sems.at[0, slot]).wait()
        pltpu.make_async_copy(down_w.at[slot], down_w.at[slot], sems.at[1, slot]).wait()

    for t in range(TILES):
        raw_copy(t).start()
    w_out_copy.start()
    for m in range(micros):
        for copy in loads(m):
            copy.start()
    fetch(0, 0)

    if remote:
        got, got_one, got_two, sum_sems = more[0:2], more[2:4], more[4:6], more[6]
        sent, got_rows, row_send, row_recv, got_att, att_side = more[7:13]
        att_send, att_recv, side_sem, z_up, z_down, z_send, z_recv = more[13:]
        total = ItemSum(dup_buf, ddown_buf, got, got_one, got_two, sum_sems)

        def side_copies():
            for t in range(TILES):
                src = att_tiles_ref.at[(micros - 1) * TILES + t, OWN:TILE]
                yield pltpu.make_async_copy(src, att_side.at[t], side_sem.at[t])

        for copy in side_copies():
            copy.start()
        meet(
            [{"dp": total.near}, {"dp": total.over_x}, {"dp": total.over_y}]
            + [{"stream": lax.rem(own_z + k, 4)} for k in range(1, 4)]
        )

        def att_copy(s):
            return pltpu.make_async_remote_copy(
                src_ref=att_last_ref,
                dst_ref=got_att.at[s],
                send_sem=att_send,
                recv_sem=att_recv.at[s],
                device_id={"stream": 3},
                device_id_type=MESH,
            )

        for s in range(3):
            pl.when(own_z == s)(lambda: att_copy(s).start())

        def row_copy(m, s):
            return pltpu.make_async_remote_copy(
                src_ref=sent.at[m, s],
                dst_ref=got_rows.at[m],
                send_sem=row_send.at[m, s],
                recv_sem=row_recv.at[m],
                device_id={"stream": s},
                device_id_type=MESH,
            )

    gain, shift = row_of(vecs_ref, GAIN2), row_of(vecs_ref, SHIFT2)
    bias = jnp.where(is_text, row_of(vecs_ref, TXT_BIAS), row_of(vecs_ref, VIS_BIAS))
    space = dy_t.shape[1] // micros
    for ref in (hid_t, dy_t):
        for m in range(micros):
            lanes = slice(m * space + rows, (m + 1) * space)
            ref[:, lanes] = jnp.zeros((width, space - rows), BF)
    for ref in (act, gup):
        ref[:, rows:space] = jnp.zeros((micros, space - rows, cols), BF)
    pad = padding(micros, False)
    for t in range(TILES):
        raw_copy(t).wait()
        padded = pad_third(pad, raw[t * PATCHES : (t + 1) * PATCHES])
        for m in range(micros):
            at = m * rows + t * OWN
            dy[at : at + OWN] = padded[m * OWN : (m + 1) * OWN]
    for m in range(micros):
        dy_t[:, m * space : m * space + rows] = dy[m * rows : (m + 1) * rows].T

    def put_rows(m, value):
        for t in range(TILES):
            tiles[m * TILES + t, 0:OWN] = value[t * OWN : (t + 1) * OWN]

    def own_rows(m):
        return jnp.concatenate([tiles[m * TILES + t, 0:OWN] for t in range(TILES)], axis=0)

    def beside(m, value):
        for t in range(TILES):
            part = value[t * (TILE - OWN) : (t + 1) * (TILE - OWN)]
            tiles[m * TILES + t, OWN:TILE] = part

    def begin(m):
        for copy in loads(m):
            copy.wait()
        if m == 0:
            w_out_copy.wait()
        at = rows_of(m)
        if remote and m == micros - 1:

            @pl.when(is_text)
            def _():
                for s in range(3):
                    att_copy(s).wait_recv()
                parts = [got_att[s] for s in range(3)] + [att_side[t] for t in range(TILES)]
                moved = t_dot(picks_ref[m], jnp.concatenate(parts, axis=0)).astype(BF)
                att[at] = (att[at].astype(F32) + moved.astype(F32)).astype(BF)

        middle = act[m, 0:rows, 0:width].astype(F32) + dot(att[at], w_out[...])
        mid[at] = middle
        normed, _ = normalize(middle)
        hidden = (normed * gain + shift).astype(BF)
        put_rows(m, hidden)
        hid_t[:, m * space : m * space + rows] = hidden.T
        acc_o[at] = middle + bias
        acc_h[at] = jnp.zeros_like(middle)

    if remote:
        for copy in side_copies():
            copy.wait()

    def deliver(slot, up_ref, down_ref):
        up, down = total.after_two(slot)
        for t in range(4):
            up_ref[t] = up[:, t * (cols // 4) : (t + 1) * (cols // 4)]
            down_ref[t] = down[t * (width // 4) : (t + 1) * (width // 4)]

    def share_copy(t, which):
        src, dst = ((z_up, got_up), (z_down, got_down))[which]
        return pltpu.make_async_remote_copy(
            src_ref=src.at[t],
            dst_ref=dst.at[own_z],
            send_sem=z_send.at[t, which],
            recv_sem=z_recv.at[own_z, which],
            device_id={"stream": t},
            device_id_type=MESH,
        )

    def share_arrival(t, which):
        dst = (got_up, got_down)[which]
        return pltpu.make_async_remote_copy(
            src_ref=dst.at[t],
            dst_ref=dst.at[t],
            send_sem=z_send.at[t, which],
            recv_sem=z_recv.at[t, which],
            device_id={"stream": t},
            device_id_type=MESH,
        )

    def own_share(t, which):
        src, dst = ((z_up, got_up), (z_down, got_down))[which]
        return pltpu.make_async_copy(src.at[t], dst.at[t], z_send.at[t, which])

    def deliver_first(slot):
        deliver(slot, z_up, z_down)
        for t in range(4):
            for which in range(2):
                pl.when(own_z != t)(lambda: share_copy(t, which).start())
                pl.when(own_z == t)(lambda: own_share(t, which).start())

    def stored(j, slot):
        return (
            pltpu.make_async_copy(dup_buf.at[slot], dup_ref.at[j], sems.at[2, slot]),
            pltpu.make_async_copy(ddown_buf.at[slot], ddown_ref.at[j], sems.at[3, slot]),
        )

    vec_ref[...] = jnp.zeros_like(vec_ref)

    def finish(m):
        at = rows_of(m)
        normed, inverse = normalize(mid[at])
        grad = acc_h[at]
        wide = dy[at].astype(F32)
        vec_ref[0:1, :] += jnp.sum(grad * normed, axis=0, keepdims=True)
        vec_ref[1:2, :] += jnp.sum(grad, axis=0, keepdims=True)
        vec_ref[2:3, :] += jnp.sum(wide, axis=0, keepdims=True)
        grad_mid = wide + norm_back(grad, normed, inverse, gain)
        mid[at] = grad_mid
        branch = grad_mid.astype(BF)
        dy[at] = branch
        put_rows(m, dot_t(branch, w_out[...]).astype(BF))
        if remote:

            @pl.when(is_text)
            def _():
                picked = dot(picks_ref[m], own_rows(m)).astype(BF)
                for s in range(3):
                    part = picked[s * 2 * SLOT : (s + 1) * 2 * SLOT]
                    if m < micros - 1:
                        sent[m, s] = part
                        row_copy(m, s).start()
                    else:
                        rows_last_ref[s] = part
                beside(m, picked[6 * SLOT :])

            if m == micros - 1:

                @pl.when(is_image)
                def _():
                    rows_last_ref[...] = jnp.zeros_like(rows_last_ref)
                    for t in range(TILES):
                        tiles[m * TILES + t, OWN:TILE] = jnp.zeros((TILE - OWN, width), BF)

                store(m, 1).start()
        else:
            store(m, 1).start()

    @pl.loop(0, STEPS)
    def _(j):
        slot = lax.rem(j, 2)
        other = 1 - slot
        pl.when(j < STEPS - 1)(lambda: fetch(j + 1, other))
        fetched(slot)

        @pl.loop(0, micros)
        def _(m):
            for n in range(micros):
                pl.when((j == 0) & (m == n))(lambda: begin(n))
            at = rows_of(m)
            up = dot(own_rows(m), up_w[slot])
            grad = dot_t(dy[at], down_w[slot])
            for t in range(TILES):
                part = slice(t * OWN, (t + 1) * OWN)
                cdf, pdf = gelu_parts(up[part])
                act[m, part] = (up[part] * cdf).astype(BF)
                gup[m, part] = (grad[part] * (cdf + up[part] * pdf)).astype(BF)
            acc_o[at] += dot(act[m, 0:rows], down_w[slot])
            acc_h[at] += dot_t(gup[m, 0:rows], up_w[slot])
            if remote:

                @pl.when(m == 0)
                def _():
                    pl.when(j > 1)(lambda: deliver_first(slot))
                    pl.when(j > 0)(lambda: total.after_core(other))


        for n in range(micros - 1):
            pl.when(j == STEPS - 1)(lambda: finish(n))
        if not remote:

            @pl.when(j > 1)
            def _():
                for copy in stored(j - 2, slot):
                    copy.wait()

        grad = dot(hid_t[...], gup[...].reshape(micros * space, cols)).astype(BF)
        if remote:
            dup_buf[slot] = grad.reshape(dup_buf.shape[1:])
            pl.when(j < STEPS - 1)(lambda: total.start(0, slot))
        else:
            dup_buf[slot] = grad
        grad = dot(dy_t[...], act[...].reshape(micros * space, cols)).astype(BF)
        if remote:
            for d in range(8):
                ddown_buf[slot, d // 4, d // 2 % 2, d % 2] = grad[:, d * piece : (d + 1) * piece]
            pl.when(j < STEPS - 1)(lambda: total.start(1, slot))
            pl.when(j > 0)(lambda: total.after_one(other))
        else:
            ddown_buf[slot] = grad
            for copy in stored(j, slot):
                copy.start()

    last = (STEPS - 1) % 2
    if remote:
        last_copies = [
            pltpu.make_async_copy(dup_buf.at[last], dup_last_ref, sems.at[2, 0]),
            pltpu.make_async_copy(ddown_buf.at[last], ddown_last_ref, sems.at[3, 0]),
        ]
        for copy in last_copies:
            copy.start()
    for m in range(micros - 1):
        store(m, 0).start()
        if remote:
            pl.when(is_text)(lambda: store(m, 1).start())
    finish(micros - 1)
    store(micros - 1, 0).start()
    for m in range(micros):
        act[m, 0:rows, 0:width] = acc_o[rows_of(m)].astype(BF)
        store(m, 2).start()
    dwout[...] = t_dot(att[...], dy[...]).astype(BF)
    dwout_copy.start()
    if remote:
        deliver(1 - last, dup_ref, ddown_ref)

        @pl.when(is_text)
        def _():
            for m in range(micros - 1):
                for s in range(3):
                    row_copy(m, s).wait_send()

        @pl.when(is_image)
        def _():
            for m in range(micros - 1):
                row_copy(m, 0).wait_recv()
                beside(m, dot(places_ref[m], got_rows[m]).astype(BF))
                store(m, 1).start()
            att_copy(0).wait_send()

        for t in range(4):
            for which in range(2):

                @pl.when(own_z != t)
                def _():
                    share_arrival(t, which).wait_recv()
                    share_copy(t, which).wait_send()

                pl.when(own_z == t)(lambda: own_share(t, which).wait())
        for copy in last_copies:
            copy.wait()
    else:
        for j in range(STEPS - 2, STEPS):
            for copy in stored(j, j % 2):
                copy.wait()
    for m in range(micros):
        for n in range(3):
            store(m, n).wait()
    dwout_copy.wait()


def expert(
    remote,
    x_tiles,
    att,
    att_tiles,
    att_last,
    dy,
    w_out,
    vecs,
    picks,
    places,
    vis_up,
    vis_down,
    txt_up,
    txt_down,
):
    rows, width = att.shape
    cols = vis_up.shape[1] // STEPS
    micros = dy.shape[1]
    space = -(-rows // micros // BLOCK) * BLOCK
    dma = pltpu.SemaphoreType.DMA
    if remote:
        shard, piece = width // 8, cols // 8
        buffers = (2, 2, 2, 2, shard, cols), (2, 2, 2, 2, width, piece)
        outs = (4, shard, cols // 4), (4, width // 4, piece)
        lasts = [buffers[0][1:], buffers[1][1:], (3, 2 * SLOT, width), *outs]
        out_specs = [HBM] * 4 + [FULL] * 3 + [HBM] * 2 + [FULL] + [HBM] * 2
        more = [
            pltpu.VMEM((2, 2, 2, shard, cols), BF),
            pltpu.VMEM((2, 2, 2, width, piece), BF),
            pltpu.VMEM((2, 2, shard, cols), BF),
            pltpu.VMEM((2, 2, width, piece), BF),
            pltpu.VMEM((2, shard, cols), BF),
            pltpu.VMEM((2, width, piece), BF),
            dma((3, 2, 2, 2)),
            pltpu.VMEM((micros - 1, 3, 2 * SLOT, width), BF),
            pltpu.VMEM((micros - 1, 2 * SLOT, width), BF),
            dma((micros - 1, 3)),
            dma((micros - 1,)),
            pltpu.VMEM((3, 2 * SLOT, width), BF),
            pltpu.VMEM((TILES, TILE - OWN, width), BF),
            dma,
            dma((3,)),
            dma((TILES,)),
            pltpu.VMEM(outs[0], BF),
            pltpu.VMEM(outs[1], BF),
            dma((4, 2)),
            dma((4, 2)),
        ]
        params = dict(collective_id=1, has_side_effects=True)
    else:
        buffers = ((2, width, cols),) * 2
        outs = ((STEPS, width, cols),) * 2
        lasts, out_specs = [], [HBM] * 4 + [FULL] + [HBM] * 2
        more, params = [], {}
    return pl.pallas_call(
        functools.partial(expert_kernel, remote),
        in_specs=[HBM] * 6 + [FULL] * 3 + [HBM] * 4,
        out_specs=out_specs,
        out_shape=[
            jax.ShapeDtypeStruct((rows, width), BF),
            jax.ShapeDtypeStruct((rows, width), F32),
            jax.ShapeDtypeStruct((rows // OWN, TILE, width), BF),
            jax.ShapeDtypeStruct((width, width), BF),
            jax.ShapeDtypeStruct((8, width), F32),
        ]
        + [jax.ShapeDtypeStruct(shape, BF) for shape in [*outs, *lasts]],
        scratch_shapes=[
            pltpu.VMEM(dy.shape, BF),
            pltpu.VMEM((rows, width), BF),
            pltpu.VMEM((rows, width), BF),
            pltpu.VMEM((width, width), BF),
            pltpu.VMEM((rows, width), F32),
            pltpu.VMEM((rows // OWN, TILE, width), BF),
            pltpu.VMEM((width, micros * space), BF),
            pltpu.VMEM((width, micros * space), BF),
            pltpu.VMEM((rows, width), F32),
            pltpu.VMEM((rows, width), F32),
            pltpu.VMEM((2, width, cols), BF),
            pltpu.VMEM((2, cols, width), BF),
            pltpu.VMEM((micros, space, cols), BF),
            pltpu.VMEM((micros, space, cols), BF),
            pltpu.VMEM(buffers[0], BF),
            pltpu.VMEM(buffers[1], BF),
            dma((4, 2)),
            dma((micros, 9)),
            dma((TILES,)),
        ]
        + more,
        compiler_params=pltpu.CompilerParams(vmem_limit_bytes=63 * 2**20, **params),
        name="expert",
    )(
        x_tiles,
        att,
        att_tiles,
        att_last,
        dy,
        w_out,
        vecs,
        picks,
        places,
        vis_up,
        vis_down,
        txt_up,
        txt_down,
    )


def project_back_kernel(x_ref, dqkv_ref, vecs_ref, w_ref, dx_ref, dw_ref, vec_ref, acc):
    i = pl.program_id(0)
    gain, shift = row_of(vecs_ref, GAIN1), row_of(vecs_ref, SHIFT1)
    normed, inverse = normalize(x_ref[0].astype(F32))
    hidden = (normed * gain + shift).astype(BF)
    dqkv = dqkv_ref[0]
    grad = dot_t(dqkv, w_ref[...])
    dx_ref[0] = norm_back(grad, normed, inverse, gain).astype(BF)
    width = x_ref.shape[2]
    part = t_dot(hidden, dqkv)
    ones = jnp.ones((8, TILE), BF)
    sums = dot(ones, dqkv)[0:1]
    vec = jnp.concatenate(
        [
            jnp.sum(grad * normed, axis=0, keepdims=True),
            jnp.sum(grad, axis=0, keepdims=True),
            sums[:, :width],
            sums[:, 2 * width :],
        ],
        axis=0,
    )

    @pl.when(i == 0)
    def _():
        acc[...] = part
        vec_ref[0:4, :] = vec

    @pl.when(i > 0)
    def _():
        acc[...] += part
        vec_ref[0:4, :] += vec

    @pl.when(i == pl.num_programs(0) - 1)
    def _():
        dw_ref[...] = acc[...].astype(BF)


def project_back(x_tiles, dqkv, vecs, w_qkv):
    tiles, _, width = x_tiles.shape

    def block(*shape):
        return pl.BlockSpec((1,) + shape, lambda i: (i,) + (0,) * len(shape))

    return pl.pallas_call(
        project_back_kernel,
        grid=(tiles,),
        in_specs=[block(TILE, width), block(TILE, 3 * width), FULL, FULL],
        out_specs=[block(TILE, width), FULL, FULL],
        out_shape=[
            jax.ShapeDtypeStruct((tiles, TILE, width), BF),
            jax.ShapeDtypeStruct((width, 3 * width), BF),
            jax.ShapeDtypeStruct((8, width), F32),
        ],
        scratch_shapes=[pltpu.VMEM((width, 3 * width), F32)],
        compiler_params=pltpu.CompilerParams(vmem_limit_bytes=56 * 2**20),
        name="project_back",
    )(x_tiles, dqkv, vecs, w_qkv)


GROUP = 256
GROUPS = 3
SLOTS = 3


def stream_blocks(count, share):
    spans = []
    for t in range(4):
        first, last = t * share // BLOCK, ((t + 1) * share - 1) // BLOCK
        spans.append(list(range(first, last + 1)))
    assert spans[-1][-1] == count - 1
    return spans


def unit_blocks(unit):
    if unit == 0:
        return list(range(6))
    g = unit - 1
    return [6 * part + 2 * g + i for part in range(3) for i in range(2)]


def back_kernel(
    x_ref,
    qkv_ref,
    p_ref,
    att_ref,
    inv_ref,
    datt_ref,
    dmid_ref,
    vecs_ref,
    w_ref,
    dwout_ref,
    zup_ref,
    zdown_ref,
    dup_last_ref,
    ddown_last_ref,
    rows_last_ref,
    vec2_ref,
    picks_ref,
    places_ref,
    dx_ref,
    sums_ref,
    got_qkv,
    got_out,
    got_up,
    got_down,
    qkv,
    x,
    att,
    inv,
    datt,
    base,
    probs,
    beside,
    got_last,
    last_a,
    last_b,
    got_last_a,
    got_last_b,
    one_last_a,
    one_last_b,
    two_last_a,
    two_last_b,
    z_last_up,
    z_last_down,
    hid_t,
    dqkv,
    w,
    sums,
    extra,
    mine,
    got_rows,
    buf_a,
    buf_b,
    got_a,
    got_b,
    one_a,
    one_b,
    two_a,
    two_b,
    held,
    dx,
    vec,
    got_vec,
    own_vec,
    z_vec,
    load_sems,
    x_sems,
    w_sem,
    last_sems,
    last_send,
    last_recv,
    last_sum_sems,
    sum_sems,
    row_send,
    row_recv,
    vec_sems,
    zvec_send,
    zvec_recv,
    expert_send,
    expert_recv,
    block_send,
    block_recv,
    dx_sems,
):
    micros = x.shape[0] // TILES
    width = x.shape[2]
    shard = width // 8
    own_z = lax.axis_index("stream")
    is_text = own_z == 3
    is_image = jnp.logical_not(is_text)
    total = ItemSum(buf_a, buf_b, (got_a, got_b), (one_a, one_b), (two_a, two_b), sum_sems)

    total_last = ItemSum(
        last_a,
        last_b,
        (got_last_a, got_last_b),
        (one_last_a, one_last_b),
        (two_last_a, two_last_b),
        last_sum_sems,
    )

    def loads(step, slot):
        m, g = lax.div(step, GROUPS), lax.rem(step, GROUPS)
        tiles = pl.ds(m * TILES, TILES)
        at = pl.multiple_of(g * GROUP, GROUP)
        copies = [pltpu.make_async_copy(p_ref.at[tiles, pl.ds(g * 4, 4)], probs.at[slot], load_sems.at[slot, 0])]
        for part in range(3):
            src = qkv_ref.at[tiles, :, pl.ds(part * width + at, GROUP)]
            dst = qkv.at[slot, :, :, pl.ds(part * GROUP, GROUP)]
            copies.append(pltpu.make_async_copy(src, dst, load_sems.at[slot, 1 + part]))
        for n, (src, dst) in enumerate(((att_ref, att), (inv_ref, inv), (datt_ref, datt))):
            src = src.at[tiles, :, pl.ds(at, GROUP)]
            copies.append(pltpu.make_async_copy(src, dst.at[slot], load_sems.at[slot, 4 + n]))
        return copies

    def micro_loads(m):
        at = pl.ds(m * TILES, TILES)
        rows = pl.ds(m * TILES * OWN, TILES * OWN)
        return [
            pltpu.make_async_copy(x_ref.at[at], x.at[at], x_sems.at[m, 0]),
            pltpu.make_async_copy(dmid_ref.at[rows], base.at[rows], x_sems.at[m, 1]),
        ]

    last_loads = [
        pltpu.make_async_copy(dup_last_ref, last_a.at[0], last_sems.at[0]),
        pltpu.make_async_copy(ddown_last_ref, last_b.at[0], last_sems.at[1]),
    ]
    w_copies = []
    for g in range(GROUPS):
        for part in range(3):
            src = w_ref.at[:, pl.ds(part * width + g * GROUP, GROUP)]
            dst = w.at[:, pl.ds((g * 3 + part) * GROUP, GROUP)]
            w_copies.append(pltpu.make_async_copy(src, dst, w_sem))
    for copy in [*loads(0, 0), *last_loads]:
        copy.start()
    meet(
        [{"dp": lax.rem(total.me + k, 8)} for k in range(1, 8)]
        + [{"stream": lax.rem(own_z + k, 4)} for k in range(1, 4)]
    )

    def last_row_copy(s):
        return pltpu.make_async_remote_copy(
            src_ref=rows_last_ref.at[s],
            dst_ref=got_last,
            send_sem=last_send.at[s],
            recv_sem=last_recv,
            device_id={"stream": s},
            device_id_type=MESH,
        )

    @pl.when(is_text)
    def _():
        for s in range(3):
            last_row_copy(s).start()

    def expert_ends(which, t, src):
        mine = zup_ref, zdown_ref, z_last_up, z_last_down
        return mine[which].at[t], (got_up, got_down)[which % 2].at[src, which // 2]

    def expert_copy(t, which):
        src, dst = expert_ends(which, t, own_z)
        return pltpu.make_async_remote_copy(
            src_ref=src,
            dst_ref=dst,
            send_sem=expert_send.at[t, which],
            recv_sem=expert_recv.at[own_z, which],
            device_id={"stream": t},
            device_id_type=MESH,
        )

    def expert_arrival(src, which):
        dst = expert_ends(which, src, src)[1]
        return pltpu.make_async_remote_copy(
            src_ref=dst,
            dst_ref=dst,
            send_sem=expert_send.at[src, which],
            recv_sem=expert_recv.at[src, which],
            device_id={"stream": src},
            device_id_type=MESH,
        )

    def expert_sends(kinds):
        for t in range(4):

            @pl.when(own_z != t)
            def _():
                for which in kinds:
                    expert_copy(t, which).start()

            @pl.when(own_z == t)
            def _():
                for which in kinds:
                    src, dst = expert_ends(which, t, t)
                    pltpu.make_async_copy(src, dst, expert_send.at[t, which]).start()

    def take_last():
        up, down = total_last.after_two(0)
        part_up, part_down = z_last_up.shape[2], z_last_down.shape[1]
        for t in range(4):
            z_last_up[t] = up[:, t * part_up : (t + 1) * part_up]
            z_last_down[t] = down[t * part_down : (t + 1) * part_down]
        expert_sends((2, 3))

    expert_sends((0, 1))

    half = buf_a.shape[-1]

    def put_unit(unit, value):
        slot = lax.rem(unit, SLOTS)
        buf_a[slot] = value[:, :half].reshape(buf_a.shape[1:])
        buf_b[slot] = value[:, half:].reshape(buf_b.shape[1:])
        total.start(0, slot)
        total.start(1, slot)

    def take_unit(unit):
        left, right = total.after_two(unit % SLOTS)
        for n in range(3):
            held[unit, n] = left[:, n * BLOCK : (n + 1) * BLOCK]
            held[unit, n + 3] = right[:, n * BLOCK : (n + 1) * BLOCK]

    def block_copy(unit, n, t, place):
        dst = got_out if unit == 0 else got_qkv
        kind = 0 if unit == 0 else 1
        return pltpu.make_async_remote_copy(
            src_ref=held.at[unit, n],
            dst_ref=dst.at[own_z, place],
            send_sem=block_send.at[kind, t, place],
            recv_sem=block_recv.at[kind, own_z, place],
            device_id={"stream": t},
            device_id_type=MESH,
        )

    def own_block_copy(unit, n, t, place):
        dst = got_out if unit == 0 else got_qkv
        kind = 0 if unit == 0 else 1
        return pltpu.make_async_copy(
            held.at[unit, n], dst.at[t, place], block_send.at[kind, t, place]
        )

    out_spans = stream_blocks(6, width // 4)
    qkv_spans = stream_blocks(18, 3 * width // 4)

    def unit_sends(unit, t):
        span = (out_spans if unit == 0 else qkv_spans)[t]
        blocks = unit_blocks(unit)
        return [(n, span.index(b)) for n, b in enumerate(blocks) if b in span]

    def send_unit(unit):
        for t in range(4):

            @pl.when(own_z != t)
            def _():
                for n, place in unit_sends(unit, t):
                    block_copy(unit, n, t, place).start()

            @pl.when(own_z == t)
            def _():
                for n, place in unit_sends(unit, t):
                    own_block_copy(unit, n, t, place).start()

    put_unit(0, dwout_ref[...])

    def row_copy(m, s):
        return pltpu.make_async_remote_copy(
            src_ref=mine.at[m],
            dst_ref=got_rows.at[m, s],
            send_sem=row_send.at[m],
            recv_sem=row_recv.at[m, s],
            device_id={"stream": 3},
            device_id_type=MESH,
        )

    low, high = pair_lanes()
    gain, shift = row_of(vecs_ref, GAIN1), row_of(vecs_ref, SHIFT1)
    vec[...] = jnp.zeros_like(vec)

    def add_vec(row, value):
        for d in range(8):
            vec[d, row : row + 1, 0:shard] += value[:, d * shard : (d + 1) * shard]

    add_vec(4, vec2_ref[0:1, :])
    add_vec(5, vec2_ref[1:2, :])
    text_scale = jnp.where(is_text, 1.0, 0.0)
    add_vec(6, vec2_ref[2:3, :] * (1.0 - text_scale))
    add_vec(7, vec2_ref[2:3, :] * text_scale)

    def input_grad(m, begin, end):
        first = m * TILES
        starts = [pl.multiple_of((first + t) * TILE + begin, 16) for t in range(TILES)]
        grads = [dqkv[pl.ds(start, end - begin), :] for start in starts]
        grad = dot_t(jnp.concatenate(grads, axis=0), w[...])
        rows = [x[first + t, begin:end] for t in range(TILES)]
        normed, inverse = normalize(jnp.concatenate(rows, axis=0).astype(F32))
        add_vec(0, jnp.sum(grad * normed, axis=0, keepdims=True))
        add_vec(1, jnp.sum(grad, axis=0, keepdims=True))
        return norm_back(grad, normed, inverse, gain)

    steps = micros * GROUPS
    span = 3 * GROUP
    hid_t[width:] = jnp.ones_like(hid_t[width:])

    @pl.loop(0, steps)
    def _(step):
        m, g = lax.div(step, GROUPS), lax.rem(step, GROUPS)
        slot = lax.rem(step, 2)
        first = m * TILES
        there = pl.multiple_of(g * span, span)

        @pl.when(step + 1 < steps)
        def _():
            for copy in loads(step + 1, 1 - slot):
                copy.start()

        @pl.when(step == 0)
        def _():
            for m in range(micros):
                for copy in micro_loads(m):
                    copy.start()
            for copy in w_copies:
                copy.start()

        for copy in loads(step, slot):
            copy.wait()

        @pl.when(step == 0)
        def _():
            for copy in last_loads:
                copy.wait()
            total_last.start(0, 0)
            total_last.start(1, 0)

        pl.when(step == 1)(lambda: total_last.after_core(0))

        @pl.when(is_image & (m == micros - 1))
        def _():
            @pl.when(g == 0)
            def _():
                last_row_copy(0).wait_recv()
                beside[...] = dot(places_ref[m], got_last[...]).astype(BF)

            cols = pl.ds(pl.multiple_of(g * GROUP, GROUP), GROUP)
            for t in range(TILES):
                datt[slot, t, OWN:TILE] = beside[t * (TILE - OWN) : (t + 1) * (TILE - OWN), cols]

        @pl.when((step >= 1) & (step <= micros))
        def _():
            first = (step - 1) * TILES
            for copy in micro_loads(step - 1):
                copy.wait()
            for t in range(TILES):
                normed, _ = normalize(x[first + t].astype(F32))
                hidden = (normed * gain + shift).astype(BF)
                at = pl.multiple_of((first + t) * TILE, TILE)
                hid_t[0:width, pl.ds(at, TILE)] = hidden.T

        def maker(t, pair):
            at = pair * BLOCK
            cols = pl.ds(at, BLOCK)
            return lambda: attend_back_pair(
                *(qkv[slot, t, :, pl.ds(part * GROUP + at, BLOCK)] for part in range(3)),
                [probs[slot, t, 2 * pair], probs[slot, t, 2 * pair + 1]],
                att[slot, t, :, cols],
                inv[slot, t, :, cols],
                datt[slot, t, :, cols],
                low,
                high,
            )

        def finish(n, results):
            t, pair = n // 2, n % 2
            rows = pl.ds(pl.multiple_of((first + t) * TILE, TILE), TILE)
            for part, value in enumerate(results):
                at = pl.multiple_of(there + part * GROUP + pair * BLOCK, BLOCK)
                dqkv[rows, pl.ds(at, BLOCK)] = value

        staggered([maker(n // 2, n % 2) for n in range(2 * TILES)], finish)

        pl.when(step == 0)(lambda: total.after_core(0))
        pl.when(step == 2)(lambda: total.after_one(0))

        @pl.when(step == 3)
        def _():
            take_unit(0)
            send_unit(0)
            total_last.after_one(0)

        pl.when(step == steps - 2)(lambda: total.after_core(1))

        @pl.when(step == steps - 1)
        def _():
            total.after_one(1)
            total.after_core(2)

        @pl.when(m == micros - 1)
        def _():
            grad = dot(hid_t[...], dqkv[:, pl.ds(there, span)])
            sums[g] = grad[width : width + 8]
            put_unit(1 + g, grad[:width].astype(BF))

        pl.when(step == steps - 2)(take_last)

        @pl.when(step == GROUPS - 1)
        def _():
            pltpu.make_async_copy(w, w, w_sem).wait()

        @pl.when(g == GROUPS - 1)
        def _():
            extra[m] = input_grad(m, OWN, TILE).astype(BF)

            @pl.when(is_image)
            def _():
                mine[m] = t_dot(places_ref[m], extra[m]).astype(BF)
                for s in range(3):

                    @pl.when(own_z == s)
                    def _():
                        row_copy(m, s).start()

    for row, at in ((2, 0), (3, 2 * GROUP)):
        cols = [sums[g, 0:1, at : at + GROUP] for g in range(GROUPS)]
        add_vec(row, jnp.concatenate(cols, axis=1))

    peers = [lax.rem(total.me + k, 8) for k in range(1, 8)]

    def vec_copy(peer):
        return pltpu.make_async_remote_copy(
            src_ref=vec.at[peer],
            dst_ref=got_vec.at[total.me],
            send_sem=vec_sems.at[0, peer],
            recv_sem=vec_sems.at[1, total.me],
            device_id={"dp": peer},
            device_id_type=MESH,
        )

    def vec_arrival(peer):
        return pltpu.make_async_remote_copy(
            src_ref=got_vec.at[peer],
            dst_ref=got_vec.at[peer],
            send_sem=vec_sems.at[0, peer],
            recv_sem=vec_sems.at[1, peer],
            device_id={"dp": peer},
            device_id_type=MESH,
        )

    def zvec_copy(t):
        return pltpu.make_async_remote_copy(
            src_ref=own_vec,
            dst_ref=z_vec.at[own_z],
            send_sem=zvec_send.at[t],
            recv_sem=zvec_recv.at[own_z],
            device_id={"stream": t},
            device_id_type=MESH,
        )

    def zvec_arrival(s):
        return pltpu.make_async_remote_copy(
            src_ref=z_vec.at[s],
            dst_ref=z_vec.at[s],
            send_sem=zvec_send.at[s],
            recv_sem=zvec_recv.at[s],
            device_id={"stream": s},
            device_id_type=MESH,
        )

    rows_all = TILES * OWN

    def dx_copy(m):
        rows = pl.ds(m * rows_all, rows_all)
        return pltpu.make_async_copy(dx.at[rows], dx_ref.at[rows], dx_sems.at[m])

    def deliver(m, scattered):
        rows = pl.ds(m * rows_all, rows_all)
        value = base[rows]
        if scattered:
            value = value + t_dot(
                picks_ref[m], jnp.concatenate([got_rows[m, s] for s in range(3)] + [extra[m]], axis=0)
            )
        dx[rows] = value.astype(BF)
        dx_copy(m).start()

    def own_part(m):
        own = pl.ds(m * rows_all, rows_all)
        base[own] += input_grad(m, 0, OWN)

    def end_rows(m):
        pl.when(is_image)(lambda: deliver(m, False))

        @pl.when(is_text)
        def _():
            for s in range(3):
                row_copy(m, s).wait_recv()
            deliver(m, True)

    take_unit(1)
    send_unit(1)
    total.after_core(0)
    for m in range(micros - 1):
        own_part(m)
    total.after_one(2)
    for m in range(micros - 1):
        end_rows(m)
    total.after_one(0)
    own_part(micros - 1)
    for peer in peers:
        vec_copy(peer).start()
    take_unit(2)
    send_unit(2)
    take_unit(3)
    send_unit(3)
    for peer in peers:
        vec_arrival(peer).wait_recv()
        vec_copy(peer).wait_send()
    own_vec[...] = vec[total.me] + sum(got_vec[peer] for peer in peers)
    for t in range(4):
        pl.when(own_z != t)(lambda: zvec_copy(t).start())

        @pl.when(own_z == t)
        def _():
            z_vec[t] = own_vec[...]

    end_rows(micros - 1)

    @pl.when(is_text)
    def _():
        for s in range(3):
            last_row_copy(s).wait_send()

    @pl.when(is_image)
    def _():
        for m in range(micros):
            row_copy(m, 0).wait_send()

    for src in range(4):

        @pl.when(own_z != src)
        def _():
            for which in range(4):
                expert_arrival(src, which).wait_recv()
                expert_copy(src, which).wait_send()

        @pl.when(own_z == src)
        def _():
            for which in range(4):
                ref, dst = expert_ends(which, src, src)
                pltpu.make_async_copy(ref, dst, expert_send.at[src, which]).wait()

    for src in range(4):

        @pl.when(own_z != src)
        def _():
            zvec_arrival(src).wait_recv()
            zvec_copy(src).wait_send()
            for unit in range(GROUPS + 1):
                for n, place in unit_sends(unit, src):
                    block_copy(unit, n, src, place).wait_send()
            for kind, dst in ((0, got_out), (1, got_qkv)):
                for place in range(dst.shape[1]):
                    pltpu.make_async_remote_copy(
                        src_ref=dst.at[src, place],
                        dst_ref=dst.at[src, place],
                        send_sem=block_send.at[kind, src, place],
                        recv_sem=block_recv.at[kind, src, place],
                        device_id={"stream": src},
                        device_id_type=MESH,
                    ).wait_recv()

        @pl.when(own_z == src)
        def _():
            for unit in range(GROUPS + 1):
                for n, place in unit_sends(unit, src):
                    own_block_copy(unit, n, src, place).wait()

    sums_ref[...] = sum(z_vec[s] for s in range(4))
    for m in range(micros):
        dx_copy(m).wait()


def back(
    x_tiles,
    qkv,
    probs,
    att,
    inv,
    datt,
    dmid,
    vecs,
    w_qkv,
    dwout,
    zup,
    zdown,
    dup_last,
    ddown_last,
    rows_last,
    vec2,
    picks,
    places,
):
    tiles, _, width = x_tiles.shape
    micros = tiles // TILES
    shard = width // 8
    half = width // 2

    def sds(*shape, dtype=F32):
        return jax.ShapeDtypeStruct(shape, dtype)

    dma = pltpu.SemaphoreType.DMA
    return pl.pallas_call(
        back_kernel,
        in_specs=[HBM] * 7 + [FULL, HBM, FULL] + [HBM] * 5 + [FULL] * 3,
        out_specs=[HBM, FULL] + [HBM] * 4,
        out_shape=[
            sds(tiles * OWN, width, dtype=BF),
            sds(8, BLOCK),
            sds(4, 5, shard, BLOCK, dtype=BF),
            sds(4, 2, shard, BLOCK, dtype=BF),
            sds(4, STEPS - 1, *zup.shape[1:], dtype=BF),
            sds(4, STEPS - 1, *zdown.shape[1:], dtype=BF),
        ],
        scratch_shapes=[
            pltpu.VMEM((2, TILES, TILE, 3 * GROUP), BF),
            pltpu.VMEM((tiles, TILE, width), BF),
            pltpu.VMEM((2, TILES, TILE, GROUP), BF),
            pltpu.VMEM((2, TILES, TILE, GROUP), BF),
            pltpu.VMEM((2, TILES, TILE, GROUP), BF),
            pltpu.VMEM((tiles * OWN, width), F32),
            pltpu.VMEM((2, TILES, 4, TILE, TILE), BF),
            pltpu.VMEM((TILES * (TILE - OWN), width), BF),
            pltpu.VMEM((2 * SLOT, width), BF),
            pltpu.VMEM((1,) + dup_last.shape, BF),
            pltpu.VMEM((1,) + ddown_last.shape, BF),
            pltpu.VMEM((1, 2, 2) + dup_last.shape[3:], BF),
            pltpu.VMEM((1, 2, 2) + ddown_last.shape[3:], BF),
            pltpu.VMEM((1, 2) + dup_last.shape[3:], BF),
            pltpu.VMEM((1, 2) + ddown_last.shape[3:], BF),
            pltpu.VMEM((1,) + dup_last.shape[3:], BF),
            pltpu.VMEM((1,) + ddown_last.shape[3:], BF),
            pltpu.VMEM(zup.shape, BF),
            pltpu.VMEM(zdown.shape, BF),
            pltpu.VMEM((width + 16, tiles * TILE), BF),
            pltpu.VMEM((tiles * TILE, 3 * width), BF),
            pltpu.VMEM((width, 3 * width), BF),
            pltpu.VMEM((GROUPS, 8, 3 * GROUP), F32),
            pltpu.VMEM((micros, TILES * (TILE - OWN), width), BF),
            pltpu.VMEM((micros, 2 * SLOT, width), BF),
            pltpu.VMEM((micros, 3, 2 * SLOT, width), BF),
            pltpu.VMEM((SLOTS, 2, 2, 2, shard, half), BF),
            pltpu.VMEM((SLOTS, 2, 2, 2, shard, half), BF),
            pltpu.VMEM((SLOTS, 2, 2, shard, half), BF),
            pltpu.VMEM((SLOTS, 2, 2, shard, half), BF),
            pltpu.VMEM((SLOTS, 2, shard, half), BF),
            pltpu.VMEM((SLOTS, 2, shard, half), BF),
            pltpu.VMEM((SLOTS, shard, half), BF),
            pltpu.VMEM((SLOTS, shard, half), BF),
            pltpu.VMEM((GROUPS + 1, 6, shard, BLOCK), BF),
            pltpu.VMEM((tiles * OWN, width), BF),
            pltpu.VMEM((8, 8, BLOCK), F32),
            pltpu.VMEM((8, 8, BLOCK), F32),
            pltpu.VMEM((8, BLOCK), F32),
            pltpu.VMEM((4, 8, BLOCK), F32),
            dma((2, 7)),
            dma((micros, 2)),
            dma,
            dma((2,)),
            dma((3,)),
            dma,
            dma((3, 2, 2, 1)),
            dma((3, 2, 2, SLOTS)),
            dma((micros,)),
            dma((micros, 3)),
            dma((2, 8)),
            dma((4,)),
            dma((4,)),
            dma((4, 4)),
            dma((4, 4)),
            dma((2, 4, 5)),
            dma((2, 4, 5)),
            dma((micros,)),
        ],
        compiler_params=pltpu.CompilerParams(
            vmem_limit_bytes=63 * 2**20, collective_id=2, has_side_effects=True
        ),
        name="back",
    )(
        x_tiles,
        qkv,
        probs,
        att,
        inv,
        datt,
        dmid,
        vecs,
        w_qkv,
        dwout,
        zup,
        zdown,
        dup_last,
        ddown_last,
        rows_last,
        vec2,
        picks,
        places,
    )


def results_kernel(
    out_hbm,
    dx_hbm,
    qkv_hbm,
    o_hbm,
    up_hbm,
    down_hbm,
    first_up_hbm,
    first_down_hbm,
    out_rows_hbm,
    dx_rows_hbm,
    dqkv_ref,
    dout_ref,
    dvup_ref,
    dvdown_ref,
    dtup_ref,
    dtdown_ref,
    out_ref,
    dx_ref,
    got_qkv,
    got_out,
    got_up,
    got_down,
    first_up,
    first_down,
    out_rows,
    dx_rows,
    sems,
):
    _, micros, width = out_rows.shape
    ins = (
        (out_hbm, out_ref),
        (dx_hbm, dx_ref),
        (up_hbm, got_up),
        (down_hbm, got_down),
        (first_up_hbm, first_up),
        (first_down_hbm, first_down),
        (qkv_hbm, got_qkv),
        (o_hbm, got_out),
    )
    loads = [pltpu.make_async_copy(src, dst, sems.at[n]) for n, (src, dst) in enumerate(ins)]
    outs = ((out_rows, out_rows_hbm), (dx_rows, dx_rows_hbm))
    stores = [pltpu.make_async_copy(src, dst, sems.at[len(ins) + n]) for n, (src, dst) in enumerate(outs)]
    for load in loads:
        load.start()
    unpad = padding(micros, True)
    for n, (src, dst) in enumerate(((out_ref, out_rows), (dx_ref, dx_rows))):
        loads[n].wait()
        for t in range(TILES):
            tiles = [src[(m * TILES + t) * OWN : (m * TILES + t + 1) * OWN] for m in range(micros)]
            rows = dot(unpad, jnp.concatenate(tiles, axis=0)).astype(BF)
            dst[t * PATCHES : (t + 1) * PATCHES] = rows.reshape(PATCHES, micros, width)
        stores[n].start()

    for load in loads[2:]:
        load.wait()
    ff_piece = got_down.shape[3]
    for j in range(STEPS):
        ups = [(first_up[s] if j == 0 else got_up[s, j - 1]).astype(F32) for s in range(4)]
        downs = [(first_down[s] if j == 0 else got_down[s, j - 1]).astype(F32) for s in range(4)]
        vis, txt = sum(ups[:3]), ups[3]
        for d in range(2):
            at = (d * STEPS + j) * ff_piece
            dvup_ref[:, at : at + ff_piece] = vis[:, d * ff_piece : (d + 1) * ff_piece]
            dtup_ref[:, at : at + ff_piece] = txt[:, d * ff_piece : (d + 1) * ff_piece]
        at = j * ff_piece
        dvdown_ref[:, at : at + ff_piece] = sum(downs[:3])
        dtdown_ref[:, at : at + ff_piece] = downs[3]

    odd = lax.rem(lax.axis_index("stream"), 2) == 1
    for got, out in ((got_qkv, dqkv_ref), (got_out, dout_ref)):
        blocks = [sum(got[s, n].astype(F32) for s in range(4)) for n in range(got.shape[1])]
        whole = jnp.concatenate(blocks, axis=1)
        moved = pltpu.roll(whole, whole.shape[1] - BLOCK // 2, 1)
        out[...] = jnp.where(odd, moved, whole)[:, : out.shape[1]]
    for store in stores:
        store.wait()


def results(micros, out, dx, got_qkv, got_out, got_up, got_down, first_up, first_down):
    arrays = out, dx, got_qkv, got_out, got_up, got_down, first_up, first_down
    width = out.shape[1]
    shard = got_up.shape[2]
    ff = 8 * STEPS * got_down.shape[3]
    rows = jax.ShapeDtypeStruct((TILES * PATCHES, micros, width), BF)
    grads = [
        (shard, 3 * width // 4),
        (shard, width // 4),
        (shard, ff // 4),
        (width // 4, ff // 8),
        (shard, ff // 4),
        (width // 4, ff // 8),
    ]
    return pl.pallas_call(
        results_kernel,
        in_specs=[HBM] * 8,
        out_specs=[HBM] * 2 + [FULL] * 6,
        out_shape=[rows, rows] + [jax.ShapeDtypeStruct(shape, F32) for shape in grads],
        scratch_shapes=[
            pltpu.VMEM(array.shape, BF) for array in arrays
        ]
        + [pltpu.VMEM(rows.shape, BF)] * 2
        + [pltpu.SemaphoreType.DMA((10,))],
        compiler_params=pltpu.CompilerParams(vmem_limit_bytes=63 * 2**20),
        name="results",
    )(*arrays)


def pad_rows(block):
    micro, rows, width = block.shape
    thirds = block.reshape(micro, TILES, PATCHES, width)
    thirds = jnp.pad(thirds, ((0, 0), (0, 0), (0, OWN - PATCHES), (0, 0)))
    return thirds.reshape(micro, TILES * OWN, width)


def unpad_rows(block):
    micro, _, width = block.shape
    thirds = block.reshape(micro, TILES, OWN, width)[:, :, :PATCHES]
    return thirds.reshape(micro, TILES * PATCHES, width)


def plan(lengths, pairs, is_text, own_stream):
    micro, items = lengths.shape
    finish = jnp.cumsum(lengths, axis=1)
    starts = finish - lengths
    numbers = jnp.arange(items, dtype=jnp.int32)
    match = pairs[:, :, None] == numbers
    start = jnp.sum(jnp.where(match, starts[:, None, :], 0), axis=2).reshape(micro, 3, TILES)
    length = jnp.sum(jnp.where(match, lengths[:, None, :], 0), axis=2).reshape(micro, 3, TILES)
    paired = (pairs >= 0).reshape(micro, 3, TILES)
    rank = jnp.where(paired, jnp.cumsum(paired.astype(jnp.int32), axis=2) - 1, -1)
    takes = rank[:, :, :, None] == jnp.arange(2)
    slot_start = jnp.sum(jnp.where(takes, start[..., None], 0), axis=2)
    slot_length = jnp.sum(jnp.where(takes, length[..., None], 0), axis=2)
    step = jnp.arange(SLOT, dtype=jnp.int32)
    slot_rows = jnp.where(step < slot_length[..., None], slot_start[..., None] + step, -1)
    pad = jnp.arange(TILE - OWN, dtype=jnp.int32)
    next_rows = PATCHES * jnp.arange(1, TILES + 1, dtype=jnp.int32)[:, None] + pad
    next_rows = jnp.where((pad < SLOT) & (next_rows < TILES * PATCHES), next_rows, -1)
    next_rows = jnp.broadcast_to(next_rows, (micro, TILES, TILE - OWN))
    wanted = jnp.concatenate([slot_rows.reshape(micro, -1), next_rows.reshape(micro, -1)], axis=1)
    place = jnp.arange(TILES * OWN, dtype=jnp.int32)
    row_at = jnp.where(place % OWN < PATCHES, place // OWN * PATCHES + place % OWN, -2)
    picks = (wanted[:, :, None] == row_at).astype(BF)
    item_paired = jnp.any(match, axis=1)
    rows = jnp.arange(TILES * PATCHES + SLOT, dtype=jnp.int32)
    member = (rows[:, None] >= starts[:, None, :]) & (rows[:, None] < finish[:, None, :])
    code = jnp.where(item_paired, -1, numbers + items * (starts // PATCHES))
    row_code = jnp.sum(jnp.where(member, code[:, None, :] + 1, 0), axis=2) - 1
    tile = jnp.arange(TILES, dtype=jnp.int32)[:, None]
    own_code = row_code[:, : TILES * PATCHES].reshape(micro, TILES, PATCHES)
    next_code = jnp.stack(
        [row_code[:, PATCHES * (t + 1) : PATCHES * (t + 1) + SLOT] for t in range(TILES)], axis=1
    )

    def here(codes):
        return jnp.where((codes >= 0) & (codes // items == tile), codes, -1)

    def lay(own, extra):
        gap = jnp.full((micro, TILES, OWN - PATCHES), -1, jnp.int32)
        end = jnp.full((micro, TILES, TILE - OWN - SLOT), -1, jnp.int32)
        return jnp.concatenate([own, gap, extra, end], axis=2)

    text_ids = lay(here(own_code), here(next_code))
    own_length = lax.dynamic_index_in_dim(length, jnp.minimum(own_stream, 2), 1, keepdims=False)
    own_takes = lax.dynamic_index_in_dim(takes, jnp.minimum(own_stream, 2), 1, keepdims=False)
    image_ids = lay(
        jnp.zeros((micro, TILES, PATCHES), jnp.int32),
        jnp.where(step < own_length[..., None], 0, -1),
    )
    ids = jnp.where(is_text, text_ids, image_ids)
    own_takes = own_takes.astype(BF)
    same = (pad[:, None] == step).astype(BF)
    places = own_takes[:, :, None, :, None] * same[:, None, :]
    places = places.reshape(micro, TILES * (TILE - OWN), 2 * SLOT)
    return picks, places, own_takes, ids.reshape(micro * TILES, 1, TILE)


def plan_kernel(length_ref, pair_ref, *refs):
    vec_refs, (picks_ref, places_ref, ids_ref, vecs_ref, starts, codes) = refs[:8], refs[8:]
    for n, ref in enumerate(vec_refs):
        rows = ref.shape[0] // BLOCK
        vecs_ref[n * rows : (n + 1) * rows] = ref[...].astype(F32).reshape(rows, BLOCK)
    micros, items = length_ref.shape
    own_z = lax.axis_index("stream")
    is_text = own_z == 3
    block = jnp.minimum(own_z, 2)
    side = TILE - OWN
    place = lax.broadcasted_iota(jnp.int32, (1, TILES * OWN), 1)
    third = third_of(place, OWN)
    inside = place - OWN * third
    row_at = jnp.where(inside < PATCHES, PATCHES * third + inside, -2)
    lane = lax.broadcasted_iota(jnp.int32, (1, TILE), 1)
    far = lax.broadcasted_iota(jnp.int32, (6 * SLOT, 1), 0)
    near = lax.broadcasted_iota(jnp.int32, (TILES * side, 1), 0)
    near_tile = third_of(near, side)
    near_step = near - side * near_tile
    near_row = PATCHES * (near_tile + 1) + near_step
    near_row = jnp.where((near_step < SLOT) & (near_row < TILES * PATCHES), near_row, -1)
    slot_at = lax.broadcasted_iota(jnp.int32, (1, 2 * SLOT), 1)
    slot_of = (slot_at >= SLOT).astype(jnp.int32)
    slot_step = slot_at - SLOT * slot_of
    for m in range(micros):
        start = jnp.int32(0)
        for item in range(items):
            starts[m, item] = start
            codes[m, item] = item + items * third_of(start, PATCHES)
            start = start + length_ref[m, item]

        def pair_of(image):
            item = pair_ref[m, image]
            known = jnp.maximum(item, 0)
            paired = item >= 0
            return paired, starts[m, known], jnp.where(paired, length_ref[m, known], 0)

        wanted = jnp.full(far.shape, -1, jnp.int32)
        for s in range(3):
            rank = jnp.int32(0)
            for t in range(TILES):
                paired, start, length = pair_of(TILES * s + t)
                step = far - SLOT * (2 * s + rank)
                wanted = jnp.where((step >= 0) & (step < length), start + step, wanted)
                rank = rank + paired.astype(jnp.int32)
        picks_ref[m, 0 : 6 * SLOT] = (wanted == row_at).astype(F32).astype(BF)
        picks_ref[m, 6 * SLOT :] = (near_row == row_at).astype(F32).astype(BF)

        rank = jnp.int32(0)
        ranks = jnp.full(near.shape, -1, jnp.int32)
        lengths = []
        for t in range(TILES):
            paired, _, length = pair_of(TILES * block + t)
            lengths.append(length)
            ranks = jnp.where((near_tile == t) & paired, rank, ranks)
            rank = rank + paired.astype(jnp.int32)
        chosen = (near_step == slot_step) & (ranks == slot_of)
        places_ref[m] = chosen.astype(F32).astype(BF)

        for image in range(3 * TILES):

            @pl.when(pair_ref[m, image] >= 0)
            def _():
                codes[m, pair_ref[m, image]] = -1

        for t in range(TILES):
            beside = lane - OWN
            image_ids = jnp.where((lane < PATCHES) | ((beside >= 0) & (beside < lengths[t])), 0, -1)
            row = jnp.where(lane < PATCHES, PATCHES * t + lane, -1)
            row = jnp.where((beside >= 0) & (beside < SLOT), PATCHES * (t + 1) + beside, row)
            text_ids = jnp.full(lane.shape, -1, jnp.int32)
            for item in range(items):
                start, code = starts[m, item], codes[m, item]
                code = jnp.where(third_of(start, PATCHES) == t, code, -1)
                member = (row >= start) & (row < start + length_ref[m, item])
                text_ids = jnp.where(member, code, text_ids)
            ids_ref[m * TILES + t] = jnp.where(is_text, text_ids, image_ids)


def plan_rows(lengths, pairs, vectors):
    micros, items = lengths.shape
    smem = pl.BlockSpec(memory_space=pltpu.SMEM)
    return pl.pallas_call(
        plan_kernel,
        in_specs=[smem, smem] + [FULL] * 8,
        out_specs=[FULL] * 4,
        out_shape=[
            jax.ShapeDtypeStruct((micros, 6 * SLOT + TILES * (TILE - OWN), TILES * OWN), BF),
            jax.ShapeDtypeStruct((micros, TILES * (TILE - OWN), 2 * SLOT), BF),
            jax.ShapeDtypeStruct((micros * TILES, 1, TILE), jnp.int32),
            jax.ShapeDtypeStruct((8 * vectors[0].shape[0] // BLOCK, BLOCK), F32),
        ],
        scratch_shapes=[
            pltpu.SMEM((micros, items), jnp.int32),
            pltpu.SMEM((micros, items), jnp.int32),
        ],
        compiler_params=pltpu.CompilerParams(vmem_limit_bytes=63 * 2**20),
        name="plan_rows",
    )(lengths, pairs, *vectors)


def spread(padded, picks, own_takes, is_text):
    micro, _, width = padded.shape
    picked = lax.dot_general(
        picks, padded, (((2,), (1,)), ((0,), (0,))), preferred_element_type=F32
    ).astype(BF)
    near = picked[:, 6 * SLOT :].reshape(micro, TILES, TILE - OWN, width)[:, :, :SLOT]
    sent = picked[:, : 6 * SLOT].reshape(micro, 3, 2 * SLOT, width)
    far = sum(lax.ppermute(sent[:, s], "stream", [(3, s)]) for s in range(3))
    far = far.reshape(micro, 1, 2, SLOT, width) * own_takes[:, :, :, None, None]
    return jnp.where(is_text, near, far[:, :, 0] + far[:, :, 1])


def collect(extra, picks, own_takes, is_text):
    micro, _, _, width = extra.shape
    mine = extra[:, :, None] * own_takes[:, :, :, None, None]
    mine = (mine[:, 0] + mine[:, 1] + mine[:, 2]).reshape(micro, 2 * SLOT, width)
    parts = [lax.ppermute(mine, "stream", [(s, 3)]) for s in range(3)]
    extra = jnp.pad(extra, ((0, 0), (0, 0), (0, TILE - OWN - SLOT), (0, 0)))
    parts.append(extra.reshape(micro, TILES * (TILE - OWN), width))
    rows = jnp.concatenate(parts, axis=1)
    scale = jnp.where(is_text, 1.0, 0.0).astype(BF)
    return lax.dot_general(
        picks * scale, rows, (((1,), (1,)), ((0,), (0,))), preferred_element_type=F32
    ).astype(BF)


def reduce_all(vectors, dw_qkv, dw_out, dup, ddown):
    width = dw_qkv.shape[0]
    shard = width // lax.axis_size("dp")
    vectors = lax.psum(vectors, ("dp", "stream"))
    vectors = lax.dynamic_slice_in_dim(vectors, lax.axis_index("dp") * shard, shard, axis=1)

    def over_items(grad, dim):
        return lax.psum_scatter(grad, "dp", scatter_dimension=dim, tiled=True)

    def over_blocks(grad):
        return lax.psum_scatter(grad, "stream", scatter_dimension=1, tiled=True).astype(F32)

    qkv = over_blocks(over_items(dw_qkv, 0))
    out = over_blocks(over_items(dw_out, 0))
    dup = over_items(jnp.concatenate(list(dup), axis=1), 0)
    ddown = over_items(jnp.concatenate(list(ddown), axis=1), 1)
    up = dup.reshape(dup.shape[0], 4, -1).transpose(1, 0, 2)
    down = ddown.reshape(4, -1, ddown.shape[1])
    up = lax.all_to_all(up, "stream", 0, 0).astype(F32)
    down = lax.all_to_all(down, "stream", 0, 0).astype(F32)
    return (
        vectors,
        qkv,
        out,
        up[0] + up[1] + up[2],
        (down[0] + down[1] + down[2]).T,
        up[3],
        down[3].T,
    )


def shards(
    remote,
    tokens,
    text_lengths,
    pair_text,
    ln1_gain,
    ln1_bias,
    w_qkv,
    q_bias,
    v_bias,
    w_out,
    ln2_gain,
    ln2_bias,
    vis_up,
    vis_down,
    vis_bias,
    txt_up,
    txt_down,
    txt_bias,
    cotangent,
):
    micro = tokens.shape[0]
    width = tokens.shape[4]
    own_stream = lax.axis_index("stream")
    is_text = own_stream == 3
    vecs = [ln1_gain, ln1_bias, q_bias, v_bias, ln2_gain, ln2_bias, vis_bias, txt_bias]
    if remote:
        picks, places, ids, vecs = plan_rows(text_lengths[:, 0], pair_text[:, 0], vecs)
    else:
        vecs = jnp.concatenate(vecs).astype(F32).reshape(-1, BLOCK)
        picks, places, own_takes, ids = plan(
            text_lengths[:, 0], pair_text[:, 0], is_text, own_stream
        )

    def tiled(own, extra):
        own = own.reshape(micro, TILES, OWN, width)
        extra = jnp.pad(extra, ((0, 0), (0, 0), (0, TILE - OWN - SLOT), (0, 0)))
        return jnp.concatenate([own, extra], axis=2).reshape(micro * TILES, TILE, width)

    def parted(tiles):
        tiles = tiles.reshape(micro, TILES, TILE, width)
        return tiles[:, :, :OWN].reshape(micro, TILES * OWN, width), tiles[:, :, OWN : OWN + SLOT]

    if remote:
        x_tiles, qkv, probs, inverse, att_tiles, att, att_last = attend_rows(
            tokens[:, 0, 0].transpose(1, 0, 2), picks, places, ids, vecs, w_qkv
        )
    else:
        x = pad_rows(tokens[:, 0, 0])
        x_tiles = tiled(x, spread(x, picks, own_takes, is_text))
        qkv, att_tiles, probs, inverse = attend(x_tiles, ids, vecs, w_qkv)
        att_own, att_extra = parted(att_tiles)
        att = att_own + collect(att_extra, picks, own_takes, is_text)
        att = att.reshape(micro * TILES * OWN, width)
        att_last = jnp.zeros((2 * SLOT, width), BF)
    out, dmid, datt_tiles, dw_out, vec2, dup, ddown, *more = expert(
        remote,
        x_tiles,
        att,
        att_tiles,
        att_last,
        cotangent[:, 0, 0].transpose(1, 0, 2),
        w_out,
        vecs,
        picks,
        places,
        vis_up,
        vis_down,
        txt_up,
        txt_down,
    )
    if remote:
        dx, vectors, *shares = back(
            x_tiles,
            qkv,
            probs,
            att_tiles,
            inverse,
            datt_tiles,
            dmid,
            vecs,
            w_qkv,
            dw_out,
            dup,
            ddown,
            *more[:3],
            vec2,
            picks,
            places,
        )
        vectors = vectors[:, : width // 8]
        out, dx, g_qkv, g_out, g_vup, g_vdown, g_tup, g_tdown = results(
            micro, out, dx, *shares, *more[3:]
        )
        out, dx = out.transpose(1, 0, 2), dx.transpose(1, 0, 2)
        g_vdown, g_tdown = g_vdown.T, g_tdown.T
    else:
        datt = parted(datt_tiles)[0]
        datt_tiles = tiled(datt, spread(datt, picks, own_takes, is_text))
        dqkv = attend_back(qkv, probs, att_tiles, inverse, datt_tiles)
        dx_tiles, dw_qkv, vec1 = project_back(x_tiles, dqkv, vecs, w_qkv)
        dx_own, dx_extra = parted(dx_tiles)
        dx = (
            dmid.reshape(micro, TILES * OWN, width)
            + dx_own.astype(F32)
            + collect(dx_extra, picks, own_takes, is_text).astype(F32)
        )
        dx = unpad_rows(dx).astype(BF)
        out = unpad_rows(out.reshape(micro, TILES * OWN, width))
        text_scale = jnp.where(is_text, 1.0, 0.0)
        vectors = jnp.concatenate(
            [vec1[0:4], vec2[0:2], vec2[2:3] * (1.0 - text_scale), vec2[2:3] * text_scale], axis=0
        )
        vectors, g_qkv, g_out, g_vup, g_vdown, g_tup, g_tdown = reduce_all(
            vectors, dw_qkv, dw_out, dup, ddown
        )
    return (
        out.reshape(tokens.shape),
        dx.reshape(tokens.shape),
        vectors[0],
        vectors[1],
        g_qkv,
        vectors[2],
        vectors[3],
        g_out,
        vectors[4],
        vectors[5],
        g_vup,
        g_vdown,
        vectors[6],
        g_tup,
        g_tdown,
        vectors[7],
    )


def solution(mesh):
    rows = P(None, "dp", "stream", None, None)
    lists = P(None, "dp", None)
    vector, matrix = P("dp"), P("dp", "stream")
    in_specs = (rows, lists, lists) + (P(),) * 14 + (rows,)
    out_specs = (
        rows,
        rows,
        vector,
        vector,
        matrix,
        vector,
        vector,
        matrix,
        vector,
        vector,
        matrix,
        matrix,
        vector,
        matrix,
        matrix,
        vector,
    )
    remote = mesh.shape["dp"] == 8
    body = functools.partial(shards, remote)
    return jax.shard_map(body, mesh=mesh, in_specs=in_specs, out_specs=out_specs, check_vma=False)
```
